32 devices in a mesh: seq: 8 (over z, y), ch: 4 (over x, core).
Axes of the slice: x: 2, y: 2, z: 4, core: 2. Of those that a mesh axis runs over, the one named last changes fastest.
Arguments:
- projected: bfloat16 [2048, 3, 8192], P('seq', None, 'ch'), may hold values from -6 to 6
- short_taps: float32 [3, 7, 8192], P(None, None, 'ch'), may hold values from -2 to 2
- filter_taps: float32 [128, 8192], P('seq', 'ch'), may hold values from -1 to 1
- decay: float32 [8192], P('ch'), may hold values from 0.003 to 0.1
- cotangent: bfloat16 [2048, 8192], P('seq', 'ch'), may hold values from -18 to 18
Outputs:
- gated: bfloat16 [2048, 8192], P('seq', 'ch')
- grad_projected: bfloat16 [2048, 3, 8192], P('seq', None, 'ch')
- grad_short: float32 [3, 7, 8192], P(None, None, 'ch')
- grad_filter: float32 [128, 8192], P('seq', 'ch')
The draws below stay inside these ranges and needn't reach their ends.
All inputs are finite; a program needn't handle non-finite values.
Results may differ from the reference program's by a relative error of at most 0.005.
Values may be sent and summed in bfloat16 or wider, within the bound.
No kernel may reach another device: no remote copies, remote signals or barrier semaphores. Data moves between devices by JAX's collectives and lax.ppermute only.
A program may use at most 128 MiB of HBM per device.

```python
import math
import jax
import jax.numpy as jnp
from jax import lax

D = 8192
K = 128
FK = 7
TOKENS = 2048


def draw_projected(key, part):
    first, second = jax.random.split(key, 2)
    base = jnp.clip(jax.random.normal(first, (TOKENS, 3, D), jnp.float32), -4.5, 4.5)
    offset = jnp.clip(0.5 * jax.random.normal(second, (1, 3, D), jnp.float32), -1.5, 1.5)
    return (base + offset).astype(jnp.bfloat16)


def draw_cotangent(key, part):
    first = jax.random.fold_in(key, 0)
    third = jax.random.fold_in(key, 2)
    channel = jnp.arange(D, dtype=jnp.float32) / D
    ramp = jnp.power(3.0, channel)[None, :]
    base = jnp.clip(jax.random.normal(first, (TOKENS, D), jnp.float32), -4.0, 4.0)
    offset = jnp.clip(0.5 * jax.random.normal(third, (1, D), jnp.float32), -1.5, 1.5)
    return ((base + offset) * ramp).astype(jnp.bfloat16)


def levels(rng, dims, shards, least, top_value):
    def one(axis_at, blocks):
        steps = jax.random.uniform(jax.random.fold_in(jax.random.fold_in(rng, 6), axis_at), (blocks,), jnp.float32, least / len(shards), top_value / len(shards))
        return jnp.repeat(jnp.exp(steps), dims[axis_at] // blocks).reshape((-1,) + (1,) * (len(dims) - axis_at - 1))

    factor_of = one(*shards[0])
    for cut in shards[1:]:
        factor_of = factor_of * one(*cut)
    return factor_of


def normal_values(own_key, dims, spread, most, cuts=(), kind=jnp.bfloat16):
    values = spread * jax.random.normal(own_key, dims, jnp.float32)
    if cuts:
        values = values * levels(own_key, dims, cuts, -0.22, 0.18)
    return jnp.clip(values, -most, most).astype(kind)


def setup_inputs(seed: int = 0) -> dict:
    key_list = jax.random.split(jax.random.key(seed), 6)
    projected = draw_projected(jax.random.fold_in(key_list[5], 71), 0)
    short_taps = normal_values(key_list[1], (3, FK, D), FK ** -0.5, 2.0, ((2, 4),), jnp.float32)
    filter_taps = normal_values(key_list[2], (K, D), (K // 3) ** -0.5, 1.0, ((0, 8), (1, 4)), jnp.float32)
    decay = jnp.clip(jnp.exp(math.log(0.1) - 3.506558 * jax.random.uniform(key_list[3], (D,), jnp.float32) ** levels(key_list[3], (D,), ((0, 4),), -0.2, 0.2)), 0.003, 0.1)
    cotangent = draw_cotangent(jax.random.fold_in(key_list[5], 71), 0)
    return dict(projected=projected, short_taps=short_taps, filter_taps=filter_taps, decay=decay, cotangent=cotangent)


def causal_short(proj, short):
    length = proj.shape[0]
    padded = jnp.concatenate([jnp.zeros((FK - 1,) + proj.shape[1:], proj.dtype), proj], axis=0)
    total = jnp.zeros_like(proj)
    for lag in range(FK):
        total = total + short[:, lag, :] * padded[FK - 1 - lag:FK - 1 - lag + length]
    return total

def long_conv(mixed, kernel):
    length = mixed.shape[0]
    extent = 2 * length
    spectrum = jnp.fft.rfft(mixed, n=extent, axis=0) * jnp.fft.rfft(kernel, n=extent, axis=0)
    return jnp.fft.irfft(spectrum, n=extent, axis=0)[:length]

def forward(proj, short, filt, decay):
    feat = causal_short(proj, short)
    lags = jnp.arange(K, dtype=jnp.float32)
    kernel = filt * jnp.exp(-decay[None, :] * lags[:, None])
    mixed = feat[:, 1, :] * feat[:, 2, :]
    return feat[:, 0, :] * long_conv(mixed, kernel)

def one_block(pieces):
    proj, short, filt, decay, cot = pieces

    def partial_forward(proj_in, short_in, filt_in):
        return forward(proj_in, short_in, filt_in, decay)
    output, pullback = jax.vjp(partial_forward, proj.astype(jnp.float32), short, filt)
    grads = pullback(cot.astype(jnp.float32))
    return (output.astype(jnp.bfloat16), grads[0].astype(jnp.bfloat16), grads[1], grads[2])

def reference(projected, short_taps, filter_taps, decay, cotangent):
    width = 512 if D % 512 == 0 else D
    blocks = D // width
    length = projected.shape[0]
    proj_b = jnp.moveaxis(projected.reshape(length, 3, blocks, width), 2, 0)
    short_b = jnp.moveaxis(short_taps.reshape(3, FK, blocks, width), 2, 0)
    filt_b = jnp.moveaxis(filter_taps.reshape(K, blocks, width), 1, 0)
    decay_b = decay.reshape(blocks, width)
    cot_b = jnp.moveaxis(cotangent.reshape(length, blocks, width), 1, 0)
    out_b, gproj_b, gshort_b, gfilt_b = lax.map(one_block, (proj_b, short_b, filt_b, decay_b, cot_b))
    gated = jnp.moveaxis(out_b, 0, 1).reshape(length, D)
    grad_projected = jnp.moveaxis(gproj_b, 0, 2).reshape(length, 3, D)
    short_raw = jnp.moveaxis(gshort_b, 0, 2).reshape(3, FK, D)
    filter_raw = jnp.moveaxis(gfilt_b, 0, 1).reshape(K, D)
    total = jnp.sum(filter_raw * filter_raw) + jnp.sum(short_raw * short_raw)
    limit = math.sqrt(K * D + 3 * FK * D)
    scale = jnp.minimum(1.0, limit / jnp.sqrt(total))
    return (gated, grad_projected, scale * short_raw, scale * filter_raw)
```

```python
import functools
import math

import jax
import jax.numpy as jnp
import ml_dtypes
import numpy as np
from jax import lax
from jax.experimental import pallas as pl
from jax.experimental.pallas import tpu as pltpu
from jax.sharding import PartitionSpec as P


FK = 7
BF16 = jnp.bfloat16
F32 = jnp.float32
HALO = 160


def from_behind(value, axis, by):
    count = lax.axis_size(axis)
    pairs = [(i, i + by) for i in range(count) if 0 <= i + by < count]
    return lax.ppermute(value, axis, pairs)


def interleaved(span, first=0, low=0):
    return np.array([first + s * span + r for r in range(low, span) for s in range(8)])


def pick(positions, count):
    out = np.zeros((len(positions), count), np.float32)
    for row, at in enumerate(positions):
        if 0 <= at < count:
            out[row, at] = 1.0
    return out.astype(ml_dtypes.bfloat16)


def halves(matrix):
    high = matrix.astype(np.float32).astype(ml_dtypes.bfloat16)
    low = (matrix - high.astype(np.float64)).astype(np.float32).astype(ml_dtypes.bfloat16)
    return np.stack([high, low])


def analysis(positions, size, pad=0):
    freq = np.arange(size // 2)[:, None]
    angle = np.pi * (((2 * freq + 1) * np.asarray(positions)[None, :]) % (2 * size)) / size
    matrix = np.concatenate([np.cos(angle), -np.sin(angle)], axis=0)
    return halves(np.pad(matrix, ((0, 0), (0, pad))))


def synthesis(positions, size):
    freq = np.arange(size // 2)[None, :]
    angle = np.pi * (((2 * freq + 1) * np.asarray(positions)[:, None]) % (2 * size)) / size
    return halves(np.concatenate([np.cos(angle), -np.sin(angle)], axis=1) * (2.0 / size))


def mm(a, b):
    return jnp.dot(a, b, preferred_element_type=F32)


def split(value):
    high = value.astype(BF16)
    return high, (value - high.astype(F32)).astype(BF16)


def product(matrix, value):
    high, low = split(value)
    return mm(matrix[0], high) + (mm(matrix[1], high) + mm(matrix[0], low))


def edges_kernel(proj, cot, short, p_tail, p_head, forward, backward):
    length, width = cot.shape
    tail, head = p_tail.shape[0] // 8 - (FK - 1), p_head.shape[0] // 8 - (FK - 1)

    def conv(x, taps, count):
        x = x.reshape(-1, 8, width)
        total = taps[0:1] * x[FK - 1 : FK - 1 + count]
        for lag in range(1, FK):
            total = total + taps[lag : lag + 1] * x[FK - 1 - lag : FK - 1 - lag + count]
        return total

    mixed = conv(mm(p_tail[...], proj[1]), short[1], tail) * conv(mm(p_tail[...], proj[2]), short[2], tail)
    ends = [proj[i, length - 16 :, :].astype(F32)[8:] for i in range(3)]
    forward[...] = jnp.concatenate(
        [mixed.reshape(tail * 8, width)] + ends + [jnp.zeros((8, width), F32)], axis=0
    ).astype(BF16)
    gate = conv(mm(p_head[...], proj[0]), short[0], head).reshape(head * 8, width)
    grad = gate * mm(p_head[(FK - 1) * 8 :, :], cot[...])
    starts = [ref[:16, :].astype(F32)[:8] for ref in (cot, proj.at[1], proj.at[2])]
    backward[...] = jnp.concatenate([grad] + starts, axis=0).astype(BF16)


def main_kernel(
    proj, cot, prev, later, short, taps, decay,
    e_own, e_prev, e_next, e_taps, s_own, s_lags, p_in, p_out,
    gated, grad_proj, filter_part, short_part,
    px, feat, grad, cots,
):
    length, width = cot.shape
    span = length // 8
    edge = FK - 1
    lanes = [slice(at, at + 128) for at in range(0, width, 128)]
    row8 = lax.broadcasted_iota(jnp.int32, (8, width), 0)

    before = prev[...].astype(F32)
    after = later[...].astype(F32)
    prev8 = [before[128 + 8 * i : 136 + 8 * i] for i in range(3)]
    cot_next = after[136:144]
    next8 = [None, after[144:152], after[152:160]]

    for i in range(3):
        x = mm(p_in[...], proj[i]).reshape(span + edge, 8, width)
        px[i, edge:] = x[edge:]
        for k in range(1, FK):
            px[i, edge - k] = jnp.where(row8 == 0, pltpu.roll(prev8[i], k, 0), x[edge - k])
    cots[...] = mm(p_in[edge * 8 :, :], cot[...]).reshape(span, 8, width)

    step = 8
    for i in range(3):
        for lane in lanes:
            weights = [jnp.broadcast_to(short[i, lag : lag + 1, lane], (8, 128)) for lag in range(FK)]
            for r in range(0, span, step):
                total = weights[0] * px[i, r + edge : r + edge + step, :, lane]
                for lag in range(1, FK):
                    total = total + weights[lag] * px[i, r + edge - lag : r + edge - lag + step, :, lane]
                feat[i, r : r + step, :, lane] = total

    def conv8(last, first, weights, whole):
        total = weights[0:1] * first if whole else jnp.zeros((8, width), F32)
        for lag in range(1, FK):
            rolled = pltpu.roll(first, lag, 0) if whole else 0.0
            total = total + weights[lag : lag + 1] * jnp.where(row8 < lag, pltpu.roll(last, lag, 0), rolled)
        return total

    ends = [proj[i, length - 16 :, :].astype(F32)[8:] for i in range(3)]
    feat_next = [None] + [conv8(ends[i], next8[i], short[i], True) for i in (1, 2)]
    mixed_next = feat_next[1] * feat_next[2]
    grad_next = after[:136]
    fix = cot_next * conv8(ends[0], None, short[0], False)
    rows = [grad_next[8 * r : 8 * r + 8] for r in range(17)]
    for r in range(edge):
        rows[r] = rows[r] + jnp.where(row8 == 0, pltpu.roll(fix, (8 - r) % 8, 0), 0.0)
    grad_next = jnp.concatenate(rows + [jnp.zeros((8, width), F32)], axis=0).astype(BF16)
    mixed_edge = jnp.concatenate([before[:128], mixed_next, jnp.zeros((8, width), F32)], axis=0).astype(BF16)

    lags = lax.broadcasted_iota(jnp.int32, (taps.shape[0], width), 0).astype(F32)
    falloff = jnp.exp(-decay[...] * lags)
    k_spec = product(e_taps, taps[...].astype(F32) * falloff)

    flat = lambda value: value.reshape(length, width)
    m_spec = product(e_own, flat(feat[1] * feat[2])) + (mm(e_prev[0], mixed_edge) + mm(e_prev[1], mixed_edge))
    g_own = product(e_own, flat(cots[...] * feat[0]))
    g_spec = g_own + (mm(e_next[0], grad_next) + mm(e_next[1], grad_next))

    half = k_spec.shape[0] // 2
    parts = lambda value: (value[:half], value[half:])
    (kr, ki), (mr, mi), (gr, gi), (hr, hi) = parts(k_spec), parts(m_spec), parts(g_spec), parts(g_own)
    lag_sums = product(s_lags, jnp.concatenate([hr * mr + hi * mi, hi * mr - hr * mi], axis=0))
    filter_part[...] = (lag_sums * falloff).astype(BF16)
    filtered = product(s_own, jnp.concatenate([mr * kr - mi * ki, mr * ki + mi * kr], axis=0))
    grad_mixed = product(s_own, jnp.concatenate([gr * kr + gi * ki, gi * kr - gr * ki], axis=0))

    own = filtered[:length].reshape(span, 8, width)
    gated[...] = mm(p_out[...], flat(feat[0] * own).astype(BF16)).astype(BF16)
    back = grad_mixed[:length].reshape(span, 8, width)
    grad[0, :span] = cots[...] * own
    grad[1, :span] = back * feat[2]
    grad[2, :span] = back * feat[1]
    back_next = grad_mixed[length:]
    edge_next = [cot_next * filtered[length:], back_next * feat_next[2], back_next * feat_next[1]]
    for i in range(3):
        for k in range(edge):
            grad[i, span + k] = jnp.where(row8 == 7, pltpu.roll(edge_next[i], 7 - k, 0), pltpu.roll(grad[i, k], 7, 0))

    for i in range(3):
        columns = []
        for lane in lanes:
            weights = [jnp.broadcast_to(short[i, lag : lag + 1, lane], (8, 128)) for lag in range(FK)]
            sums = [jnp.zeros((8, 128), F32)] * FK
            chunks = []
            for r in range(0, span, step):
                total = jnp.zeros((step, 8, 128), F32)
                here = px[i, r + edge : r + edge + step, :, lane]
                for lag in range(FK):
                    value = grad[i, r + lag : r + lag + step, :, lane]
                    total = total + weights[lag] * value
                    sums[lag] = sums[lag] + jnp.sum(here * value, axis=0)
                chunks.append(total)
            columns.append(jnp.concatenate(chunks, axis=0))
            for lag in range(FK):
                short_part[i, lag : lag + 1, lane] = jnp.sum(sums[lag], axis=0, keepdims=True)
        short_part[i, FK:, :] = jnp.zeros((1, width), F32)
        result = flat(jnp.concatenate(columns, axis=2)).astype(BF16)
        grad_proj[i] = mm(p_out[...], result).astype(BF16)


def whole(array):
    return pl.BlockSpec(array.shape, lambda c: (0,) * array.ndim)


def columns(rows, width):
    lead = (0,) * len(rows)
    return pl.BlockSpec(tuple(rows) + (width,), lambda c: lead + (c,))


def edges(proj, cot, short, width):
    length, channels = cot.shape
    p_tail = jnp.asarray(pick(interleaved(16, length - 128, 1 - FK), length))
    p_head = jnp.asarray(pick(interleaved(17, 0, 1 - FK), length))
    return pl.pallas_call(
        edges_kernel,
        grid=(channels // width,),
        in_specs=[
            columns((3, length), width), columns((length,), width), columns((3, FK), width),
            whole(p_tail), whole(p_head),
        ],
        out_specs=[columns((HALO,), width)] * 2,
        out_shape=[jax.ShapeDtypeStruct((HALO, channels), BF16)] * 2,
        compiler_params=pltpu.CompilerParams(vmem_limit_bytes=48 << 20),
        name="edges",
    )(proj, cot, short, p_tail, p_head)


def main(proj, cot, prev, later, short, taps, decay, width):
    length, channels = cot.shape
    count = taps.shape[0]
    size = 2 * length
    own = interleaved(length // 8)
    constants = [
        analysis(own, size),
        analysis(np.concatenate([interleaved(16, -128), length + np.arange(8)]), size, 8),
        analysis(interleaved(17, length), size, 8),
        analysis(np.arange(count), size),
        synthesis(np.concatenate([own, length + np.arange(8)]), size),
        synthesis(np.arange(count), size),
        pick(interleaved(length // 8, 0, 1 - FK), length),
        pick(own, length).T,
    ]
    constants = [jnp.asarray(constant) for constant in constants]
    span = length // 8
    return pl.pallas_call(
        main_kernel,
        grid=(channels // width,),
        in_specs=[
            columns((3, length), width), columns((length,), width), columns((HALO,), width),
            columns((HALO,), width), columns((3, FK), width), columns((count,), width), columns((1,), width),
        ] + [whole(constant) for constant in constants],
        out_specs=[
            columns((length,), width), columns((3, length), width), columns((count,), width),
            columns((3, FK + 1), width),
        ],
        out_shape=[
            jax.ShapeDtypeStruct((length, channels), BF16),
            jax.ShapeDtypeStruct((3, length, channels), BF16),
            jax.ShapeDtypeStruct((count, channels), BF16),
            jax.ShapeDtypeStruct((3, FK + 1, channels), F32),
        ],
        scratch_shapes=[
            pltpu.VMEM((3, span + FK - 1, 8, width), F32),
            pltpu.VMEM((3, span, 8, width), F32),
            pltpu.VMEM((3, span + FK - 1, 8, width), F32),
            pltpu.VMEM((span, 8, width), F32),
        ],
        compiler_params=pltpu.CompilerParams(vmem_limit_bytes=56 << 20),
        name="operator",
    )(proj, cot, prev, later, short, taps, decay, *constants)


def everyone(value, axis, count):
    return lax.all_to_all(jnp.broadcast_to(value[None], (count,) + value.shape), axis, 0, 0)


def shards(projected, short_taps, filter_taps, decay, cotangent):
    length, _, channels = projected.shape
    ranks = lax.axis_size("seq")
    rows = filter_taps.shape[0]
    width = min(256, channels)
    proj = jnp.transpose(projected, (1, 0, 2))
    forward, backward = edges(proj, cotangent, short_taps, width)
    prev = from_behind(forward, "seq", 1)
    later = from_behind(backward, "seq", -1)
    taps = everyone(filter_taps.astype(BF16), "seq", ranks).reshape(rows * ranks, channels)
    gated, grad_proj, filter_part, short_part = main(
        proj, cotangent, prev, later, short_taps, taps, decay[None], width
    )
    filter_all = lax.all_to_all(filter_part.reshape(ranks, rows, channels), "seq", 0, 0)
    filter_raw = jnp.sum(filter_all.astype(F32), axis=0)
    share = channels // ranks
    short_all = jnp.transpose(short_part.reshape(3 * (FK + 1), ranks, share), (1, 0, 2))
    short_raw = jnp.sum(lax.all_to_all(short_all, "seq", 0, 0), axis=0)
    squares = jnp.sum(filter_raw * filter_raw) + jnp.sum(short_raw * short_raw)
    total = jnp.sum(everyone(jnp.full((8, 128), squares), ("seq", "ch"), ranks * lax.axis_size("ch"))[:, 0, 0])
    short_sum = jnp.transpose(everyone(short_raw, "seq", ranks), (1, 0, 2)).reshape(3, FK + 1, channels)[:, :FK]
    entries = (rows * ranks + 3 * FK) * channels * lax.axis_size("ch")
    scale = jnp.minimum(1.0, math.sqrt(entries) / jnp.sqrt(total))
    return (gated, jnp.transpose(grad_proj, (1, 0, 2)), scale * short_sum, scale * filter_raw)


def solution(mesh):
    placed = (P("seq", None, "ch"), P(None, None, "ch"), P("seq", "ch"), P("ch"), P("seq", "ch"))
    return jax.shard_map(
        shards,
        mesh=mesh,
        in_specs=placed,
        out_specs=(P("seq", "ch"), P("seq", None, "ch"), P(None, None, "ch"), P("seq", "ch")),
        check_vma=False,
    )
```

```python
import functools
import math

import jax
import jax.numpy as jnp
import ml_dtypes
import numpy as np
from jax import lax
from jax.experimental import pallas as pl
from jax.experimental.pallas import tpu as pltpu
from jax.sharding import PartitionSpec as P


FK = 7
BF16 = jnp.bfloat16
F32 = jnp.float32
CHUNKS = 4


def from_behind(value, axis, by):
    count = lax.axis_size(axis)
    pairs = [(i, i + by) for i in range(count) if 0 <= i + by < count]
    return lax.ppermute(value, axis, pairs)


def interleaved(span, first=0, low=0):
    return np.array([first + s * span + r for r in range(low, span) for s in range(8)])


def pick(positions, count):
    out = np.zeros((len(positions), count), np.float32)
    for row, at in enumerate(positions):
        if 0 <= at < count:
            out[row, at] = 1.0
    return out.astype(ml_dtypes.bfloat16)


def halves(matrix):
    high = matrix.astype(np.float32).astype(ml_dtypes.bfloat16)
    low = (matrix - high.astype(np.float64)).astype(np.float32).astype(ml_dtypes.bfloat16)
    return np.stack([high, low])


def analysis(positions, size, pad=0):
    freq = np.arange(size // 2)[:, None]
    angle = np.pi * (((2 * freq + 1) * np.asarray(positions)[None, :]) % (2 * size)) / size
    matrix = np.concatenate([np.cos(angle), -np.sin(angle)], axis=0)
    return halves(np.pad(matrix, ((0, 0), (0, pad))))


def synthesis(positions, size):
    freq = np.arange(size // 2)[None, :]
    angle = np.pi * (((2 * freq + 1) * np.asarray(positions)[:, None]) % (2 * size)) / size
    return halves(np.concatenate([np.cos(angle), -np.sin(angle)], axis=1) * (2.0 / size))


def mm(a, b):
    return jnp.dot(a, b, preferred_element_type=F32)


def edges_kernel(proj, cot, short, p_tail, p_head, *refs):
    forward, backward = refs[-2:]
    length, width = cot.shape
    tail, head = p_tail.shape[0] // 8 - (FK - 1), p_head.shape[0] // 8 - (FK - 1)

    def conv(x, taps, count):
        x = x.reshape(-1, 8, width)
        total = taps[0:1] * x[FK - 1 : FK - 1 + count]
        for lag in range(1, FK):
            total = total + taps[lag : lag + 1] * x[FK - 1 - lag : FK - 1 - lag + count]
        return total

    mixed = conv(mm(p_tail[...], proj[1]), short[1], tail) * conv(mm(p_tail[...], proj[2]), short[2], tail)
    ends = [proj[i, length - 16 :, :].astype(F32)[8:] for i in range(3)]
    forward[...] = jnp.concatenate([mixed.reshape(tail * 8, width)] + ends, axis=0).astype(BF16)
    gate = conv(mm(p_head[...], proj[0]), short[0], head).reshape(head * 8, width)
    grad = gate * mm(p_head[(FK - 1) * 8 :, :], cot[...])
    starts = [ref[:16, :].astype(F32)[:8] for ref in (cot, proj.at[1], proj.at[2])]
    backward[...] = jnp.concatenate([grad] + starts, axis=0).astype(BF16)
    if len(refs) > 2:
        taps, spread = refs[:2]
        spread[...] = jnp.broadcast_to(taps[...].astype(BF16)[None], spread.shape)


def main_kernel(
    proj, cot, prev, later, short, taps, decay,
    e_own, e_prev, e_next, e_taps, s_own, s_lags, p_in, p_out, *refs,
):
    gated, grad_proj, sums_out, px, feat, grad, cots = refs[-7:]
    length, width = cot.shape
    span = length // 8
    edge = FK - 1
    lanes = [slice(at, at + 128) for at in range(0, width, 128)]
    row8 = lax.broadcasted_iota(jnp.int32, (8, width), 0)

    before = prev[...].astype(F32)
    after = later[...].astype(F32)
    prev8 = [before[128 + 8 * i : 136 + 8 * i] for i in range(3)]
    cot_next = after[136:144]
    next8 = [None, after[144:152], after[152:160]]

    lags = lax.broadcasted_iota(jnp.int32, (taps.shape[0], width), 0).astype(F32)
    falloff = jnp.exp(-decay[...] * lags)
    kernel = taps[...].astype(F32) * falloff
    high = kernel.astype(BF16)
    low = (kernel - high.astype(F32)).astype(BF16)
    k_spec = mm(e_taps[...], jnp.concatenate([high, high, low], axis=0))

    for i in range(3):
        x = mm(p_in[...], proj[i]).reshape(span + edge, 8, width)
        px[i, edge:] = x[edge:]
        for k in range(1, FK):
            px[i, edge - k] = jnp.where(row8 == 0, pltpu.roll(prev8[i], k, 0), x[edge - k])
    cots[...] = mm(p_in[edge * 8 :, :], cot[...]).reshape(span, 8, width)

    step = 8
    for i in range(3):
        for lane in lanes:
            weights = [jnp.broadcast_to(short[i, lag : lag + 1, lane], (8, 128)) for lag in range(FK)]
            for r in range(0, span, step):
                total = weights[0] * px[i, r + edge : r + edge + step, :, lane]
                for lag in range(1, FK):
                    total = total + weights[lag] * px[i, r + edge - lag : r + edge - lag + step, :, lane]
                feat[i, r : r + step, :, lane] = total

    def conv8(last, first, weights, whole):
        total = weights[0:1] * first if whole else jnp.zeros((8, width), F32)
        for lag in range(1, FK):
            rolled = pltpu.roll(first, lag, 0) if whole else 0.0
            total = total + weights[lag : lag + 1] * jnp.where(row8 < lag, pltpu.roll(last, lag, 0), rolled)
        return total

    ends = [proj[i, length - 16 :, :].astype(F32)[8:] for i in range(3)]
    feat_next = [None] + [conv8(ends[i], next8[i], short[i], True) for i in (1, 2)]
    mixed_next = feat_next[1] * feat_next[2]
    grad_next = after[:136]
    fix = cot_next * conv8(ends[0], None, short[0], False)
    rows = [grad_next[8 * r : 8 * r + 8] for r in range(17)]
    for r in range(edge):
        rows[r] = rows[r] + jnp.where(row8 == 0, pltpu.roll(fix, (8 - r) % 8, 0), 0.0)
    grad_next = jnp.concatenate(rows + [jnp.zeros((8, width), F32)], axis=0).astype(BF16)
    mixed_edge = jnp.concatenate([before[:128], mixed_next, jnp.zeros((8, width), F32)], axis=0).astype(BF16)

    flat = lambda value: value.reshape(length, width)
    mixed = flat(feat[1] * feat[2]).astype(BF16)
    grad_own = flat(cots[...] * feat[0]).astype(BF16)
    m_spec = mm(e_own[...], jnp.concatenate([mixed, mixed], axis=0)) + mm(e_prev[...], mixed_edge)
    g_own = mm(e_own[...], jnp.concatenate([grad_own, grad_own], axis=0))
    g_spec = g_own + mm(e_next[...], grad_next)

    half = k_spec.shape[0] // 2
    parts = lambda value: (value[:half], value[half:])
    (kr, ki), (mr, mi), (gr, gi), (hr, hi) = parts(k_spec), parts(m_spec), parts(g_spec), parts(g_own)

    def back_to(matrix, real, imaginary):
        spectrum = jnp.concatenate([real, imaginary], axis=0).astype(BF16)
        return mm(matrix[...], jnp.concatenate([spectrum, spectrum], axis=0))

    filtered = back_to(s_own, mr * kr - mi * ki, mr * ki + mi * kr)
    grad_mixed = back_to(s_own, gr * kr + gi * ki, gi * kr - gr * ki)
    filter_sums = back_to(s_lags, hr * mr + hi * mi, hi * mr - hr * mi) * falloff

    own = filtered[:length].reshape(span, 8, width)
    gated[...] = mm(p_out[...], flat(feat[0] * own).astype(BF16)).astype(BF16)
    back = grad_mixed[:length].reshape(span, 8, width)
    grad[0, :span] = cots[...] * own
    grad[1, :span] = back * feat[2]
    grad[2, :span] = back * feat[1]
    back_next = grad_mixed[length:]
    edge_next = [cot_next * filtered[length:], back_next * feat_next[2], back_next * feat_next[1]]
    for i in range(3):
        for k in range(edge):
            grad[i, span + k] = jnp.where(row8 == 7, pltpu.roll(edge_next[i], 7 - k, 0), pltpu.roll(grad[i, k], 7, 0))

    short_rows = []
    for i in range(3):
        columns, rows = [], [[] for _ in range(FK)]
        for lane in lanes:
            weights = [jnp.broadcast_to(short[i, lag : lag + 1, lane], (8, 128)) for lag in range(FK)]
            sums = [jnp.zeros((8, 128), F32)] * FK
            chunks = []
            for r in range(0, span, step):
                total = jnp.zeros((step, 8, 128), F32)
                here = px[i, r + edge : r + edge + step, :, lane]
                for lag in range(FK):
                    value = grad[i, r + lag : r + lag + step, :, lane]
                    total = total + weights[lag] * value
                    sums[lag] = sums[lag] + jnp.sum(here * value, axis=0)
                chunks.append(total)
            columns.append(jnp.concatenate(chunks, axis=0))
            for lag in range(FK):
                rows[lag].append(jnp.sum(sums[lag], axis=0, keepdims=True))
        short_rows += [jnp.concatenate(row, axis=1) for row in rows] + [jnp.zeros((1, width), F32)]
        result = flat(jnp.concatenate(columns, axis=2)).astype(BF16)
        grad_proj[i] = mm(p_out[...], result).astype(BF16)

    ranks, slots, _ = sums_out.shape
    per, each = filter_sums.shape[0] // ranks, -(-len(short_rows) // ranks)
    short_rows += [jnp.zeros((1, width), F32)] * (ranks * each - len(short_rows))
    empty = [jnp.zeros((slots - per - each, width), F32)]
    blocks = []
    for rank in range(ranks):
        blocks += [filter_sums[rank * per : rank * per + per]] + short_rows[rank * each : rank * each + each] + empty
    sums_out[...] = jnp.concatenate(blocks, axis=0).reshape(ranks, slots, width).astype(BF16)


def resident(array):
    return pl.BlockSpec(memory_space=pltpu.VMEM)


def columns(rows, width, first=0):
    lead = (0,) * len(rows)
    return pl.BlockSpec(tuple(rows) + (width,), lambda c: lead + (first + c,))


def edges(proj, cot, short, width, first, blocks, taps=None, ranks=None):
    length = cot.shape[0]
    constants = [
        jnp.asarray(pick(interleaved(16, length - 128, 1 - FK), length)),
        jnp.asarray(pick(interleaved(17, 0, 1 - FK), length)),
    ]
    in_specs = [
        columns((3, length), width, first), columns((length,), width, first), columns((3, FK), width, first),
    ] + [resident(constant) for constant in constants]
    out_specs = [columns((152,), width), columns((160,), width)]
    out_shape = [jax.ShapeDtypeStruct((rows, blocks * width), BF16) for rows in (152, 160)]
    operands = [proj, cot, short] + constants
    if taps is not None:
        rows, channels = taps.shape
        in_specs.append(columns((rows,), channels // blocks))
        operands.append(taps)
        out_specs.insert(0, columns((ranks, rows), channels // blocks))
        out_shape.insert(0, pltpu.HBM((ranks, rows, channels), BF16))
    return pl.pallas_call(
        edges_kernel,
        grid=(blocks,),
        in_specs=in_specs,
        out_specs=out_specs,
        out_shape=out_shape,
        compiler_params=pltpu.CompilerParams(vmem_limit_bytes=32 << 20),
        cost_estimate=pl.CostEstimate(flops=0, bytes_accessed=blocks * width * 10000, transcendentals=0),
        name="edges",
    )(*operands)


def main(proj, cot, prev, later, short, taps, decay, width, first, blocks, ranks, slots, group, at, held):
    length, channels = cot.shape
    count = taps.shape[0]
    size = 2 * length
    span = length // 8
    own = interleaved(span)
    high, low = analysis(own, size)
    k_high, k_low = analysis(np.arange(count), size)
    constants = [
        np.concatenate([high, low], axis=1),
        analysis(np.concatenate([interleaved(16, -128), length + np.arange(8)]), size, 8)[0],
        analysis(interleaved(17, length), size, 8)[0],
        np.concatenate([k_high, k_low, k_high], axis=1),
        np.concatenate(list(synthesis(np.concatenate([own, length + np.arange(8)]), size)), axis=1),
        np.concatenate(list(synthesis(np.arange(count), size)), axis=1),
        pick(interleaved(span, 0, 1 - FK), length),
        pick(own, length).T,
    ]
    constants = [jnp.asarray(constant) for constant in constants]
    operands = [proj, cot, prev, later, short, taps, decay] + constants
    aliases = {}
    for index, value in enumerate(held):
        if value is not None:
            aliases[len(operands)] = index
            operands.append(value)
    return pl.pallas_call(
        main_kernel,
        grid=(blocks,),
        in_specs=[
            columns((3, length), width, first), columns((length,), width, first), columns((prev.shape[0],), width),
            columns((later.shape[0],), width), columns((3, FK), width, first), columns((count,), width, first),
            columns((1,), width, first),
        ] + [resident(constant) for constant in constants] + [pl.BlockSpec(memory_space=pl.ANY)] * len(aliases),
        out_specs=[
            columns((length,), width, first), columns((3, length), width, first), columns((ranks, slots), width, at),
        ],
        out_shape=[
            jax.ShapeDtypeStruct((length, channels), BF16),
            jax.ShapeDtypeStruct((3, length, channels), BF16),
            pltpu.HBM((ranks, slots, group), BF16),
        ],
        scratch_shapes=[
            pltpu.VMEM((3, span + FK - 1, 8, width), F32),
            pltpu.VMEM((3, span, 8, width), F32),
            pltpu.VMEM((3, span + FK - 1, 8, width), F32),
            pltpu.VMEM((span, 8, width), F32),
        ],
        input_output_aliases=aliases,
        compiler_params=pltpu.CompilerParams(vmem_limit_bytes=40 << 20),
        cost_estimate=pl.CostEstimate(flops=blocks * 4 * 10**9, bytes_accessed=blocks * 2 * 10**6, transcendentals=0),
        name="operator",
    )(*operands)


def everyone(value, axis, count):
    return lax.all_to_all(jnp.broadcast_to(value[None], (count,) + value.shape), axis, 0, 0)


def shards(projected, short_taps, filter_taps, decay, cotangent):
    length, _, channels = projected.shape
    ranks = lax.axis_size("seq")
    rows = filter_taps.shape[0]
    width = min(256, channels // CHUNKS)
    blocks = channels // width // CHUNKS
    chunk = blocks * width
    proj = pltpu.with_memory_space_constraint(jnp.transpose(projected, (1, 0, 2)), pltpu.HBM)
    cotangent = pltpu.with_memory_space_constraint(cotangent, pltpu.HBM)

    each = -(-3 * (FK + 1) // ranks)
    slots = -(-(rows + each) // 8) * 8

    sent, prev, later, spread = [], [], [], None
    for k in range(CHUNKS):
        made = edges(
            proj, cotangent, short_taps, width, k * blocks, blocks, filter_taps if k == 1 else None, ranks
        )
        if k == 1:
            spread = made[0]
        sent.append(made[-2:])
    for k in range(CHUNKS):
        forward, backward = sent[k]
        if k:
            forward, prev[k - 1] = lax.optimization_barrier((forward, prev[k - 1]))
            backward, later[k - 1] = lax.optimization_barrier((backward, later[k - 1]))
        prev.append(from_behind(forward, "seq", 1))
        later.append(from_behind(backward, "seq", -1))
    taps = lax.all_to_all(spread, "seq", 0, 0).reshape(rows * ranks, channels)

    gated = grad_proj = sums = None
    groups = []
    for k in range(CHUNKS):
        last = k == CHUNKS - 1
        gated, grad_proj, sums = main(
            proj, cotangent, prev[k], later[k], short_taps, taps, decay[None], width, k * blocks, blocks, ranks,
            slots, chunk if last else chunk * (CHUNKS - 1), 0 if last else k * blocks,
            [gated, grad_proj, None if last else sums],
        )
        if k >= CHUNKS - 2:
            groups.append(lax.all_to_all(sums, "seq", 0, 0))

    raw = [jnp.sum(group.astype(F32), axis=0) for group in groups]
    total = sum(jnp.sum(part[: rows + each] * part[: rows + each]) for part in raw)
    filter_raw = jnp.concatenate([part[:rows] for part in raw], axis=1)
    short_raw = jnp.concatenate([part[rows : rows + each] for part in raw], axis=1)
    short_raw, total = lax.optimization_barrier((short_raw, total))
    totals = everyone(jnp.full((8, 128), total), ("seq", "ch"), ranks * lax.axis_size("ch"))
    short_all = everyone(short_raw.reshape(8 * each, channels // 8), "seq", ranks)
    short_all = short_all.reshape(ranks * each, channels)[: 3 * (FK + 1)].reshape(3, FK + 1, channels)[:, :FK]
    entries = (rows * ranks + 3 * FK) * channels * lax.axis_size("ch")
    scale = jnp.minimum(1.0, math.sqrt(entries) / jnp.sqrt(jnp.sum(totals[:, 0, 0])))
    return (gated, jnp.transpose(grad_proj, (1, 0, 2)), scale * short_all, scale * filter_raw)


def solution(mesh):
    placed = (P("seq", None, "ch"), P(None, None, "ch"), P("seq", "ch"), P("ch"), P("seq", "ch"))
    return jax.shard_map(
        shards,
        mesh=mesh,
        in_specs=placed,
        out_specs=(P("seq", "ch"), P("seq", None, "ch"), P(None, None, "ch"), P("seq", "ch")),
        check_vma=False,
    )
```

```python
import functools
import math

import jax
import jax.numpy as jnp
import ml_dtypes
import numpy as np
from jax import lax
from jax.experimental import pallas as pl
from jax.experimental.pallas import tpu as pltpu
from jax.sharding import PartitionSpec as P


FK = 7
BF16 = jnp.bfloat16
F32 = jnp.float32
CHUNKS = 2


def from_behind(value, axis, by):
    count = lax.axis_size(axis)
    pairs = [(i, i + by) for i in range(count) if 0 <= i + by < count]
    return lax.ppermute(value, axis, pairs)


def interleaved(span, first=0, low=0):
    return np.array([first + s * span + r for r in range(low, span) for s in range(8)])


def pick(positions, count):
    out = np.zeros((len(positions), count), np.float32)
    for row, at in enumerate(positions):
        if 0 <= at < count:
            out[row, at] = 1.0
    return out.astype(ml_dtypes.bfloat16)


def halves(matrix):
    high = matrix.astype(np.float32).astype(ml_dtypes.bfloat16)
    low = (matrix - high.astype(np.float64)).astype(np.float32).astype(ml_dtypes.bfloat16)
    return np.stack([high, low])


def analysis(positions, size, pad=0):
    freq = np.arange(size // 2)[:, None]
    angle = np.pi * (((2 * freq + 1) * np.asarray(positions)[None, :]) % (2 * size)) / size
    matrix = np.concatenate([np.cos(angle), -np.sin(angle)], axis=0)
    return halves(np.pad(matrix, ((0, 0), (0, pad))))


def synthesis(positions, size):
    freq = np.arange(size // 2)[None, :]
    angle = np.pi * (((2 * freq + 1) * np.asarray(positions)[:, None]) % (2 * size)) / size
    return halves(np.concatenate([np.cos(angle), -np.sin(angle)], axis=1) * (2.0 / size))


def mm(a, b):
    return jnp.dot(a, b, preferred_element_type=F32)


def picked(span, first, length):
    shape = ((span + FK - 1) * 8, length)
    row, column = (lax.broadcasted_iota(jnp.int32, shape, axis) for axis in (0, 1))
    position = first + (row & 7) * span + (row >> 3) - (FK - 1)
    return jnp.where(position == column, 1.0, 0.0).astype(BF16)


def edges_kernel(proj, cot, short, *refs):
    forward, backward = refs[-2:]
    length, width = cot.shape
    tail, head = 16, 17
    p_tail, p_head = picked(tail, length - 128, length), picked(head, 0, length)

    def conv(x, taps, count):
        x = x.reshape(-1, 8, width)
        total = taps[0:1] * x[FK - 1 : FK - 1 + count]
        for lag in range(1, FK):
            total = total + taps[lag : lag + 1] * x[FK - 1 - lag : FK - 1 - lag + count]
        return total

    mixed = conv(mm(p_tail, proj[1]), short[1], tail) * conv(mm(p_tail, proj[2]), short[2], tail)
    ends = [proj[i, length - 16 :, :].astype(F32)[8:] for i in range(3)]
    forward[...] = jnp.concatenate([mixed.reshape(tail * 8, width)] + ends, axis=0).astype(BF16)
    gate = conv(mm(p_head, proj[0]), short[0], head).reshape(head * 8, width)
    grad = gate * mm(p_head[(FK - 1) * 8 :], cot[...])
    starts = [ref[:16, :].astype(F32)[:8] for ref in (cot, proj.at[1], proj.at[2])]
    backward[...] = jnp.concatenate([grad] + starts, axis=0).astype(BF16)
    if len(refs) > 2:
        taps, spread = refs[:2]
        spread[...] = jnp.broadcast_to(taps[...].astype(BF16)[None], spread.shape)


def main_kernel(
    proj, cot, prev, later, short, taps, decay,
    e_own, e_prev, e_next, e_taps, s_own, s_lags, p_in, p_out, *refs,
):
    gated, grad_proj, sums_out, px, feat, grad, cots = refs[-7:]
    length, width = cot.shape
    span = length // 8
    edge = FK - 1
    lanes = [slice(at, at + 128) for at in range(0, width, 128)]
    row8 = lax.broadcasted_iota(jnp.int32, (8, width), 0)

    before = prev[...].astype(F32)
    after = later[...].astype(F32)
    prev8 = [before[128 + 8 * i : 136 + 8 * i] for i in range(3)]
    cot_next = after[136:144]
    next8 = [None, after[144:152], after[152:160]]

    lags = lax.broadcasted_iota(jnp.int32, (taps.shape[0], width), 0).astype(F32)
    falloff = jnp.exp(-decay[...] * lags)
    kernel = taps[...].astype(F32) * falloff
    high = kernel.astype(BF16)
    low = (kernel - high.astype(F32)).astype(BF16)
    k_spec = mm(e_taps[...], jnp.concatenate([high, high, low], axis=0))

    for i in range(3):
        x = mm(p_in[...], proj[i]).reshape(span + edge, 8, width)
        px[i, edge:] = x[edge:]
        for k in range(1, FK):
            px[i, edge - k] = jnp.where(row8 == 0, pltpu.roll(prev8[i], k, 0), x[edge - k])
    cots[...] = mm(p_in[edge * 8 :, :], cot[...]).reshape(span, 8, width)

    step = 8
    for i in range(3):
        for lane in lanes:
            weights = [jnp.broadcast_to(short[i, lag : lag + 1, lane], (8, 128)) for lag in range(FK)]
            for r in range(0, span, step):
                total = weights[0] * px[i, r + edge : r + edge + step, :, lane]
                for lag in range(1, FK):
                    total = total + weights[lag] * px[i, r + edge - lag : r + edge - lag + step, :, lane]
                feat[i, r : r + step, :, lane] = total

    def conv8(last, first, weights, whole):
        total = weights[0:1] * first if whole else jnp.zeros((8, width), F32)
        for lag in range(1, FK):
            rolled = pltpu.roll(first, lag, 0) if whole else 0.0
            total = total + weights[lag : lag + 1] * jnp.where(row8 < lag, pltpu.roll(last, lag, 0), rolled)
        return total

    ends = [proj[i, length - 16 :, :].astype(F32)[8:] for i in range(3)]
    feat_next = [None] + [conv8(ends[i], next8[i], short[i], True) for i in (1, 2)]
    mixed_next = feat_next[1] * feat_next[2]
    grad_next = after[:136]
    fix = cot_next * conv8(ends[0], None, short[0], False)
    rows = [grad_next[8 * r : 8 * r + 8] for r in range(17)]
    for r in range(edge):
        rows[r] = rows[r] + jnp.where(row8 == 0, pltpu.roll(fix, (8 - r) % 8, 0), 0.0)
    grad_next = jnp.concatenate(rows + [jnp.zeros((8, width), F32)], axis=0).astype(BF16)
    mixed_edge = jnp.concatenate([before[:128], mixed_next, jnp.zeros((8, width), F32)], axis=0).astype(BF16)

    flat = lambda value: value.reshape(length, width)
    mixed = flat(feat[1] * feat[2]).astype(BF16)
    grad_own = flat(cots[...] * feat[0]).astype(BF16)
    m_spec = mm(e_own[...], jnp.concatenate([mixed, mixed], axis=0)) + mm(e_prev[...], mixed_edge)
    g_own = mm(e_own[...], jnp.concatenate([grad_own, grad_own], axis=0))
    g_spec = g_own + mm(e_next[...], grad_next)

    half = k_spec.shape[0] // 2
    parts = lambda value: (value[:half], value[half:])
    (kr, ki), (mr, mi), (gr, gi), (hr, hi) = parts(k_spec), parts(m_spec), parts(g_spec), parts(g_own)

    def back_to(matrix, real, imaginary):
        spectrum = jnp.concatenate([real, imaginary], axis=0).astype(BF16)
        return mm(matrix[...], jnp.concatenate([spectrum, spectrum], axis=0))

    filtered = back_to(s_own, mr * kr - mi * ki, mr * ki + mi * kr)
    grad_mixed = back_to(s_own, gr * kr + gi * ki, gi * kr - gr * ki)
    filter_sums = back_to(s_lags, hr * mr + hi * mi, hi * mr - hr * mi) * falloff

    own = filtered[:length].reshape(span, 8, width)
    gated[...] = mm(p_out[...], flat(feat[0] * own).astype(BF16)).astype(BF16)
    back = grad_mixed[:length].reshape(span, 8, width)
    grad[0, :span] = cots[...] * own
    grad[1, :span] = back * feat[2]
    grad[2, :span] = back * feat[1]
    back_next = grad_mixed[length:]
    edge_next = [cot_next * filtered[length:], back_next * feat_next[2], back_next * feat_next[1]]
    for i in range(3):
        for k in range(edge):
            grad[i, span + k] = jnp.where(row8 == 7, pltpu.roll(edge_next[i], 7 - k, 0), pltpu.roll(grad[i, k], 7, 0))

    short_rows = []
    for i in range(3):
        columns, rows = [], [[] for _ in range(FK)]
        for lane in lanes:
            weights = [jnp.broadcast_to(short[i, lag : lag + 1, lane], (8, 128)) for lag in range(FK)]
            sums = [jnp.zeros((8, 128), F32)] * FK
            chunks = []
            for r in range(0, span, step):
                total = jnp.zeros((step, 8, 128), F32)
                here = px[i, r + edge : r + edge + step, :, lane]
                for lag in range(FK):
                    value = grad[i, r + lag : r + lag + step, :, lane]
                    total = total + weights[lag] * value
                    sums[lag] = sums[lag] + jnp.sum(here * value, axis=0)
                chunks.append(total)
            columns.append(jnp.concatenate(chunks, axis=0))
            for lag in range(FK):
                rows[lag].append(jnp.sum(sums[lag], axis=0, keepdims=True))
        short_rows += [jnp.concatenate(row, axis=1) for row in rows] + [jnp.zeros((1, width), F32)]
        result = flat(jnp.concatenate(columns, axis=2)).astype(BF16)
        grad_proj[i] = mm(p_out[...], result).astype(BF16)

    ranks, slots, _ = sums_out.shape
    per, each = filter_sums.shape[0] // ranks, -(-len(short_rows) // ranks)
    short_rows += [jnp.zeros((1, width), F32)] * (ranks * each - len(short_rows))
    gaps = [-per % 8, -each % 8]
    gaps = [[jnp.zeros((gap, width), F32)] if gap else [] for gap in gaps]
    blocks = []
    for rank in range(ranks):
        blocks += [filter_sums[rank * per : rank * per + per]] + gaps[0]
        blocks += short_rows[rank * each : rank * each + each] + gaps[1]
    sums_out[...] = jnp.concatenate(blocks, axis=0).reshape(ranks, slots, width).astype(BF16)


def resident(array):
    return pl.BlockSpec(memory_space=pltpu.VMEM)


def columns(rows, width, first=0):
    lead = (0,) * len(rows)
    return pl.BlockSpec(tuple(rows) + (width,), lambda c: lead + (first + c,))


def edges(proj, cot, short, width, first, blocks, taps=None, ranks=None):
    length = cot.shape[0]
    in_specs = [
        columns((3, length), width, first), columns((length,), width, first), columns((3, FK), width, first),
    ]
    out_specs = [columns((152,), width), columns((160,), width)]
    out_shape = [jax.ShapeDtypeStruct((rows, blocks * width), BF16) for rows in (152, 160)]
    operands = [proj, cot, short]
    if taps is not None:
        rows, channels = taps.shape
        in_specs.append(columns((rows,), channels // blocks))
        operands.append(taps)
        out_specs.insert(0, columns((ranks, rows), channels // blocks))
        out_shape.insert(0, pltpu.HBM((ranks, rows, channels), BF16))
    return pl.pallas_call(
        edges_kernel,
        grid=(blocks,),
        in_specs=in_specs,
        out_specs=out_specs,
        out_shape=out_shape,
        compiler_params=pltpu.CompilerParams(vmem_limit_bytes=32 << 20),
        cost_estimate=pl.CostEstimate(flops=0, bytes_accessed=blocks * width * 10000, transcendentals=0),
        name="edges",
    )(*operands)


def main(proj, cot, prev, later, short, taps, decay, width, first, blocks, ranks, slots, held):
    length, channels = cot.shape
    count = taps.shape[0]
    size = 2 * length
    span = length // 8
    own = interleaved(span)
    high, low = analysis(own, size)
    k_high, k_low = analysis(np.arange(count), size)
    constants = [
        np.concatenate([high, low], axis=1),
        analysis(np.concatenate([interleaved(16, -128), length + np.arange(8)]), size, 8)[0],
        analysis(interleaved(17, length), size, 8)[0],
        np.concatenate([k_high, k_low, k_high], axis=1),
        np.concatenate(list(synthesis(np.concatenate([own, length + np.arange(8)]), size)), axis=1),
        np.concatenate(list(synthesis(np.arange(count), size)), axis=1),
        pick(interleaved(span, 0, 1 - FK), length),
        pick(own, length).T,
    ]
    constants = [jnp.asarray(constant) for constant in constants]
    operands = [proj, cot, prev, later, short, taps, decay] + constants
    aliases = {}
    for index, value in enumerate(held):
        if value is not None:
            aliases[len(operands)] = index
            operands.append(value)
    return pl.pallas_call(
        main_kernel,
        grid=(blocks,),
        in_specs=[
            columns((3, length), width, first), columns((length,), width, first), columns((prev.shape[0],), width),
            columns((later.shape[0],), width), columns((3, FK), width, first), columns((count,), width, first),
            columns((1,), width, first),
        ] + [resident(constant) for constant in constants] + [pl.BlockSpec(memory_space=pl.ANY)] * len(aliases),
        out_specs=[
            columns((length,), width, first), columns((3, length), width, first), columns((ranks, slots), width, first),
        ],
        out_shape=[
            jax.ShapeDtypeStruct((length, channels), BF16),
            jax.ShapeDtypeStruct((3, length, channels), BF16),
            pltpu.HBM((ranks, slots, channels), BF16),
        ],
        scratch_shapes=[
            pltpu.VMEM((3, span + FK - 1, 8, width), F32),
            pltpu.VMEM((3, span, 8, width), F32),
            pltpu.VMEM((3, span + FK - 1, 8, width), F32),
            pltpu.VMEM((span, 8, width), F32),
        ],
        input_output_aliases=aliases,
        compiler_params=pltpu.CompilerParams(vmem_limit_bytes=40 << 20),
        cost_estimate=pl.CostEstimate(flops=blocks * 4 * 10**9, bytes_accessed=blocks * 2 * 10**6, transcendentals=0),
        name="operator",
    )(*operands)


def squares_kernel(sums, raw, payload):
    ranks, slots, channels = sums.shape
    total = sums[0].astype(F32)
    for rank in range(1, ranks):
        total = total + sums[rank].astype(F32)
    raw[...] = total
    squares = jnp.sum(total * total, keepdims=True)
    high = squares.astype(BF16).astype(F32)
    everyone, rows, width = payload.shape
    each, cuts = rows // 8 - 1, channels // width
    first = slots - 8 * (-(-each // 8))
    pieces = [
        total[row : row + 1, cut * width : (cut + 1) * width]
        for row in range(first, first + each)
        for cut in range(cuts)
    ]
    half = (8, width // 2)
    ends = [jnp.broadcast_to(high, half), jnp.broadcast_to(squares - high, half)]
    block = jnp.concatenate(pieces + [jnp.concatenate(ends, axis=1)], axis=0).astype(BF16)
    for other in range(everyone):
        payload[other] = block


def scale_kernel(entries, mine, raw, gathered, grad_short, grad_filter):
    everyone, rows, width = gathered.shape
    each, channels = rows // 8 - 1, raw.shape[1]
    cuts = channels // width
    total = jnp.zeros((8, width), F32)
    for other in range(everyone):
        total = total + gathered[other].astype(F32)[rows - 8 :]
    total = total[:1, :1] + total[:1, width // 2 : width // 2 + 1]
    scale = jnp.minimum(1.0, math.sqrt(entries) / jnp.sqrt(total))
    grad_filter[...] = scale * raw[: grad_filter.shape[0], :]
    step = mine[1]
    for i in range(3):
        for lag in range(FK):
            rank, row = divmod(i * (FK + 1) + lag, each)
            block = gathered[rank * step + mine[0]].astype(F32) * scale
            for cut in range(cuts):
                at = row * cuts + cut
                grad_short[i, lag : lag + 1, cut * width : (cut + 1) * width] = block[at : at + 1]


def shards(projected, short_taps, filter_taps, decay, cotangent):
    length, _, channels = projected.shape
    ranks, groups = lax.axis_size("seq"), lax.axis_size("ch")
    rows = filter_taps.shape[0]
    width = min(256, channels // CHUNKS)
    blocks = channels // width // CHUNKS
    proj = jnp.transpose(projected, (1, 0, 2))
    proj, cotangent, short_taps, filter_taps, decay = (
        pltpu.with_memory_space_constraint(array, pltpu.HBM)
        for array in (proj, cotangent, short_taps, filter_taps, decay[None])
    )

    each = -(-3 * (FK + 1) // ranks)
    slots = -(-rows // 8) * 8 + -(-each // 8) * 8

    prev, later, spread = [], [], None
    for k in range(CHUNKS):
        last = k == CHUNKS - 1
        made = edges(proj, cotangent, short_taps, width, k * blocks, blocks, filter_taps if last else None, ranks)
        spread = made[0] if last else None
        prev.append(from_behind(made[-2], "seq", 1))
        later.append(from_behind(made[-1], "seq", -1))
    taps = lax.all_to_all(spread, "seq", 0, 0).reshape(rows * ranks, channels)

    held = [None] * 3
    for k in range(CHUNKS):
        held = main(
            proj, cotangent, prev[k], later[k], short_taps, taps, decay, width, k * blocks, blocks, ranks, slots, held
        )
    gated, grad_proj, sums = held
    sums = lax.all_to_all(sums, "seq", 0, 0)

    vmem = pl.BlockSpec(memory_space=pltpu.VMEM)
    raw, payload = pl.pallas_call(
        squares_kernel,
        in_specs=[vmem],
        out_specs=[vmem] * 2,
        out_shape=[
            jax.ShapeDtypeStruct((slots, channels), F32),
            jax.ShapeDtypeStruct((ranks * groups, 8 * each + 8, channels // 8), BF16),
        ],
        compiler_params=pltpu.CompilerParams(vmem_limit_bytes=32 << 20),
        name="squares",
    )(sums)
    gathered = lax.all_to_all(payload, ("seq", "ch"), 0, 0)
    mine = jnp.stack([lax.axis_index("ch"), jnp.int32(groups)])
    entries = (rows * ranks + 3 * FK) * channels * groups
    grad_short, grad_filter = pl.pallas_call(
        functools.partial(scale_kernel, entries),
        in_specs=[pl.BlockSpec(memory_space=pltpu.SMEM), vmem, vmem],
        out_specs=[vmem] * 2,
        out_shape=[
            jax.ShapeDtypeStruct((3, FK, channels), F32),
            jax.ShapeDtypeStruct((rows, channels), F32),
        ],
        compiler_params=pltpu.CompilerParams(vmem_limit_bytes=32 << 20),
        name="scale",
    )(mine, raw, gathered)
    return (gated, jnp.transpose(grad_proj, (1, 0, 2)), grad_short, grad_filter)


def solution(mesh):
    placed = (P("seq", None, "ch"), P(None, None, "ch"), P("seq", "ch"), P("ch"), P("seq", "ch"))
    return jax.shard_map(
        shards,
        mesh=mesh,
        in_specs=placed,
        out_specs=(P("seq", "ch"), P("seq", None, "ch"), P(None, None, "ch"), P("seq", "ch")),
        check_vma=False,
    )
```

```python
import functools
import math

import jax
import jax.numpy as jnp
import ml_dtypes
import numpy as np
from jax import lax
from jax.experimental import pallas as pl
from jax.experimental.pallas import tpu as pltpu
from jax.sharding import PartitionSpec as P


FK = 7
BF16 = jnp.bfloat16
F32 = jnp.float32
CHUNKS = 2
SHORT = 32


def from_behind(value, axis, by):
    count = lax.axis_size(axis)
    pairs = [(i, i + by) for i in range(count) if 0 <= i + by < count]
    return lax.ppermute(value, axis, pairs)


def interleaved(span, first=0, low=0):
    return np.array([first + s * span + r for r in range(low, span) for s in range(8)])


def pick(positions, count):
    out = np.zeros((len(positions), count), np.float32)
    for row, at in enumerate(positions):
        if 0 <= at < count:
            out[row, at] = 1.0
    return out.astype(ml_dtypes.bfloat16)


def halves(matrix):
    high = matrix.astype(np.float32).astype(ml_dtypes.bfloat16)
    low = (matrix - high.astype(np.float64)).astype(np.float32).astype(ml_dtypes.bfloat16)
    return np.stack([high, low])


def analysis(positions, size, pad=0):
    freq = np.arange(size // 2)[:, None]
    angle = np.pi * (((2 * freq + 1) * np.asarray(positions)[None, :]) % (2 * size)) / size
    matrix = np.concatenate([np.cos(angle), -np.sin(angle)], axis=0)
    return halves(np.pad(matrix, ((0, 0), (0, pad))))


def synthesis(positions, size):
    freq = np.arange(size // 2)[None, :]
    angle = np.pi * (((2 * freq + 1) * np.asarray(positions)[:, None]) % (2 * size)) / size
    return halves(np.concatenate([np.cos(angle), -np.sin(angle)], axis=1) * (2.0 / size))


def mm(a, b):
    return jnp.dot(a, b, preferred_element_type=F32)


def picked(span, first, length):
    shape = ((span + FK - 1) * 8, length)
    row, column = (lax.broadcasted_iota(jnp.int32, shape, axis) for axis in (0, 1))
    position = first + (row & 7) * span + (row >> 3) - (FK - 1)
    return jnp.where(position == column, 1.0, 0.0).astype(BF16)


def edges_kernel(proj, cot, short, forward, backward):
    length, width = cot.shape
    tail, head = 16, 17
    p_tail, p_head = picked(tail, length - 128, length), picked(head, 0, length)

    def conv(x, taps, count):
        x = x.reshape(-1, 8, width)
        total = taps[0:1] * x[FK - 1 : FK - 1 + count]
        for lag in range(1, FK):
            total = total + taps[lag : lag + 1] * x[FK - 1 - lag : FK - 1 - lag + count]
        return total

    mixed = conv(mm(p_tail, proj[1]), short[1], tail) * conv(mm(p_tail, proj[2]), short[2], tail)
    ends = [proj[i, length - 16 :, :].astype(F32)[8:] for i in range(3)]
    forward[...] = jnp.concatenate([mixed.reshape(tail * 8, width)] + ends, axis=0).astype(BF16)
    gate = conv(mm(p_head, proj[0]), short[0], head).reshape(head * 8, width)
    grad = gate * mm(p_head[(FK - 1) * 8 :], cot[...])
    starts = [ref[:16, :].astype(F32)[:8] for ref in (cot, proj.at[1], proj.at[2])]
    backward[...] = jnp.concatenate([grad] + starts, axis=0).astype(BF16)


def spread_kernel(taps, spread):
    spread[...] = jnp.broadcast_to(taps[...].astype(BF16)[None], spread.shape)


def main_kernel(
    first, proj, cot, prev, later, short, taps, decay,
    e_own, e_prev, e_next, e_taps, s_own, s_lags, p_in, p_out, *refs,
):
    gated, grad_proj, sums_out, px, feat, grad, cots, filter_held, short_held, done = refs[-10:]
    length, width = cot.shape
    span = length // 8
    edge = FK - 1
    lanes = [slice(at, at + 128) for at in range(0, width, 128)]
    row8 = lax.broadcasted_iota(jnp.int32, (8, width), 0)

    before = prev[...].astype(F32)
    after = later[...].astype(F32)
    prev8 = [before[128 + 8 * i : 136 + 8 * i] for i in range(3)]
    cot_next = after[136:144]
    next8 = [None, after[144:152], after[152:160]]

    lags = lax.broadcasted_iota(jnp.int32, (taps.shape[0], width), 0).astype(F32)
    falloff = jnp.exp(-decay[...] * lags)
    kernel = taps[...].astype(F32) * falloff
    high = kernel.astype(BF16)
    low = (kernel - high.astype(F32)).astype(BF16)
    k_spec = mm(e_taps[...], jnp.concatenate([high, high, low], axis=0))

    for i in range(3):
        x = mm(p_in[...], proj[i]).reshape(span + edge, 8, width)
        px[i, edge:] = x[edge:]
        for k in range(1, FK):
            px[i, edge - k] = jnp.where(row8 == 0, pltpu.roll(prev8[i], k, 0), x[edge - k])
    cots[...] = mm(p_in[edge * 8 :, :], cot[...]).reshape(span, 8, width)

    step = 8
    for i in range(3):
        for lane in lanes:
            weights = [jnp.broadcast_to(short[i, lag : lag + 1, lane], (8, 128)) for lag in range(FK)]
            for r in range(0, span, step):
                total = weights[0] * px[i, r + edge : r + edge + step, :, lane]
                for lag in range(1, FK):
                    total = total + weights[lag] * px[i, r + edge - lag : r + edge - lag + step, :, lane]
                feat[i, r : r + step, :, lane] = total

    def conv8(last, first, weights, whole):
        total = weights[0:1] * first if whole else jnp.zeros((8, width), F32)
        for lag in range(1, FK):
            rolled = pltpu.roll(first, lag, 0) if whole else 0.0
            total = total + weights[lag : lag + 1] * jnp.where(row8 < lag, pltpu.roll(last, lag, 0), rolled)
        return total

    ends = [proj[i, length - 16 :, :].astype(F32)[8:] for i in range(3)]
    feat_next = [None] + [conv8(ends[i], next8[i], short[i], True) for i in (1, 2)]
    mixed_next = feat_next[1] * feat_next[2]
    grad_next = after[:136]
    fix = cot_next * conv8(ends[0], None, short[0], False)
    rows = [grad_next[8 * r : 8 * r + 8] for r in range(17)]
    for r in range(edge):
        rows[r] = rows[r] + jnp.where(row8 == 0, pltpu.roll(fix, (8 - r) % 8, 0), 0.0)
    grad_next = jnp.concatenate(rows + [jnp.zeros((8, width), F32)], axis=0).astype(BF16)
    mixed_edge = jnp.concatenate([before[:128], mixed_next, jnp.zeros((8, width), F32)], axis=0).astype(BF16)

    flat = lambda value: value.reshape(length, width)
    mixed = flat(feat[1] * feat[2]).astype(BF16)
    grad_own = flat(cots[...] * feat[0]).astype(BF16)
    m_spec = mm(e_own[...], jnp.concatenate([mixed, mixed], axis=0)) + mm(e_prev[...], mixed_edge)
    g_own = mm(e_own[...], jnp.concatenate([grad_own, grad_own], axis=0))
    g_spec = g_own + mm(e_next[...], grad_next)

    half = k_spec.shape[0] // 2
    parts = lambda value: (value[:half], value[half:])
    (kr, ki), (mr, mi), (gr, gi), (hr, hi) = parts(k_spec), parts(m_spec), parts(g_spec), parts(g_own)

    def back_to(matrix, real, imaginary):
        spectrum = jnp.concatenate([real, imaginary], axis=0).astype(BF16)
        return mm(matrix[...], jnp.concatenate([spectrum, spectrum], axis=0))

    filtered = back_to(s_own, mr * kr - mi * ki, mr * ki + mi * kr)
    grad_mixed = back_to(s_own, gr * kr + gi * ki, gi * kr - gr * ki)
    filter_sums = back_to(s_lags, hr * mr + hi * mi, hi * mr - hr * mi) * falloff

    own = filtered[:length].reshape(span, 8, width)
    gated[...] = mm(p_out[...], flat(feat[0] * own).astype(BF16)).astype(BF16)
    back = grad_mixed[:length].reshape(span, 8, width)
    grad[0, :span] = cots[...] * own
    grad[1, :span] = back * feat[2]
    grad[2, :span] = back * feat[1]
    back_next = grad_mixed[length:]
    edge_next = [cot_next * filtered[length:], back_next * feat_next[2], back_next * feat_next[1]]
    for i in range(3):
        for k in range(edge):
            grad[i, span + k] = jnp.where(row8 == 7, pltpu.roll(edge_next[i], 7 - k, 0), pltpu.roll(grad[i, k], 7, 0))

    short_rows = []
    for i in range(3):
        columns, rows = [], [[] for _ in range(FK)]
        for lane in lanes:
            weights = [jnp.broadcast_to(short[i, lag : lag + 1, lane], (8, 128)) for lag in range(FK)]
            sums = [jnp.zeros((8, 128), F32)] * FK
            chunks = []
            for r in range(0, span, step):
                total = jnp.zeros((step, 8, 128), F32)
                here = px[i, r + edge : r + edge + step, :, lane]
                for lag in range(FK):
                    value = grad[i, r + lag : r + lag + step, :, lane]
                    total = total + weights[lag] * value
                    sums[lag] = sums[lag] + jnp.sum(here * value, axis=0)
                chunks.append(total)
            columns.append(jnp.concatenate(chunks, axis=0))
            for lag in range(FK):
                rows[lag].append(jnp.sum(sums[lag], axis=0, keepdims=True))
        short_rows += [jnp.concatenate(row, axis=1) for row in rows]
        result = flat(jnp.concatenate(columns, axis=2)).astype(BF16)
        grad_proj[i] = mm(p_out[...], result).astype(BF16)

    step, block = pl.program_id(0), first + pl.program_id(0)
    ranks, slot, _ = filter_held.shape
    per, share = filter_sums.shape[0] // ranks, short_held.shape[0]
    copies = [
        pltpu.make_async_copy(
            filter_held, sums_out.at[:, pl.ds(pl.multiple_of(block * slot, slot), slot), :], done.at[0]
        ),
        pltpu.make_async_copy(
            short_held,
            sums_out.at[pl.ds(block * share, share), pl.ds(sums_out.shape[1] - SHORT, SHORT), :],
            done.at[1],
        ),
    ]

    @pl.when(step > 0)
    def _():
        for copy in copies:
            copy.wait()

    by_rank = filter_sums.reshape(ranks, per, width) if per % 8 == 0 else jnp.stack(
        [filter_sums[rank * per : rank * per + per] for rank in range(ranks)]
    )
    if slot > per:
        by_rank = jnp.concatenate([by_rank, jnp.zeros((ranks, slot - per, width), F32)], axis=1)
    filter_held[...] = by_rank.astype(BF16)
    sums = jnp.concatenate(short_rows + [jnp.zeros((SHORT - len(short_rows), width), F32)], axis=0)
    for rank in range(share):
        held = pltpu.roll(sums, width - rank * (width // share), 1) if rank else sums
        short_held[rank] = held.astype(BF16)
    for copy in copies:
        copy.start()

    @pl.when(step == pl.num_programs(0) - 1)
    def _():
        for copy in copies:
            copy.wait()


def whole(array):
    return pl.BlockSpec(array.shape, lambda c: (0,) * array.ndim)


def columns(rows, width, first=0):
    lead = (0,) * len(rows)
    return pl.BlockSpec(tuple(rows) + (width,), lambda c: lead + (first + c,))


def edges(proj, cot, short, width, first, blocks):
    length = cot.shape[0]
    return pl.pallas_call(
        edges_kernel,
        grid=(blocks,),
        in_specs=[
            columns((3, length), width, first), columns((length,), width, first), columns((3, FK), width, first),
        ],
        out_specs=[columns((152,), width), columns((160,), width)],
        out_shape=[jax.ShapeDtypeStruct((rows, blocks * width), BF16) for rows in (152, 160)],
        compiler_params=pltpu.CompilerParams(vmem_limit_bytes=32 << 20),
        cost_estimate=pl.CostEstimate(flops=0, bytes_accessed=blocks * width * 10000, transcendentals=0),
        name="edges",
    )(proj, cot, short)


def main(proj, cot, prev, later, short, taps, decay, width, first, blocks, ranks, slot, held):
    length, channels = cot.shape
    count = taps.shape[0]
    size = 2 * length
    span = length // 8
    share = ranks * width // channels
    own = interleaved(span)
    high, low = analysis(own, size)
    k_high, k_low = analysis(np.arange(count), size)
    constants = [
        np.concatenate([high, low], axis=1),
        analysis(np.concatenate([interleaved(16, -128), length + np.arange(8)]), size, 8)[0],
        analysis(interleaved(17, length), size, 8)[0],
        np.concatenate([k_high, k_low, k_high], axis=1),
        np.concatenate(list(synthesis(np.concatenate([own, length + np.arange(8)]), size)), axis=1),
        np.concatenate(list(synthesis(np.arange(count), size)), axis=1),
        pick(interleaved(span, 0, 1 - FK), length),
        pick(own, length).T,
    ]
    constants = [pltpu.with_memory_space_constraint(jnp.asarray(constant), pltpu.HBM) for constant in constants]
    operands = [proj, cot, prev, later, short, taps, decay] + constants
    aliases = {}
    for index, value in enumerate(held):
        if value is not None:
            aliases[len(operands)] = index
            operands.append(value)
    return pl.pallas_call(
        functools.partial(main_kernel, first),
        grid=(blocks,),
        in_specs=[
            columns((3, length), width, first), columns((length,), width, first), columns((prev.shape[0],), width),
            columns((later.shape[0],), width), columns((3, FK), width, first), columns((count,), width, first),
            columns((1,), width, first),
        ] + [whole(constant) for constant in constants] + [pl.BlockSpec(memory_space=pl.ANY)] * len(aliases),
        out_specs=[
            columns((length,), width, first), columns((3, length), width, first), pl.BlockSpec(memory_space=pl.ANY),
        ],
        out_shape=[
            jax.ShapeDtypeStruct((length, channels), BF16),
            jax.ShapeDtypeStruct((3, length, channels), BF16),
            pltpu.HBM((ranks, channels // width * slot + SHORT, width), BF16),
        ],
        scratch_shapes=[
            pltpu.VMEM((3, span + FK - 1, 8, width), F32),
            pltpu.VMEM((3, span, 8, width), F32),
            pltpu.VMEM((3, span + FK - 1, 8, width), F32),
            pltpu.VMEM((span, 8, width), F32),
            pltpu.VMEM((ranks, slot, width), BF16),
            pltpu.VMEM((share, SHORT, width), BF16),
            pltpu.SemaphoreType.DMA((2,)),
        ],
        input_output_aliases=aliases,
        compiler_params=pltpu.CompilerParams(vmem_limit_bytes=40 << 20),
        cost_estimate=pl.CostEstimate(flops=blocks * 4 * 10**9, bytes_accessed=blocks * 2 * 10**6, transcendentals=0),
        name="operator",
    )(*operands)


def squares_kernel(rows, share, sums, raw, payload):
    ranks, slots, width = sums.shape
    total = sums[0].astype(F32)
    for rank in range(1, ranks):
        total = total + sums[rank].astype(F32)
    slot = -(-rows // 16) * 16
    pieces = [total[at : at + rows] for at in range(0, slots - SHORT, slot)]
    raw[...] = jnp.concatenate(pieces, axis=1)
    lane = lax.broadcasted_iota(jnp.int32, (SHORT, width), 1)
    short = jnp.where(lane < share, total[slots - SHORT :], 0.0)
    squares = jnp.sum(short * short, keepdims=True)
    for piece in pieces:
        squares = squares + jnp.sum(piece * piece, keepdims=True)
    high = squares.astype(BF16).astype(F32)
    row = lax.broadcasted_iota(jnp.int32, (24, width), 0)
    block = jnp.where(row < 3 * FK, short[:24], jnp.where(row == 3 * FK, high, squares - high)).astype(BF16)
    for other in range(payload.shape[0]):
        payload[other] = block


def scale_kernel(entries, share, mine, raw, gathered, grad_short, grad_filter):
    everyone, rows, width = gathered.shape
    total = jnp.zeros((8, width), F32)
    for other in range(everyone):
        total = total + gathered[other].astype(F32)[16:]
    total = total[5:6, :1] + total[6:7, :1]
    scale = jnp.minimum(1.0, math.sqrt(entries) / jnp.sqrt(total))
    grad_filter[...] = scale * raw[...]
    step = mine[1]
    for rank in range(raw.shape[1] // share):
        block = gathered[rank * step + mine[0]].astype(F32) * scale
        for i in range(3):
            grad_short[i, :, rank * share : (rank + 1) * share] = block[i * FK : (i + 1) * FK, :share]


def shards(projected, short_taps, filter_taps, decay, cotangent):
    length, _, channels = projected.shape
    ranks, groups = lax.axis_size("seq"), lax.axis_size("ch")
    rows = filter_taps.shape[0]
    width = min(256, channels // CHUNKS)
    blocks = channels // width // CHUNKS
    proj = jnp.transpose(projected, (1, 0, 2))
    proj, cotangent, short_taps, decay = (
        pltpu.with_memory_space_constraint(array, pltpu.HBM)
        for array in (proj, cotangent, short_taps, decay[None])
    )

    slot = -(-rows // 16) * 16
    share = channels // ranks

    def constrained(*values):
        return lax.optimization_barrier(values)

    prev, later = [], []
    for k in range(CHUNKS):
        forward, backward = edges(proj, cotangent, short_taps, width, k * blocks, blocks)
        if k:
            forward, backward, later[-1] = constrained(forward, backward, later[-1])
        prev.append(from_behind(forward, "seq", 1))
        later.append(from_behind(backward, "seq", -1))
    filter_taps, prev[0] = constrained(filter_taps, prev[0])
    spread = pl.pallas_call(
        spread_kernel,
        out_shape=pltpu.HBM((ranks, rows, channels), BF16),
        name="spread",
    )(filter_taps)
    taps = lax.all_to_all(spread, "seq", 0, 0).reshape(rows * ranks, channels)

    held = [None] * 3
    for k in range(CHUNKS):
        held = main(
            proj, cotangent, prev[k], later[k], short_taps, taps, decay, width, k * blocks, blocks, ranks, slot, held
        )
    gated, grad_proj, sums = held
    sums = lax.all_to_all(sums, "seq", 0, 0)

    vmem = pl.BlockSpec(memory_space=pltpu.VMEM)
    raw, payload = pl.pallas_call(
        functools.partial(squares_kernel, rows, share),
        in_specs=[vmem],
        out_specs=[vmem] * 2,
        out_shape=[
            jax.ShapeDtypeStruct((rows, channels), F32),
            jax.ShapeDtypeStruct((ranks * groups, 24, width), BF16),
        ],
        compiler_params=pltpu.CompilerParams(vmem_limit_bytes=32 << 20),
        name="squares",
    )(sums)
    gathered = lax.all_to_all(payload, ("seq", "ch"), 0, 0)
    mine = jnp.stack([lax.axis_index("ch"), jnp.int32(groups)])
    entries = (rows * ranks + 3 * FK) * channels * groups
    grad_short, grad_filter = pl.pallas_call(
        functools.partial(scale_kernel, entries, share),
        in_specs=[pl.BlockSpec(memory_space=pltpu.SMEM), vmem, vmem],
        out_specs=[vmem] * 2,
        out_shape=[
            jax.ShapeDtypeStruct((3, FK, channels), F32),
            jax.ShapeDtypeStruct((rows, channels), F32),
        ],
        compiler_params=pltpu.CompilerParams(vmem_limit_bytes=32 << 20),
        name="scale",
    )(mine, raw, gathered)
    return (gated, jnp.transpose(grad_proj, (1, 0, 2)), grad_short, grad_filter)


def solution(mesh):
    placed = (P("seq", None, "ch"), P(None, None, "ch"), P("seq", "ch"), P("ch"), P("seq", "ch"))
    return jax.shard_map(
        shards,
        mesh=mesh,
        in_specs=placed,
        out_specs=(P("seq", "ch"), P("seq", None, "ch"), P(None, None, "ch"), P("seq", "ch")),
        check_vma=False,
    )
```

```python
import functools
import math

import jax
import jax.numpy as jnp
import ml_dtypes
import numpy as np
from jax import lax
from jax.experimental import pallas as pl
from jax.experimental.pallas import tpu as pltpu
from jax.sharding import PartitionSpec as P


FK = 7
BF16 = jnp.bfloat16
F32 = jnp.float32
SHORT = 32


def from_behind(value, axis, by):
    count = lax.axis_size(axis)
    pairs = [(i, i + by) for i in range(count) if 0 <= i + by < count]
    return lax.ppermute(value, axis, pairs)


def interleaved(span, first=0, low=0):
    return np.array([first + s * span + r for r in range(low, span) for s in range(8)])


def pick(positions, count):
    out = np.zeros((len(positions), count), np.float32)
    for row, at in enumerate(positions):
        if 0 <= at < count:
            out[row, at] = 1.0
    return out.astype(ml_dtypes.bfloat16)


def halves(matrix):
    high = matrix.astype(np.float32).astype(ml_dtypes.bfloat16)
    low = (matrix - high.astype(np.float64)).astype(np.float32).astype(ml_dtypes.bfloat16)
    return np.stack([high, low])


def analysis(positions, size, pad=0):
    freq = np.arange(size // 2)[:, None]
    angle = np.pi * (((2 * freq + 1) * np.asarray(positions)[None, :]) % (2 * size)) / size
    matrix = np.concatenate([np.cos(angle), -np.sin(angle)], axis=0)
    return halves(np.pad(matrix, ((0, 0), (0, pad))))


def synthesis(positions, size):
    freq = np.arange(size // 2)[None, :]
    angle = np.pi * (((2 * freq + 1) * np.asarray(positions)[:, None]) % (2 * size)) / size
    return halves(np.concatenate([np.cos(angle), -np.sin(angle)], axis=1) * (2.0 / size))


def mm(a, b):
    return jnp.dot(a, b, preferred_element_type=F32)


def picked(span, first, length):
    shape = ((span + FK - 1) * 8, length)
    row, column = (lax.broadcasted_iota(jnp.int32, shape, axis) for axis in (0, 1))
    position = first + (row & 7) * span + (row >> 3) - (FK - 1)
    return jnp.where(position == column, 1.0, 0.0).astype(BF16)


def edges_kernel(proj, cot, short, taps, forward, backward, spread):
    length, width = cot.shape
    tail, head = 16, 17
    p_tail, p_head = picked(tail, length - 128, length), picked(head, 0, length)

    def conv(x, taps, count):
        x = x.reshape(-1, 8, width)
        total = taps[0:1] * x[FK - 1 : FK - 1 + count]
        for lag in range(1, FK):
            total = total + taps[lag : lag + 1] * x[FK - 1 - lag : FK - 1 - lag + count]
        return total

    mixed = conv(mm(p_tail, proj[1]), short[1], tail) * conv(mm(p_tail, proj[2]), short[2], tail)
    ends = [proj[i, length - 16 :, :].astype(F32)[8:] for i in range(3)]
    forward[...] = jnp.concatenate([mixed.reshape(tail * 8, width)] + ends, axis=0).astype(BF16)
    gate = conv(mm(p_head, proj[0]), short[0], head).reshape(head * 8, width)
    grad = gate * mm(p_head[(FK - 1) * 8 :], cot[...])
    starts = [ref[:16, :].astype(F32)[:8] for ref in (cot, proj.at[1], proj.at[2])]
    backward[...] = jnp.concatenate([grad] + starts, axis=0).astype(BF16)
    spread[...] = jnp.broadcast_to(taps[...].astype(BF16)[None], spread.shape)


def conv8(last, first, taps):
    row = lax.broadcasted_iota(jnp.int32, last.shape, 0)
    total = jnp.zeros(last.shape, F32) if first is None else taps[0:1] * first
    for lag in range(1, FK):
        rolled = 0.0 if first is None else pltpu.roll(first, lag, 0)
        total = total + taps[lag : lag + 1] * jnp.where(row < lag, pltpu.roll(last, lag, 0), rolled)
    return total


def own_kernel(proj, cot, short, taps, decay, e_own, e_taps, p_in, feat, px, cots, m_part, g_part, k_spec):
    length, width = cot.shape
    span = length // 8
    edge = FK - 1
    lags = lax.broadcasted_iota(jnp.int32, (taps.shape[0], width), 0).astype(F32)
    kernel = taps[...].astype(F32) * jnp.exp(-decay[...] * lags)
    high = kernel.astype(BF16)
    low = (kernel - high.astype(F32)).astype(BF16)
    k_spec[...] = mm(e_taps[...], jnp.concatenate([high, high, low], axis=0))

    step = 8
    for i in range(3):
        x = mm(p_in[...], proj[i])
        px[i] = x[edge * 8 :].astype(BF16)
        x = x.reshape(span + edge, 8, width)
        for at in range(0, width, 128):
            lane = slice(at, at + 128)
            weights = [jnp.broadcast_to(short[i, lag : lag + 1, lane], (8, 128)) for lag in range(FK)]
            for r in range(0, span, step):
                total = weights[0] * x[r + edge : r + edge + step, :, lane]
                for lag in range(1, FK):
                    total = total + weights[lag] * x[r + edge - lag : r + edge - lag + step, :, lane]
                feat[i, r * 8 : (r + step) * 8, lane] = total.reshape(step * 8, 128)
    moved = mm(p_in[edge * 8 :, :], cot[...])
    cots[...] = moved.astype(BF16)
    mixed = (feat[1] * feat[2]).astype(BF16)
    m_part[...] = mm(e_own[...], jnp.concatenate([mixed, mixed], axis=0))
    grad = (moved * feat[0]).astype(BF16)
    g_part[...] = mm(e_own[...], jnp.concatenate([grad, grad], axis=0))


def finish_kernel(
    prev, later, feat, px, cots, m_part, g_part, k_spec, ends, starts, short, decay,
    e_prev, e_next, e_first, s_own, s_lags,
    product, grad, sums_out, filter_held, short_held, done,
):
    length, width = cots.shape
    span = length // 8
    edge = FK - 1
    step, steps = pl.program_id(0), pl.num_programs(0)
    row8 = lax.broadcasted_iota(jnp.int32, (8, width), 0)
    before = prev[...].astype(F32)
    after = later[...].astype(F32)
    prev8 = [before[128 + 8 * i : 136 + 8 * i] for i in range(3)]
    cot_next = after[136:144]
    next8 = [None, after[144:152], after[152:160]]
    ends8 = [ends[i].astype(F32)[8:] for i in range(3)]
    cot_first = starts[...].astype(F32)[:8]

    fixes = [conv8(prev8[i], None, short[i]) for i in range(3)]
    heads = []
    for i in range(3):
        rows, natural = [], jnp.zeros((8, width), F32)
        for r in range(edge):
            part = feat[i, 8 * r : 8 * r + 8, :]
            natural = natural + jnp.where(row8 == r, pltpu.roll(part, r, 0) if r else part, 0.0)
            moved = pltpu.roll(fixes[i], 8 - r, 0) if r else fixes[i]
            rows.append(part + jnp.where(row8 == 0, moved, 0.0))
        heads.append((jnp.concatenate(rows, axis=0), natural))
    features = lambda i: jnp.concatenate([heads[i][0], feat[i, edge * 8 :, :]], axis=0)
    inside = row8 < edge
    (first1, first2), (fix1, fix2) = (heads[1][1], heads[2][1]), fixes[1:]
    mixed_fix = jnp.where(inside, (first1 + fix1) * (first2 + fix2) - first1 * first2, 0.0)
    grad_fix = jnp.where(inside, cot_first * fixes[0], 0.0)

    feat_next = [None] + [conv8(ends8[i], next8[i], short[i]) for i in (1, 2)]
    fix = cot_next * conv8(ends8[0], None, short[0])
    rows = [after[8 * r : 8 * r + 8] for r in range(17)]
    for r in range(edge):
        rows[r] = rows[r] + jnp.where(row8 == 0, pltpu.roll(fix, (8 - r) % 8, 0), 0.0)
    grad_edge = jnp.concatenate(rows + [grad_fix], axis=0).astype(BF16)
    mixed_edge = jnp.concatenate([before[:128], feat_next[1] * feat_next[2], mixed_fix], axis=0).astype(BF16)
    grad_first = jnp.concatenate([grad_fix, jnp.zeros((8, width), F32)], axis=0).astype(BF16)

    m_spec = m_part[...] + mm(e_prev[...], mixed_edge)
    g_own = g_part[...] + mm(e_first[...], grad_first)
    g_spec = g_part[...] + mm(e_next[...], grad_edge)

    half = k_spec.shape[0] // 2
    parts = lambda value: (value[:half], value[half:])
    (kr, ki), (mr, mi), (gr, gi), (hr, hi) = parts(k_spec[...]), parts(m_spec), parts(g_spec), parts(g_own)

    def back_to(matrix, real, imaginary):
        spectrum = jnp.concatenate([real, imaginary], axis=0).astype(BF16)
        return mm(matrix[...], jnp.concatenate([spectrum, spectrum], axis=0))

    filtered = back_to(s_own, mr * kr - mi * ki, mr * ki + mi * kr)
    grad_mixed = back_to(s_own, gr * kr + gi * ki, gi * kr - gr * ki)
    filter_sums = back_to(s_lags, hr * mr + hi * mi, hi * mr - hr * mi)
    lags = lax.broadcasted_iota(jnp.int32, filter_sums.shape, 0).astype(F32)
    filter_sums = filter_sums * jnp.exp(-decay[...] * lags)

    own, back = filtered[:length], grad_mixed[:length]
    product[...] = (features(0) * own).astype(BF16)
    grad[0, :length] = cots[...].astype(F32) * own
    grad[1, :length] = back * features(2)
    grad[2, :length] = back * features(1)
    back_next = grad_mixed[length:]
    edge_next = [cot_next * filtered[length:], back_next * feat_next[2], back_next * feat_next[1]]
    for i in range(3):
        for k in range(edge):
            at = length + 8 * k
            moved = pltpu.roll(grad[i, 8 * k : 8 * k + 8, :], 7, 0)
            grad[i, at : at + 8, :] = jnp.where(row8 == 7, pltpu.roll(edge_next[i], 7 - k, 0), moved)

    short_rows = []
    chunk = 64
    for i in range(3):
        rows = [[] for _ in range(FK)]
        for at in range(0, width, 128):
            lane = slice(at, at + 128)
            sums = [jnp.zeros((8, 128), F32)] * FK
            for r in range(0, length, chunk):
                here = px[i, r : r + chunk, lane].astype(F32).reshape(chunk // 8, 8, 128)
                for lag in range(FK):
                    value = grad[i, r + 8 * lag : r + 8 * lag + chunk, lane].reshape(chunk // 8, 8, 128)
                    sums[lag] = sums[lag] + jnp.sum(here * value, axis=0)
            for lag in range(FK):
                rows[lag].append(jnp.sum(sums[lag], axis=0, keepdims=True))
        short_rows += [jnp.concatenate(row, axis=1) for row in rows]

    ranks, slot, _ = filter_held.shape
    per, share = filter_sums.shape[0] // ranks, short_held.shape[0]
    copies = [
        pltpu.make_async_copy(
            filter_held, sums_out.at[:, pl.ds(pl.multiple_of(step * slot, slot), slot), :], done.at[0]
        ),
        pltpu.make_async_copy(
            short_held,
            sums_out.at[pl.ds(step * share, share), pl.ds(sums_out.shape[1] - SHORT, SHORT), :],
            done.at[1],
        ),
    ]

    @pl.when(step > 0)
    def _():
        for copy in copies:
            copy.wait()

    if per % 8 == 0:
        by_rank = filter_sums.reshape(ranks, per, width)
    else:
        by_rank = jnp.stack([filter_sums[rank * per : rank * per + per] for rank in range(ranks)])
    if slot > per:
        by_rank = jnp.concatenate([by_rank, jnp.zeros((ranks, slot - per, width), F32)], axis=1)
    filter_held[...] = by_rank.astype(BF16)
    sums = jnp.concatenate(short_rows + [jnp.zeros((SHORT - len(short_rows), width), F32)], axis=0)
    for rank in range(share):
        held = pltpu.roll(sums, width - rank * (width // share), 1) if rank else sums
        short_held[rank] = held.astype(BF16)
    for copy in copies:
        copy.start()

    @pl.when(step == steps - 1)
    def _():
        for copy in copies:
            copy.wait()


def outputs_kernel(product, grad, short, p_out, gated, grad_proj):
    length, width = product.shape
    gated[...] = mm(p_out[...], product[...]).astype(BF16)
    chunk = 64
    for i in range(3):
        columns = []
        for at in range(0, width, 128):
            lane = slice(at, at + 128)
            weights = [jnp.broadcast_to(short[i, lag : lag + 1, lane], (8, 128)) for lag in range(FK)]
            chunks = []
            for r in range(0, length, chunk):
                total = jnp.zeros((chunk // 8, 8, 128), F32)
                for lag in range(FK):
                    value = grad[i, r + 8 * lag : r + 8 * lag + chunk, lane].reshape(chunk // 8, 8, 128)
                    total = total + weights[lag] * value
                chunks.append(total.reshape(chunk, 128))
            columns.append(jnp.concatenate(chunks, axis=0))
        result = jnp.concatenate(columns, axis=1).astype(BF16)
        grad_proj[i] = mm(p_out[...], result).astype(BF16)


def whole(array):
    return pl.BlockSpec(array.shape, lambda c: (0,) * array.ndim)


def columns(rows, width, first=0):
    lead = (0,) * len(rows)
    return pl.BlockSpec(tuple(rows) + (width,), lambda c: lead + (first + c,))


def call(kernel, name, operands, outputs, width, constants=(), cost=1, **options):
    spec = lambda rows: rows if isinstance(rows, pl.BlockSpec) else columns(rows, width)
    constants = [pltpu.with_memory_space_constraint(jnp.asarray(constant), pltpu.HBM) for constant in constants]
    operands = [
        (pltpu.with_memory_space_constraint(array, pltpu.HBM) if array.dtype == F32 else array, rows)
        for array, rows in operands
    ]
    return pl.pallas_call(
        kernel,
        grid=(operands[0][0].shape[-1] // width,),
        in_specs=[spec(rows) for _, rows in operands] + [whole(constant) for constant in constants],
        out_specs=[spec(rows) for _, rows in outputs],
        out_shape=[shape for shape, _ in outputs],
        compiler_params=pltpu.CompilerParams(vmem_limit_bytes=40 << 20),
        cost_estimate=pl.CostEstimate(flops=cost * 10**9, bytes_accessed=10**6, transcendentals=0),
        name=name,
        **options,
    )(*[array for array, _ in operands], *constants)


def squares_kernel(rows, share, sums, raw, payload):
    ranks, slots, width = sums.shape
    total = sums[0].astype(F32)
    for rank in range(1, ranks):
        total = total + sums[rank].astype(F32)
    slot = -(-rows // 16) * 16
    pieces = [total[at : at + rows] for at in range(0, slots - SHORT, slot)]
    raw[...] = jnp.concatenate(pieces, axis=1)
    lane = lax.broadcasted_iota(jnp.int32, (SHORT, width), 1)
    short = jnp.where(lane < share, total[slots - SHORT :], 0.0)
    squares = jnp.sum(short * short, keepdims=True)
    for piece in pieces:
        squares = squares + jnp.sum(piece * piece, keepdims=True)
    high = squares.astype(BF16).astype(F32)
    row = lax.broadcasted_iota(jnp.int32, (24, width), 0)
    block = jnp.where(row < 3 * FK, short[:24], jnp.where(row == 3 * FK, high, squares - high)).astype(BF16)
    for other in range(payload.shape[0]):
        payload[other] = block


def scale_kernel(entries, share, mine, raw, gathered, grad_short, grad_filter):
    everyone, rows, width = gathered.shape
    total = jnp.zeros((8, width), F32)
    for other in range(everyone):
        total = total + gathered[other].astype(F32)[16:]
    total = total[5:6, :1] + total[6:7, :1]
    scale = jnp.minimum(1.0, math.sqrt(entries) / jnp.sqrt(total))
    grad_filter[...] = scale * raw[...]
    step = mine[1]
    for rank in range(raw.shape[1] // share):
        block = gathered[rank * step + mine[0]].astype(F32) * scale
        for i in range(3):
            grad_short[i, :, rank * share : (rank + 1) * share] = block[i * FK : (i + 1) * FK, :share]


def shards(projected, short_taps, filter_taps, decay, cotangent):
    length, _, channels = projected.shape
    ranks, groups = lax.axis_size("seq"), lax.axis_size("ch")
    rows = filter_taps.shape[0]
    count = rows * ranks
    width = min(256, channels)
    share = channels // ranks
    slot = -(-rows // 16) * 16
    size, span = 2 * length, length // 8
    extended = length + 8 * (FK - 1)
    proj, cot, short, decay = (
        pltpu.with_memory_space_constraint(array, pltpu.HBM)
        for array in (jnp.transpose(projected, (1, 0, 2)), cotangent, short_taps, decay[None])
    )
    floats = lambda *shape: pltpu.HBM(shape + (channels,), F32)
    halves_of = lambda *shape: jax.ShapeDtypeStruct(shape + (channels,), BF16)
    own = interleaved(span)
    after = length + np.arange(8)

    forward, backward, spread = call(
        edges_kernel, "edges",
        [(proj, (3, length)), (cot, (length,)), (short, (3, FK)), (filter_taps, (rows,))],
        [
            (halves_of(152), (152,)), (halves_of(160), (160,)),
            (pltpu.HBM((ranks, rows, channels), BF16), (ranks, rows)),
        ],
        width, cost=3,
    )
    taps = lax.all_to_all(spread, "seq", 0, 0).reshape(count, channels)
    prev = from_behind(forward, "seq", 1)
    later = from_behind(backward, "seq", -1)

    e_high, e_low = analysis(own, size)
    k_high, k_low = analysis(np.arange(count), size)
    feat, px, cots, m_part, g_part, k_spec = call(
        own_kernel, "own",
        [(proj, (3, length)), (cot, (length,)), (short, (3, FK)), (taps, (count,)), (decay, (1,))],
        [
            (floats(3, length), (3, length)), (halves_of(3, length), (3, length)), (halves_of(length), (length,)),
            (floats(size), (size,)), (floats(size), (size,)), (floats(size), (size,)),
        ],
        width,
        [
            np.concatenate([e_high, e_low], axis=1), np.concatenate([k_high, k_low, k_high], axis=1),
            pick(interleaved(span, 0, 1 - FK), length),
        ],
        cost=10,
    )

    s_own = synthesis(np.concatenate([own, after]), size)
    s_lags = synthesis(np.arange(count), size)
    product, grad, sums = call(
        finish_kernel, "finish",
        [
            (prev, (152,)), (later, (160,)), (feat, (3, length)), (px, (3, length)), (cots, (length,)),
            (m_part, (size,)), (g_part, (size,)), (k_spec, (size,)),
            (proj, pl.BlockSpec((3, 16, width), lambda c: (0, length // 16 - 1, c))), (cot, (16,)),
            (short, (3, FK)), (decay, (1,)),
        ],
        [
            (halves_of(length), (length,)), (floats(3, extended), (3, extended)),
            (pltpu.HBM((ranks, channels // width * slot + SHORT, width), BF16), pl.BlockSpec(memory_space=pl.ANY)),
        ],
        width,
        [
            analysis(np.concatenate([interleaved(16, -128), after, np.arange(8)]), size)[0],
            analysis(np.concatenate([interleaved(17, length), np.arange(8)]), size)[0],
            analysis(np.arange(8), size, 8)[0],
            np.concatenate(list(s_own), axis=1), np.concatenate(list(s_lags), axis=1),
        ],
        cost=12,
        scratch_shapes=[
            pltpu.VMEM((ranks, slot, width), BF16),
            pltpu.VMEM((ranks * width // channels, SHORT, width), BF16),
            pltpu.SemaphoreType.DMA((2,)),
        ],
    )
    gated, grad_proj = call(
        outputs_kernel, "outputs",
        [(product, (length,)), (grad, (3, extended)), (short, (3, FK))],
        [(halves_of(length), (length,)), (halves_of(3, length), (3, length))],
        width, [pick(own, length).T], cost=8,
    )
    sums, gated, grad_proj = lax.optimization_barrier((lax.all_to_all(sums, "seq", 0, 0), gated, grad_proj))

    vmem = pl.BlockSpec(memory_space=pltpu.VMEM)
    raw, payload = pl.pallas_call(
        functools.partial(squares_kernel, rows, share),
        in_specs=[vmem],
        out_specs=[vmem] * 2,
        out_shape=[
            jax.ShapeDtypeStruct((rows, channels), F32),
            jax.ShapeDtypeStruct((ranks * groups, 24, width), BF16),
        ],
        compiler_params=pltpu.CompilerParams(vmem_limit_bytes=32 << 20),
        name="squares",
    )(sums)
    gathered = lax.all_to_all(payload, ("seq", "ch"), 0, 0)
    mine = jnp.stack([lax.axis_index("ch"), jnp.int32(groups)])
    entries = (rows * ranks + 3 * FK) * channels * groups
    grad_short, grad_filter = pl.pallas_call(
        functools.partial(scale_kernel, entries, share),
        in_specs=[pl.BlockSpec(memory_space=pltpu.SMEM), vmem, vmem],
        out_specs=[vmem] * 2,
        out_shape=[
            jax.ShapeDtypeStruct((3, FK, channels), F32),
            jax.ShapeDtypeStruct((rows, channels), F32),
        ],
        compiler_params=pltpu.CompilerParams(vmem_limit_bytes=32 << 20),
        name="scale",
    )(mine, raw, gathered)
    return (gated, jnp.transpose(grad_proj, (1, 0, 2)), grad_short, grad_filter)


def solution(mesh):
    placed = (P("seq", None, "ch"), P(None, None, "ch"), P("seq", "ch"), P("ch"), P("seq", "ch"))
    return jax.shard_map(
        shards,
        mesh=mesh,
        in_specs=placed,
        out_specs=(P("seq", "ch"), P("seq", None, "ch"), P(None, None, "ch"), P("seq", "ch")),
        check_vma=False,
    )
```

```python
import functools
import math

import jax
import jax.numpy as jnp
import ml_dtypes
import numpy as np
from jax import lax
from jax.experimental import pallas as pl
from jax.experimental.pallas import tpu as pltpu
from jax.sharding import PartitionSpec as P


FK = 7
BF16 = jnp.bfloat16
F32 = jnp.float32
CHUNKS = 2
SHORT = 32


def from_behind(value, axis, by):
    count = lax.axis_size(axis)
    pairs = [(i, i + by) for i in range(count) if 0 <= i + by < count]
    return lax.ppermute(value, axis, pairs)


def interleaved(span, first=0, low=0):
    return np.array([first + s * span + r for r in range(low, span) for s in range(8)])


def pick(positions, count):
    out = np.zeros((len(positions), count), np.float32)
    for row, at in enumerate(positions):
        if 0 <= at < count:
            out[row, at] = 1.0
    return out.astype(ml_dtypes.bfloat16)


def halves(matrix):
    high = matrix.astype(np.float32).astype(ml_dtypes.bfloat16)
    low = (matrix - high.astype(np.float64)).astype(np.float32).astype(ml_dtypes.bfloat16)
    return np.stack([high, low])


def analysis(positions, size, pad=0):
    freq = np.arange(size // 2)[:, None]
    angle = np.pi * (((2 * freq + 1) * np.asarray(positions)[None, :]) % (2 * size)) / size
    matrix = np.concatenate([np.cos(angle), -np.sin(angle)], axis=0)
    return halves(np.pad(matrix, ((0, 0), (0, pad))))


def synthesis(positions, size):
    freq = np.arange(size // 2)[None, :]
    angle = np.pi * (((2 * freq + 1) * np.asarray(positions)[:, None]) % (2 * size)) / size
    return halves(np.concatenate([np.cos(angle), -np.sin(angle)], axis=1) * (2.0 / size))


def mm(a, b):
    return jnp.dot(a, b, preferred_element_type=F32)


def picked(span, first, length):
    shape = ((span + FK - 1) * 8, length)
    row, column = (lax.broadcasted_iota(jnp.int32, shape, axis) for axis in (0, 1))
    position = first + (row & 7) * span + (row >> 3) - (FK - 1)
    return jnp.where(position == column, 1.0, 0.0).astype(BF16)


def edges_kernel(proj, cot, short, *refs):
    forward, backward = refs[-4:-2]
    p_tail, p_head = refs[-2:]
    length, width = cot.shape
    tail, head = 16, 17

    @pl.when(pl.program_id(0) == 0)
    def _():
        p_tail[...] = picked(tail, length - 128, length)
        p_head[...] = picked(head, 0, length)


    def conv(x, taps, count):
        x = x.reshape(-1, 8, width)
        total = taps[0:1] * x[FK - 1 : FK - 1 + count]
        for lag in range(1, FK):
            total = total + taps[lag : lag + 1] * x[FK - 1 - lag : FK - 1 - lag + count]
        return total

    mixed = conv(mm(p_tail[...], proj[1]), short[1], tail) * conv(mm(p_tail[...], proj[2]), short[2], tail)
    ends = [proj[i, length - 16 :, :].astype(F32)[8:] for i in range(3)]
    forward[...] = jnp.concatenate([mixed.reshape(tail * 8, width)] + ends, axis=0).astype(BF16)
    gate = conv(mm(p_head[...], proj[0]), short[0], head).reshape(head * 8, width)
    grad = gate * mm(p_head[(FK - 1) * 8 :, :], cot[...])
    starts = [ref[:16, :].astype(F32)[:8] for ref in (cot, proj.at[1], proj.at[2])]
    backward[...] = jnp.concatenate([grad] + starts, axis=0).astype(BF16)
    if len(refs) > 4:
        taps, spread = refs[:2]
        spread[...] = jnp.broadcast_to(taps[...].astype(BF16)[None], spread.shape)


def conv8(last, first, taps):
    row = lax.broadcasted_iota(jnp.int32, last.shape, 0)
    total = jnp.zeros(last.shape, F32) if first is None else taps[0:1] * first
    for lag in range(1, FK):
        rolled = 0.0 if first is None else pltpu.roll(first, lag, 0)
        total = total + taps[lag : lag + 1] * jnp.where(row < lag, pltpu.roll(last, lag, 0), rolled)
    return total


def own_kernel(proj, cot, short, e_own, p_in, feat, px, cots, m_part, g_part):
    length, width = cot.shape
    span = length // 8
    edge = FK - 1
    step = 8
    for i in range(3):
        x = mm(p_in[...], proj[i])
        px[i] = x[edge * 8 :].astype(BF16)
        x = x.reshape(span + edge, 8, width)
        for at in range(0, width, 128):
            lane = slice(at, at + 128)
            weights = [jnp.broadcast_to(short[i, lag : lag + 1, lane], (8, 128)) for lag in range(FK)]
            for r in range(0, span, step):
                total = weights[0] * x[r + edge : r + edge + step, :, lane]
                for lag in range(1, FK):
                    total = total + weights[lag] * x[r + edge - lag : r + edge - lag + step, :, lane]
                feat[i, r * 8 : (r + step) * 8, lane] = total.reshape(step * 8, 128)
    moved = mm(p_in[edge * 8 :, :], cot[...])
    cots[...] = moved.astype(BF16)
    mixed = (feat[1] * feat[2]).astype(BF16)
    m_part[...] = mm(e_own[...], jnp.concatenate([mixed, mixed], axis=0))
    grad = (moved * feat[0]).astype(BF16)
    g_part[...] = mm(e_own[...], jnp.concatenate([grad, grad], axis=0))


def finish_kernel(
    first, prev, later, feat, px, cots, m_part, g_part, taps, ends, starts, short, decay,
    e_prev, e_next, e_first, e_taps, s_own, s_lags, *refs,
):
    product, grad, sums_out, filter_held, short_held, done = refs[-6:]
    length, width = cots.shape
    span = length // 8
    edge = FK - 1
    step, steps = pl.program_id(0), pl.num_programs(0)
    row8 = lax.broadcasted_iota(jnp.int32, (8, width), 0)
    before = prev[...].astype(F32)
    after = later[...].astype(F32)
    prev8 = [before[128 + 8 * i : 136 + 8 * i] for i in range(3)]
    cot_next = after[136:144]
    next8 = [None, after[144:152], after[152:160]]
    ends8 = [ends[i].astype(F32)[8:] for i in range(3)]
    cot_first = starts[...].astype(F32)[:8]

    fixes = [conv8(prev8[i], None, short[i]) for i in range(3)]
    heads = []
    for i in range(3):
        rows, natural = [], jnp.zeros((8, width), F32)
        for r in range(edge):
            part = feat[i, 8 * r : 8 * r + 8, :]
            natural = natural + jnp.where(row8 == r, pltpu.roll(part, r, 0) if r else part, 0.0)
            moved = pltpu.roll(fixes[i], 8 - r, 0) if r else fixes[i]
            rows.append(part + jnp.where(row8 == 0, moved, 0.0))
        heads.append((jnp.concatenate(rows, axis=0), natural))
    features = lambda i: jnp.concatenate([heads[i][0], feat[i, edge * 8 :, :]], axis=0)
    inside = row8 < edge
    (first1, first2), (fix1, fix2) = (heads[1][1], heads[2][1]), fixes[1:]
    mixed_fix = jnp.where(inside, (first1 + fix1) * (first2 + fix2) - first1 * first2, 0.0)
    grad_fix = jnp.where(inside, cot_first * fixes[0], 0.0)

    feat_next = [None] + [conv8(ends8[i], next8[i], short[i]) for i in (1, 2)]
    fix = cot_next * conv8(ends8[0], None, short[0])
    rows = [after[8 * r : 8 * r + 8] for r in range(17)]
    for r in range(edge):
        rows[r] = rows[r] + jnp.where(row8 == 0, pltpu.roll(fix, (8 - r) % 8, 0), 0.0)
    grad_edge = jnp.concatenate(rows + [grad_fix], axis=0).astype(BF16)
    mixed_edge = jnp.concatenate([before[:128], feat_next[1] * feat_next[2], mixed_fix], axis=0).astype(BF16)
    grad_first = jnp.concatenate([grad_fix, jnp.zeros((8, width), F32)], axis=0).astype(BF16)

    m_spec = m_part[...] + mm(e_prev[...], mixed_edge)
    g_own = g_part[...] + mm(e_first[...], grad_first)
    g_spec = g_part[...] + mm(e_next[...], grad_edge)

    lags = lax.broadcasted_iota(jnp.int32, (taps.shape[0], width), 0).astype(F32)
    falloff = jnp.exp(-decay[...] * lags)
    kernel = taps[...].astype(F32) * falloff
    high = kernel.astype(BF16)
    low = (kernel - high.astype(F32)).astype(BF16)
    k_spec = mm(e_taps[...], jnp.concatenate([high, high, low], axis=0))

    half = k_spec.shape[0] // 2
    parts = lambda value: (value[:half], value[half:])
    (kr, ki), (mr, mi), (gr, gi), (hr, hi) = parts(k_spec), parts(m_spec), parts(g_spec), parts(g_own)

    def back_to(matrix, real, imaginary):
        spectrum = jnp.concatenate([real, imaginary], axis=0).astype(BF16)
        return mm(matrix[...], jnp.concatenate([spectrum, spectrum], axis=0))

    filtered = back_to(s_own, mr * kr - mi * ki, mr * ki + mi * kr)
    grad_mixed = back_to(s_own, gr * kr + gi * ki, gi * kr - gr * ki)
    filter_sums = back_to(s_lags, hr * mr + hi * mi, hi * mr - hr * mi) * falloff

    own, back = filtered[:length], grad_mixed[:length]
    product[...] = (features(0) * own).astype(BF16)
    grad[0, :length] = cots[...].astype(F32) * own
    grad[1, :length] = back * features(2)
    grad[2, :length] = back * features(1)
    back_next = grad_mixed[length:]
    edge_next = [cot_next * filtered[length:], back_next * feat_next[2], back_next * feat_next[1]]
    for i in range(3):
        for k in range(edge):
            at = length + 8 * k
            moved = pltpu.roll(grad[i, 8 * k : 8 * k + 8, :], 7, 0)
            grad[i, at : at + 8, :] = jnp.where(row8 == 7, pltpu.roll(edge_next[i], 7 - k, 0), moved)

    short_rows = []
    chunk = 64
    for i in range(3):
        rows = [[] for _ in range(FK)]
        for at in range(0, width, 128):
            lane = slice(at, at + 128)
            sums = [jnp.zeros((8, 128), F32)] * FK
            for r in range(0, length, chunk):
                here = px[i, r : r + chunk, lane].astype(F32).reshape(chunk // 8, 8, 128)
                for lag in range(FK):
                    value = grad[i, r + 8 * lag : r + 8 * lag + chunk, lane].reshape(chunk // 8, 8, 128)
                    sums[lag] = sums[lag] + jnp.sum(here * value, axis=0)
            for lag in range(FK):
                rows[lag].append(jnp.sum(sums[lag], axis=0, keepdims=True))
        short_rows += [jnp.concatenate(row, axis=1) for row in rows]

    ranks, slot, _ = filter_held.shape
    per, share, block = filter_sums.shape[0] // ranks, short_held.shape[0], first + step
    copies = [
        pltpu.make_async_copy(
            filter_held, sums_out.at[:, pl.ds(pl.multiple_of(block * slot, slot), slot), :], done.at[0]
        ),
        pltpu.make_async_copy(
            short_held,
            sums_out.at[pl.ds(block * share, share), pl.ds(sums_out.shape[1] - SHORT, SHORT), :],
            done.at[1],
        ),
    ]

    @pl.when(step > 0)
    def _():
        for copy in copies:
            copy.wait()

    if per % 8 == 0:
        by_rank = filter_sums.reshape(ranks, per, width)
    else:
        by_rank = jnp.stack([filter_sums[rank * per : rank * per + per] for rank in range(ranks)])
    if slot > per:
        by_rank = jnp.concatenate([by_rank, jnp.zeros((ranks, slot - per, width), F32)], axis=1)
    filter_held[...] = by_rank.astype(BF16)
    sums = jnp.concatenate(short_rows + [jnp.zeros((SHORT - len(short_rows), width), F32)], axis=0)
    for rank in range(share):
        held = pltpu.roll(sums, width - rank * (width // share), 1) if rank else sums
        short_held[rank] = held.astype(BF16)
    for copy in copies:
        copy.start()

    @pl.when(step == steps - 1)
    def _():
        for copy in copies:
            copy.wait()


def outputs_kernel(product, grad, short, p_out, gated, grad_proj):
    length, width = product.shape
    gated[...] = mm(p_out[...], product[...]).astype(BF16)
    chunk = 64
    for i in range(3):
        columns = []
        for at in range(0, width, 128):
            lane = slice(at, at + 128)
            weights = [jnp.broadcast_to(short[i, lag : lag + 1, lane], (8, 128)) for lag in range(FK)]
            chunks = []
            for r in range(0, length, chunk):
                total = jnp.zeros((chunk // 8, 8, 128), F32)
                for lag in range(FK):
                    value = grad[i, r + 8 * lag : r + 8 * lag + chunk, lane].reshape(chunk // 8, 8, 128)
                    total = total + weights[lag] * value
                chunks.append(total.reshape(chunk, 128))
            columns.append(jnp.concatenate(chunks, axis=0))
        result = jnp.concatenate(columns, axis=1).astype(BF16)
        grad_proj[i] = mm(p_out[...], result).astype(BF16)


def whole(array):
    return pl.BlockSpec(array.shape, lambda c: (0,) * array.ndim)


def columns(rows, width, first=0):
    lead = (0,) * len(rows)
    return pl.BlockSpec(tuple(rows) + (width,), lambda c: lead + (first + c,))


def call(kernel, name, operands, outputs, width, constants=(), cost=1, first=0, blocks=None, held=(), **options):
    spec = lambda rows: rows if isinstance(rows, pl.BlockSpec) else columns(rows, width, first)
    aliases = {len(operands) + len(constants) + at: at for at in range(len(held))}
    constants = [pltpu.with_memory_space_constraint(jnp.asarray(constant), pltpu.HBM) for constant in constants]
    operands = [
        (pltpu.with_memory_space_constraint(array, pltpu.HBM) if array.dtype == F32 else array, rows)
        for array, rows in operands
    ]
    return pl.pallas_call(
        kernel,
        grid=(blocks or operands[0][0].shape[-1] // width,),
        in_specs=[spec(rows) for _, rows in operands] + [whole(constant) for constant in constants]
        + [pl.BlockSpec(memory_space=pl.ANY)] * len(held),
        out_specs=[spec(rows) for _, rows in outputs],
        out_shape=[shape for shape, _ in outputs],
        compiler_params=pltpu.CompilerParams(vmem_limit_bytes=40 << 20),
        cost_estimate=pl.CostEstimate(flops=cost * 10**9, bytes_accessed=10**6, transcendentals=0),
        input_output_aliases=aliases,
        name=name,
        **options,
    )(*[array for array, _ in operands], *constants, *held)


def squares_kernel(rows, share, sums, raw, payload):
    ranks, slots, width = sums.shape
    total = sums[0].astype(F32)
    for rank in range(1, ranks):
        total = total + sums[rank].astype(F32)
    slot = -(-rows // 16) * 16
    pieces = [total[at : at + rows] for at in range(0, slots - SHORT, slot)]
    raw[...] = jnp.concatenate(pieces, axis=1)
    lane = lax.broadcasted_iota(jnp.int32, (SHORT, width), 1)
    short = jnp.where(lane < share, total[slots - SHORT :], 0.0)
    squares = jnp.sum(short * short, keepdims=True)
    for piece in pieces:
        squares = squares + jnp.sum(piece * piece, keepdims=True)
    high = squares.astype(BF16).astype(F32)
    row = lax.broadcasted_iota(jnp.int32, (24, width), 0)
    block = jnp.where(row < 3 * FK, short[:24], jnp.where(row == 3 * FK, high, squares - high)).astype(BF16)
    for other in range(payload.shape[0]):
        payload[other] = block


def scale_kernel(entries, share, mine, raw, gathered, grad_short, grad_filter):
    everyone, rows, width = gathered.shape
    total = jnp.zeros((8, width), F32)
    for other in range(everyone):
        total = total + gathered[other].astype(F32)[16:]
    total = total[5:6, :1] + total[6:7, :1]
    scale = jnp.minimum(1.0, math.sqrt(entries) / jnp.sqrt(total))
    grad_filter[...] = scale * raw[...]
    step = mine[1]
    for rank in range(raw.shape[1] // share):
        block = gathered[rank * step + mine[0]].astype(F32) * scale
        for i in range(3):
            grad_short[i, :, rank * share : (rank + 1) * share] = block[i * FK : (i + 1) * FK, :share]


def shards(projected, short_taps, filter_taps, decay, cotangent):
    length, _, channels = projected.shape
    ranks, groups = lax.axis_size("seq"), lax.axis_size("ch")
    rows = filter_taps.shape[0]
    count = rows * ranks
    width = min(256, channels // CHUNKS)
    share = channels // ranks
    slot = -(-rows // 16) * 16
    size, span = 2 * length, length // 8
    extended = length + 8 * (FK - 1)
    proj, cot, short, decay = (
        pltpu.with_memory_space_constraint(array, pltpu.HBM)
        for array in (jnp.transpose(projected, (1, 0, 2)), cotangent, short_taps, decay[None])
    )
    floats = lambda *shape: pltpu.HBM(shape + (channels,), F32)
    halves_of = lambda *shape: jax.ShapeDtypeStruct(shape + (channels,), BF16)
    own = interleaved(span)
    after = length + np.arange(8)

    blocks = channels // width // CHUNKS
    prev, later, taps = [], [], None
    for k in range(CHUNKS):
        operands = [(proj, (3, length)), (cot, (length,)), (short, (3, FK))]
        results = [
            (jax.ShapeDtypeStruct((count, blocks * width), BF16), columns((count,), width)) for count in (152, 160)
        ]
        if k == 0:
            operands.append((filter_taps, columns((rows,), channels // blocks)))
            results.insert(0, (pltpu.HBM((ranks, rows, channels), BF16), columns((ranks, rows), channels // blocks)))
        *spread, forward, backward = call(
            edges_kernel, "edges", operands, results, width, cost=1, first=k * blocks, blocks=blocks,
            scratch_shapes=[pltpu.VMEM(((at + FK - 1) * 8, length), BF16) for at in (16, 17)],
        )
        if k == 0:
            taps = lax.all_to_all(spread[0], "seq", 0, 0).reshape(count, channels)
        else:
            forward, backward, prev[-1], later[-1] = lax.optimization_barrier((forward, backward, prev[-1], later[-1]))
        prev.append(from_behind(forward, "seq", 1))
        later.append(from_behind(backward, "seq", -1))

    feat, px, cots, m_part, g_part = call(
        own_kernel, "own",
        [(proj, (3, length)), (cot, (length,)), (short, (3, FK))],
        [
            (floats(3, length), (3, length)), (halves_of(3, length), (3, length)), (halves_of(length), (length,)),
            (floats(size), (size,)), (floats(size), (size,)),
        ],
        width,
        [np.concatenate(list(analysis(own, size)), axis=1), pick(interleaved(span, 0, 1 - FK), length)],
        cost=10,
    )

    k_high, k_low = analysis(np.arange(count), size)
    constants = [
        analysis(np.concatenate([interleaved(16, -128), after, np.arange(8)]), size)[0],
        analysis(np.concatenate([interleaved(17, length), np.arange(8)]), size)[0],
        analysis(np.arange(8), size, 8)[0],
        np.concatenate([k_high, k_low, k_high], axis=1),
        np.concatenate(list(synthesis(np.concatenate([own, after]), size)), axis=1),
        np.concatenate(list(synthesis(np.arange(count), size)), axis=1),
    ]
    held = ()
    for k in range(CHUNKS):
        first = k * blocks
        held = call(
            functools.partial(finish_kernel, first), "finish",
            [
                (prev[k], columns((152,), width)), (later[k], columns((160,), width)), (feat, (3, length)),
                (px, (3, length)), (cots, (length,)), (m_part, (size,)), (g_part, (size,)), (taps, (count,)),
                (proj, pl.BlockSpec((3, 16, width), lambda c, first=first: (0, length // 16 - 1, first + c))),
                (cot, (16,)), (short, (3, FK)), (decay, (1,)),
            ],
            [
                (halves_of(length), (length,)), (floats(3, extended), (3, extended)),
                (
                    pltpu.HBM((ranks, channels // width * slot + SHORT, width), BF16),
                    pl.BlockSpec(memory_space=pl.ANY),
                ),
            ],
            width, constants, cost=6, first=first, blocks=blocks, held=held,
            scratch_shapes=[
                pltpu.VMEM((ranks, slot, width), BF16),
                pltpu.VMEM((ranks * width // channels, SHORT, width), BF16),
                pltpu.SemaphoreType.DMA((2,)),
            ],
        )
    product, grad, sums = held
    gated, grad_proj = call(
        outputs_kernel, "outputs",
        [(product, (length,)), (grad, (3, extended)), (short, (3, FK))],
        [(halves_of(length), (length,)), (halves_of(3, length), (3, length))],
        width, [pick(own, length).T], cost=8,
    )
    sums, gated, grad_proj = lax.optimization_barrier((lax.all_to_all(sums, "seq", 0, 0), gated, grad_proj))

    vmem = pl.BlockSpec(memory_space=pltpu.VMEM)
    raw, payload = pl.pallas_call(
        functools.partial(squares_kernel, rows, share),
        in_specs=[vmem],
        out_specs=[vmem] * 2,
        out_shape=[
            jax.ShapeDtypeStruct((rows, channels), F32),
            jax.ShapeDtypeStruct((ranks * groups, 24, width), BF16),
        ],
        compiler_params=pltpu.CompilerParams(vmem_limit_bytes=32 << 20),
        name="squares",
    )(sums)
    gathered = lax.all_to_all(payload, ("seq", "ch"), 0, 0)
    mine = jnp.stack([lax.axis_index("ch"), jnp.int32(groups)])
    entries = (rows * ranks + 3 * FK) * channels * groups
    grad_short, grad_filter = pl.pallas_call(
        functools.partial(scale_kernel, entries, share),
        in_specs=[pl.BlockSpec(memory_space=pltpu.SMEM), vmem, vmem],
        out_specs=[vmem] * 2,
        out_shape=[
            jax.ShapeDtypeStruct((3, FK, channels), F32),
            jax.ShapeDtypeStruct((rows, channels), F32),
        ],
        compiler_params=pltpu.CompilerParams(vmem_limit_bytes=32 << 20),
        name="scale",
    )(mine, raw, gathered)
    return (gated, jnp.transpose(grad_proj, (1, 0, 2)), grad_short, grad_filter)


def solution(mesh):
    placed = (P("seq", None, "ch"), P(None, None, "ch"), P("seq", "ch"), P("ch"), P("seq", "ch"))
    return jax.shard_map(
        shards,
        mesh=mesh,
        in_specs=placed,
        out_specs=(P("seq", "ch"), P("seq", None, "ch"), P(None, None, "ch"), P("seq", "ch")),
        check_vma=False,
    )
```

```python
import functools
import math

import jax
import jax.numpy as jnp
import ml_dtypes
import numpy as np
from jax import lax
from jax.experimental import pallas as pl
from jax.experimental.pallas import tpu as pltpu
from jax.sharding import PartitionSpec as P


FK = 7
BF16 = jnp.bfloat16
F32 = jnp.float32
CHUNKS = 1
SHORT = 32
STEP = 64


def from_behind(value, axis, by):
    count = lax.axis_size(axis)
    pairs = [(i, i + by) for i in range(count) if 0 <= i + by < count]
    return lax.ppermute(value, axis, pairs)


def interleaved(span, first=0, low=0):
    return np.array([first + s * span + r for r in range(low, span) for s in range(8)])


def pick(positions, count):
    out = np.zeros((len(positions), count), np.float32)
    for row, at in enumerate(positions):
        if 0 <= at < count:
            out[row, at] = 1.0
    return out.astype(ml_dtypes.bfloat16)


def halves(matrix):
    high = matrix.astype(np.float32).astype(ml_dtypes.bfloat16)
    low = (matrix - high.astype(np.float64)).astype(np.float32).astype(ml_dtypes.bfloat16)
    return np.stack([high, low])


def analysis(positions, size, pad=0):
    freq = np.arange(size // 2)[:, None]
    angle = np.pi * (((2 * freq + 1) * np.asarray(positions)[None, :]) % (2 * size)) / size
    matrix = np.concatenate([np.cos(angle), -np.sin(angle)], axis=0)
    return halves(np.pad(matrix, ((0, 0), (0, pad))))


def synthesis(positions, size):
    freq = np.arange(size // 2)[None, :]
    angle = np.pi * (((2 * freq + 1) * np.asarray(positions)[:, None]) % (2 * size)) / size
    return halves(np.concatenate([np.cos(angle), -np.sin(angle)], axis=1) * (2.0 / size))


def mm(a, b):
    return jnp.dot(a, b, preferred_element_type=F32)


def picked(span, first, length):
    shape = ((span + FK - 1) * 8, length)
    row, column = (lax.broadcasted_iota(jnp.int32, shape, axis) for axis in (0, 1))
    position = first + (row & 7) * span + (row >> 3) - (FK - 1)
    return jnp.where(position == column, 1.0, 0.0).astype(BF16)


def lanes_of(width):
    return [slice(at, at + 128) for at in range(0, width, 128)]


def featurized(x, taps, lane, row, rows):
    total = None
    for lag in range(FK):
        at = row + 8 * (FK - 1 - lag)
        part = x[at : at + rows, lane].reshape(rows // 8, 8, 128) * taps[lag]
        total = part if total is None else total + part
    return total


def spread_taps(short, i, lane):
    return [jnp.broadcast_to(short[i, lag : lag + 1, lane], (8, 128)) for lag in range(FK)]


def edges_kernel(proj, cot, short, *refs):
    forward, backward = refs[-8:-6]
    p_tail, p_head, first, second, zeroth, held = refs[-6:]
    length, width = cot.shape
    tail, head = 16, 17

    @pl.when(pl.program_id(0) == 0)
    def _():
        p_tail[...] = picked(tail, length - 128, length)
        p_head[...] = picked(head, 0, length)

    first[...] = mm(p_tail[...], proj[1])
    second[...] = mm(p_tail[...], proj[2])
    zeroth[...] = mm(p_head[...], proj[0])
    held[...] = mm(p_head[(FK - 1) * 8 :, :], cot[...])
    for lane in lanes_of(width):
        taps = [spread_taps(short, i, lane) for i in range(3)]
        for r in range(0, 8 * tail, STEP):
            mixed = featurized(first, taps[1], lane, r, STEP) * featurized(second, taps[2], lane, r, STEP)
            forward[r : r + STEP, lane] = mixed.reshape(STEP, 128).astype(BF16)
        for r in range(0, 8 * head, STEP):
            rows = min(STEP, 8 * head - r)
            grad = featurized(zeroth, taps[0], lane, r, rows).reshape(rows, 128) * held[r : r + rows, lane]
            if rows < STEP:
                starts = [ref[:16, lane].astype(F32)[:8] for ref in (cot, proj.at[1], proj.at[2])]
                backward[r:, lane] = jnp.concatenate([grad] + starts, axis=0).astype(BF16)
            else:
                backward[r : r + rows, lane] = grad.astype(BF16)
    ends = [proj[i, length - 16 :, :].astype(F32)[8:] for i in range(3)]
    forward[8 * tail :, :] = jnp.concatenate(ends, axis=0).astype(BF16)
    if len(refs) > 8:
        taps, spread = refs[:2]
        spread[...] = jnp.broadcast_to(taps[...].astype(BF16)[None], spread.shape)


def conv8(last, first, taps):
    row = lax.broadcasted_iota(jnp.int32, last.shape, 0)
    total = jnp.zeros(last.shape, F32) if first is None else taps[0:1] * first
    for lag in range(1, FK):
        rolled = 0.0 if first is None else pltpu.roll(first, lag, 0)
        total = total + taps[lag : lag + 1] * jnp.where(row < lag, pltpu.roll(last, lag, 0), rolled)
    return total


def own_kernel(proj, cot, short, e_own, p_in, feat, px, cots, m_part, g_part, x, moved, mixed, grads):
    length, width = cot.shape
    edge = FK - 1
    for i in range(3):
        x[i] = mm(p_in[...], proj[i])
    moved[...] = mm(p_in[edge * 8 :, :], cot[...])
    for lane in lanes_of(width):
        taps = [spread_taps(short, i, lane) for i in range(3)]
        for r in range(0, length, STEP):
            rows = slice(r, r + STEP)
            parts = []
            for i in range(3):
                px[i, rows, lane] = x[i, r + 8 * edge : r + 8 * edge + STEP, lane].astype(BF16)
                part = featurized(x.at[i], taps[i], lane, r, STEP).reshape(STEP, 128)
                feat[i, rows, lane] = part
                parts.append(part)
            here = moved[rows, lane]
            cots[rows, lane] = here.astype(BF16)
            mixed[rows, lane] = (parts[1] * parts[2]).astype(BF16)
            grads[rows, lane] = (here * parts[0]).astype(BF16)
    for out, value in ((m_part, mixed), (g_part, grads)):
        value = value[...]
        out[...] = mm(e_own[...], jnp.concatenate([value, value], axis=0))


def finish_kernel(
    first, prev, later, feat, px, cots, m_part, g_part, taps, ends, starts, short, decay,
    e_prev, e_next, e_first, e_taps, s_own, s_lags, *refs,
):
    product, grad, sums_out, filter_held, short_held, done = refs[-17:-11]
    fixed, ms, gs, hs, ks, ys, zs, cs, filtered, grad_mixed, decays = refs[-11:]
    length, width = cots.shape
    span = length // 8
    edge = FK - 1
    step, steps = pl.program_id(0), pl.num_programs(0)
    row8 = lax.broadcasted_iota(jnp.int32, (8, width), 0)
    before = prev[...].astype(F32)
    after = later[...].astype(F32)
    prev8 = [before[128 + 8 * i : 136 + 8 * i] for i in range(3)]
    cot_next = after[136:144]
    next8 = [None, after[144:152], after[152:160]]
    ends8 = [ends[i].astype(F32)[8:] for i in range(3)]
    cot_first = starts[...].astype(F32)[:8]

    fixes = [conv8(prev8[i], None, short[i]) for i in range(3)]
    heads = []
    for i in range(3):
        rows, natural = [], jnp.zeros((8, width), F32)
        for r in range(edge):
            part = feat[i, 8 * r : 8 * r + 8, :]
            natural = natural + jnp.where(row8 == r, pltpu.roll(part, r, 0) if r else part, 0.0)
            moved = pltpu.roll(fixes[i], 8 - r, 0) if r else fixes[i]
            rows.append(part + jnp.where(row8 == 0, moved, 0.0))
        heads.append((jnp.concatenate(rows, axis=0), natural))
    for i in range(3):
        fixed[i, : 8 * edge] = heads[i][0]
        fixed[i, 8 * edge :] = feat[i, 8 * edge : STEP, :]
    inside = row8 < edge
    (first1, first2), (fix1, fix2) = (heads[1][1], heads[2][1]), fixes[1:]
    mixed_fix = jnp.where(inside, (first1 + fix1) * (first2 + fix2) - first1 * first2, 0.0)
    grad_fix = jnp.where(inside, cot_first * fixes[0], 0.0)

    feat_next = [None] + [conv8(ends8[i], next8[i], short[i]) for i in (1, 2)]
    fix = cot_next * conv8(ends8[0], None, short[0])
    rows = [after[8 * r : 8 * r + 8] for r in range(17)]
    for r in range(edge):
        rows[r] = rows[r] + jnp.where(row8 == 0, pltpu.roll(fix, (8 - r) % 8, 0), 0.0)
    grad_edge = jnp.concatenate(rows + [grad_fix], axis=0).astype(BF16)
    mixed_edge = jnp.concatenate([before[:128], feat_next[1] * feat_next[2], mixed_fix], axis=0).astype(BF16)
    grad_first = jnp.concatenate([grad_fix, jnp.zeros((8, width), F32)], axis=0).astype(BF16)

    ms[...] = mm(e_prev[...], mixed_edge)
    hs[...] = mm(e_first[...], grad_first)
    gs[...] = mm(e_next[...], grad_edge)
    lags = lax.broadcasted_iota(jnp.int32, (taps.shape[0], width), 0).astype(F32)
    decays[...] = jnp.exp(-decay[...] * lags)
    kernel = taps[...].astype(F32) * decays[...]
    high = kernel.astype(BF16)
    low = (kernel - high.astype(F32)).astype(BF16)
    ks[...] = mm(e_taps[...], jnp.concatenate([high, high, low], axis=0))

    half = ks.shape[0] // 2
    for lane in lanes_of(width):
        for f in range(0, half, 32):
            real, imag = slice(f, f + 32), slice(half + f, half + f + 32)
            kr, ki = ks[real, lane], ks[imag, lane]
            mr, mi = m_part[real, lane] + ms[real, lane], m_part[imag, lane] + ms[imag, lane]
            ys[real, lane] = (mr * kr - mi * ki).astype(BF16)
            ys[imag, lane] = (mr * ki + mi * kr).astype(BF16)
            pr, pi = g_part[real, lane], g_part[imag, lane]
            hr, hi = pr + hs[real, lane], pi + hs[imag, lane]
            cs[real, lane] = (hr * mr + hi * mi).astype(BF16)
            cs[imag, lane] = (hi * mr - hr * mi).astype(BF16)
            gr, gi = pr + gs[real, lane], pi + gs[imag, lane]
            zs[real, lane] = (gr * kr + gi * ki).astype(BF16)
            zs[imag, lane] = (gi * kr - gr * ki).astype(BF16)

    def back_to(matrix, spectrum):
        spectrum = spectrum[...]
        return mm(matrix[...], jnp.concatenate([spectrum, spectrum], axis=0))

    filtered[...] = back_to(s_own, ys)
    grad_mixed[...] = back_to(s_own, zs)
    filter_sums = back_to(s_lags, cs) * decays[...]

    for lane in lanes_of(width):
        for r in range(0, length, STEP):
            rows = slice(r, r + STEP)
            features = [fixed[i, :, lane] if r == 0 else feat[i, rows, lane] for i in range(3)]
            own, back = filtered[rows, lane], grad_mixed[rows, lane]
            product[rows, lane] = (features[0] * own).astype(BF16)
            grad[0, rows, lane] = cots[rows, lane].astype(F32) * own
            grad[1, rows, lane] = back * features[2]
            grad[2, rows, lane] = back * features[1]
    own_next, back_next = filtered[length:, :], grad_mixed[length:, :]
    edge_next = [cot_next * own_next, back_next * feat_next[2], back_next * feat_next[1]]
    for i in range(3):
        for k in range(edge):
            at = length + 8 * k
            moved = pltpu.roll(grad[i, 8 * k : 8 * k + 8, :], 7, 0)
            grad[i, at : at + 8, :] = jnp.where(row8 == 7, pltpu.roll(edge_next[i], 7 - k, 0), moved)

    short_rows = []
    chunk = 64
    for i in range(3):
        rows = [[] for _ in range(FK)]
        for at in range(0, width, 128):
            lane = slice(at, at + 128)
            sums = [jnp.zeros((8, 128), F32)] * FK
            for r in range(0, length, chunk):
                here = px[i, r : r + chunk, lane].astype(F32).reshape(chunk // 8, 8, 128)
                for lag in range(FK):
                    value = grad[i, r + 8 * lag : r + 8 * lag + chunk, lane].reshape(chunk // 8, 8, 128)
                    sums[lag] = sums[lag] + jnp.sum(here * value, axis=0)
            for lag in range(FK):
                rows[lag].append(jnp.sum(sums[lag], axis=0, keepdims=True))
        short_rows += [jnp.concatenate(row, axis=1) for row in rows]

    ranks, slot, _ = filter_held.shape
    per, share, block = filter_sums.shape[0] // ranks, short_held.shape[0], first + step
    copies = [
        pltpu.make_async_copy(
            filter_held, sums_out.at[:, pl.ds(pl.multiple_of(block * slot, slot), slot), :], done.at[0]
        ),
        pltpu.make_async_copy(
            short_held,
            sums_out.at[pl.ds(block * share, share), pl.ds(sums_out.shape[1] - SHORT, SHORT), :],
            done.at[1],
        ),
    ]

    @pl.when(step > 0)
    def _():
        for copy in copies:
            copy.wait()

    if per % 8 == 0:
        by_rank = filter_sums.reshape(ranks, per, width)
    else:
        by_rank = jnp.stack([filter_sums[rank * per : rank * per + per] for rank in range(ranks)])
    if slot > per:
        by_rank = jnp.concatenate([by_rank, jnp.zeros((ranks, slot - per, width), F32)], axis=1)
    filter_held[...] = by_rank.astype(BF16)
    sums = jnp.concatenate(short_rows + [jnp.zeros((SHORT - len(short_rows), width), F32)], axis=0)
    for rank in range(share):
        held = pltpu.roll(sums, width - rank * (width // share), 1) if rank else sums
        short_held[rank] = held.astype(BF16)
    for copy in copies:
        copy.start()

    @pl.when(step == steps - 1)
    def _():
        for copy in copies:
            copy.wait()


def outputs_kernel(product, grad, short, p_out, gated, grad_proj, held):
    length, width = product.shape
    gated[...] = mm(p_out[...], product[...]).astype(BF16)
    for i in range(3):
        for lane in lanes_of(width):
            taps = spread_taps(short, i, lane)
            for r in range(0, length, STEP):
                total = None
                for lag in range(FK):
                    part = grad[i, r + 8 * lag : r + 8 * lag + STEP, lane].reshape(STEP // 8, 8, 128) * taps[lag]
                    total = part if total is None else total + part
                held[i, r : r + STEP, lane] = total.reshape(STEP, 128).astype(BF16)
        grad_proj[i] = mm(p_out[...], held[i]).astype(BF16)


def whole(array):
    return pl.BlockSpec(array.shape, lambda c: (0,) * array.ndim)


def columns(rows, width, first=0):
    lead = (0,) * len(rows)
    return pl.BlockSpec(tuple(rows) + (width,), lambda c: lead + (first + c,))


def call(kernel, name, operands, outputs, width, constants=(), cost=1, first=0, blocks=None, held=(), **options):
    spec = lambda rows: rows if isinstance(rows, pl.BlockSpec) else columns(rows, width, first)
    aliases = {len(operands) + len(constants) + at: at for at in range(len(held))}
    constants = [pltpu.with_memory_space_constraint(jnp.asarray(constant), pltpu.HBM) for constant in constants]
    operands = [
        (array if isinstance(rows, pl.BlockSpec) else pltpu.with_memory_space_constraint(array, pltpu.HBM), rows)
        for array, rows in operands
    ]
    return pl.pallas_call(
        kernel,
        grid=(blocks or operands[0][0].shape[-1] // width,),
        in_specs=[spec(rows) for _, rows in operands] + [whole(constant) for constant in constants]
        + [pl.BlockSpec(memory_space=pl.ANY)] * len(held),
        out_specs=[spec(rows) for _, rows in outputs],
        out_shape=[shape for shape, _ in outputs],
        compiler_params=pltpu.CompilerParams(vmem_limit_bytes=40 << 20),
        cost_estimate=pl.CostEstimate(flops=cost * 10**9, bytes_accessed=10**6, transcendentals=0),
        input_output_aliases=aliases,
        name=name,
        **options,
    )(*[array for array, _ in operands], *constants, *held)


def squares_kernel(rows, share, sums, raw, payload):
    ranks, slots, width = sums.shape
    total = sums[0].astype(F32)
    for rank in range(1, ranks):
        total = total + sums[rank].astype(F32)
    slot = -(-rows // 16) * 16
    pieces = [total[at : at + rows] for at in range(0, slots - SHORT, slot)]
    raw[...] = jnp.concatenate(pieces, axis=1)
    lane = lax.broadcasted_iota(jnp.int32, (SHORT, width), 1)
    short = jnp.where(lane < share, total[slots - SHORT :], 0.0)
    squares = jnp.sum(short * short, keepdims=True)
    for piece in pieces:
        squares = squares + jnp.sum(piece * piece, keepdims=True)
    high = squares.astype(BF16).astype(F32)
    row = lax.broadcasted_iota(jnp.int32, (24, width), 0)
    block = jnp.where(row < 3 * FK, short[:24], jnp.where(row == 3 * FK, high, squares - high)).astype(BF16)
    for other in range(payload.shape[0]):
        payload[other] = block


def scale_kernel(entries, share, mine, raw, gathered, grad_short, grad_filter):
    everyone, rows, width = gathered.shape
    total = jnp.zeros((8, width), F32)
    for other in range(everyone):
        total = total + gathered[other].astype(F32)[16:]
    total = total[5:6, :1] + total[6:7, :1]
    scale = jnp.minimum(1.0, math.sqrt(entries) / jnp.sqrt(total))
    grad_filter[...] = scale * raw[...]
    step = mine[1]
    for rank in range(raw.shape[1] // share):
        block = gathered[rank * step + mine[0]].astype(F32) * scale
        for i in range(3):
            grad_short[i, :, rank * share : (rank + 1) * share] = block[i * FK : (i + 1) * FK, :share]


def shards(projected, short_taps, filter_taps, decay, cotangent):
    length, _, channels = projected.shape
    ranks, groups = lax.axis_size("seq"), lax.axis_size("ch")
    rows = filter_taps.shape[0]
    count = rows * ranks
    width = min(256, channels // CHUNKS)
    share = channels // ranks
    slot = -(-rows // 16) * 16
    size, span = 2 * length, length // 8
    extended = length + 8 * (FK - 1)
    proj, cot, short, decay = (
        pltpu.with_memory_space_constraint(array, pltpu.HBM)
        for array in (jnp.transpose(projected, (1, 0, 2)), cotangent, short_taps, decay[None])
    )
    floats = lambda *shape: pltpu.HBM(shape + (channels,), F32)
    halves_of = lambda *shape: pltpu.HBM(shape + (channels,), BF16)
    own = interleaved(span)
    after = length + np.arange(8)

    blocks = channels // width // CHUNKS
    prev, later, taps = [], [], None
    for k in range(CHUNKS):
        operands = [(proj, (3, length)), (cot, (length,)), (short, (3, FK))]
        results = [
            (jax.ShapeDtypeStruct((count, blocks * width), BF16), columns((count,), width)) for count in (152, 160)
        ]
        if k == 0:
            operands.append((filter_taps, columns((rows,), channels // blocks)))
            results.insert(0, (pltpu.HBM((ranks, rows, channels), BF16), columns((ranks, rows), channels // blocks)))
        *spread, forward, backward = call(
            edges_kernel, "edges", operands, results, width, cost=1, first=k * blocks, blocks=blocks,
            scratch_shapes=[pltpu.VMEM(((at + FK - 1) * 8, length), BF16) for at in (16, 17)]
            + [pltpu.VMEM((at * 8, width), F32) for at in (15 + FK, 15 + FK, 16 + FK, 17)],
        )
        if k == 0:
            taps = lax.all_to_all(spread[0], "seq", 0, 0).reshape(count, channels)
        else:
            forward, backward, prev[-1], later[-1] = lax.optimization_barrier((forward, backward, prev[-1], later[-1]))
        prev.append(from_behind(forward, "seq", 1))
        later.append(from_behind(backward, "seq", -1))

    feat, px, cots, m_part, g_part = call(
        own_kernel, "own",
        [(proj, (3, length)), (cot, (length,)), (short, (3, FK))],
        [
            (floats(3, length), (3, length)), (halves_of(3, length), (3, length)), (halves_of(length), (length,)),
            (floats(size), (size,)), (floats(size), (size,)),
        ],
        width,
        [np.concatenate(list(analysis(own, size)), axis=1), pick(interleaved(span, 0, 1 - FK), length)],
        cost=10,
        scratch_shapes=[
            pltpu.VMEM((3, extended, width), F32), pltpu.VMEM((length, width), F32),
            pltpu.VMEM((length, width), BF16), pltpu.VMEM((length, width), BF16),
        ],
    )

    k_high, k_low = analysis(np.arange(count), size)
    constants = [
        analysis(np.concatenate([interleaved(16, -128), after, np.arange(8)]), size)[0],
        analysis(np.concatenate([interleaved(17, length), np.arange(8)]), size)[0],
        analysis(np.arange(8), size, 8)[0],
        np.concatenate([k_high, k_low, k_high], axis=1),
        np.concatenate(list(synthesis(np.concatenate([own, after]), size)), axis=1),
        np.concatenate(list(synthesis(np.arange(count), size)), axis=1),
    ]
    held = ()
    for k in range(CHUNKS):
        first = k * blocks
        held = call(
            functools.partial(finish_kernel, first), "finish",
            [
                (prev[k], columns((152,), width)), (later[k], columns((160,), width)), (feat, (3, length)),
                (px, (3, length)), (cots, (length,)), (m_part, (size,)), (g_part, (size,)), (taps, columns((count,), width, first)),
                (proj, pl.BlockSpec((3, 16, width), lambda c, first=first: (0, length // 16 - 1, first + c))),
                (cot, (16,)), (short, (3, FK)), (decay, (1,)),
            ],
            [
                (halves_of(length), (length,)), (floats(3, extended), (3, extended)),
                (
                    pltpu.HBM((ranks, channels // width * slot + SHORT, width), BF16),
                    pl.BlockSpec(memory_space=pl.ANY),
                ),
            ],
            width, constants, cost=6, first=first, blocks=blocks, held=held,
            scratch_shapes=[
                pltpu.VMEM((ranks, slot, width), BF16),
                pltpu.VMEM((ranks * width // channels, SHORT, width), BF16),
                pltpu.SemaphoreType.DMA((2,)),
                pltpu.VMEM((3, STEP, width), F32),
            ] + [pltpu.VMEM((size, width), F32)] * 4 + [pltpu.VMEM((size, width), BF16)] * 3
            + [pltpu.VMEM((length + 8, width), F32)] * 2 + [pltpu.VMEM((count, width), F32)],
        )
    product, grad, sums = held
    gated, grad_proj = call(
        outputs_kernel, "outputs",
        [(product, (length,)), (grad, (3, extended)), (short, (3, FK))],
        [(halves_of(length), (length,)), (halves_of(3, length), (3, length))],
        width, [pick(own, length).T], cost=8, scratch_shapes=[pltpu.VMEM((3, length, width), BF16)],
    )
    sums, gated, grad_proj = lax.optimization_barrier((lax.all_to_all(sums, "seq", 0, 0), gated, grad_proj))

    vmem = pl.BlockSpec(memory_space=pltpu.VMEM)
    raw, payload = pl.pallas_call(
        functools.partial(squares_kernel, rows, share),
        in_specs=[vmem],
        out_specs=[vmem] * 2,
        out_shape=[
            jax.ShapeDtypeStruct((rows, channels), F32),
            jax.ShapeDtypeStruct((ranks * groups, 24, width), BF16),
        ],
        compiler_params=pltpu.CompilerParams(vmem_limit_bytes=32 << 20),
        name="squares",
    )(sums)
    gathered = lax.all_to_all(payload, ("seq", "ch"), 0, 0)
    mine = jnp.stack([lax.axis_index("ch"), jnp.int32(groups)])
    entries = (rows * ranks + 3 * FK) * channels * groups
    grad_short, grad_filter = pl.pallas_call(
        functools.partial(scale_kernel, entries, share),
        in_specs=[pl.BlockSpec(memory_space=pltpu.SMEM), vmem, vmem],
        out_specs=[vmem] * 2,
        out_shape=[
            jax.ShapeDtypeStruct((3, FK, channels), F32),
            jax.ShapeDtypeStruct((rows, channels), F32),
        ],
        compiler_params=pltpu.CompilerParams(vmem_limit_bytes=32 << 20),
        name="scale",
    )(mine, raw, gathered)
    return (gated, jnp.transpose(grad_proj, (1, 0, 2)), grad_short, grad_filter)


def solution(mesh):
    placed = (P("seq", None, "ch"), P(None, None, "ch"), P("seq", "ch"), P("ch"), P("seq", "ch"))
    return jax.shard_map(
        shards,
        mesh=mesh,
        in_specs=placed,
        out_specs=(P("seq", "ch"), P("seq", None, "ch"), P(None, None, "ch"), P("seq", "ch")),
        check_vma=False,
    )
```

```python
import functools
import math

import jax
import jax.numpy as jnp
import ml_dtypes
import numpy as np
from jax import lax
from jax.experimental import pallas as pl
from jax.experimental.pallas import tpu as pltpu
from jax.sharding import PartitionSpec as P


FK = 7
BF16 = jnp.bfloat16
F32 = jnp.float32
SHORT = 32
STEP = 64


def from_behind(value, axis, by):
    count = lax.axis_size(axis)
    pairs = [(i, i + by) for i in range(count) if 0 <= i + by < count]
    return lax.ppermute(value, axis, pairs)


def interleaved(span, first=0, low=0):
    return np.array([first + s * span + r for r in range(low, span) for s in range(8)])


def pick(positions, count):
    out = np.zeros((len(positions), count), np.float32)
    for row, at in enumerate(positions):
        if 0 <= at < count:
            out[row, at] = 1.0
    return out.astype(ml_dtypes.bfloat16)


def halves(matrix):
    high = matrix.astype(np.float32).astype(ml_dtypes.bfloat16)
    low = (matrix - high.astype(np.float64)).astype(np.float32).astype(ml_dtypes.bfloat16)
    return np.stack([high, low])


def analysis(positions, size, pad=0):
    freq = np.arange(size // 2)[:, None]
    angle = np.pi * (((2 * freq + 1) * np.asarray(positions)[None, :]) % (2 * size)) / size
    matrix = np.concatenate([np.cos(angle), -np.sin(angle)], axis=0)
    return halves(np.pad(matrix, ((0, 0), (0, pad))))


def synthesis(positions, size):
    freq = np.arange(size // 2)[None, :]
    angle = np.pi * (((2 * freq + 1) * np.asarray(positions)[:, None]) % (2 * size)) / size
    return halves(np.concatenate([np.cos(angle), -np.sin(angle)], axis=1) * (2.0 / size))


def mm(a, b):
    return jnp.dot(a, b, preferred_element_type=F32)


def picked(span, first, length):
    shape = ((span + FK - 1) * 8, length)
    row, column = (lax.broadcasted_iota(jnp.int32, shape, axis) for axis in (0, 1))
    position = first + (row & 7) * span + (row >> 3) - (FK - 1)
    return jnp.where(position == column, 1.0, 0.0).astype(BF16)


def lanes_of(width):
    return [slice(at, at + 128) for at in range(0, width, 128)]


def featurized(x, taps, lane, row, rows):
    total = None
    for lag in range(FK):
        at = row + 8 * (FK - 1 - lag)
        part = x[at : at + rows, lane].reshape(rows // 8, 8, 128) * taps[lag]
        total = part if total is None else total + part
    return total


def spread_taps(short, i, lane):
    return [jnp.broadcast_to(short[i, lag : lag + 1, lane], (8, 128)) for lag in range(FK)]


def fetch(pairs, semaphores):
    copies = [pltpu.make_async_copy(source, into, semaphores.at[at]) for at, (source, into) in enumerate(pairs)]
    for copy in copies:
        copy.start()
    return copies


def window(block, width):
    return pl.ds(pl.multiple_of(block * width, width), width)


def edges_kernel(
    proj, cot, short, forward, backward,
    tails, heads, few, taps_held, p_tail, p_head, first, second, zeroth, held, semaphores,
):
    length, channels = cot.shape
    some, width = p_tail.shape[1], first.shape[1]
    tail, head = 16, 17
    copies = fetch(
        [
            (proj.at[1, length - some :, :], tails.at[0]),
            (proj.at[2, length - some :, :], tails.at[1]),
            (proj.at[0, :some, :], heads.at[0]),
            (cot.at[:some, :], heads.at[1]),
            (proj.at[0, length - 16 :, :], few.at[0]),
            (proj.at[1, :16, :], few.at[1]),
            (proj.at[2, :16, :], few.at[2]),
            (short, taps_held),
        ],
        semaphores,
    )
    p_tail[...] = picked(tail, some - 128, some)
    p_head[...] = picked(head, 0, some)
    for copy in copies:
        copy.wait()

    def block(c, _):
        columns = window(c, width)
        first[...] = mm(p_tail[...], tails[0, :, columns])
        second[...] = mm(p_tail[...], tails[1, :, columns])
        zeroth[...] = mm(p_head[...], heads[0, :, columns])
        held[...] = mm(p_head[(FK - 1) * 8 :, :], heads[1, :, columns])
        for lane in lanes_of(width):
            wide = pl.ds(pl.multiple_of(c * width + lane.start, 128), 128)
            taps = [spread_taps(taps_held, i, wide) for i in range(3)]
            for r in range(0, 8 * tail, STEP):
                mixed = featurized(first, taps[1], lane, r, STEP) * featurized(second, taps[2], lane, r, STEP)
                forward[r : r + STEP, wide] = mixed.reshape(STEP, 128).astype(BF16)
            ends = [few[0, :, wide], tails[0, some - 16 :, wide], tails[1, some - 16 :, wide]]
            ends = [end.astype(F32)[8:] for end in ends]
            forward[8 * tail :, wide] = jnp.concatenate(ends, axis=0).astype(BF16)
            for r in range(0, 8 * head, STEP):
                rows = min(STEP, 8 * head - r)
                grad = featurized(zeroth, taps[0], lane, r, rows).reshape(rows, 128) * held[r : r + rows, lane]
                if rows < STEP:
                    starts = [heads[1, :16, wide], few[1, :, wide], few[2, :, wide]]
                    starts = [start.astype(F32)[:8] for start in starts]
                    backward[r:, wide] = jnp.concatenate([grad] + starts, axis=0).astype(BF16)
                else:
                    backward[r : r + rows, wide] = grad.astype(BF16)
        return 0

    lax.fori_loop(0, channels // width, block, 0)


def spread_kernel(taps, spread):
    spread[...] = jnp.broadcast_to(taps[...].astype(BF16)[None], spread.shape)


def conv8(last, first, taps):
    row = lax.broadcasted_iota(jnp.int32, last.shape, 0)
    total = jnp.zeros(last.shape, F32) if first is None else taps[0:1] * first
    for lag in range(1, FK):
        rolled = 0.0 if first is None else pltpu.roll(first, lag, 0)
        total = total + taps[lag : lag + 1] * jnp.where(row < lag, pltpu.roll(last, lag, 0), rolled)
    return total


def own_kernel(
    proj_far, cot_far, short_far, e_own_far, p_in_far, feat, px, cots, m_part, g_part,
    proj, cot, short, e_own, p_in, x, moved, mixed, grads, semaphores,
):
    length, channels = cot.shape
    width = x.shape[2]
    edge = FK - 1
    copies = fetch(
        [(proj_far.at[i], proj.at[i]) for i in range(3)]
        + [(cot_far, cot), (short_far, short), (p_in_far, p_in), (e_own_far, e_own)],
        semaphores,
    )
    for copy in copies:
        copy.wait()

    def block(c, _):
        columns = window(c, width)
        for i in range(3):
            x[i] = mm(p_in[...], proj[i, :, columns])
        moved[...] = mm(p_in[edge * 8 :, :], cot[:, columns])
        for lane in lanes_of(width):
            wide = pl.ds(pl.multiple_of(c * width + lane.start, 128), 128)
            taps = [spread_taps(short, i, wide) for i in range(3)]
            for r in range(0, length, STEP):
                rows = slice(r, r + STEP)
                parts = []
                for i in range(3):
                    px[c, i, rows, lane] = x[i, r + 8 * edge : r + 8 * edge + STEP, lane].astype(BF16)
                    part = featurized(x.at[i], taps[i], lane, r, STEP).reshape(STEP, 128)
                    feat[c, i, rows, lane] = part
                    parts.append(part)
                here = moved[rows, lane]
                cots[c, rows, lane] = here.astype(BF16)
                mixed[rows, lane] = (parts[1] * parts[2]).astype(BF16)
                grads[rows, lane] = (here * parts[0]).astype(BF16)
        for out, value in ((m_part, mixed), (g_part, grads)):
            value = value[...]
            out[c] = mm(e_own[...], jnp.concatenate([value, value], axis=0))
        return 0

    lax.fori_loop(0, channels // width, block, 0)


def finish_kernel(
    prev_all, later_all, feat_all, px_all, cots_all, m_all, g_all, taps_all, proj_far, cot_far, short_far, decay_far,
    e_prev_far, e_next_far, e_first_far, e_taps_far, s_own_far, s_lags_far,
    product_all, grad_all, sums_out,
    ends_all, starts_all, short_all, decay_all, e_prev, e_next, e_first, e_taps, s_own, s_lags,
    fixed, ms, gs, hs, ks, ys, zs, cs, filtered, grad_mixed, decays, semaphores,
):
    length, width = cots_all.shape[1:]
    pairs = [
        (proj_far.at[:, length - 16 :, :], ends_all), (cot_far.at[:16, :], starts_all), (short_far, short_all),
        (decay_far, decay_all), (e_prev_far, e_prev), (e_first_far, e_first), (e_next_far, e_next),
        (e_taps_far, e_taps), (s_own_far, s_own), (s_lags_far, s_lags),
    ]
    copies = fetch(pairs, semaphores)
    for copy in copies:
        copy.wait()

    def block(c, _):
        columns = window(c, width)
        narrow = [prev_all, later_all, taps_all, starts_all, decay_all]
        prev, later, taps, starts, decay = [ref.at[:, columns] for ref in narrow]
        ends, short = ends_all.at[:, :, columns], short_all.at[:, :, columns]
        feat, px, cots, m_part, g_part, product, grad = [
            ref.at[c] for ref in (feat_all, px_all, cots_all, m_all, g_all, product_all, grad_all)
        ]
        finish_block(
            c, prev, later, feat, px, cots, m_part, g_part, taps, ends, starts, short, decay,
            e_prev, e_next, e_first, e_taps, s_own, s_lags, product, grad, sums_out,
            fixed, ms, gs, hs, ks, ys, zs, cs, filtered, grad_mixed, decays,
        )
        return 0

    lax.fori_loop(0, cots_all.shape[0], block, 0)


def finish_block(
    block, prev, later, feat, px, cots, m_part, g_part, taps, ends, starts, short, decay,
    e_prev, e_next, e_first, e_taps, s_own, s_lags, product, grad, sums_out,
    fixed, ms, gs, hs, ks, ys, zs, cs, filtered, grad_mixed, decays,
):
    length, width = 8 * (grad.shape[1] // 8 - FK + 1), ms.shape[1]
    edge = FK - 1
    row8 = lax.broadcasted_iota(jnp.int32, (8, width), 0)
    before = prev[...].astype(F32)
    after = later[...].astype(F32)
    prev8 = [before[128 + 8 * i : 136 + 8 * i] for i in range(3)]
    cot_next = after[136:144]
    next8 = [None, after[144:152], after[152:160]]
    ends8 = [ends[i].astype(F32)[8:] for i in range(3)]
    cot_first = starts[...].astype(F32)[:8]
    short = [short[i] for i in range(3)]

    fixes = [conv8(prev8[i], None, short[i]) for i in range(3)]
    heads = []
    for i in range(3):
        rows, natural = [], jnp.zeros((8, width), F32)
        for r in range(edge):
            part = feat[i, 8 * r : 8 * r + 8, :]
            natural = natural + jnp.where(row8 == r, pltpu.roll(part, r, 0) if r else part, 0.0)
            moved = pltpu.roll(fixes[i], 8 - r, 0) if r else fixes[i]
            rows.append(part + jnp.where(row8 == 0, moved, 0.0))
        heads.append((jnp.concatenate(rows, axis=0), natural))
    for i in range(3):
        fixed[i, : 8 * edge] = heads[i][0]
        fixed[i, 8 * edge :] = feat[i, 8 * edge : STEP, :]
    inside = row8 < edge
    (first1, first2), (fix1, fix2) = (heads[1][1], heads[2][1]), fixes[1:]
    mixed_fix = jnp.where(inside, (first1 + fix1) * (first2 + fix2) - first1 * first2, 0.0)
    grad_fix = jnp.where(inside, cot_first * fixes[0], 0.0)

    feat_next = [None] + [conv8(ends8[i], next8[i], short[i]) for i in (1, 2)]
    fix = cot_next * conv8(ends8[0], None, short[0])
    rows = [after[8 * r : 8 * r + 8] for r in range(17)]
    for r in range(edge):
        rows[r] = rows[r] + jnp.where(row8 == 0, pltpu.roll(fix, (8 - r) % 8, 0), 0.0)
    grad_edge = jnp.concatenate(rows + [grad_fix], axis=0).astype(BF16)
    mixed_edge = jnp.concatenate([before[:128], feat_next[1] * feat_next[2], mixed_fix], axis=0).astype(BF16)
    grad_first = jnp.concatenate([grad_fix, jnp.zeros((8, width), F32)], axis=0).astype(BF16)

    ms[...] = mm(e_prev[...], mixed_edge)
    hs[...] = mm(e_first[...], grad_first)
    gs[...] = mm(e_next[...], grad_edge)
    lags = lax.broadcasted_iota(jnp.int32, decays.shape, 0).astype(F32)
    decays[...] = jnp.exp(-decay[...] * lags)
    kernel = taps[...].astype(F32) * decays[...]
    high = kernel.astype(BF16)
    low = (kernel - high.astype(F32)).astype(BF16)
    ks[...] = mm(e_taps[...], jnp.concatenate([high, high, low], axis=0))

    half = ks.shape[0] // 2
    for lane in lanes_of(width):
        for f in range(0, half, 32):
            real, imag = slice(f, f + 32), slice(half + f, half + f + 32)
            kr, ki = ks[real, lane], ks[imag, lane]
            mr, mi = m_part[real, lane] + ms[real, lane], m_part[imag, lane] + ms[imag, lane]
            ys[real, lane] = (mr * kr - mi * ki).astype(BF16)
            ys[imag, lane] = (mr * ki + mi * kr).astype(BF16)
            pr, pi = g_part[real, lane], g_part[imag, lane]
            hr, hi = pr + hs[real, lane], pi + hs[imag, lane]
            cs[real, lane] = (hr * mr + hi * mi).astype(BF16)
            cs[imag, lane] = (hi * mr - hr * mi).astype(BF16)
            gr, gi = pr + gs[real, lane], pi + gs[imag, lane]
            zs[real, lane] = (gr * kr + gi * ki).astype(BF16)
            zs[imag, lane] = (gi * kr - gr * ki).astype(BF16)

    def back_to(matrix, spectrum):
        spectrum = spectrum[...]
        return mm(matrix[...], jnp.concatenate([spectrum, spectrum], axis=0))

    filtered[...] = back_to(s_own, ys)
    grad_mixed[...] = back_to(s_own, zs)
    filter_sums = back_to(s_lags, cs) * decays[...]

    for lane in lanes_of(width):
        for r in range(0, length, STEP):
            rows = slice(r, r + STEP)
            features = [fixed[i, :, lane] if r == 0 else feat[i, rows, lane] for i in range(3)]
            own, back = filtered[rows, lane], grad_mixed[rows, lane]
            product[rows, lane] = (features[0] * own).astype(BF16)
            grad[0, rows, lane] = cots[rows, lane].astype(F32) * own
            grad[1, rows, lane] = back * features[2]
            grad[2, rows, lane] = back * features[1]
    own_next, back_next = filtered[length:, :], grad_mixed[length:, :]
    edge_next = [cot_next * own_next, back_next * feat_next[2], back_next * feat_next[1]]
    for i in range(3):
        for k in range(edge):
            at = length + 8 * k
            moved = pltpu.roll(grad[i, 8 * k : 8 * k + 8, :], 7, 0)
            grad[i, at : at + 8, :] = jnp.where(row8 == 7, pltpu.roll(edge_next[i], 7 - k, 0), moved)

    short_rows = []
    chunk = 64
    for i in range(3):
        rows = [[] for _ in range(FK)]
        for at in range(0, width, 128):
            lane = slice(at, at + 128)
            sums = [jnp.zeros((8, 128), F32)] * FK
            for r in range(0, length, chunk):
                here = px[i, r : r + chunk, lane].astype(F32).reshape(chunk // 8, 8, 128)
                for lag in range(FK):
                    value = grad[i, r + 8 * lag : r + 8 * lag + chunk, lane].reshape(chunk // 8, 8, 128)
                    sums[lag] = sums[lag] + jnp.sum(here * value, axis=0)
            for lag in range(FK):
                rows[lag].append(jnp.sum(sums[lag], axis=0, keepdims=True))
        short_rows += [jnp.concatenate(row, axis=1) for row in rows]

    ranks, total, _ = sums_out.shape
    per = filter_sums.shape[0] // ranks
    slot = -(-per // 16) * 16
    share = ranks * slot // (total - SHORT)
    if per % 8 == 0:
        by_rank = filter_sums.reshape(ranks, per, width)
    else:
        by_rank = jnp.stack([filter_sums[rank * per : rank * per + per] for rank in range(ranks)])
    if slot > per:
        by_rank = jnp.concatenate([by_rank, jnp.zeros((ranks, slot - per, width), F32)], axis=1)
    sums_out[:, pl.ds(pl.multiple_of(block * slot, slot), slot), :] = by_rank.astype(BF16)
    sums = jnp.concatenate(short_rows + [jnp.zeros((SHORT - len(short_rows), width), F32)], axis=0)
    for rank in range(share):
        held = pltpu.roll(sums, width - rank * (width // share), 1) if rank else sums
        sums_out[block * share + rank, total - SHORT :, :] = held.astype(BF16)


def outputs_kernel(product, grad, short, p_out, gated, grad_proj, held):
    c = pl.program_id(0)
    length, width = product.shape[1:]
    gated[...] = mm(p_out[...], product[c]).astype(BF16)
    for i in range(3):
        for lane in lanes_of(width):
            taps = spread_taps(short, i, lane)
            for r in range(0, length, STEP):
                total = None
                for lag in range(FK):
                    at = slice(r + 8 * lag, r + 8 * lag + STEP)
                    part = grad[c, i, at, lane].reshape(STEP // 8, 8, 128) * taps[lag]
                    total = part if total is None else total + part
                held[i, r : r + STEP, lane] = total.reshape(STEP, 128).astype(BF16)
        grad_proj[i] = mm(p_out[...], held[i]).astype(BF16)


def whole(array):
    return pl.BlockSpec(array.shape, lambda c: (0,) * array.ndim)


def columns(rows, width, first=0):
    lead = (0,) * len(rows)
    return pl.BlockSpec(tuple(rows) + (width,), lambda c: lead + (first + c,))


def call(kernel, name, operands, outputs, cost=1, limit=24, **options):
    vmem, far = pl.BlockSpec(memory_space=pltpu.VMEM), pl.BlockSpec(memory_space=pl.ANY)
    if "in_specs" not in options:
        options["in_specs"] = [far if stays else vmem for _, stays in operands]
        options["out_specs"] = [vmem] * len(outputs)
    arrays = [pltpu.with_memory_space_constraint(array, pltpu.HBM) if stays else array for array, stays in operands]
    return pl.pallas_call(
        kernel,
        out_shape=outputs,
        compiler_params=pltpu.CompilerParams(vmem_limit_bytes=limit << 20),
        cost_estimate=pl.CostEstimate(flops=cost * 10**9, bytes_accessed=10**6, transcendentals=0),
        name=name,
        **options,
    )(*arrays)


def squares_kernel(rows, share, sums, raw, payload):
    ranks, slots, width = sums.shape
    total = sums[0].astype(F32)
    for rank in range(1, ranks):
        total = total + sums[rank].astype(F32)
    slot = -(-rows // 16) * 16
    pieces = [total[at : at + rows] for at in range(0, slots - SHORT, slot)]
    raw[...] = jnp.concatenate(pieces, axis=1)
    lane = lax.broadcasted_iota(jnp.int32, (SHORT, width), 1)
    short = jnp.where(lane < share, total[slots - SHORT :], 0.0)
    squares = jnp.sum(short * short, keepdims=True)
    for piece in pieces:
        squares = squares + jnp.sum(piece * piece, keepdims=True)
    high = squares.astype(BF16).astype(F32)
    row = lax.broadcasted_iota(jnp.int32, (24, width), 0)
    block = jnp.where(row < 3 * FK, short[:24], jnp.where(row == 3 * FK, high, squares - high)).astype(BF16)
    for other in range(payload.shape[0]):
        payload[other] = block


def scale_kernel(entries, share, mine, raw, gathered, grad_short, grad_filter):
    everyone, rows, width = gathered.shape
    total = jnp.zeros((8, width), F32)
    for other in range(everyone):
        total = total + gathered[other].astype(F32)[16:]
    total = total[5:6, :1] + total[6:7, :1]
    scale = jnp.minimum(1.0, math.sqrt(entries) / jnp.sqrt(total))
    grad_filter[...] = scale * raw[...]
    step = mine[1]
    for rank in range(raw.shape[1] // share):
        block = gathered[rank * step + mine[0]].astype(F32) * scale
        for i in range(3):
            grad_short[i, :, rank * share : (rank + 1) * share] = block[i * FK : (i + 1) * FK, :share]


def shards(projected, short_taps, filter_taps, decay, cotangent):
    length, _, channels = projected.shape
    ranks, groups = lax.axis_size("seq"), lax.axis_size("ch")
    rows = filter_taps.shape[0]
    count = rows * ranks
    width = min(256, channels)
    blocks = channels // width
    share = channels // ranks
    slot = -(-rows // 16) * 16
    size, span = 2 * length, length // 8
    extended = length + 8 * (FK - 1)
    some = 144
    proj, cot, short, decay = jnp.transpose(projected, (1, 0, 2)), cotangent, short_taps, decay[None]
    full = lambda kind, *shape: jax.ShapeDtypeStruct(shape, kind)
    vmem = lambda kind, *shape: pltpu.VMEM(shape, kind)
    copied = lambda array: pltpu.VMEM(array.shape, array.dtype)
    semaphores = pltpu.SemaphoreType.DMA((10,))
    own = interleaved(span)
    after = length + np.arange(8)

    forward, backward = call(
        edges_kernel, "edges", [(proj, True), (cot, True), (short, True)],
        [full(BF16, 152, channels), full(BF16, 160, channels)],
        scratch_shapes=[
            vmem(BF16, 2, some, channels), vmem(BF16, 2, some, channels), vmem(BF16, 3, 16, channels), copied(short),
            vmem(BF16, 8 * (15 + FK), some), vmem(BF16, 8 * (16 + FK), some), vmem(F32, 8 * (15 + FK), width),
            vmem(F32, 8 * (15 + FK), width), vmem(F32, 8 * (16 + FK), width), vmem(F32, 8 * 17, width), semaphores,
        ],
    )
    filter_taps, forward = lax.optimization_barrier((filter_taps, forward))
    prev = from_behind(forward, "seq", 1)
    later = from_behind(backward, "seq", -1)
    spread = pl.pallas_call(
        spread_kernel,
        out_shape=pltpu.HBM((ranks, rows, channels), BF16),
        cost_estimate=pl.CostEstimate(flops=0, bytes_accessed=10**6, transcendentals=0),
        name="spread",
    )(filter_taps)
    taps = lax.all_to_all(spread, "seq", 0, 0).reshape(count, channels)

    e_own = jnp.asarray(np.concatenate(list(analysis(own, size)), axis=1))
    p_in = jnp.asarray(pick(interleaved(span, 0, 1 - FK), length))
    feat, px, cots, m_part, g_part = call(
        own_kernel, "own", [(array, True) for array in (proj, cot, short, e_own, p_in)],
        [
            full(F32, blocks, 3, length, width), full(BF16, blocks, 3, length, width),
            full(BF16, blocks, length, width), full(F32, blocks, size, width), full(F32, blocks, size, width),
        ],
        cost=10,
        scratch_shapes=[copied(array) for array in (proj, cot, short, e_own, p_in)] + [
            vmem(F32, 3, extended, width), vmem(F32, length, width), vmem(BF16, length, width),
            vmem(BF16, length, width), semaphores,
        ],
    )

    k_high, k_low = analysis(np.arange(count), size)
    constants = [
        analysis(np.concatenate([interleaved(16, -128), after, np.arange(8)]), size)[0],
        analysis(np.concatenate([interleaved(17, length), np.arange(8)]), size)[0],
        analysis(np.arange(8), size, 8)[0],
        np.concatenate([k_high, k_low, k_high], axis=1),
        np.concatenate(list(synthesis(np.concatenate([own, after]), size)), axis=1),
        np.concatenate(list(synthesis(np.arange(count), size)), axis=1),
    ]
    constants = [jnp.asarray(constant) for constant in constants]
    product, grad, sums = call(
        finish_kernel, "finish",
        [(array, False) for array in (prev, later, feat, px, cots, m_part, g_part, taps)]
        + [(array, True) for array in [proj, cot, short, decay] + constants],
        [
            full(BF16, blocks, length, width), full(F32, blocks, 3, extended, width),
            full(BF16, ranks, blocks * slot + SHORT, width),
        ],
        cost=12,
        scratch_shapes=[vmem(BF16, 3, 16, channels), vmem(BF16, 16, channels), copied(short), copied(decay)]
        + [copied(constant) for constant in constants]
        + [vmem(F32, 3, STEP, width)] + [vmem(F32, size, width)] * 4 + [vmem(BF16, size, width)] * 3
        + [vmem(F32, length + 8, width)] * 2 + [vmem(F32, count, width), semaphores],
    )
    p_out = jnp.asarray(pick(own, length).T)
    inside = pl.BlockSpec(memory_space=pltpu.VMEM)
    gated, grad_proj = call(
        outputs_kernel, "outputs", [(product, False), (grad, False), (short, True), (p_out, True)],
        [full(BF16, length, channels), full(BF16, 3, length, channels)], cost=8,
        grid=(blocks,), in_specs=[inside, inside, columns((3, FK), width), whole(p_out)],
        out_specs=[columns((length,), width), columns((3, length), width)],
        scratch_shapes=[vmem(BF16, 3, length, width)],
    )
    sums, gated, grad_proj = lax.optimization_barrier((lax.all_to_all(sums, "seq", 0, 0), gated, grad_proj))

    vmem = pl.BlockSpec(memory_space=pltpu.VMEM)
    raw, payload = pl.pallas_call(
        functools.partial(squares_kernel, rows, share),
        in_specs=[vmem],
        out_specs=[vmem] * 2,
        out_shape=[
            jax.ShapeDtypeStruct((rows, channels), F32),
            jax.ShapeDtypeStruct((ranks * groups, 24, width), BF16),
        ],
        compiler_params=pltpu.CompilerParams(vmem_limit_bytes=32 << 20),
        name="squares",
    )(sums)
    gathered = lax.all_to_all(payload, ("seq", "ch"), 0, 0)
    mine = jnp.stack([lax.axis_index("ch"), jnp.int32(groups)])
    entries = (rows * ranks + 3 * FK) * channels * groups
    grad_short, grad_filter = pl.pallas_call(
        functools.partial(scale_kernel, entries, share),
        in_specs=[pl.BlockSpec(memory_space=pltpu.SMEM), vmem, vmem],
        out_specs=[vmem] * 2,
        out_shape=[
            jax.ShapeDtypeStruct((3, FK, channels), F32),
            jax.ShapeDtypeStruct((rows, channels), F32),
        ],
        compiler_params=pltpu.CompilerParams(vmem_limit_bytes=32 << 20),
        name="scale",
    )(mine, raw, gathered)
    return (gated, jnp.transpose(grad_proj, (1, 0, 2)), grad_short, grad_filter)


def solution(mesh):
    placed = (P("seq", None, "ch"), P(None, None, "ch"), P("seq", "ch"), P("ch"), P("seq", "ch"))
    return jax.shard_map(
        shards,
        mesh=mesh,
        in_specs=placed,
        out_specs=(P("seq", "ch"), P("seq", None, "ch"), P(None, None, "ch"), P("seq", "ch")),
        check_vma=False,
    )
```

```python
import functools
import math

import jax
import jax.numpy as jnp
import ml_dtypes
import numpy as np
from jax import lax
from jax.experimental import pallas as pl
from jax.experimental.pallas import tpu as pltpu
from jax.sharding import PartitionSpec as P


FK = 7
BF16 = jnp.bfloat16
F32 = jnp.float32
SHORT = 32
STEP = 64


def from_behind(value, axis, by):
    count = lax.axis_size(axis)
    pairs = [(i, i + by) for i in range(count) if 0 <= i + by < count]
    return lax.ppermute(value, axis, pairs)


def interleaved(span, first=0, low=0):
    return np.array([first + s * span + r for r in range(low, span) for s in range(8)])


def pick(positions, count):
    out = np.zeros((len(positions), count), np.float32)
    for row, at in enumerate(positions):
        if 0 <= at < count:
            out[row, at] = 1.0
    return out.astype(ml_dtypes.bfloat16)


def halves(matrix):
    high = matrix.astype(np.float32).astype(ml_dtypes.bfloat16)
    low = (matrix - high.astype(np.float64)).astype(np.float32).astype(ml_dtypes.bfloat16)
    return np.stack([high, low])


def analysis(positions, size, pad=0):
    freq = np.arange(size // 2)[:, None]
    angle = np.pi * (((2 * freq + 1) * np.asarray(positions)[None, :]) % (2 * size)) / size
    matrix = np.concatenate([np.cos(angle), -np.sin(angle)], axis=0)
    return halves(np.pad(matrix, ((0, 0), (0, pad))))


def synthesis(positions, size):
    freq = np.arange(size // 2)[None, :]
    angle = np.pi * (((2 * freq + 1) * np.asarray(positions)[:, None]) % (2 * size)) / size
    return halves(np.concatenate([np.cos(angle), -np.sin(angle)], axis=1) * (2.0 / size))


def mm(a, b):
    return jnp.dot(a, b, preferred_element_type=F32)


def picked(span, first, length):
    shape = ((span + FK - 1) * 8, length)
    row, column = (lax.broadcasted_iota(jnp.int32, shape, axis) for axis in (0, 1))
    position = first + (row & 7) * span + (row >> 3) - (FK - 1)
    return jnp.where(position == column, 1.0, 0.0).astype(BF16)


def lanes_of(width):
    return [slice(at, at + 128) for at in range(0, width, 128)]


def featurized(x, taps, lane, row, rows):
    total = None
    for lag in range(FK):
        at = row + 8 * (FK - 1 - lag)
        part = x[at : at + rows, lane].reshape(rows // 8, 8, 128) * taps[lag]
        total = part if total is None else total + part
    return total


def spread_taps(short, i, lane):
    return [jnp.broadcast_to(short[i, lag : lag + 1, lane], (8, 128)) for lag in range(FK)]


def fetch(pairs, semaphores):
    copies = [pltpu.make_async_copy(source, into, semaphores.at[at]) for at, (source, into) in enumerate(pairs)]
    for copy in copies:
        copy.start()
    return copies


def fetch_first(pairs, semaphores, when):
    @pl.when(when)
    def _():
        for copy in fetch(pairs, semaphores):
            copy.wait()


def window(block, width):
    return pl.ds(pl.multiple_of(block * width, width), width)


def edges_kernel(
    proj, cot, short, taps, forward, backward, spread,
    all_taps, all_spread, tails, heads, few, taps_held, p_tail, p_head, first, second, zeroth, held, semaphores,
):
    length, channels = cot.shape
    some, width = p_tail.shape[1], first.shape[1]
    tail, head = 16, 17
    copies = fetch(
        [
            (proj.at[1, length - some :, :], tails.at[0]),
            (proj.at[2, length - some :, :], tails.at[1]),
            (proj.at[0, :some, :], heads.at[0]),
            (cot.at[:some, :], heads.at[1]),
            (proj.at[0, length - 16 :, :], few.at[0]),
            (proj.at[1, :16, :], few.at[1]),
            (proj.at[2, :16, :], few.at[2]),
            (short, taps_held),
            (taps, all_taps),
        ],
        semaphores,
    )
    p_tail[...] = picked(tail, some - 128, some)
    p_head[...] = picked(head, 0, some)
    copies.pop().wait()
    all_spread[...] = jnp.broadcast_to(all_taps[...].astype(BF16)[None], all_spread.shape)
    sent = pltpu.make_async_copy(all_spread, spread, semaphores.at[9])
    sent.start()
    for copy in copies:
        copy.wait()

    def block(c, _):
        columns = window(c, width)
        first[...] = mm(p_tail[...], tails[0, :, columns])
        second[...] = mm(p_tail[...], tails[1, :, columns])
        zeroth[...] = mm(p_head[...], heads[0, :, columns])
        held[...] = mm(p_head[(FK - 1) * 8 :, :], heads[1, :, columns])
        for lane in lanes_of(width):
            wide = pl.ds(pl.multiple_of(c * width + lane.start, 128), 128)
            taps = [spread_taps(taps_held, i, wide) for i in range(3)]
            for r in range(0, 8 * tail, STEP):
                mixed = featurized(first, taps[1], lane, r, STEP) * featurized(second, taps[2], lane, r, STEP)
                forward[r : r + STEP, wide] = mixed.reshape(STEP, 128).astype(BF16)
            ends = [few[0, :, wide], tails[0, some - 16 :, wide], tails[1, some - 16 :, wide]]
            ends = [end.astype(F32)[8:] for end in ends]
            forward[8 * tail :, wide] = jnp.concatenate(ends, axis=0).astype(BF16)
            for r in range(0, 8 * head, STEP):
                rows = min(STEP, 8 * head - r)
                grad = featurized(zeroth, taps[0], lane, r, rows).reshape(rows, 128) * held[r : r + rows, lane]
                if rows < STEP:
                    starts = [heads[1, :16, wide], few[1, :, wide], few[2, :, wide]]
                    starts = [start.astype(F32)[:8] for start in starts]
                    backward[r:, wide] = jnp.concatenate([grad] + starts, axis=0).astype(BF16)
                else:
                    backward[r : r + rows, wide] = grad.astype(BF16)
        return 0

    lax.fori_loop(0, channels // width, block, 0)
    sent.wait()


def conv8(last, first, taps):
    row = lax.broadcasted_iota(jnp.int32, last.shape, 0)
    total = jnp.zeros(last.shape, F32) if first is None else taps[0:1] * first
    for lag in range(1, FK):
        rolled = 0.0 if first is None else pltpu.roll(first, lag, 0)
        total = total + taps[lag : lag + 1] * jnp.where(row < lag, pltpu.roll(last, lag, 0), rolled)
    return total


def own_kernel(
    proj_far, cot_far, short_far, e_own_far, p_in_far, feat, px, cots, m_part, g_part,
    proj, cot, short, e_own, p_in, x, moved, mixed, grads, semaphores,
):
    length, channels = cot.shape
    width = x.shape[2]
    edge = FK - 1
    c = pl.program_id(0)
    fetch_first(
        [(proj_far.at[i], proj.at[i]) for i in range(3)]
        + [(cot_far, cot), (short_far, short), (p_in_far, p_in), (e_own_far, e_own)],
        semaphores,
        c == 0,
    )
    columns = window(c, width)
    for i in range(3):
        x[i] = mm(p_in[...], proj[i, :, columns])
    moved[...] = mm(p_in[edge * 8 :, :], cot[:, columns])
    for lane in lanes_of(width):
        wide = pl.ds(pl.multiple_of(c * width + lane.start, 128), 128)
        taps = [spread_taps(short, i, wide) for i in range(3)]
        for r in range(0, length, STEP):
            rows = slice(r, r + STEP)
            parts = []
            for i in range(3):
                px[0, i, rows, lane] = x[i, r + 8 * edge : r + 8 * edge + STEP, lane].astype(BF16)
                part = featurized(x.at[i], taps[i], lane, r, STEP).reshape(STEP, 128)
                feat[0, i, rows, lane] = part
                parts.append(part)
            here = moved[rows, lane]
            cots[0, rows, lane] = here.astype(BF16)
            mixed[rows, lane] = (parts[1] * parts[2]).astype(BF16)
            grads[rows, lane] = (here * parts[0]).astype(BF16)
    for out, value in ((m_part, mixed), (g_part, grads)):
        value = value[...]
        out[0] = mm(e_own[...], jnp.concatenate([value, value], axis=0))


def taps_kernel(taps, decay, e_taps, k_spec, decays):
    lags = lax.broadcasted_iota(jnp.int32, taps.shape, 0).astype(F32)
    falloff = jnp.exp(-decay[...] * lags)
    decays[0] = falloff
    kernel = taps[...].astype(F32) * falloff
    high = kernel.astype(BF16)
    low = (kernel - high.astype(F32)).astype(BF16)
    k_spec[0] = mm(e_taps[...], jnp.concatenate([high, high, low], axis=0))


def finish_kernel(
    prev_all, later_all, feat, px, cots, m_part, g_part, ks, decays, proj_far, cot_far, short_far,
    e_prev_far, e_next_far, e_first_far, s_own_far, s_lags_far,
    product, grad, sums_out,
    ends_all, starts_all, short_all, e_prev, e_next, e_first, s_own, s_lags, semaphores, *held,
):
    length, width = cots.shape[1:]
    c = pl.program_id(0)
    pairs = [
        (proj_far.at[:, length - 16 :, :], ends_all), (cot_far.at[:16, :], starts_all), (short_far, short_all),
        (e_prev_far, e_prev), (e_first_far, e_first), (e_next_far, e_next), (s_own_far, s_own), (s_lags_far, s_lags),
    ]
    fetch_first(pairs, semaphores, c == 0)
    columns = window(c, width)
    prev, later, starts = [ref.at[:, columns] for ref in (prev_all, later_all, starts_all)]
    ends, short = ends_all.at[:, :, columns], short_all.at[:, :, columns]
    feat, px, cots, m_part, g_part, ks, decays, product, grad = [
        ref.at[0] for ref in (feat, px, cots, m_part, g_part, ks, decays, product, grad)
    ]
    finish_block(
        c, prev, later, feat, px, cots, m_part, g_part, ks, decays, ends, starts, short,
        e_prev, e_next, e_first, s_own, s_lags, product, grad, sums_out, *held,
    )


def finish_block(
    block, prev, later, feat, px, cots, m_part, g_part, ks, decays, ends, starts, short,
    e_prev, e_next, e_first, s_own, s_lags, product, grad, sums_out,
    fixed, ms, gs, hs, ys, zs, cs, filtered, grad_mixed,
):
    length, width = 8 * (grad.shape[1] // 8 - FK + 1), ms.shape[1]
    edge = FK - 1
    row8 = lax.broadcasted_iota(jnp.int32, (8, width), 0)
    before = prev[...].astype(F32)
    after = later[...].astype(F32)
    prev8 = [before[128 + 8 * i : 136 + 8 * i] for i in range(3)]
    cot_next = after[136:144]
    next8 = [None, after[144:152], after[152:160]]
    ends8 = [ends[i].astype(F32)[8:] for i in range(3)]
    cot_first = starts[...].astype(F32)[:8]
    short = [short[i] for i in range(3)]

    fixes = [conv8(prev8[i], None, short[i]) for i in range(3)]
    heads = []
    for i in range(3):
        rows, natural = [], jnp.zeros((8, width), F32)
        for r in range(edge):
            part = feat[i, 8 * r : 8 * r + 8, :]
            natural = natural + jnp.where(row8 == r, pltpu.roll(part, r, 0) if r else part, 0.0)
            moved = pltpu.roll(fixes[i], 8 - r, 0) if r else fixes[i]
            rows.append(part + jnp.where(row8 == 0, moved, 0.0))
        heads.append((jnp.concatenate(rows, axis=0), natural))
    for i in range(3):
        fixed[i, : 8 * edge] = heads[i][0]
        fixed[i, 8 * edge :] = feat[i, 8 * edge : STEP, :]
    inside = row8 < edge
    (first1, first2), (fix1, fix2) = (heads[1][1], heads[2][1]), fixes[1:]
    mixed_fix = jnp.where(inside, (first1 + fix1) * (first2 + fix2) - first1 * first2, 0.0)
    grad_fix = jnp.where(inside, cot_first * fixes[0], 0.0)

    feat_next = [None] + [conv8(ends8[i], next8[i], short[i]) for i in (1, 2)]
    fix = cot_next * conv8(ends8[0], None, short[0])
    rows = [after[8 * r : 8 * r + 8] for r in range(17)]
    for r in range(edge):
        rows[r] = rows[r] + jnp.where(row8 == 0, pltpu.roll(fix, (8 - r) % 8, 0), 0.0)
    grad_edge = jnp.concatenate(rows + [grad_fix], axis=0).astype(BF16)
    mixed_edge = jnp.concatenate([before[:128], feat_next[1] * feat_next[2], mixed_fix], axis=0).astype(BF16)
    grad_first = jnp.concatenate([grad_fix, jnp.zeros((8, width), F32)], axis=0).astype(BF16)

    ms[...] = mm(e_prev[...], mixed_edge)
    hs[...] = mm(e_first[...], grad_first)
    gs[...] = mm(e_next[...], grad_edge)
    half = ks.shape[0] // 2
    for lane in lanes_of(width):
        for f in range(0, half, 32):
            real, imag = slice(f, f + 32), slice(half + f, half + f + 32)
            kr, ki = ks[real, lane], ks[imag, lane]
            mr, mi = m_part[real, lane] + ms[real, lane], m_part[imag, lane] + ms[imag, lane]
            ys[real, lane] = (mr * kr - mi * ki).astype(BF16)
            ys[imag, lane] = (mr * ki + mi * kr).astype(BF16)
            pr, pi = g_part[real, lane], g_part[imag, lane]
            hr, hi = pr + hs[real, lane], pi + hs[imag, lane]
            cs[real, lane] = (hr * mr + hi * mi).astype(BF16)
            cs[imag, lane] = (hi * mr - hr * mi).astype(BF16)
            gr, gi = pr + gs[real, lane], pi + gs[imag, lane]
            zs[real, lane] = (gr * kr + gi * ki).astype(BF16)
            zs[imag, lane] = (gi * kr - gr * ki).astype(BF16)

    def back_to(matrix, spectrum):
        spectrum = spectrum[...]
        return mm(matrix[...], jnp.concatenate([spectrum, spectrum], axis=0))

    filtered[...] = back_to(s_own, ys)
    grad_mixed[...] = back_to(s_own, zs)
    filter_sums = back_to(s_lags, cs) * decays[...]

    for lane in lanes_of(width):
        for r in range(0, length, STEP):
            rows = slice(r, r + STEP)
            features = [fixed[i, :, lane] if r == 0 else feat[i, rows, lane] for i in range(3)]
            own, back = filtered[rows, lane], grad_mixed[rows, lane]
            product[rows, lane] = (features[0] * own).astype(BF16)
            grad[0, rows, lane] = cots[rows, lane].astype(F32) * own
            grad[1, rows, lane] = back * features[2]
            grad[2, rows, lane] = back * features[1]
    own_next, back_next = filtered[length:, :], grad_mixed[length:, :]
    edge_next = [cot_next * own_next, back_next * feat_next[2], back_next * feat_next[1]]
    for i in range(3):
        for k in range(edge):
            at = length + 8 * k
            moved = pltpu.roll(grad[i, 8 * k : 8 * k + 8, :], 7, 0)
            grad[i, at : at + 8, :] = jnp.where(row8 == 7, pltpu.roll(edge_next[i], 7 - k, 0), moved)

    short_rows = []
    chunk = 64
    for i in range(3):
        rows = [[] for _ in range(FK)]
        for at in range(0, width, 128):
            lane = slice(at, at + 128)
            sums = [jnp.zeros((8, 128), F32)] * FK
            for r in range(0, length, chunk):
                here = px[i, r : r + chunk, lane].astype(F32).reshape(chunk // 8, 8, 128)
                for lag in range(FK):
                    value = grad[i, r + 8 * lag : r + 8 * lag + chunk, lane].reshape(chunk // 8, 8, 128)
                    sums[lag] = sums[lag] + jnp.sum(here * value, axis=0)
            for lag in range(FK):
                rows[lag].append(jnp.sum(sums[lag], axis=0, keepdims=True))
        short_rows += [jnp.concatenate(row, axis=1) for row in rows]

    ranks, total, _ = sums_out.shape
    per = filter_sums.shape[0] // ranks
    slot = -(-per // 16) * 16
    share = ranks * slot // (total - SHORT)
    if per % 8 == 0:
        by_rank = filter_sums.reshape(ranks, per, width)
    else:
        by_rank = jnp.stack([filter_sums[rank * per : rank * per + per] for rank in range(ranks)])
    if slot > per:
        by_rank = jnp.concatenate([by_rank, jnp.zeros((ranks, slot - per, width), F32)], axis=1)
    sums_out[:, pl.ds(pl.multiple_of(block * slot, slot), slot), :] = by_rank.astype(BF16)
    sums = jnp.concatenate(short_rows + [jnp.zeros((SHORT - len(short_rows), width), F32)], axis=0)
    for rank in range(share):
        held = pltpu.roll(sums, width - rank * (width // share), 1) if rank else sums
        sums_out[block * share + rank, total - SHORT :, :] = held.astype(BF16)


def outputs_kernel(product, grad, short, p_out, gated, grad_proj, held):
    length, width = product.shape[1:]
    gated[...] = mm(p_out[...], product[0]).astype(BF16)
    for i in range(3):
        for lane in lanes_of(width):
            taps = spread_taps(short, i, lane)
            for r in range(0, length, STEP):
                total = None
                for lag in range(FK):
                    at = slice(r + 8 * lag, r + 8 * lag + STEP)
                    part = grad[0, i, at, lane].reshape(STEP // 8, 8, 128) * taps[lag]
                    total = part if total is None else total + part
                held[i, r : r + STEP, lane] = total.reshape(STEP, 128).astype(BF16)
        grad_proj[i] = mm(p_out[...], held[i]).astype(BF16)


def whole(array):
    return pl.BlockSpec(array.shape, lambda c: (0,) * array.ndim)


def columns(rows, width):
    lead = (0,) * len(rows)
    return pl.BlockSpec(tuple(rows) + (width,), lambda c: lead + (c,))


def one_of(array):
    tail = (0,) * (len(array.shape) - 1)
    return pl.BlockSpec((1,) + tuple(array.shape[1:]), lambda c: (c,) + tail)


IN_VMEM = pl.BlockSpec(memory_space=pltpu.VMEM)
FAR = pl.BlockSpec(memory_space=pl.ANY)


def call(kernel, name, operands, outputs, cost=1, **options):
    arrays = [
        array if spec is IN_VMEM else pltpu.with_memory_space_constraint(array, pltpu.HBM) for array, spec in operands
    ]
    return pl.pallas_call(
        kernel,
        in_specs=[spec for _, spec in operands],
        out_specs=[spec for _, spec in outputs],
        out_shape=[shape for shape, _ in outputs],
        compiler_params=pltpu.CompilerParams(vmem_limit_bytes=32 << 20),
        cost_estimate=pl.CostEstimate(flops=cost * 10**9, bytes_accessed=10**6, transcendentals=0),
        name=name,
        **options,
    )(*arrays)


def squares_kernel(rows, share, sums, raw, payload):
    ranks, slots, width = sums.shape
    total = sums[0].astype(F32)
    for rank in range(1, ranks):
        total = total + sums[rank].astype(F32)
    slot = -(-rows // 16) * 16
    pieces = [total[at : at + rows] for at in range(0, slots - SHORT, slot)]
    raw[...] = jnp.concatenate(pieces, axis=1)
    lane = lax.broadcasted_iota(jnp.int32, (SHORT, width), 1)
    short = jnp.where(lane < share, total[slots - SHORT :], 0.0)
    squares = jnp.sum(short * short, keepdims=True)
    for piece in pieces:
        squares = squares + jnp.sum(piece * piece, keepdims=True)
    high = squares.astype(BF16).astype(F32)
    row = lax.broadcasted_iota(jnp.int32, (24, width), 0)
    block = jnp.where(row < 3 * FK, short[:24], jnp.where(row == 3 * FK, high, squares - high)).astype(BF16)
    for other in range(payload.shape[0]):
        payload[other] = block


def scale_kernel(entries, share, mine, raw, gathered, grad_short, grad_filter):
    everyone, rows, width = gathered.shape
    total = jnp.zeros((8, width), F32)
    for other in range(everyone):
        total = total + gathered[other].astype(F32)[16:]
    total = total[5:6, :1] + total[6:7, :1]
    scale = jnp.minimum(1.0, math.sqrt(entries) / jnp.sqrt(total))
    grad_filter[...] = scale * raw[...]
    step = mine[1]
    for rank in range(raw.shape[1] // share):
        block = gathered[rank * step + mine[0]].astype(F32) * scale
        for i in range(3):
            grad_short[i, :, rank * share : (rank + 1) * share] = block[i * FK : (i + 1) * FK, :share]


def shards(projected, short_taps, filter_taps, decay, cotangent):
    length, _, channels = projected.shape
    ranks, groups = lax.axis_size("seq"), lax.axis_size("ch")
    rows = filter_taps.shape[0]
    count = rows * ranks
    width = min(256, channels)
    blocks = channels // width
    share = channels // ranks
    slot = -(-rows // 16) * 16
    size, span = 2 * length, length // 8
    extended = length + 8 * (FK - 1)
    some = 144
    proj, cot, short, decay = jnp.transpose(projected, (1, 0, 2)), cotangent, short_taps, decay[None]
    full = lambda kind, *shape: (jax.ShapeDtypeStruct(shape, kind), IN_VMEM)
    by_block = lambda kind, *shape: (pltpu.HBM((blocks,) + shape, kind), one_of(np.empty((blocks,) + shape, np.bool_)))
    vmem = lambda kind, *shape: pltpu.VMEM(shape, kind)
    copied = lambda array: pltpu.VMEM(array.shape, array.dtype)
    far = lambda *arrays: [(array, FAR) for array in arrays]
    pieces = lambda *arrays: [(array, one_of(array)) for array in arrays]
    semaphores = pltpu.SemaphoreType.DMA((10,))
    own = interleaved(span)
    after = length + np.arange(8)

    forward, backward, spread = call(
        edges_kernel, "edges", far(proj, cot, short, filter_taps),
        [full(BF16, 152, channels), full(BF16, 160, channels), (pltpu.HBM((ranks, rows, channels), BF16), FAR)],
        scratch_shapes=[
            copied(filter_taps), vmem(BF16, ranks, rows, channels),
            vmem(BF16, 2, some, channels), vmem(BF16, 2, some, channels), vmem(BF16, 3, 16, channels), copied(short),
            vmem(BF16, 8 * (15 + FK), some), vmem(BF16, 8 * (16 + FK), some), vmem(F32, 8 * (15 + FK), width),
            vmem(F32, 8 * (15 + FK), width), vmem(F32, 8 * (16 + FK), width), vmem(F32, 8 * 17, width), semaphores,
        ],
    )
    prev = from_behind(forward, "seq", 1)
    later = from_behind(backward, "seq", -1)
    taps = lax.all_to_all(spread, "seq", 0, 0).reshape(count, channels)

    e_own = jnp.asarray(np.concatenate(list(analysis(own, size)), axis=1))
    p_in = jnp.asarray(pick(interleaved(span, 0, 1 - FK), length))
    inputs = (proj, cot, short, e_own, p_in)
    feat, px, cots, m_part, g_part = call(
        own_kernel, "own", far(*inputs),
        [
            by_block(F32, 3, length, width), by_block(BF16, 3, length, width), by_block(BF16, length, width),
            by_block(F32, size, width), by_block(F32, size, width),
        ],
        cost=10,
        grid=(blocks,),
        scratch_shapes=[copied(array) for array in inputs] + [
            vmem(F32, 3, extended, width), vmem(F32, length, width), vmem(BF16, length, width),
            vmem(BF16, length, width), semaphores,
        ],
    )

    taps, cots = lax.optimization_barrier((taps, cots))
    k_high, k_low = analysis(np.arange(count), size)
    e_taps = jnp.asarray(np.concatenate([k_high, k_low, k_high], axis=1))
    k_spec, decays = call(
        taps_kernel, "taps",
        [(taps, columns((count,), width)), (decay, columns((1,), width)), (e_taps, whole(e_taps))],
        [by_block(F32, size, width), by_block(F32, count, width)],
        cost=3,
        grid=(blocks,),
    )
    constants = [
        analysis(np.concatenate([interleaved(16, -128), after, np.arange(8)]), size)[0],
        analysis(np.concatenate([interleaved(17, length), np.arange(8)]), size)[0],
        analysis(np.arange(8), size, 8)[0],
        np.concatenate(list(synthesis(np.concatenate([own, after]), size)), axis=1),
        np.concatenate(list(synthesis(np.arange(count), size)), axis=1),
    ]
    constants = [jnp.asarray(constant) for constant in constants]
    product, grad, sums = call(
        finish_kernel, "finish",
        [(prev, IN_VMEM), (later, IN_VMEM)] + pieces(feat, px, cots, m_part, g_part, k_spec, decays)
        + far(proj, cot, short, *constants),
        [by_block(BF16, length, width), by_block(F32, 3, extended, width), full(BF16, ranks, blocks * slot + SHORT, width)],
        cost=12,
        grid=(blocks,),
        scratch_shapes=[vmem(BF16, 3, 16, channels), vmem(BF16, 16, channels), copied(short)]
        + [copied(constant) for constant in constants] + [semaphores]
        + [vmem(F32, 3, STEP, width)] + [vmem(F32, size, width)] * 3 + [vmem(BF16, size, width)] * 3
        + [vmem(F32, length + 8, width)] * 2,
    )
    p_out = jnp.asarray(pick(own, length).T)
    gated, grad_proj = call(
        outputs_kernel, "outputs",
        pieces(product, grad) + [(short, columns((3, FK), width)), (p_out, whole(p_out))],
        [
            (jax.ShapeDtypeStruct((length, channels), BF16), columns((length,), width)),
            (jax.ShapeDtypeStruct((3, length, channels), BF16), columns((3, length), width)),
        ],
        cost=8,
        grid=(blocks,),
        scratch_shapes=[vmem(BF16, 3, length, width)],
    )
    sums, gated, grad_proj = lax.optimization_barrier((lax.all_to_all(sums, "seq", 0, 0), gated, grad_proj))

    vmem = pl.BlockSpec(memory_space=pltpu.VMEM)
    raw, payload = pl.pallas_call(
        functools.partial(squares_kernel, rows, share),
        in_specs=[vmem],
        out_specs=[vmem] * 2,
        out_shape=[
            jax.ShapeDtypeStruct((rows, channels), F32),
            jax.ShapeDtypeStruct((ranks * groups, 24, width), BF16),
        ],
        compiler_params=pltpu.CompilerParams(vmem_limit_bytes=32 << 20),
        name="squares",
    )(sums)
    gathered = lax.all_to_all(payload, ("seq", "ch"), 0, 0)
    mine = jnp.stack([lax.axis_index("ch"), jnp.int32(groups)])
    entries = (rows * ranks + 3 * FK) * channels * groups
    grad_short, grad_filter = pl.pallas_call(
        functools.partial(scale_kernel, entries, share),
        in_specs=[pl.BlockSpec(memory_space=pltpu.SMEM), vmem, vmem],
        out_specs=[vmem] * 2,
        out_shape=[
            jax.ShapeDtypeStruct((3, FK, channels), F32),
            jax.ShapeDtypeStruct((rows, channels), F32),
        ],
        compiler_params=pltpu.CompilerParams(vmem_limit_bytes=32 << 20),
        name="scale",
    )(mine, raw, gathered)
    return (gated, jnp.transpose(grad_proj, (1, 0, 2)), grad_short, grad_filter)


def solution(mesh):
    placed = (P("seq", None, "ch"), P(None, None, "ch"), P("seq", "ch"), P("ch"), P("seq", "ch"))
    return jax.shard_map(
        shards,
        mesh=mesh,
        in_specs=placed,
        out_specs=(P("seq", "ch"), P("seq", None, "ch"), P(None, None, "ch"), P("seq", "ch")),
        check_vma=False,
    )
```

```python
import functools
import math

import jax
import jax.numpy as jnp
import ml_dtypes
import numpy as np
from jax import lax
from jax.experimental import pallas as pl
from jax.experimental.pallas import tpu as pltpu
from jax.sharding import PartitionSpec as P


FK = 7
BF16 = jnp.bfloat16
F32 = jnp.float32
SHORT = 32
STEP = 64


def from_behind(value, axis, by):
    count = lax.axis_size(axis)
    pairs = [(i, i + by) for i in range(count) if 0 <= i + by < count]
    return lax.ppermute(value, axis, pairs)


def interleaved(span, first=0, low=0):
    return np.array([first + s * span + r for r in range(low, span) for s in range(8)])


def pick(positions, count):
    out = np.zeros((len(positions), count), np.float32)
    for row, at in enumerate(positions):
        if 0 <= at < count:
            out[row, at] = 1.0
    return out.astype(ml_dtypes.bfloat16)


def halves(matrix):
    high = matrix.astype(np.float32).astype(ml_dtypes.bfloat16)
    low = (matrix - high.astype(np.float64)).astype(np.float32).astype(ml_dtypes.bfloat16)
    return np.stack([high, low])


def analysis(positions, size, pad=0):
    freq = np.arange(size // 2)[:, None]
    angle = np.pi * (((2 * freq + 1) * np.asarray(positions)[None, :]) % (2 * size)) / size
    matrix = np.concatenate([np.cos(angle), -np.sin(angle)], axis=0)
    return halves(np.pad(matrix, ((0, 0), (0, pad))))


def synthesis(positions, size):
    freq = np.arange(size // 2)[None, :]
    angle = np.pi * (((2 * freq + 1) * np.asarray(positions)[:, None]) % (2 * size)) / size
    return halves(np.concatenate([np.cos(angle), -np.sin(angle)], axis=1) * (2.0 / size))


def mm(a, b):
    return jnp.dot(a, b, preferred_element_type=F32)


def picked(span, first, length):
    shape = ((span + FK - 1) * 8, length)
    row, column = (lax.broadcasted_iota(jnp.int32, shape, axis) for axis in (0, 1))
    position = first + (row & 7) * span + (row >> 3) - (FK - 1)
    return jnp.where(position == column, 1.0, 0.0).astype(BF16)


def lanes_of(width):
    return [slice(at, at + 128) for at in range(0, width, 128)]


def featurized(x, taps, lane, row, rows):
    total = None
    for lag in range(FK):
        at = row + 8 * (FK - 1 - lag)
        part = x[at : at + rows, lane].reshape(rows // 8, 8, 128) * taps[lag]
        total = part if total is None else total + part
    return total


def spread_taps(short, i, lane):
    return [jnp.broadcast_to(short[i, lag : lag + 1, lane], (8, 128)) for lag in range(FK)]


def fetch(pairs, semaphores):
    copies = [pltpu.make_async_copy(source, into, semaphores.at[at]) for at, (source, into) in enumerate(pairs)]
    for copy in copies:
        copy.start()
    return copies


def fetch_first(pairs, semaphores, when):
    @pl.when(when)
    def _():
        for copy in fetch(pairs, semaphores):
            copy.wait()


def window(block, width):
    return pl.ds(pl.multiple_of(block * width, width), width)


def edges_kernel(
    proj, cot, short, taps, forward, backward, spread,
    all_taps, all_spread, tails, heads, few, taps_held, p_tail, p_head, first, second, zeroth, held, semaphores,
):
    length, channels = cot.shape
    some, width = p_tail.shape[1], first.shape[1]
    tail, head = 16, 17
    copies = fetch(
        [
            (proj.at[1, length - some :, :], tails.at[0]),
            (proj.at[2, length - some :, :], tails.at[1]),
            (proj.at[0, :some, :], heads.at[0]),
            (cot.at[:some, :], heads.at[1]),
            (proj.at[0, length - 16 :, :], few.at[0]),
            (proj.at[1, :16, :], few.at[1]),
            (proj.at[2, :16, :], few.at[2]),
            (short, taps_held),
            (taps, all_taps),
        ],
        semaphores,
    )
    p_tail[...] = picked(tail, some - 128, some)
    p_head[...] = picked(head, 0, some)
    copies.pop().wait()
    all_spread[...] = jnp.broadcast_to(all_taps[...].astype(BF16)[None], all_spread.shape)
    sent = pltpu.make_async_copy(all_spread, spread, semaphores.at[9])
    sent.start()
    for copy in copies:
        copy.wait()

    def block(c, _):
        columns = window(c, width)
        first[...] = mm(p_tail[...], tails[0, :, columns])
        second[...] = mm(p_tail[...], tails[1, :, columns])
        zeroth[...] = mm(p_head[...], heads[0, :, columns])
        held[...] = mm(p_head[(FK - 1) * 8 :, :], heads[1, :, columns])
        for lane in lanes_of(width):
            wide = pl.ds(pl.multiple_of(c * width + lane.start, 128), 128)
            taps = [spread_taps(taps_held, i, wide) for i in range(3)]
            for r in range(0, 8 * tail, STEP):
                mixed = featurized(first, taps[1], lane, r, STEP) * featurized(second, taps[2], lane, r, STEP)
                forward[r : r + STEP, wide] = mixed.reshape(STEP, 128).astype(BF16)
            ends = [few[0, :, wide], tails[0, some - 16 :, wide], tails[1, some - 16 :, wide]]
            ends = [end.astype(F32)[8:] for end in ends]
            forward[8 * tail :, wide] = jnp.concatenate(ends, axis=0).astype(BF16)
            for r in range(0, 8 * head, STEP):
                rows = min(STEP, 8 * head - r)
                grad = featurized(zeroth, taps[0], lane, r, rows).reshape(rows, 128) * held[r : r + rows, lane]
                if rows < STEP:
                    starts = [heads[1, :16, wide], few[1, :, wide], few[2, :, wide]]
                    starts = [start.astype(F32)[:8] for start in starts]
                    backward[r:, wide] = jnp.concatenate([grad] + starts, axis=0).astype(BF16)
                else:
                    backward[r : r + rows, wide] = grad.astype(BF16)
        return 0

    lax.fori_loop(0, channels // width, block, 0)
    sent.wait()


def conv8(last, first, taps):
    row = lax.broadcasted_iota(jnp.int32, last.shape, 0)
    total = jnp.zeros(last.shape, F32) if first is None else taps[0:1] * first
    for lag in range(1, FK):
        rolled = 0.0 if first is None else pltpu.roll(first, lag, 0)
        total = total + taps[lag : lag + 1] * jnp.where(row < lag, pltpu.roll(last, lag, 0), rolled)
    return total


def own_kernel(
    proj_far, cot_far, short_far, e_own_far, p_in_far, feat, px, cots, m_part, g_part,
    proj, cot, short, e_own, p_in, x, moved, mixed, grads, semaphores,
):
    length, channels = cot.shape
    width = x.shape[2]
    edge = FK - 1
    c = pl.program_id(0)
    fetch_first(
        [(proj_far.at[i], proj.at[i]) for i in range(3)]
        + [(cot_far, cot), (short_far, short), (p_in_far, p_in), (e_own_far, e_own)],
        semaphores,
        c == 0,
    )
    columns = window(c, width)
    for i in range(3):
        x[i] = mm(p_in[...], proj[i, :, columns])
    moved[...] = mm(p_in[edge * 8 :, :], cot[:, columns])
    for lane in lanes_of(width):
        wide = pl.ds(pl.multiple_of(c * width + lane.start, 128), 128)
        taps = [spread_taps(short, i, wide) for i in range(3)]
        for r in range(0, length, STEP):
            rows = slice(r, r + STEP)
            parts = []
            for i in range(3):
                px[0, i, rows, lane] = x[i, r + 8 * edge : r + 8 * edge + STEP, lane].astype(BF16)
                part = featurized(x.at[i], taps[i], lane, r, STEP).reshape(STEP, 128)
                feat[0, i, rows, lane] = part
                parts.append(part)
            here = moved[rows, lane]
            cots[0, rows, lane] = here.astype(BF16)
            mixed[rows, lane] = (parts[1] * parts[2]).astype(BF16)
            grads[rows, lane] = (here * parts[0]).astype(BF16)
    for out, value in ((m_part, mixed), (g_part, grads)):
        value = value[...]
        out[0] = mm(e_own[...], jnp.concatenate([value, value], axis=0))


def started(part, fix, rows):
    row8 = lax.broadcasted_iota(jnp.int32, fix.shape, 0)
    groups, natural = [], jnp.zeros(fix.shape, F32)
    for r in range(FK - 1):
        here = part[8 * r : 8 * r + 8, :]
        natural = natural + jnp.where(row8 == r, pltpu.roll(here, r, 0) if r else here, 0.0)
        groups.append(here + jnp.where(row8 == 0, pltpu.roll(fix, 8 - r, 0) if r else fix, 0.0))
    rest = [part[8 * (FK - 1) : rows, :]]
    return jnp.concatenate(groups + rest, axis=0), natural


def short_sums(px, grad, length):
    width = px.shape[-1]
    rows = [[] for _ in range(FK)]
    for lane in lanes_of(width):
        sums = [jnp.zeros((8, 128), F32)] * FK
        for r in range(0, length, STEP):
            here = px[r : r + STEP, lane].astype(F32).reshape(STEP // 8, 8, 128)
            for lag in range(FK):
                value = grad[r + 8 * lag : r + 8 * lag + STEP, lane].reshape(STEP // 8, 8, 128)
                sums[lag] = sums[lag] + jnp.sum(here * value, axis=0)
        for lag in range(FK):
            rows[lag].append(jnp.sum(sums[lag], axis=0, keepdims=True))
    return [jnp.concatenate(row, axis=1) for row in rows]


def back_to(matrix, spectrum):
    spectrum = spectrum[...]
    return mm(matrix[...], jnp.concatenate([spectrum, spectrum], axis=0))


def forwards_kernel(
    prev_all, feat0, feat1, feat2, px0, cots, m_part, g_part, taps, decay, cot_far, short_far,
    e_prev_far, e_first_far, e_taps_far, s_own_far, s_lags_far,
    product, grad0, grad0_end, filter_out, short0, next_out, k_out,
    starts_all, short_all, e_prev, e_first, e_taps, s_own, s_lags, semaphores,
    fixed, ms, hs, ys, cs, filtered, grad,
):
    length, width = cots.shape[1:]
    edge = FK - 1
    c = pl.program_id(0)
    pairs = [
        (cot_far.at[:16, :], starts_all), (short_far, short_all), (e_prev_far, e_prev), (e_first_far, e_first),
        (e_taps_far, e_taps), (s_own_far, s_own), (s_lags_far, s_lags),
    ]
    fetch_first(pairs, semaphores, c == 0)
    columns = window(c, width)
    row8 = lax.broadcasted_iota(jnp.int32, (8, width), 0)
    before = prev_all[:, columns].astype(F32)
    fixes = [conv8(before[128 + 8 * i : 136 + 8 * i], None, short_all[i, :, columns]) for i in range(3)]
    fixed[...], _ = started(feat0.at[0, 0], fixes[0], STEP)
    first1, first2 = [started(ref.at[0, 0], fix, STEP)[1] for ref, fix in ((feat1, fixes[1]), (feat2, fixes[2]))]
    inside = row8 < edge
    mixed_fix = jnp.where(inside, (first1 + fixes[1]) * (first2 + fixes[2]) - first1 * first2, 0.0)
    grad_fix = jnp.where(inside, starts_all[:, columns].astype(F32)[:8] * fixes[0], 0.0)
    empty = jnp.zeros((8, width), F32)
    ms[...] = mm(e_prev[...], jnp.concatenate([before[:128], mixed_fix, empty], axis=0).astype(BF16))
    hs[...] = mm(e_first[...], jnp.concatenate([grad_fix, empty], axis=0).astype(BF16))

    lags = lax.broadcasted_iota(jnp.int32, taps.shape, 0).astype(F32)
    falloff = jnp.exp(-decay[...] * lags)
    kernel = taps[...].astype(F32) * falloff
    high = kernel.astype(BF16)
    low = (kernel - high.astype(F32)).astype(BF16)
    k_out[0] = mm(e_taps[...], jnp.concatenate([high, high, low], axis=0))

    half = ms.shape[0] // 2
    for lane in lanes_of(width):
        for f in range(0, half, 32):
            real, imag = slice(f, f + 32), slice(half + f, half + f + 32)
            kr, ki = k_out[0, real, lane], k_out[0, imag, lane]
            mr, mi = m_part[0, real, lane] + ms[real, lane], m_part[0, imag, lane] + ms[imag, lane]
            ys[real, lane] = (mr * kr - mi * ki).astype(BF16)
            ys[imag, lane] = (mr * ki + mi * kr).astype(BF16)
            hr, hi = g_part[0, real, lane] + hs[real, lane], g_part[0, imag, lane] + hs[imag, lane]
            cs[real, lane] = (hr * mr + hi * mi).astype(BF16)
            cs[imag, lane] = (hi * mr - hr * mi).astype(BF16)
    filtered[...] = back_to(s_own, ys)
    filter_sums = back_to(s_lags, cs) * falloff

    for lane in lanes_of(width):
        for r in range(0, length, STEP):
            rows = slice(r, r + STEP)
            own = filtered[rows, lane]
            feature = fixed[:, lane] if r == 0 else feat0[0, 0, rows, lane]
            product[0, rows, lane] = (feature * own).astype(BF16)
            value = cots[0, rows, lane].astype(F32) * own
            grad[rows, lane] = value
            grad0[0, rows, lane] = value
    next_out[0] = filtered[length:, :]
    for k in range(edge):
        at = slice(8 * k, 8 * k + 8)
        value = jnp.where(row8 == 7, 0.0, pltpu.roll(grad[at, :], 7, 0))
        grad[length + at.start : length + at.stop, :] = value
        grad0_end[0, at, :] = value
    short0[0] = jnp.concatenate(short_sums(px0.at[0, 0], grad, length) + [empty[:1]], axis=0)

    ranks, slot = filter_out.shape[1:3]
    per = filter_sums.shape[0] // ranks
    if per % 8 == 0:
        by_rank = filter_sums.reshape(ranks, per, width)
    else:
        by_rank = jnp.stack([filter_sums[rank * per : rank * per + per] for rank in range(ranks)])
    if slot > per:
        by_rank = jnp.concatenate([by_rank, jnp.zeros((ranks, slot - per, width), F32)], axis=1)
    filter_out[0] = by_rank.astype(BF16)


def backwards_kernel(
    prev_all, later_all, feat1, feat2, px1, px2, g_part, k_spec, grad0_end, filter_in, short0, next_in, taps, decay,
    proj_far, cot_far, short_far, e_next_far, s_own_far,
    grad, grad0_out, sums_out,
    ends_all, starts_all, short_all, e_next, s_own, semaphores,
    fixed, gs, zs, grad_mixed,
):
    length, width = feat1.shape[2:]
    edge = FK - 1
    c = pl.program_id(0)
    pairs = [
        (proj_far.at[:, length - 16 :, :], ends_all), (cot_far.at[:16, :], starts_all), (short_far, short_all),
        (e_next_far, e_next), (s_own_far, s_own),
    ]
    fetch_first(pairs, semaphores, c == 0)
    columns = window(c, width)
    row8 = lax.broadcasted_iota(jnp.int32, (8, width), 0)
    before = prev_all[:, columns].astype(F32)[128:]
    after = later_all[:, columns].astype(F32)
    cot_next, next8 = after[136:144], [None, after[144:152], after[152:160]]
    short = [short_all[i, :, columns] for i in range(3)]
    ends8 = [ends_all[i, :, columns].astype(F32)[8:] for i in range(3)]
    fixes = [conv8(before[8 * i : 8 * i + 8], None, short[i]) for i in range(3)]
    for i, ref in ((0, feat1), (1, feat2)):
        fixed[i], _ = started(ref.at[0, 0], fixes[i + 1], STEP)
    grad_fix = jnp.where(row8 < edge, starts_all[:, columns].astype(F32)[:8] * fixes[0], 0.0)

    feat_next = [None] + [conv8(ends8[i], next8[i], short[i]) for i in (1, 2)]
    fix = cot_next * conv8(ends8[0], None, short[0])
    rows = [after[8 * r : 8 * r + 8] for r in range(17)]
    for r in range(edge):
        rows[r] = rows[r] + jnp.where(row8 == 0, pltpu.roll(fix, (8 - r) % 8, 0), 0.0)
    gs[...] = mm(e_next[...], jnp.concatenate(rows + [grad_fix], axis=0).astype(BF16))

    half = gs.shape[0] // 2
    for lane in lanes_of(width):
        for f in range(0, half, 32):
            real, imag = slice(f, f + 32), slice(half + f, half + f + 32)
            kr, ki = k_spec[0, real, lane], k_spec[0, imag, lane]
            gr, gi = g_part[0, real, lane] + gs[real, lane], g_part[0, imag, lane] + gs[imag, lane]
            zs[real, lane] = (gr * kr + gi * ki).astype(BF16)
            zs[imag, lane] = (gi * kr - gr * ki).astype(BF16)
    grad_mixed[...] = back_to(s_own, zs)

    for lane in lanes_of(width):
        for r in range(0, length, STEP):
            at = slice(r, r + STEP)
            back = grad_mixed[at, lane]
            one, two = [fixed[i, :, lane] if r == 0 else ref[0, 0, at, lane] for i, ref in ((0, feat1), (1, feat2))]
            grad[0, 0, at, lane] = back * two
            grad[0, 1, at, lane] = back * one

    own_next, mixed_next = next_in[0], feat_next[1] * feat_next[2]
    for lag in range(edge):
        tap = taps[...].astype(F32)[lag : lag + 1] * jnp.exp(-decay[...] * float(lag))
        moved = pltpu.roll(mixed_next, lag, 0) if lag else mixed_next
        own_next = own_next + tap * jnp.where(row8 >= lag, moved, 0.0)
    back_next = grad_mixed[length:, :]
    edge_next = [cot_next * own_next, back_next * feat_next[2], back_next * feat_next[1]]
    for k in range(edge):
        at = slice(8 * k, 8 * k + 8)
        grad0_out[0, at, :] = jnp.where(row8 == 7, pltpu.roll(edge_next[0], 7 - k, 0), grad0_end[0, at, :])
        for i in range(2):
            moved = pltpu.roll(grad[0, i, at, :], 7, 0)
            value = jnp.where(row8 == 7, pltpu.roll(edge_next[i + 1], 7 - k, 0), moved)
            grad[0, i, length + at.start : length + at.stop, :] = value

    short_rows = [short0[0, :1, :]]
    for lag in range(1, FK):
        pair = jnp.where(row8 < lag, pltpu.roll(ends8[0], lag, 0), 0.0) * edge_next[0]
        short_rows.append(short0[0, lag : lag + 1, :] + jnp.sum(pair, axis=0, keepdims=True))
    for i, px in ((0, px1), (1, px2)):
        short_rows += short_sums(px.at[0, 0], grad.at[0, i], length)

    ranks, total, _ = sums_out.shape
    slot = filter_in.shape[2]
    share = ranks * slot // (total - SHORT)
    sums_out[:, pl.ds(pl.multiple_of(c * slot, slot), slot), :] = filter_in[0]
    sums = jnp.concatenate(short_rows + [jnp.zeros((SHORT - len(short_rows), width), F32)], axis=0)
    for rank in range(share):
        held = pltpu.roll(sums, width - rank * (width // share), 1) if rank else sums
        sums_out[c * share + rank, total - SHORT :, :] = held.astype(BF16)


def outputs_kernel(product, grad0, grad0_end, grad, short, p_out, gated, grad_proj, plane, held):
    length, width = product.shape[1:]
    gated[...] = mm(p_out[...], product[0]).astype(BF16)
    plane[:length] = grad0[0]
    plane[length:] = grad0_end[0]
    for i in range(3):
        source = plane if i == 0 else grad.at[0, i - 1]
        for lane in lanes_of(width):
            taps = spread_taps(short, i, lane)
            for r in range(0, length, STEP):
                total = None
                for lag in range(FK):
                    at = slice(r + 8 * lag, r + 8 * lag + STEP)
                    part = source[at, lane].reshape(STEP // 8, 8, 128) * taps[lag]
                    total = part if total is None else total + part
                held[i, r : r + STEP, lane] = total.reshape(STEP, 128).astype(BF16)
        grad_proj[i] = mm(p_out[...], held[i]).astype(BF16)


def whole(array):
    return pl.BlockSpec(array.shape, lambda c: (0,) * array.ndim)


def columns(rows, width):
    lead = (0,) * len(rows)
    return pl.BlockSpec(tuple(rows) + (width,), lambda c: lead + (c,))


def one_of(array):
    tail = (0,) * (len(array.shape) - 1)
    return pl.BlockSpec((1,) + tuple(array.shape[1:]), lambda c: (c,) + tail)


IN_VMEM = pl.BlockSpec(memory_space=pltpu.VMEM)
FAR = pl.BlockSpec(memory_space=pl.ANY)


def call(kernel, name, operands, outputs, cost=1, **options):
    arrays = [
        array if spec is IN_VMEM else pltpu.with_memory_space_constraint(array, pltpu.HBM) for array, spec in operands
    ]
    return pl.pallas_call(
        kernel,
        in_specs=[spec for _, spec in operands],
        out_specs=[spec for _, spec in outputs],
        out_shape=[shape for shape, _ in outputs],
        compiler_params=pltpu.CompilerParams(vmem_limit_bytes=32 << 20),
        cost_estimate=pl.CostEstimate(flops=cost * 10**9, bytes_accessed=10**6, transcendentals=0),
        name=name,
        **options,
    )(*arrays)


def squares_kernel(rows, share, sums, raw, payload):
    ranks, slots, width = sums.shape
    total = sums[0].astype(F32)
    for rank in range(1, ranks):
        total = total + sums[rank].astype(F32)
    slot = -(-rows // 16) * 16
    pieces = [total[at : at + rows] for at in range(0, slots - SHORT, slot)]
    raw[...] = jnp.concatenate(pieces, axis=1)
    lane = lax.broadcasted_iota(jnp.int32, (SHORT, width), 1)
    short = jnp.where(lane < share, total[slots - SHORT :], 0.0)
    squares = jnp.sum(short * short, keepdims=True)
    for piece in pieces:
        squares = squares + jnp.sum(piece * piece, keepdims=True)
    high = squares.astype(BF16).astype(F32)
    row = lax.broadcasted_iota(jnp.int32, (24, width), 0)
    block = jnp.where(row < 3 * FK, short[:24], jnp.where(row == 3 * FK, high, squares - high)).astype(BF16)
    for other in range(payload.shape[0]):
        payload[other] = block


def scale_kernel(entries, share, mine, raw, gathered, grad_short, grad_filter):
    everyone, rows, width = gathered.shape
    total = jnp.zeros((8, width), F32)
    for other in range(everyone):
        total = total + gathered[other].astype(F32)[16:]
    total = total[5:6, :1] + total[6:7, :1]
    scale = jnp.minimum(1.0, math.sqrt(entries) / jnp.sqrt(total))
    grad_filter[...] = scale * raw[...]
    step = mine[1]
    for rank in range(raw.shape[1] // share):
        block = gathered[rank * step + mine[0]].astype(F32) * scale
        for i in range(3):
            grad_short[i, :, rank * share : (rank + 1) * share] = block[i * FK : (i + 1) * FK, :share]


def shards(projected, short_taps, filter_taps, decay, cotangent):
    length, _, channels = projected.shape
    ranks, groups = lax.axis_size("seq"), lax.axis_size("ch")
    rows = filter_taps.shape[0]
    count = rows * ranks
    width = min(256, channels)
    blocks = channels // width
    share = channels // ranks
    slot = -(-rows // 16) * 16
    size, span = 2 * length, length // 8
    extended = length + 8 * (FK - 1)
    some = 144
    proj, cot, short, decay = jnp.transpose(projected, (1, 0, 2)), cotangent, short_taps, decay[None]
    full = lambda kind, *shape: (jax.ShapeDtypeStruct(shape, kind), IN_VMEM)
    by_block = lambda kind, *shape: (pltpu.HBM((blocks,) + shape, kind), one_of(np.empty((blocks,) + shape, np.bool_)))
    vmem = lambda kind, *shape: pltpu.VMEM(shape, kind)
    copied = lambda array: pltpu.VMEM(array.shape, array.dtype)
    far = lambda *arrays: [(array, FAR) for array in arrays]
    pieces = lambda *arrays: [(array, one_of(array)) for array in arrays]
    semaphores = pltpu.SemaphoreType.DMA((10,))
    own = interleaved(span)
    after = length + np.arange(8)

    forward, backward, spread = call(
        edges_kernel, "edges", far(proj, cot, short, filter_taps),
        [full(BF16, 152, channels), full(BF16, 160, channels), (pltpu.HBM((ranks, rows, channels), BF16), FAR)],
        scratch_shapes=[
            copied(filter_taps), vmem(BF16, ranks, rows, channels),
            vmem(BF16, 2, some, channels), vmem(BF16, 2, some, channels), vmem(BF16, 3, 16, channels), copied(short),
            vmem(BF16, 8 * (15 + FK), some), vmem(BF16, 8 * (16 + FK), some), vmem(F32, 8 * (15 + FK), width),
            vmem(F32, 8 * (15 + FK), width), vmem(F32, 8 * (16 + FK), width), vmem(F32, 8 * 17, width), semaphores,
        ],
    )
    prev = from_behind(forward, "seq", 1)
    prev, backward = lax.optimization_barrier((prev, backward))
    later = from_behind(backward, "seq", -1)
    taps = lax.all_to_all(spread, "seq", 0, 0).reshape(count, channels)

    e_own = jnp.asarray(np.concatenate(list(analysis(own, size)), axis=1))
    p_in = jnp.asarray(pick(interleaved(span, 0, 1 - FK), length))
    inputs = (proj, cot, short, e_own, p_in)
    feat, px, cots, m_part, g_part = call(
        own_kernel, "own", far(*inputs),
        [
            by_block(F32, 3, length, width), by_block(BF16, 3, length, width), by_block(BF16, length, width),
            by_block(F32, size, width), by_block(F32, size, width),
        ],
        cost=10,
        grid=(blocks,),
        scratch_shapes=[copied(array) for array in inputs] + [
            vmem(F32, 3, extended, width), vmem(F32, length, width), vmem(BF16, length, width),
            vmem(BF16, length, width), semaphores,
        ],
    )

    k_high, k_low = analysis(np.arange(count), size)
    e_prev = analysis(np.concatenate([interleaved(16, -128), np.arange(8)]), size, 8)[0]
    e_next = analysis(np.concatenate([interleaved(17, length), np.arange(8)]), size)[0]
    e_first = analysis(np.arange(8), size, 8)[0]
    e_taps = np.concatenate([k_high, k_low, k_high], axis=1)
    s_own = np.concatenate(list(synthesis(np.concatenate([own, after]), size)), axis=1)
    s_lags = np.concatenate(list(synthesis(np.arange(count), size)), axis=1)
    e_prev, e_next, e_first, e_taps, s_own, s_lags = [
        jnp.asarray(constant) for constant in (e_prev, e_next, e_first, e_taps, s_own, s_lags)
    ]

    def plane(array, i, some=length):
        return [(array, pl.BlockSpec((1, 1, some, width), lambda c: (c, i, 0, 0)))]

    few = [(taps, columns((16,), width)), (decay, columns((1,), width))]
    constants = (e_prev, e_first, e_taps, s_own, s_lags)
    product, grad0, grad0_end, filter_sums, short0, filtered_next, k_spec = call(
        forwards_kernel, "forwards",
        [(prev, IN_VMEM)] + plane(feat, 0) + plane(feat, 1, STEP) + plane(feat, 2, STEP) + plane(px, 0)
        + pieces(cots, m_part, g_part) + [(taps, columns((count,), width)), (decay, columns((1,), width))]
        + far(cot, short, *constants),
        [
            by_block(BF16, length, width), by_block(F32, length, width), by_block(F32, extended - length, width),
            by_block(BF16, ranks, slot, width), by_block(F32, 8, width), by_block(F32, 8, width),
            by_block(F32, size, width),
        ],
        cost=10,
        grid=(blocks,),
        scratch_shapes=[vmem(BF16, 16, channels), copied(short)] + [copied(constant) for constant in constants]
        + [semaphores, vmem(F32, STEP, width)] + [vmem(F32, size, width)] * 2 + [vmem(BF16, size, width)] * 2
        + [vmem(F32, length + 8, width), vmem(F32, extended, width)],
    )
    grad, grad0_end, sums = call(
        backwards_kernel, "backwards",
        [(prev, IN_VMEM), (later, IN_VMEM)] + plane(feat, 1) + plane(feat, 2) + plane(px, 1) + plane(px, 2)
        + pieces(g_part, k_spec, grad0_end, filter_sums, short0, filtered_next) + few
        + far(proj, cot, short, e_next, s_own),
        [
            by_block(F32, 2, extended, width), by_block(F32, extended - length, width),
            full(BF16, ranks, blocks * slot + SHORT, width),
        ],
        cost=10,
        grid=(blocks,),
        scratch_shapes=[
            vmem(BF16, 3, 16, channels), vmem(BF16, 16, channels), copied(short), copied(e_next), copied(s_own),
            semaphores, vmem(F32, 2, STEP, width), vmem(F32, size, width), vmem(BF16, size, width),
            vmem(F32, length + 8, width),
        ],
    )
    p_out = jnp.asarray(pick(own, length).T)
    gated, grad_proj = call(
        outputs_kernel, "outputs",
        pieces(product, grad0, grad0_end, grad) + [(short, columns((3, FK), width)), (p_out, whole(p_out))],
        [
            (jax.ShapeDtypeStruct((length, channels), BF16), columns((length,), width)),
            (jax.ShapeDtypeStruct((3, length, channels), BF16), columns((3, length), width)),
        ],
        cost=8,
        grid=(blocks,),
        scratch_shapes=[vmem(F32, extended, width), vmem(BF16, 3, length, width)],
    )
    sums, gated, grad_proj = lax.optimization_barrier((lax.all_to_all(sums, "seq", 0, 0), gated, grad_proj))

    vmem = pl.BlockSpec(memory_space=pltpu.VMEM)
    raw, payload = pl.pallas_call(
        functools.partial(squares_kernel, rows, share),
        in_specs=[vmem],
        out_specs=[vmem] * 2,
        out_shape=[
            jax.ShapeDtypeStruct((rows, channels), F32),
            jax.ShapeDtypeStruct((ranks * groups, 24, width), BF16),
        ],
        compiler_params=pltpu.CompilerParams(vmem_limit_bytes=32 << 20),
        name="squares",
    )(sums)
    gathered = lax.all_to_all(payload, ("seq", "ch"), 0, 0)
    mine = jnp.stack([lax.axis_index("ch"), jnp.int32(groups)])
    entries = (rows * ranks + 3 * FK) * channels * groups
    grad_short, grad_filter = pl.pallas_call(
        functools.partial(scale_kernel, entries, share),
        in_specs=[pl.BlockSpec(memory_space=pltpu.SMEM), vmem, vmem],
        out_specs=[vmem] * 2,
        out_shape=[
            jax.ShapeDtypeStruct((3, FK, channels), F32),
            jax.ShapeDtypeStruct((rows, channels), F32),
        ],
        compiler_params=pltpu.CompilerParams(vmem_limit_bytes=32 << 20),
        name="scale",
    )(mine, raw, gathered)
    return (gated, jnp.transpose(grad_proj, (1, 0, 2)), grad_short, grad_filter)


def solution(mesh):
    placed = (P("seq", None, "ch"), P(None, None, "ch"), P("seq", "ch"), P("ch"), P("seq", "ch"))
    return jax.shard_map(
        shards,
        mesh=mesh,
        in_specs=placed,
        out_specs=(P("seq", "ch"), P("seq", None, "ch"), P(None, None, "ch"), P("seq", "ch")),
        check_vma=False,
    )
```

```python
import functools
import math

import jax
import jax.numpy as jnp
import ml_dtypes
import numpy as np
from jax import lax
from jax.experimental import pallas as pl
from jax.experimental.pallas import tpu as pltpu
from jax.sharding import PartitionSpec as P


FK = 7
BF16 = jnp.bfloat16
F32 = jnp.float32
CHUNKS = 2
SHORT = 32
STEP = 64


def from_behind(value, axis, by):
    count = lax.axis_size(axis)
    pairs = [(i, i + by) for i in range(count) if 0 <= i + by < count]
    return lax.ppermute(value, axis, pairs)


def interleaved(span, first=0, low=0):
    return np.array([first + s * span + r for r in range(low, span) for s in range(8)])


def pick(positions, count):
    out = np.zeros((len(positions), count), np.float32)
    for row, at in enumerate(positions):
        if 0 <= at < count:
            out[row, at] = 1.0
    return out.astype(ml_dtypes.bfloat16)


def halves(matrix):
    high = matrix.astype(np.float32).astype(ml_dtypes.bfloat16)
    low = (matrix - high.astype(np.float64)).astype(np.float32).astype(ml_dtypes.bfloat16)
    return np.stack([high, low])


def analysis(positions, size, pad=0):
    freq = np.arange(size // 2)[:, None]
    angle = np.pi * (((2 * freq + 1) * np.asarray(positions)[None, :]) % (2 * size)) / size
    matrix = np.concatenate([np.cos(angle), -np.sin(angle)], axis=0)
    return halves(np.pad(matrix, ((0, 0), (0, pad))))


def synthesis(positions, size):
    freq = np.arange(size // 2)[None, :]
    angle = np.pi * (((2 * freq + 1) * np.asarray(positions)[:, None]) % (2 * size)) / size
    return halves(np.concatenate([np.cos(angle), -np.sin(angle)], axis=1) * (2.0 / size))


def mm(a, b):
    return jnp.dot(a, b, preferred_element_type=F32)


def picked(span, first, length):
    shape = ((span + FK - 1) * 8, length)
    row, column = (lax.broadcasted_iota(jnp.int32, shape, axis) for axis in (0, 1))
    position = first + (row & 7) * span + (row >> 3) - (FK - 1)
    return jnp.where(position == column, 1.0, 0.0).astype(BF16)


def lanes_of(width):
    return [slice(at, at + 128) for at in range(0, width, 128)]


def featurized(x, taps, lane, row, rows):
    total = None
    for lag in range(FK):
        at = row + 8 * (FK - 1 - lag)
        part = x[at : at + rows, lane].reshape(rows // 8, 8, 128) * taps[lag]
        total = part if total is None else total + part
    return total


def spread_taps(short, i, lane):
    return [jnp.broadcast_to(short[i, lag : lag + 1, lane], (8, 128)) for lag in range(FK)]


def fetch(pairs, semaphores):
    copies = [pltpu.make_async_copy(source, into, semaphores.at[at]) for at, (source, into) in enumerate(pairs)]
    for copy in copies:
        copy.start()
    return copies


def window(block, width):
    return pl.ds(pl.multiple_of(block * width, width), width)


def edges_kernel(at, proj, cot, short, *refs):
    tails, heads, few, taps_held, p_tail, p_head, first, second, zeroth, held, semaphores = refs[-11:]
    with_taps = len(refs) > 13
    if with_taps:
        taps, forward, backward, spread, all_taps, all_spread = refs[:6]
    else:
        forward, backward = refs[:2]
    length, channels = cot.shape[0], forward.shape[1]
    here = pl.ds(at, channels)
    some, width = p_tail.shape[1], first.shape[1]
    tail, head = 16, 17
    pairs = [
        (proj.at[1, length - some :, here], tails.at[0]),
        (proj.at[2, length - some :, here], tails.at[1]),
        (proj.at[0, :some, here], heads.at[0]),
        (cot.at[:some, here], heads.at[1]),
        (proj.at[0, length - 16 :, here], few.at[0]),
        (proj.at[1, :16, here], few.at[1]),
        (proj.at[2, :16, here], few.at[2]),
        (short.at[:, :, here], taps_held),
    ]
    copies = fetch(pairs + [(taps, all_taps)] if with_taps else pairs, semaphores)
    p_tail[...] = picked(tail, some - 128, some)
    p_head[...] = picked(head, 0, some)
    if with_taps:
        copies.pop().wait()
        all_spread[...] = jnp.broadcast_to(all_taps[...].astype(BF16)[None], all_spread.shape)
        sent = pltpu.make_async_copy(all_spread, spread, semaphores.at[9])
        sent.start()
    for copy in copies:
        copy.wait()

    def block(c, _):
        columns = window(c, width)
        first[...] = mm(p_tail[...], tails[0, :, columns])
        second[...] = mm(p_tail[...], tails[1, :, columns])
        zeroth[...] = mm(p_head[...], heads[0, :, columns])
        held[...] = mm(p_head[(FK - 1) * 8 :, :], heads[1, :, columns])
        for lane in lanes_of(width):
            wide = pl.ds(pl.multiple_of(c * width + lane.start, 128), 128)
            taps = [spread_taps(taps_held, i, wide) for i in range(3)]
            for r in range(0, 8 * tail, STEP):
                mixed = featurized(first, taps[1], lane, r, STEP) * featurized(second, taps[2], lane, r, STEP)
                forward[r : r + STEP, wide] = mixed.reshape(STEP, 128).astype(BF16)
            ends = [few[0, :, wide], tails[0, some - 16 :, wide], tails[1, some - 16 :, wide]]
            ends = [end.astype(F32)[8:] for end in ends]
            forward[8 * tail :, wide] = jnp.concatenate(ends, axis=0).astype(BF16)
            for r in range(0, 8 * head, STEP):
                rows = min(STEP, 8 * head - r)
                grad = featurized(zeroth, taps[0], lane, r, rows).reshape(rows, 128) * held[r : r + rows, lane]
                if rows < STEP:
                    starts = [heads[1, :16, wide], few[1, :, wide], few[2, :, wide]]
                    starts = [start.astype(F32)[:8] for start in starts]
                    backward[r:, wide] = jnp.concatenate([grad] + starts, axis=0).astype(BF16)
                else:
                    backward[r : r + rows, wide] = grad.astype(BF16)
        return 0

    lax.fori_loop(0, channels // width, block, 0)
    if with_taps:
        sent.wait()


def operator_kernel(
    first, proj, cot, prev, later, short, taps, decay,
    e_own, e_prev, e_next, e_taps, s_own, s_lags, p_in, *refs,
):
    product, grad, sums_out, px, feat, cots, filter_held, short_held, done = refs[-9:]
    grad = grad.at[0]
    length, width = cot.shape
    span = length // 8
    edge = FK - 1
    lanes = [slice(at, at + 128) for at in range(0, width, 128)]
    row8 = lax.broadcasted_iota(jnp.int32, (8, width), 0)

    before = prev[...].astype(F32)
    after = later[...].astype(F32)
    prev8 = [before[128 + 8 * i : 136 + 8 * i] for i in range(3)]
    cot_next = after[136:144]
    next8 = [None, after[144:152], after[152:160]]

    lags = lax.broadcasted_iota(jnp.int32, (taps.shape[0], width), 0).astype(F32)
    falloff = jnp.exp(-decay[...] * lags)
    kernel = taps[...].astype(F32) * falloff
    high = kernel.astype(BF16)
    low = (kernel - high.astype(F32)).astype(BF16)
    k_spec = mm(e_taps[...], jnp.concatenate([high, high, low], axis=0))

    for i in range(3):
        x = mm(p_in[...], proj[i]).reshape(span + edge, 8, width)
        px[i, edge:] = x[edge:]
        for k in range(1, FK):
            px[i, edge - k] = jnp.where(row8 == 0, pltpu.roll(prev8[i], k, 0), x[edge - k])
    cots[...] = mm(p_in[edge * 8 :, :], cot[...]).reshape(span, 8, width)

    step = 8
    for i in range(3):
        for lane in lanes:
            weights = [jnp.broadcast_to(short[i, lag : lag + 1, lane], (8, 128)) for lag in range(FK)]
            for r in range(0, span, step):
                total = weights[0] * px[i, r + edge : r + edge + step, :, lane]
                for lag in range(1, FK):
                    total = total + weights[lag] * px[i, r + edge - lag : r + edge - lag + step, :, lane]
                feat[i, r : r + step, :, lane] = total

    def conv8(last, first, weights, whole):
        total = weights[0:1] * first if whole else jnp.zeros((8, width), F32)
        for lag in range(1, FK):
            rolled = pltpu.roll(first, lag, 0) if whole else 0.0
            total = total + weights[lag : lag + 1] * jnp.where(row8 < lag, pltpu.roll(last, lag, 0), rolled)
        return total

    ends = [proj[i, length - 16 :, :].astype(F32)[8:] for i in range(3)]
    feat_next = [None] + [conv8(ends[i], next8[i], short[i], True) for i in (1, 2)]
    mixed_next = feat_next[1] * feat_next[2]
    grad_next = after[:136]
    fix = cot_next * conv8(ends[0], None, short[0], False)
    rows = [grad_next[8 * r : 8 * r + 8] for r in range(17)]
    for r in range(edge):
        rows[r] = rows[r] + jnp.where(row8 == 0, pltpu.roll(fix, (8 - r) % 8, 0), 0.0)
    grad_next = jnp.concatenate(rows + [jnp.zeros((8, width), F32)], axis=0).astype(BF16)
    mixed_edge = jnp.concatenate([before[:128], mixed_next, jnp.zeros((8, width), F32)], axis=0).astype(BF16)

    flat = lambda value: value.reshape(length, width)
    mixed = flat(feat[1] * feat[2]).astype(BF16)
    grad_own = flat(cots[...] * feat[0]).astype(BF16)
    m_spec = mm(e_own[...], jnp.concatenate([mixed, mixed], axis=0)) + mm(e_prev[...], mixed_edge)
    g_own = mm(e_own[...], jnp.concatenate([grad_own, grad_own], axis=0))
    g_spec = g_own + mm(e_next[...], grad_next)

    half = k_spec.shape[0] // 2
    parts = lambda value: (value[:half], value[half:])
    (kr, ki), (mr, mi), (gr, gi), (hr, hi) = parts(k_spec), parts(m_spec), parts(g_spec), parts(g_own)

    def back_to(matrix, real, imaginary):
        spectrum = jnp.concatenate([real, imaginary], axis=0).astype(BF16)
        return mm(matrix[...], jnp.concatenate([spectrum, spectrum], axis=0))

    filtered = back_to(s_own, mr * kr - mi * ki, mr * ki + mi * kr)
    grad_mixed = back_to(s_own, gr * kr + gi * ki, gi * kr - gr * ki)
    filter_sums = back_to(s_lags, hr * mr + hi * mi, hi * mr - hr * mi) * falloff

    own = filtered[:length].reshape(span, 8, width)
    product[0] = flat(feat[0] * own).astype(BF16)
    back = grad_mixed[:length].reshape(span, 8, width)
    grad[0, :span] = cots[...] * own
    grad[1, :span] = back * feat[2]
    grad[2, :span] = back * feat[1]
    back_next = grad_mixed[length:]
    edge_next = [cot_next * filtered[length:], back_next * feat_next[2], back_next * feat_next[1]]
    for i in range(3):
        for k in range(edge):
            grad[i, span + k] = jnp.where(row8 == 7, pltpu.roll(edge_next[i], 7 - k, 0), pltpu.roll(grad[i, k], 7, 0))

    short_rows = []
    for i in range(3):
        rows = [[] for _ in range(FK)]
        for lane in lanes:
            sums = [jnp.zeros((8, 128), F32)] * FK
            for r in range(0, span, step):
                here = px[i, r + edge : r + edge + step, :, lane]
                for lag in range(FK):
                    value = grad[i, r + lag : r + lag + step, :, lane]
                    sums[lag] = sums[lag] + jnp.sum(here * value, axis=0)
            for lag in range(FK):
                rows[lag].append(jnp.sum(sums[lag], axis=0, keepdims=True))
        short_rows += [jnp.concatenate(row, axis=1) for row in rows]

    step, block = pl.program_id(0), first + pl.program_id(0)
    ranks, slot, _ = filter_held.shape
    per, share = filter_sums.shape[0] // ranks, short_held.shape[0]
    copies = [
        pltpu.make_async_copy(
            filter_held, sums_out.at[:, pl.ds(pl.multiple_of(block * slot, slot), slot), :], done.at[0]
        ),
        pltpu.make_async_copy(
            short_held,
            sums_out.at[pl.ds(block * share, share), pl.ds(sums_out.shape[1] - SHORT, SHORT), :],
            done.at[1],
        ),
    ]

    @pl.when(step > 0)
    def _():
        for copy in copies:
            copy.wait()

    by_rank = filter_sums.reshape(ranks, per, width) if per % 8 == 0 else jnp.stack(
        [filter_sums[rank * per : rank * per + per] for rank in range(ranks)]
    )
    if slot > per:
        by_rank = jnp.concatenate([by_rank, jnp.zeros((ranks, slot - per, width), F32)], axis=1)
    filter_held[...] = by_rank.astype(BF16)
    sums = jnp.concatenate(short_rows + [jnp.zeros((SHORT - len(short_rows), width), F32)], axis=0)
    for rank in range(share):
        held = pltpu.roll(sums, width - rank * (width // share), 1) if rank else sums
        short_held[rank] = held.astype(BF16)
    for copy in copies:
        copy.start()

    @pl.when(step == pl.num_programs(0) - 1)
    def _():
        for copy in copies:
            copy.wait()


def outputs_kernel(product, grad, short, p_out, gated, grad_proj):
    length, width = product.shape[1:]
    span = length // 8
    gated[...] = mm(p_out[...], product[0]).astype(BF16)
    for i in range(3):
        lanes = []
        for lane in lanes_of(width):
            taps = spread_taps(short, i, lane)
            chunks = []
            for r in range(0, span, 8):
                total = None
                for lag in range(FK):
                    part = grad[0, i, r + lag : r + lag + 8, :, lane] * taps[lag]
                    total = part if total is None else total + part
                chunks.append(total)
            lanes.append(jnp.concatenate(chunks, axis=0))
        result = jnp.concatenate(lanes, axis=2).reshape(length, width).astype(BF16)
        grad_proj[i] = mm(p_out[...], result).astype(BF16)


def whole(array):
    return pl.BlockSpec(array.shape, lambda c: (0,) * array.ndim)


def columns(rows, width, first=0):
    lead = (0,) * len(rows)
    return pl.BlockSpec(tuple(rows) + (width,), lambda c: lead + (first + c,))


def one_of(array, first=0):
    tail = (0,) * (len(array.shape) - 1)
    return pl.BlockSpec((1,) + tuple(array.shape[1:]), lambda c: (first + c,) + tail)


IN_VMEM = pl.BlockSpec(memory_space=pltpu.VMEM)
FAR = pl.BlockSpec(memory_space=pl.ANY)


def call(kernel, name, operands, outputs, cost=1, held=(), free=(), **options):
    arrays = [
        array if at in free else pltpu.with_memory_space_constraint(array, pltpu.HBM)
        for at, (array, _) in enumerate(operands)
    ]
    return pl.pallas_call(
        kernel,
        in_specs=[spec for _, spec in operands] + [FAR] * len(held),
        out_specs=[spec for _, spec in outputs],
        out_shape=[shape for shape, _ in outputs],
        input_output_aliases={len(operands) + at: at for at in range(len(held))},
        compiler_params=pltpu.CompilerParams(vmem_limit_bytes=40 << 20),
        cost_estimate=pl.CostEstimate(flops=cost * 10**9, bytes_accessed=10**6, transcendentals=0),
        name=name,
        **options,
    )(*arrays, *held)


def squares_kernel(rows, share, sums, raw, payload):
    ranks, slots, width = sums.shape
    total = sums[0].astype(F32)
    for rank in range(1, ranks):
        total = total + sums[rank].astype(F32)
    slot = -(-rows // 16) * 16
    pieces = [total[at : at + rows] for at in range(0, slots - SHORT, slot)]
    raw[...] = jnp.concatenate(pieces, axis=1)
    lane = lax.broadcasted_iota(jnp.int32, (SHORT, width), 1)
    short = jnp.where(lane < share, total[slots - SHORT :], 0.0)
    squares = jnp.sum(short * short, keepdims=True)
    for piece in pieces:
        squares = squares + jnp.sum(piece * piece, keepdims=True)
    high = squares.astype(BF16).astype(F32)
    row = lax.broadcasted_iota(jnp.int32, (24, width), 0)
    block = jnp.where(row < 3 * FK, short[:24], jnp.where(row == 3 * FK, high, squares - high)).astype(BF16)
    for other in range(payload.shape[0]):
        payload[other] = block


def scale_kernel(entries, share, mine, raw, gathered, grad_short, grad_filter):
    everyone, rows, width = gathered.shape
    total = jnp.zeros((8, width), F32)
    for other in range(everyone):
        total = total + gathered[other].astype(F32)[16:]
    total = total[5:6, :1] + total[6:7, :1]
    scale = jnp.minimum(1.0, math.sqrt(entries) / jnp.sqrt(total))
    grad_filter[...] = scale * raw[...]
    step = mine[1]
    for rank in range(raw.shape[1] // share):
        block = gathered[rank * step + mine[0]].astype(F32) * scale
        for i in range(3):
            grad_short[i, :, rank * share : (rank + 1) * share] = block[i * FK : (i + 1) * FK, :share]


def shards(projected, short_taps, filter_taps, decay, cotangent):
    length, _, channels = projected.shape
    ranks, groups = lax.axis_size("seq"), lax.axis_size("ch")
    rows = filter_taps.shape[0]
    count = rows * ranks
    width = min(256, channels // CHUNKS)
    share = channels // ranks
    slot = -(-rows // 16) * 16
    size, span = 2 * length, length // 8
    some = 144
    proj, cot, short, decay = jnp.transpose(projected, (1, 0, 2)), cotangent, short_taps, decay[None]
    full = lambda kind, *shape: (jax.ShapeDtypeStruct(shape, kind), IN_VMEM)
    vmem = lambda kind, *shape: pltpu.VMEM(shape, kind)
    far = lambda *arrays: [(array, FAR) for array in arrays]
    semaphores = pltpu.SemaphoreType.DMA((10,))
    own = interleaved(span)
    after = length + np.arange(8)
    chunk = channels // CHUNKS
    blocks = chunk // width

    prev, later, taps = [], [], None
    for k in range(CHUNKS):
        operands = far(proj, cot, short)
        results = [full(BF16, 152, chunk), full(BF16, 160, chunk)]
        scratch = [
            vmem(BF16, 2, some, chunk), vmem(BF16, 2, some, chunk), vmem(BF16, 3, 16, chunk), vmem(F32, 3, FK, chunk),
            vmem(BF16, 8 * (15 + FK), some), vmem(BF16, 8 * (16 + FK), some), vmem(F32, 8 * (15 + FK), width),
            vmem(F32, 8 * (15 + FK), width), vmem(F32, 8 * (16 + FK), width), vmem(F32, 8 * 17, width), semaphores,
        ]
        if k == 0:
            operands += far(filter_taps)
            results.append((pltpu.HBM((ranks, rows, channels), BF16), FAR))
            scratch = [vmem(F32, rows, channels), vmem(BF16, ranks, rows, channels)] + scratch
        forward, backward, *spread = call(
            functools.partial(edges_kernel, k * chunk), "edges", operands, results, scratch_shapes=scratch
        )
        if k == 0:
            taps = lax.all_to_all(spread[0], "seq", 0, 0).reshape(count, channels)
        else:
            forward, backward, prev[-1], later[-1] = lax.optimization_barrier((forward, backward, prev[-1], later[-1]))
        prev.append(from_behind(forward, "seq", 1))
        later.append(from_behind(backward, "seq", -1))

    high, low = analysis(own, size)
    k_high, k_low = analysis(np.arange(count), size)
    constants = [
        np.concatenate([high, low], axis=1),
        analysis(np.concatenate([interleaved(16, -128), after]), size, 8)[0],
        analysis(interleaved(17, length), size, 8)[0],
        np.concatenate([k_high, k_low, k_high], axis=1),
        np.concatenate(list(synthesis(np.concatenate([own, after]), size)), axis=1),
        np.concatenate(list(synthesis(np.arange(count), size)), axis=1),
        pick(interleaved(span, 0, 1 - FK), length),
    ]
    constants = [(jnp.asarray(constant), whole(constant)) for constant in constants]
    held = ()
    for k in range(CHUNKS):
        first = k * blocks
        results = [
            pltpu.HBM((CHUNKS * blocks, length, width), BF16),
            pltpu.HBM((CHUNKS * blocks, 3, span + FK - 1, 8, width), F32),
        ]
        held = call(
            functools.partial(operator_kernel, first), "operator",
            [
                (proj, columns((3, length), width, first)), (cot, columns((length,), width, first)),
                (prev[k], columns((152,), width)), (later[k], columns((160,), width)),
                (short, columns((3, FK), width, first)), (taps, columns((count,), width, first)),
                (decay, columns((1,), width, first)),
            ] + constants,
            [(result, one_of(result, first)) for result in results]
            + [(pltpu.HBM((ranks, CHUNKS * blocks * slot + SHORT, width), BF16), FAR)],
            cost=12,
            held=held,
            free=(2, 3, 5),
            grid=(blocks,),
            scratch_shapes=[
                vmem(F32, 3, span + FK - 1, 8, width), vmem(F32, 3, span, 8, width), vmem(F32, span, 8, width),
                vmem(BF16, ranks, slot, width), vmem(BF16, ranks * width // channels, SHORT, width),
                pltpu.SemaphoreType.DMA((2,)),
            ],
        )
    product, grad, sums = held
    p_out = jnp.asarray(pick(own, length).T)
    gated, grad_proj = call(
        outputs_kernel, "outputs",
        [(product, one_of(product)), (grad, one_of(grad)), (short, columns((3, FK), width)), (p_out, whole(p_out))],
        [
            (jax.ShapeDtypeStruct((length, channels), BF16), columns((length,), width)),
            (jax.ShapeDtypeStruct((3, length, channels), BF16), columns((3, length), width)),
        ],
        cost=8,
        grid=(CHUNKS * blocks,),
    )
    sums, gated, grad_proj = lax.optimization_barrier((lax.all_to_all(sums, "seq", 0, 0), gated, grad_proj))

    vmem = pl.BlockSpec(memory_space=pltpu.VMEM)
    raw, payload = pl.pallas_call(
        functools.partial(squares_kernel, rows, share),
        in_specs=[vmem],
        out_specs=[vmem] * 2,
        out_shape=[
            jax.ShapeDtypeStruct((rows, channels), F32),
            jax.ShapeDtypeStruct((ranks * groups, 24, width), BF16),
        ],
        compiler_params=pltpu.CompilerParams(vmem_limit_bytes=32 << 20),
        name="squares",
    )(sums)
    gathered = lax.all_to_all(payload, ("seq", "ch"), 0, 0)
    mine = jnp.stack([lax.axis_index("ch"), jnp.int32(groups)])
    entries = (rows * ranks + 3 * FK) * channels * groups
    grad_short, grad_filter = pl.pallas_call(
        functools.partial(scale_kernel, entries, share),
        in_specs=[pl.BlockSpec(memory_space=pltpu.SMEM), vmem, vmem],
        out_specs=[vmem] * 2,
        out_shape=[
            jax.ShapeDtypeStruct((3, FK, channels), F32),
            jax.ShapeDtypeStruct((rows, channels), F32),
        ],
        compiler_params=pltpu.CompilerParams(vmem_limit_bytes=32 << 20),
        name="scale",
    )(mine, raw, gathered)
    return (gated, jnp.transpose(grad_proj, (1, 0, 2)), grad_short, grad_filter)


def solution(mesh):
    placed = (P("seq", None, "ch"), P(None, None, "ch"), P("seq", "ch"), P("ch"), P("seq", "ch"))
    return jax.shard_map(
        shards,
        mesh=mesh,
        in_specs=placed,
        out_specs=(P("seq", "ch"), P("seq", None, "ch"), P(None, None, "ch"), P("seq", "ch")),
        check_vma=False,
    )
```

```python
import functools
import math

import jax
import jax.numpy as jnp
import ml_dtypes
import numpy as np
from jax import lax
from jax.experimental import pallas as pl
from jax.experimental.pallas import tpu as pltpu
from jax.sharding import PartitionSpec as P


FK = 7
BF16 = jnp.bfloat16
F32 = jnp.float32
CHUNKS = 2
SHORT = 32
STEP = 64


def from_behind(value, axis, by):
    count = lax.axis_size(axis)
    pairs = [(i, i + by) for i in range(count) if 0 <= i + by < count]
    return lax.ppermute(value, axis, pairs)


def interleaved(span, first=0, low=0):
    return np.array([first + s * span + r for r in range(low, span) for s in range(8)])


def pick(positions, count):
    out = np.zeros((len(positions), count), np.float32)
    for row, at in enumerate(positions):
        if 0 <= at < count:
            out[row, at] = 1.0
    return out.astype(ml_dtypes.bfloat16)


def halves(matrix):
    high = matrix.astype(np.float32).astype(ml_dtypes.bfloat16)
    low = (matrix - high.astype(np.float64)).astype(np.float32).astype(ml_dtypes.bfloat16)
    return np.stack([high, low])


def analysis(positions, size, pad=0):
    freq = np.arange(size // 2)[:, None]
    angle = np.pi * (((2 * freq + 1) * np.asarray(positions)[None, :]) % (2 * size)) / size
    matrix = np.concatenate([np.cos(angle), -np.sin(angle)], axis=0)
    return halves(np.pad(matrix, ((0, 0), (0, pad))))


def synthesis(positions, size):
    freq = np.arange(size // 2)[None, :]
    angle = np.pi * (((2 * freq + 1) * np.asarray(positions)[:, None]) % (2 * size)) / size
    return halves(np.concatenate([np.cos(angle), -np.sin(angle)], axis=1) * (2.0 / size))


def mm(a, b):
    return jnp.dot(a, b, preferred_element_type=F32)


def picked(span, first, length):
    shape = ((span + FK - 1) * 8, length)
    row, column = (lax.broadcasted_iota(jnp.int32, shape, axis) for axis in (0, 1))
    position = first + (row & 7) * span + (row >> 3) - (FK - 1)
    return jnp.where(position == column, 1.0, 0.0).astype(BF16)


def lanes_of(width):
    return [slice(at, at + 128) for at in range(0, width, 128)]


def featurized(x, taps, lane, row, rows):
    total = None
    for lag in range(FK):
        at = row + 8 * (FK - 1 - lag)
        part = x[at : at + rows, lane].reshape(rows // 8, 8, 128) * taps[lag]
        total = part if total is None else total + part
    return total


def spread_taps(short, i, lane):
    return [jnp.broadcast_to(short[i, lag : lag + 1, lane], (8, 128)) for lag in range(FK)]


def fetch(pairs, semaphores):
    copies = [pltpu.make_async_copy(source, into, semaphores.at[at]) for at, (source, into) in enumerate(pairs)]
    for copy in copies:
        copy.start()
    return copies


def window(block, width):
    return pl.ds(pl.multiple_of(block * width, width), width)


def edges_kernel(at, proj, cot, short, *refs):
    tails, heads, few, taps_held, p_tail, p_head, first, second, zeroth, held, semaphores = refs[-11:]
    with_taps = len(refs) > 13
    if with_taps:
        taps, forward, backward, spread, all_taps, all_spread = refs[:6]
    else:
        forward, backward = refs[:2]
    length, channels = cot.shape[0], forward.shape[1]
    here = pl.ds(at, channels)
    some, width = p_tail.shape[1], first.shape[1]
    tail, head = 16, 17
    pairs = [
        (proj.at[1, length - some :, here], tails.at[0]),
        (proj.at[2, length - some :, here], tails.at[1]),
        (proj.at[0, :some, here], heads.at[0]),
        (cot.at[:some, here], heads.at[1]),
        (proj.at[0, length - 16 :, here], few.at[0]),
        (proj.at[1, :16, here], few.at[1]),
        (proj.at[2, :16, here], few.at[2]),
        (short.at[:, :, here], taps_held),
    ]
    copies = fetch(pairs + [(taps, all_taps)] if with_taps else pairs, semaphores)
    p_tail[...] = picked(tail, some - 128, some)
    p_head[...] = picked(head, 0, some)
    if with_taps:
        copies.pop().wait()
        all_spread[...] = jnp.broadcast_to(all_taps[...].astype(BF16)[None], all_spread.shape)
        sent = pltpu.make_async_copy(all_spread, spread, semaphores.at[9])
        sent.start()
    for copy in copies:
        copy.wait()

    def block(c, _):
        columns = window(c, width)
        first[...] = mm(p_tail[...], tails[0, :, columns])
        second[...] = mm(p_tail[...], tails[1, :, columns])
        zeroth[...] = mm(p_head[...], heads[0, :, columns])
        held[...] = mm(p_head[(FK - 1) * 8 :, :], heads[1, :, columns])
        for lane in lanes_of(width):
            wide = pl.ds(pl.multiple_of(c * width + lane.start, 128), 128)
            taps = [spread_taps(taps_held, i, wide) for i in range(3)]
            for r in range(0, 8 * tail, STEP):
                mixed = featurized(first, taps[1], lane, r, STEP) * featurized(second, taps[2], lane, r, STEP)
                forward[r : r + STEP, wide] = mixed.reshape(STEP, 128).astype(BF16)
            ends = [few[0, :, wide], tails[0, some - 16 :, wide], tails[1, some - 16 :, wide]]
            ends = [end.astype(F32)[8:] for end in ends]
            forward[8 * tail :, wide] = jnp.concatenate(ends, axis=0).astype(BF16)
            for r in range(0, 8 * head, STEP):
                rows = min(STEP, 8 * head - r)
                grad = featurized(zeroth, taps[0], lane, r, rows).reshape(rows, 128) * held[r : r + rows, lane]
                if rows < STEP:
                    starts = [heads[1, :16, wide], few[1, :, wide], few[2, :, wide]]
                    starts = [start.astype(F32)[:8] for start in starts]
                    backward[r:, wide] = jnp.concatenate([grad] + starts, axis=0).astype(BF16)
                else:
                    backward[r : r + rows, wide] = grad.astype(BF16)
        return 0

    lax.fori_loop(0, channels // width, block, 0)
    if with_taps:
        sent.wait()


def operator_kernel(
    first, proj, cot, prev, later, short, taps, decay,
    e_own, e_prev, e_next, e_taps, s_own, s_lags, p_in, *refs,
):
    product, grad, sums_out, px, feat, cots, filter_held, short_held, done = refs[-9:]
    grad = grad.at[0]
    length, width = cot.shape
    span = length // 8
    edge = FK - 1
    lanes = [slice(at, at + 128) for at in range(0, width, 128)]
    row8 = lax.broadcasted_iota(jnp.int32, (8, width), 0)

    before = prev[...].astype(F32)
    after = later[...].astype(F32)
    prev8 = [before[128 + 8 * i : 136 + 8 * i] for i in range(3)]
    cot_next = after[136:144]
    next8 = [None, after[144:152], after[152:160]]

    lags = lax.broadcasted_iota(jnp.int32, (taps.shape[0], width), 0).astype(F32)
    falloff = jnp.exp(-decay[...] * lags)
    kernel = taps[...].astype(F32) * falloff
    high = kernel.astype(BF16)
    low = (kernel - high.astype(F32)).astype(BF16)
    k_spec = mm(e_taps[...], jnp.concatenate([high, high, low], axis=0))

    for i in range(3):
        x = mm(p_in[...], proj[i]).reshape(span + edge, 8, width)
        px[i, edge:] = x[edge:]
        for k in range(1, FK):
            px[i, edge - k] = jnp.where(row8 == 0, pltpu.roll(prev8[i], k, 0), x[edge - k])
    cots[...] = mm(p_in[edge * 8 :, :], cot[...]).reshape(span, 8, width)

    step = 8
    for i in range(3):
        for lane in lanes:
            weights = [jnp.broadcast_to(short[i, lag : lag + 1, lane], (8, 128)) for lag in range(FK)]
            for r in range(0, span, step):
                total = weights[0] * px[i, r + edge : r + edge + step, :, lane]
                for lag in range(1, FK):
                    total = total + weights[lag] * px[i, r + edge - lag : r + edge - lag + step, :, lane]
                feat[i, r : r + step, :, lane] = total

    def conv8(last, first, weights, whole):
        total = weights[0:1] * first if whole else jnp.zeros((8, width), F32)
        for lag in range(1, FK):
            rolled = pltpu.roll(first, lag, 0) if whole else 0.0
            total = total + weights[lag : lag + 1] * jnp.where(row8 < lag, pltpu.roll(last, lag, 0), rolled)
        return total

    ends = [proj[i, length - 16 :, :].astype(F32)[8:] for i in range(3)]
    feat_next = [None] + [conv8(ends[i], next8[i], short[i], True) for i in (1, 2)]
    mixed_next = feat_next[1] * feat_next[2]
    grad_next = after[:136]
    fix = cot_next * conv8(ends[0], None, short[0], False)
    rows = [grad_next[8 * r : 8 * r + 8] for r in range(17)]
    for r in range(edge):
        rows[r] = rows[r] + jnp.where(row8 == 0, pltpu.roll(fix, (8 - r) % 8, 0), 0.0)
    grad_next = jnp.concatenate(rows + [jnp.zeros((8, width), F32)], axis=0).astype(BF16)
    mixed_edge = jnp.concatenate([before[:128], mixed_next, jnp.zeros((8, width), F32)], axis=0).astype(BF16)

    flat = lambda value: value.reshape(length, width)
    mixed = flat(feat[1] * feat[2]).astype(BF16)
    grad_own = flat(cots[...] * feat[0]).astype(BF16)
    m_spec = mm(e_own[...], jnp.concatenate([mixed, mixed], axis=0)) + mm(e_prev[...], mixed_edge)
    g_own = mm(e_own[...], jnp.concatenate([grad_own, grad_own], axis=0))
    g_spec = g_own + mm(e_next[...], grad_next)

    half = k_spec.shape[0] // 2
    parts = lambda value: (value[:half], value[half:])
    (kr, ki), (mr, mi), (gr, gi), (hr, hi) = parts(k_spec), parts(m_spec), parts(g_spec), parts(g_own)

    def back_to(matrix, real, imaginary):
        spectrum = jnp.concatenate([real, imaginary], axis=0).astype(BF16)
        return mm(matrix[...], jnp.concatenate([spectrum, spectrum], axis=0))

    filtered = back_to(s_own, mr * kr - mi * ki, mr * ki + mi * kr)
    grad_mixed = back_to(s_own, gr * kr + gi * ki, gi * kr - gr * ki)
    filter_sums = back_to(s_lags, hr * mr + hi * mi, hi * mr - hr * mi) * falloff

    own = filtered[:length].reshape(span, 8, width)
    product[0] = flat(feat[0] * own).astype(BF16)
    back = grad_mixed[:length].reshape(span, 8, width)
    grad[0, :span] = cots[...] * own
    grad[1, :span] = back * feat[2]
    grad[2, :span] = back * feat[1]
    back_next = grad_mixed[length:]
    edge_next = [cot_next * filtered[length:], back_next * feat_next[2], back_next * feat_next[1]]
    for i in range(3):
        for k in range(edge):
            grad[i, span + k] = jnp.where(row8 == 7, pltpu.roll(edge_next[i], 7 - k, 0), pltpu.roll(grad[i, k], 7, 0))

    short_rows = []
    for i in range(3):
        rows = [[] for _ in range(FK)]
        for lane in lanes:
            sums = [jnp.zeros((8, 128), F32)] * FK
            for r in range(0, span, step):
                here = px[i, r + edge : r + edge + step, :, lane]
                for lag in range(FK):
                    value = grad[i, r + lag : r + lag + step, :, lane]
                    sums[lag] = sums[lag] + jnp.sum(here * value, axis=0)
            for lag in range(FK):
                rows[lag].append(jnp.sum(sums[lag], axis=0, keepdims=True))
        short_rows += [jnp.concatenate(row, axis=1) for row in rows]

    step, block = pl.program_id(0), first + pl.program_id(0)
    ranks, slot, _ = filter_held.shape
    per, share = filter_sums.shape[0] // ranks, short_held.shape[0]
    copies = [
        pltpu.make_async_copy(
            filter_held, sums_out.at[:, pl.ds(pl.multiple_of(block * slot, slot), slot), :], done.at[0]
        ),
        pltpu.make_async_copy(
            short_held,
            sums_out.at[pl.ds(block * share, share), pl.ds(sums_out.shape[1] - SHORT, SHORT), :],
            done.at[1],
        ),
    ]

    @pl.when(step > 0)
    def _():
        for copy in copies:
            copy.wait()

    by_rank = filter_sums.reshape(ranks, per, width) if per % 8 == 0 else jnp.stack(
        [filter_sums[rank * per : rank * per + per] for rank in range(ranks)]
    )
    if slot > per:
        by_rank = jnp.concatenate([by_rank, jnp.zeros((ranks, slot - per, width), F32)], axis=1)
    filter_held[...] = by_rank.astype(BF16)
    sums = jnp.concatenate(short_rows + [jnp.zeros((SHORT - len(short_rows), width), F32)], axis=0)
    for rank in range(share):
        held = pltpu.roll(sums, width - rank * (width // share), 1) if rank else sums
        short_held[rank] = held.astype(BF16)
    for copy in copies:
        copy.start()

    @pl.when(step == pl.num_programs(0) - 1)
    def _():
        for copy in copies:
            copy.wait()


def outputs_kernel(product, grad, short, p_out, gated, grad_proj):
    length, width = product.shape[1:]
    span = length // 8
    gated[...] = mm(p_out[...], product[0]).astype(BF16)
    for i in range(3):
        lanes = []
        for lane in lanes_of(width):
            taps = spread_taps(short, i, lane)
            chunks = []
            for r in range(0, span, 8):
                total = None
                for lag in range(FK):
                    part = grad[0, i, r + lag : r + lag + 8, :, lane] * taps[lag]
                    total = part if total is None else total + part
                chunks.append(total)
            lanes.append(jnp.concatenate(chunks, axis=0))
        result = jnp.concatenate(lanes, axis=2).reshape(length, width).astype(BF16)
        grad_proj[i] = mm(p_out[...], result).astype(BF16)


def whole(array):
    return pl.BlockSpec(array.shape, lambda c: (0,) * array.ndim)


def columns(rows, width, first=0):
    lead = (0,) * len(rows)
    return pl.BlockSpec(tuple(rows) + (width,), lambda c: lead + (first + c,))


def one_of(array, first=0):
    tail = (0,) * (len(array.shape) - 1)
    return pl.BlockSpec((1,) + tuple(array.shape[1:]), lambda c: (first + c,) + tail)


IN_VMEM = pl.BlockSpec(memory_space=pltpu.VMEM)
FAR = pl.BlockSpec(memory_space=pl.ANY)


def call(kernel, name, operands, outputs, cost=1, held=(), free=(), **options):
    arrays = [
        array if at in free else pltpu.with_memory_space_constraint(array, pltpu.HBM)
        for at, (array, _) in enumerate(operands)
    ]
    return pl.pallas_call(
        kernel,
        in_specs=[spec for _, spec in operands] + [FAR] * len(held),
        out_specs=[spec for _, spec in outputs],
        out_shape=[shape for shape, _ in outputs],
        input_output_aliases={len(operands) + at: at for at in range(len(held))},
        compiler_params=pltpu.CompilerParams(vmem_limit_bytes=40 << 20),
        cost_estimate=pl.CostEstimate(flops=cost * 10**9, bytes_accessed=10**6, transcendentals=0),
        name=name,
        **options,
    )(*arrays, *held)


def squares_kernel(rows, share, sums, raw, payload):
    ranks, slots, width = sums.shape
    total = sums[0].astype(F32)
    for rank in range(1, ranks):
        total = total + sums[rank].astype(F32)
    slot = -(-rows // 16) * 16
    pieces = [total[at : at + rows] for at in range(0, slots - SHORT, slot)]
    raw[...] = jnp.concatenate(pieces, axis=1)
    lane = lax.broadcasted_iota(jnp.int32, (SHORT, width), 1)
    short = jnp.where(lane < share, total[slots - SHORT :], 0.0)
    squares = jnp.sum(short * short, keepdims=True)
    for piece in pieces:
        squares = squares + jnp.sum(piece * piece, keepdims=True)
    high = squares.astype(BF16).astype(F32)
    row = lax.broadcasted_iota(jnp.int32, (24, width), 0)
    block = jnp.where(row < 3 * FK, short[:24], jnp.where(row == 3 * FK, high, squares - high)).astype(BF16)
    for other in range(payload.shape[0]):
        payload[other] = block


def scale_kernel(entries, share, mine, raw, gathered, grad_short, grad_filter):
    everyone, rows, width = gathered.shape
    total = jnp.zeros((8, width), F32)
    for other in range(everyone):
        total = total + gathered[other].astype(F32)[16:]
    total = total[5:6, :1] + total[6:7, :1]
    scale = jnp.minimum(1.0, math.sqrt(entries) / jnp.sqrt(total))
    grad_filter[...] = scale * raw[...]
    step = mine[1]
    for rank in range(raw.shape[1] // share):
        block = gathered[rank * step + mine[0]].astype(F32) * scale
        for i in range(3):
            grad_short[i, :, rank * share : (rank + 1) * share] = block[i * FK : (i + 1) * FK, :share]


def shards(projected, short_taps, filter_taps, decay, cotangent):
    length, _, channels = projected.shape
    ranks, groups = lax.axis_size("seq"), lax.axis_size("ch")
    rows = filter_taps.shape[0]
    count = rows * ranks
    width = min(256, channels // CHUNKS)
    share = channels // ranks
    slot = -(-rows // 16) * 16
    size, span = 2 * length, length // 8
    some = 144
    proj, cot, short, decay = jnp.transpose(projected, (1, 0, 2)), cotangent, short_taps, decay[None]
    full = lambda kind, *shape: (jax.ShapeDtypeStruct(shape, kind), IN_VMEM)
    vmem = lambda kind, *shape: pltpu.VMEM(shape, kind)
    far = lambda *arrays: [(array, FAR) for array in arrays]
    semaphores = pltpu.SemaphoreType.DMA((10,))
    own = interleaved(span)
    after = length + np.arange(8)
    chunk = channels // CHUNKS
    blocks = chunk // width

    prev, later, taps = [], [], None
    for k in range(CHUNKS):
        operands = far(proj, cot, short)
        results = [full(BF16, 152, chunk), full(BF16, 160, chunk)]
        scratch = [
            vmem(BF16, 2, some, chunk), vmem(BF16, 2, some, chunk), vmem(BF16, 3, 16, chunk), vmem(F32, 3, FK, chunk),
            vmem(BF16, 8 * (15 + FK), some), vmem(BF16, 8 * (16 + FK), some), vmem(F32, 8 * (15 + FK), width),
            vmem(F32, 8 * (15 + FK), width), vmem(F32, 8 * (16 + FK), width), vmem(F32, 8 * 17, width), semaphores,
        ]
        if k == 0:
            operands += far(filter_taps)
            results.append((pltpu.HBM((ranks, rows, channels), BF16), FAR))
            scratch = [vmem(F32, rows, channels), vmem(BF16, ranks, rows, channels)] + scratch
        forward, backward, *spread = call(
            functools.partial(edges_kernel, k * chunk), "edges", operands, results, cost=10 if k else 1,
            scratch_shapes=scratch,
        )
        if k == 0:
            taps = lax.all_to_all(spread[0], "seq", 0, 0).reshape(count, channels)
        else:
            forward, backward, prev[-1], later[-1] = lax.optimization_barrier((forward, backward, prev[-1], later[-1]))
        prev.append(from_behind(forward, "seq", 1))
        later.append(from_behind(backward, "seq", -1))

    high, low = analysis(own, size)
    k_high, k_low = analysis(np.arange(count), size)
    constants = [
        np.concatenate([high, low], axis=1),
        analysis(np.concatenate([interleaved(16, -128), after]), size, 8)[0],
        analysis(interleaved(17, length), size, 8)[0],
        np.concatenate([k_high, k_low, k_high], axis=1),
        np.concatenate(list(synthesis(np.concatenate([own, after]), size)), axis=1),
        np.concatenate(list(synthesis(np.arange(count), size)), axis=1),
        pick(interleaved(span, 0, 1 - FK), length),
    ]
    constants = [(jnp.asarray(constant), whole(constant)) for constant in constants]
    held = ()
    for k in range(CHUNKS):
        first = k * blocks
        results = [
            pltpu.HBM((CHUNKS * blocks, length, width), BF16),
            pltpu.HBM((CHUNKS * blocks, 3, span + FK - 1, 8, width), F32),
        ]
        held = call(
            functools.partial(operator_kernel, first), "operator",
            [
                (proj, columns((3, length), width, first)), (cot, columns((length,), width, first)),
                (prev[k], columns((152,), width)), (later[k], columns((160,), width)),
                (short, columns((3, FK), width, first)), (taps, columns((count,), width, first)),
                (decay, columns((1,), width, first)),
            ] + constants,
            [(result, one_of(result, first)) for result in results]
            + [(pltpu.HBM((ranks, CHUNKS * blocks * slot + SHORT, width), BF16), FAR)],
            cost=12,
            held=held,
            free=(2, 3, 5),
            grid=(blocks,),
            scratch_shapes=[
                vmem(F32, 3, span + FK - 1, 8, width), vmem(F32, 3, span, 8, width), vmem(F32, span, 8, width),
                vmem(BF16, ranks, slot, width), vmem(BF16, ranks * width // channels, SHORT, width),
                pltpu.SemaphoreType.DMA((2,)),
            ],
        )
    product, grad, sums = held
    p_out = jnp.asarray(pick(own, length).T)
    gated, grad_proj = call(
        outputs_kernel, "outputs",
        [(product, one_of(product)), (grad, one_of(grad)), (short, columns((3, FK), width)), (p_out, whole(p_out))],
        [
            (jax.ShapeDtypeStruct((length, channels), BF16), columns((length,), width)),
            (jax.ShapeDtypeStruct((3, length, channels), BF16), columns((3, length), width)),
        ],
        cost=8,
        grid=(CHUNKS * blocks,),
    )
    sums, gated, grad_proj = lax.optimization_barrier((lax.all_to_all(sums, "seq", 0, 0), gated, grad_proj))

    vmem = pl.BlockSpec(memory_space=pltpu.VMEM)
    raw, payload = pl.pallas_call(
        functools.partial(squares_kernel, rows, share),
        in_specs=[vmem],
        out_specs=[vmem] * 2,
        out_shape=[
            jax.ShapeDtypeStruct((rows, channels), F32),
            jax.ShapeDtypeStruct((ranks * groups, 24, width), BF16),
        ],
        compiler_params=pltpu.CompilerParams(vmem_limit_bytes=32 << 20),
        name="squares",
    )(sums)
    gathered = lax.all_to_all(payload, ("seq", "ch"), 0, 0)
    mine = jnp.stack([lax.axis_index("ch"), jnp.int32(groups)])
    entries = (rows * ranks + 3 * FK) * channels * groups
    grad_short, grad_filter = pl.pallas_call(
        functools.partial(scale_kernel, entries, share),
        in_specs=[pl.BlockSpec(memory_space=pltpu.SMEM), vmem, vmem],
        out_specs=[vmem] * 2,
        out_shape=[
            jax.ShapeDtypeStruct((3, FK, channels), F32),
            jax.ShapeDtypeStruct((rows, channels), F32),
        ],
        compiler_params=pltpu.CompilerParams(vmem_limit_bytes=32 << 20),
        name="scale",
    )(mine, raw, gathered)
    return (gated, jnp.transpose(grad_proj, (1, 0, 2)), grad_short, grad_filter)


def solution(mesh):
    placed = (P("seq", None, "ch"), P(None, None, "ch"), P("seq", "ch"), P("ch"), P("seq", "ch"))
    return jax.shard_map(
        shards,
        mesh=mesh,
        in_specs=placed,
        out_specs=(P("seq", "ch"), P("seq", None, "ch"), P(None, None, "ch"), P("seq", "ch")),
        check_vma=False,
    )
```

```python
import functools
import math

import jax
import jax.numpy as jnp
import ml_dtypes
import numpy as np
from jax import lax
from jax.experimental import pallas as pl
from jax.experimental.pallas import tpu as pltpu
from jax.sharding import PartitionSpec as P


FK = 7
BF16 = jnp.bfloat16
F32 = jnp.float32
CHUNKS = 2
SHORT = 32
STEP = 64


def from_behind(value, axis, by):
    count = lax.axis_size(axis)
    pairs = [(i, i + by) for i in range(count) if 0 <= i + by < count]
    return lax.ppermute(value, axis, pairs)


def interleaved(span, first=0, low=0):
    return np.array([first + s * span + r for r in range(low, span) for s in range(8)])


def pick(positions, count):
    out = np.zeros((len(positions), count), np.float32)
    for row, at in enumerate(positions):
        if 0 <= at < count:
            out[row, at] = 1.0
    return out.astype(ml_dtypes.bfloat16)


def halves(matrix):
    high = matrix.astype(np.float32).astype(ml_dtypes.bfloat16)
    low = (matrix - high.astype(np.float64)).astype(np.float32).astype(ml_dtypes.bfloat16)
    return np.stack([high, low])


def analysis(positions, size, pad=0):
    freq = np.arange(size // 2)[:, None]
    angle = np.pi * (((2 * freq + 1) * np.asarray(positions)[None, :]) % (2 * size)) / size
    matrix = np.concatenate([np.cos(angle), -np.sin(angle)], axis=0)
    return halves(np.pad(matrix, ((0, 0), (0, pad))))


def synthesis(positions, size):
    freq = np.arange(size // 2)[None, :]
    angle = np.pi * (((2 * freq + 1) * np.asarray(positions)[:, None]) % (2 * size)) / size
    return halves(np.concatenate([np.cos(angle), -np.sin(angle)], axis=1) * (2.0 / size))


def mm(a, b):
    return jnp.dot(a, b, preferred_element_type=F32)


def picked(span, first, length):
    shape = ((span + FK - 1) * 8, length)
    row, column = (lax.broadcasted_iota(jnp.int32, shape, axis) for axis in (0, 1))
    position = first + (row & 7) * span + (row >> 3) - (FK - 1)
    return jnp.where(position == column, 1.0, 0.0).astype(BF16)


def lanes_of(width):
    return [slice(at, at + 128) for at in range(0, width, 128)]


def featurized(x, taps, lane, row, rows):
    total = None
    for lag in range(FK):
        at = row + 8 * (FK - 1 - lag)
        part = x[at : at + rows, lane].reshape(rows // 8, 8, 128) * taps[lag]
        total = part if total is None else total + part
    return total


def spread_taps(short, i, lane):
    return [jnp.broadcast_to(short[i, lag : lag + 1, lane], (8, 128)) for lag in range(FK)]


def fetch(pairs, semaphores):
    copies = [pltpu.make_async_copy(source, into, semaphores.at[at]) for at, (source, into) in enumerate(pairs)]
    for copy in copies:
        copy.start()
    return copies


def window(block, width):
    return pl.ds(pl.multiple_of(block * width, width), width)


def edges_kernel(at, proj, cot, short, *refs):
    tails, heads, few, taps_held, p_tail, p_head, first, second, zeroth, held, semaphores = refs[-11:]
    with_taps = len(refs) > 13
    if with_taps:
        taps, forward, backward, spread, all_taps, all_spread = refs[:6]
    else:
        forward, backward = refs[:2]
    length, channels = cot.shape[0], forward.shape[1]
    here = pl.ds(at, channels)
    some, width = p_tail.shape[1], first.shape[1]
    tail, head = 16, 17
    pairs = [
        (proj.at[1, length - some :, here], tails.at[0]),
        (proj.at[2, length - some :, here], tails.at[1]),
        (proj.at[0, :some, here], heads.at[0]),
        (cot.at[:some, here], heads.at[1]),
        (proj.at[0, length - 16 :, here], few.at[0]),
        (proj.at[1, :16, here], few.at[1]),
        (proj.at[2, :16, here], few.at[2]),
        (short.at[:, :, here], taps_held),
    ]
    copies = fetch(pairs + [(taps, all_taps)] if with_taps else pairs, semaphores)
    p_tail[...] = picked(tail, some - 128, some)
    p_head[...] = picked(head, 0, some)
    if with_taps:
        copies.pop().wait()
        all_spread[...] = jnp.broadcast_to(all_taps[...].astype(BF16)[None], all_spread.shape)
        sent = pltpu.make_async_copy(all_spread, spread, semaphores.at[9])
        sent.start()
    for copy in copies:
        copy.wait()

    def block(c, _):
        columns = window(c, width)
        first[...] = mm(p_tail[...], tails[0, :, columns])
        second[...] = mm(p_tail[...], tails[1, :, columns])
        zeroth[...] = mm(p_head[...], heads[0, :, columns])
        held[...] = mm(p_head[(FK - 1) * 8 :, :], heads[1, :, columns])
        for lane in lanes_of(width):
            wide = pl.ds(pl.multiple_of(c * width + lane.start, 128), 128)
            taps = [spread_taps(taps_held, i, wide) for i in range(3)]
            for r in range(0, 8 * tail, STEP):
                mixed = featurized(first, taps[1], lane, r, STEP) * featurized(second, taps[2], lane, r, STEP)
                forward[r : r + STEP, wide] = mixed.reshape(STEP, 128).astype(BF16)
            ends = [few[0, :, wide], tails[0, some - 16 :, wide], tails[1, some - 16 :, wide]]
            ends = [end.astype(F32)[8:] for end in ends]
            forward[8 * tail :, wide] = jnp.concatenate(ends, axis=0).astype(BF16)
            for r in range(0, 8 * head, STEP):
                rows = min(STEP, 8 * head - r)
                grad = featurized(zeroth, taps[0], lane, r, rows).reshape(rows, 128) * held[r : r + rows, lane]
                if rows < STEP:
                    starts = [heads[1, :16, wide], few[1, :, wide], few[2, :, wide]]
                    starts = [start.astype(F32)[:8] for start in starts]
                    backward[r:, wide] = jnp.concatenate([grad] + starts, axis=0).astype(BF16)
                else:
                    backward[r : r + rows, wide] = grad.astype(BF16)
        return 0

    lax.fori_loop(0, channels // width, block, 0)
    if with_taps:
        sent.wait()


def operator_kernel(
    first, proj, cot, prev, later, short, taps, decay,
    e_own, e_prev, e_next, e_taps, s_own, s_lags, p_in, *refs,
):
    product, grad, sums_out, px, feat, cots, filter_held, short_held, done = refs[-9:]
    grad = grad.at[0]
    length, width = cot.shape
    span = length // 8
    edge = FK - 1
    lanes = [slice(at, at + 128) for at in range(0, width, 128)]
    row8 = lax.broadcasted_iota(jnp.int32, (8, width), 0)

    before = prev[...].astype(F32)
    after = later[...].astype(F32)
    prev8 = [before[128 + 8 * i : 136 + 8 * i] for i in range(3)]
    cot_next = after[136:144]
    next8 = [None, after[144:152], after[152:160]]

    lags = lax.broadcasted_iota(jnp.int32, (taps.shape[0], width), 0).astype(F32)
    falloff = jnp.exp(-decay[...] * lags)
    kernel = taps[...].astype(F32) * falloff
    high = kernel.astype(BF16)
    low = (kernel - high.astype(F32)).astype(BF16)
    k_spec = mm(e_taps[...], jnp.concatenate([high, high, low], axis=0))

    for i in range(3):
        x = mm(p_in[...], proj[i]).reshape(span + edge, 8, width)
        px[i, edge:] = x[edge:]
        for k in range(1, FK):
            px[i, edge - k] = jnp.where(row8 == 0, pltpu.roll(prev8[i], k, 0), x[edge - k])
    cots[...] = mm(p_in[edge * 8 :, :], cot[...]).reshape(span, 8, width)

    step = 8
    for i in range(3):
        for lane in lanes:
            weights = [jnp.broadcast_to(short[i, lag : lag + 1, lane], (8, 128)) for lag in range(FK)]
            for r in range(0, span, step):
                total = weights[0] * px[i, r + edge : r + edge + step, :, lane]
                for lag in range(1, FK):
                    total = total + weights[lag] * px[i, r + edge - lag : r + edge - lag + step, :, lane]
                feat[i, r : r + step, :, lane] = total

    def conv8(last, first, weights, whole):
        total = weights[0:1] * first if whole else jnp.zeros((8, width), F32)
        for lag in range(1, FK):
            rolled = pltpu.roll(first, lag, 0) if whole else 0.0
            total = total + weights[lag : lag + 1] * jnp.where(row8 < lag, pltpu.roll(last, lag, 0), rolled)
        return total

    ends = [proj[i, length - 16 :, :].astype(F32)[8:] for i in range(3)]
    feat_next = [None] + [conv8(ends[i], next8[i], short[i], True) for i in (1, 2)]
    mixed_next = feat_next[1] * feat_next[2]
    grad_next = after[:136]
    fix = cot_next * conv8(ends[0], None, short[0], False)
    rows = [grad_next[8 * r : 8 * r + 8] for r in range(17)]
    for r in range(edge):
        rows[r] = rows[r] + jnp.where(row8 == 0, pltpu.roll(fix, (8 - r) % 8, 0), 0.0)
    grad_next = jnp.concatenate(rows + [jnp.zeros((8, width), F32)], axis=0).astype(BF16)
    mixed_edge = jnp.concatenate([before[:128], mixed_next, jnp.zeros((8, width), F32)], axis=0).astype(BF16)

    flat = lambda value: value.reshape(length, width)
    mixed = flat(feat[1] * feat[2]).astype(BF16)
    grad_own = flat(cots[...] * feat[0]).astype(BF16)
    m_spec = mm(e_own[...], jnp.concatenate([mixed, mixed], axis=0)) + mm(e_prev[...], mixed_edge)
    g_own = mm(e_own[...], jnp.concatenate([grad_own, grad_own], axis=0))
    g_spec = g_own + mm(e_next[...], grad_next)

    half = k_spec.shape[0] // 2
    parts = lambda value: (value[:half], value[half:])
    (kr, ki), (mr, mi), (gr, gi), (hr, hi) = parts(k_spec), parts(m_spec), parts(g_spec), parts(g_own)

    def back_to(matrix, real, imaginary):
        spectrum = jnp.concatenate([real, imaginary], axis=0).astype(BF16)
        return mm(matrix[...], jnp.concatenate([spectrum, spectrum], axis=0))

    filtered = back_to(s_own, mr * kr - mi * ki, mr * ki + mi * kr)
    grad_mixed = back_to(s_own, gr * kr + gi * ki, gi * kr - gr * ki)
    filter_sums = back_to(s_lags, hr * mr + hi * mi, hi * mr - hr * mi) * falloff

    own = filtered[:length].reshape(span, 8, width)
    product[0] = flat(feat[0] * own).astype(BF16)
    back = grad_mixed[:length].reshape(span, 8, width)
    grad[0, :span] = cots[...] * own
    grad[1, :span] = back * feat[2]
    grad[2, :span] = back * feat[1]
    back_next = grad_mixed[length:]
    edge_next = [cot_next * filtered[length:], back_next * feat_next[2], back_next * feat_next[1]]
    for i in range(3):
        for k in range(edge):
            grad[i, span + k] = jnp.where(row8 == 7, pltpu.roll(edge_next[i], 7 - k, 0), pltpu.roll(grad[i, k], 7, 0))

    short_rows = []
    for i in range(3):
        rows = [[] for _ in range(FK)]
        for lane in lanes:
            sums = [jnp.zeros((8, 128), F32)] * FK
            for r in range(0, span, step):
                here = px[i, r + edge : r + edge + step, :, lane]
                for lag in range(FK):
                    value = grad[i, r + lag : r + lag + step, :, lane]
                    sums[lag] = sums[lag] + jnp.sum(here * value, axis=0)
            for lag in range(FK):
                rows[lag].append(jnp.sum(sums[lag], axis=0, keepdims=True))
        short_rows += [jnp.concatenate(row, axis=1) for row in rows]

    step, block = pl.program_id(0), first + pl.program_id(0)
    ranks, slot, _ = filter_held.shape
    per, share = filter_sums.shape[0] // ranks, short_held.shape[0]
    copies = [
        pltpu.make_async_copy(
            filter_held, sums_out.at[:, pl.ds(pl.multiple_of(block * slot, slot), slot), :], done.at[0]
        ),
        pltpu.make_async_copy(
            short_held,
            sums_out.at[pl.ds(block * share, share), pl.ds(sums_out.shape[1] - SHORT, SHORT), :],
            done.at[1],
        ),
    ]

    @pl.when(step > 0)
    def _():
        for copy in copies:
            copy.wait()

    by_rank = filter_sums.reshape(ranks, per, width) if per % 8 == 0 else jnp.stack(
        [filter_sums[rank * per : rank * per + per] for rank in range(ranks)]
    )
    if slot > per:
        by_rank = jnp.concatenate([by_rank, jnp.zeros((ranks, slot - per, width), F32)], axis=1)
    filter_held[...] = by_rank.astype(BF16)
    sums = jnp.concatenate(short_rows + [jnp.zeros((SHORT - len(short_rows), width), F32)], axis=0)
    for rank in range(share):
        held = pltpu.roll(sums, width - rank * (width // share), 1) if rank else sums
        short_held[rank] = held.astype(BF16)
    for copy in copies:
        copy.start()

    @pl.when(step == pl.num_programs(0) - 1)
    def _():
        for copy in copies:
            copy.wait()


def outputs_kernel(product, grad, short, p_out, gated, grad_proj):
    length, width = product.shape[1:]
    span = length // 8
    gated[...] = mm(p_out[...], product[0]).astype(BF16)
    for i in range(3):
        lanes = []
        for lane in lanes_of(width):
            taps = spread_taps(short, i, lane)
            chunks = []
            for r in range(0, span, 8):
                total = None
                for lag in range(FK):
                    part = grad[0, i, r + lag : r + lag + 8, :, lane] * taps[lag]
                    total = part if total is None else total + part
                chunks.append(total)
            lanes.append(jnp.concatenate(chunks, axis=0))
        result = jnp.concatenate(lanes, axis=2).reshape(length, width).astype(BF16)
        grad_proj[i] = mm(p_out[...], result).astype(BF16)


def whole(array):
    return pl.BlockSpec(array.shape, lambda c: (0,) * array.ndim)


def columns(rows, width, first=0):
    lead = (0,) * len(rows)
    return pl.BlockSpec(tuple(rows) + (width,), lambda c: lead + (first + c,))


def one_of(array, first=0):
    tail = (0,) * (len(array.shape) - 1)
    return pl.BlockSpec((1,) + tuple(array.shape[1:]), lambda c: (first + c,) + tail)


IN_VMEM = pl.BlockSpec(memory_space=pltpu.VMEM)
FAR = pl.BlockSpec(memory_space=pl.ANY)


def call(kernel, name, operands, outputs, cost=1, held=(), free=(), **options):
    arrays = [
        array if at in free else pltpu.with_memory_space_constraint(array, pltpu.HBM)
        for at, (array, _) in enumerate(operands)
    ]
    return pl.pallas_call(
        kernel,
        in_specs=[spec for _, spec in operands] + [FAR] * len(held),
        out_specs=[spec for _, spec in outputs],
        out_shape=[shape for shape, _ in outputs],
        input_output_aliases={len(operands) + at: at for at in range(len(held))},
        compiler_params=pltpu.CompilerParams(vmem_limit_bytes=40 << 20),
        cost_estimate=pl.CostEstimate(flops=cost * 10**9, bytes_accessed=10**6, transcendentals=0),
        name=name,
        **options,
    )(*arrays, *held)


def squares_kernel(rows, share, sums, raw, payload):
    ranks, slots, width = sums.shape
    total = sums[0].astype(F32)
    for rank in range(1, ranks):
        total = total + sums[rank].astype(F32)
    slot = -(-rows // 16) * 16
    pieces = [total[at : at + rows] for at in range(0, slots - SHORT, slot)]
    raw[...] = jnp.concatenate(pieces, axis=1)
    lane = lax.broadcasted_iota(jnp.int32, (SHORT, width), 1)
    short = jnp.where(lane < share, total[slots - SHORT :], 0.0)
    squares = jnp.sum(short * short, keepdims=True)
    for piece in pieces:
        squares = squares + jnp.sum(piece * piece, keepdims=True)
    high = squares.astype(BF16).astype(F32)
    row = lax.broadcasted_iota(jnp.int32, (24, width), 0)
    block = jnp.where(row < 3 * FK, short[:24], jnp.where(row == 3 * FK, high, squares - high)).astype(BF16)
    for other in range(payload.shape[0]):
        payload[other] = block


def scale_kernel(entries, share, mine, raw, gathered, grad_short, grad_filter):
    everyone, rows, width = gathered.shape
    total = jnp.zeros((8, width), F32)
    for other in range(everyone):
        total = total + gathered[other].astype(F32)[16:]
    total = total[5:6, :1] + total[6:7, :1]
    scale = jnp.minimum(1.0, math.sqrt(entries) / jnp.sqrt(total))
    grad_filter[...] = scale * raw[...]
    step = mine[1]
    for rank in range(raw.shape[1] // share):
        block = gathered[rank * step + mine[0]].astype(F32) * scale
        for i in range(3):
            grad_short[i, :, rank * share : (rank + 1) * share] = block[i * FK : (i + 1) * FK, :share]


def shards(projected, short_taps, filter_taps, decay, cotangent):
    length, _, channels = projected.shape
    ranks, groups = lax.axis_size("seq"), lax.axis_size("ch")
    rows = filter_taps.shape[0]
    count = rows * ranks
    width = min(256, channels // CHUNKS)
    share = channels // ranks
    slot = -(-rows // 16) * 16
    size, span = 2 * length, length // 8
    some = 144
    proj, cot, short, decay = jnp.transpose(projected, (1, 0, 2)), cotangent, short_taps, decay[None]
    full = lambda kind, *shape: (jax.ShapeDtypeStruct(shape, kind), IN_VMEM)
    vmem = lambda kind, *shape: pltpu.VMEM(shape, kind)
    far = lambda *arrays: [(array, FAR) for array in arrays]
    semaphores = pltpu.SemaphoreType.DMA((10,))
    own = interleaved(span)
    after = length + np.arange(8)
    chunk = channels // CHUNKS
    blocks = chunk // width

    prev, later, taps = [], [], None
    for k in range(CHUNKS):
        operands = far(proj, cot, short)
        results = [full(BF16, 152, chunk), full(BF16, 160, chunk)]
        scratch = [
            vmem(BF16, 2, some, chunk), vmem(BF16, 2, some, chunk), vmem(BF16, 3, 16, chunk), vmem(F32, 3, FK, chunk),
            vmem(BF16, 8 * (15 + FK), some), vmem(BF16, 8 * (16 + FK), some), vmem(F32, 8 * (15 + FK), width),
            vmem(F32, 8 * (15 + FK), width), vmem(F32, 8 * (16 + FK), width), vmem(F32, 8 * 17, width), semaphores,
        ]
        if k == 0:
            operands += far(filter_taps)
            results.append((pltpu.HBM((ranks, rows, channels), BF16), FAR))
            scratch = [vmem(F32, rows, channels), vmem(BF16, ranks, rows, channels)] + scratch
        forward, backward, *spread = call(
            functools.partial(edges_kernel, k * chunk), "edges", operands, results, cost=10 if k else 1,
            scratch_shapes=scratch,
        )
        if k == 0:
            taps = lax.all_to_all(spread[0], "seq", 0, 0).reshape(count, channels)
        prev.append(from_behind(forward, "seq", 1))
        later.append(from_behind(backward, "seq", -1))

    high, low = analysis(own, size)
    k_high, k_low = analysis(np.arange(count), size)
    constants = [
        np.concatenate([high, low], axis=1),
        analysis(np.concatenate([interleaved(16, -128), after]), size, 8)[0],
        analysis(interleaved(17, length), size, 8)[0],
        np.concatenate([k_high, k_low, k_high], axis=1),
        np.concatenate(list(synthesis(np.concatenate([own, after]), size)), axis=1),
        np.concatenate(list(synthesis(np.arange(count), size)), axis=1),
        pick(interleaved(span, 0, 1 - FK), length),
    ]
    constants = [(jnp.asarray(constant), whole(constant)) for constant in constants]
    held = ()
    for k in range(CHUNKS):
        first = k * blocks
        results = [
            pltpu.HBM((CHUNKS * blocks, length, width), BF16),
            pltpu.HBM((CHUNKS * blocks, 3, span + FK - 1, 8, width), F32),
        ]
        held = call(
            functools.partial(operator_kernel, first), "operator",
            [
                (proj, columns((3, length), width, first)), (cot, columns((length,), width, first)),
                (prev[k], columns((152,), width)), (later[k], columns((160,), width)),
                (short, columns((3, FK), width, first)), (taps, columns((count,), width, first)),
                (decay, columns((1,), width, first)),
            ] + constants,
            [(result, one_of(result, first)) for result in results]
            + [(pltpu.HBM((ranks, CHUNKS * blocks * slot + SHORT, width), BF16), FAR)],
            cost=12,
            held=held,
            free=(2, 3, 5),
            grid=(blocks,),
            scratch_shapes=[
                vmem(F32, 3, span + FK - 1, 8, width), vmem(F32, 3, span, 8, width), vmem(F32, span, 8, width),
                vmem(BF16, ranks, slot, width), vmem(BF16, ranks * width // channels, SHORT, width),
                pltpu.SemaphoreType.DMA((2,)),
            ],
        )
    product, grad, sums = held
    p_out = jnp.asarray(pick(own, length).T)
    gated, grad_proj = call(
        outputs_kernel, "outputs",
        [(product, one_of(product)), (grad, one_of(grad)), (short, columns((3, FK), width)), (p_out, whole(p_out))],
        [
            (jax.ShapeDtypeStruct((length, channels), BF16), columns((length,), width)),
            (jax.ShapeDtypeStruct((3, length, channels), BF16), columns((3, length), width)),
        ],
        cost=8,
        grid=(CHUNKS * blocks,),
    )
    sums, gated, grad_proj = lax.optimization_barrier((lax.all_to_all(sums, "seq", 0, 0), gated, grad_proj))

    vmem = pl.BlockSpec(memory_space=pltpu.VMEM)
    raw, payload = pl.pallas_call(
        functools.partial(squares_kernel, rows, share),
        in_specs=[vmem],
        out_specs=[vmem] * 2,
        out_shape=[
            jax.ShapeDtypeStruct((rows, channels), F32),
            jax.ShapeDtypeStruct((ranks * groups, 24, width), BF16),
        ],
        compiler_params=pltpu.CompilerParams(vmem_limit_bytes=32 << 20),
        name="squares",
    )(sums)
    gathered = lax.all_to_all(payload, ("seq", "ch"), 0, 0)
    mine = jnp.stack([lax.axis_index("ch"), jnp.int32(groups)])
    entries = (rows * ranks + 3 * FK) * channels * groups
    grad_short, grad_filter = pl.pallas_call(
        functools.partial(scale_kernel, entries, share),
        in_specs=[pl.BlockSpec(memory_space=pltpu.SMEM), vmem, vmem],
        out_specs=[vmem] * 2,
        out_shape=[
            jax.ShapeDtypeStruct((3, FK, channels), F32),
            jax.ShapeDtypeStruct((rows, channels), F32),
        ],
        compiler_params=pltpu.CompilerParams(vmem_limit_bytes=32 << 20),
        name="scale",
    )(mine, raw, gathered)
    return (gated, jnp.transpose(grad_proj, (1, 0, 2)), grad_short, grad_filter)


def solution(mesh):
    placed = (P("seq", None, "ch"), P(None, None, "ch"), P("seq", "ch"), P("ch"), P("seq", "ch"))
    return jax.shard_map(
        shards,
        mesh=mesh,
        in_specs=placed,
        out_specs=(P("seq", "ch"), P("seq", None, "ch"), P(None, None, "ch"), P("seq", "ch")),
        check_vma=False,
    )
```

```python
import functools
import math

import jax
import jax.numpy as jnp
import ml_dtypes
import numpy as np
from jax import lax
from jax.experimental import pallas as pl
from jax.experimental.pallas import tpu as pltpu
from jax.sharding import PartitionSpec as P


FK = 7
BF16 = jnp.bfloat16
F32 = jnp.float32
CHUNKS = 2
SHORT = 32
STEP = 64


def from_behind(value, axis, by):
    count = lax.axis_size(axis)
    pairs = [(i, i + by) for i in range(count) if 0 <= i + by < count]
    return lax.ppermute(value, axis, pairs)


def interleaved(span, first=0, low=0):
    return np.array([first + s * span + r for r in range(low, span) for s in range(8)])


def pick(positions, count):
    out = np.zeros((len(positions), count), np.float32)
    for row, at in enumerate(positions):
        if 0 <= at < count:
            out[row, at] = 1.0
    return out.astype(ml_dtypes.bfloat16)


def halves(matrix):
    high = matrix.astype(np.float32).astype(ml_dtypes.bfloat16)
    low = (matrix - high.astype(np.float64)).astype(np.float32).astype(ml_dtypes.bfloat16)
    return np.stack([high, low])


def analysis(positions, size, pad=0):
    freq = np.arange(size // 2)[:, None]
    angle = np.pi * (((2 * freq + 1) * np.asarray(positions)[None, :]) % (2 * size)) / size
    matrix = np.concatenate([np.cos(angle), -np.sin(angle)], axis=0)
    return halves(np.pad(matrix, ((0, 0), (0, pad))))


def synthesis(positions, size):
    freq = np.arange(size // 2)[None, :]
    angle = np.pi * (((2 * freq + 1) * np.asarray(positions)[:, None]) % (2 * size)) / size
    return halves(np.concatenate([np.cos(angle), -np.sin(angle)], axis=1) * (2.0 / size))


def mm(a, b):
    return jnp.dot(a, b, preferred_element_type=F32)


def picked(span, first, length):
    shape = ((span + FK - 1) * 8, length)
    row, column = (lax.broadcasted_iota(jnp.int32, shape, axis) for axis in (0, 1))
    position = first + (row & 7) * span + (row >> 3) - (FK - 1)
    return jnp.where(position == column, 1.0, 0.0).astype(BF16)


def lanes_of(width):
    return [slice(at, at + 128) for at in range(0, width, 128)]


def featurized(x, taps, lane, row, rows):
    total = None
    for lag in range(FK):
        at = row + 8 * (FK - 1 - lag)
        part = x[at : at + rows, lane].reshape(rows // 8, 8, 128) * taps[lag]
        total = part if total is None else total + part
    return total


def spread_taps(short, i, lane):
    return [jnp.broadcast_to(short[i, lag : lag + 1, lane], (8, 128)) for lag in range(FK)]


def fetch(pairs, semaphores):
    copies = [pltpu.make_async_copy(source, into, semaphores.at[at]) for at, (source, into) in enumerate(pairs)]
    for copy in copies:
        copy.start()
    return copies


def window(block, width):
    return pl.ds(pl.multiple_of(block * width, width), width)


def edges_kernel(at, proj, cot, short, *refs):
    tails, heads, few, taps_held, p_tail, p_head, first, second, zeroth, held, semaphores = refs[-11:]
    with_taps = len(refs) > 13
    if with_taps:
        taps, forward, backward, spread, all_taps, all_spread = refs[:6]
    else:
        forward, backward = refs[:2]
    length, channels = cot.shape[0], forward.shape[1]
    here = pl.ds(at, channels)
    some, width = p_tail.shape[1], first.shape[1]
    tail, head = 16, 17
    pairs = [
        (proj.at[1, length - some :, here], tails.at[0]),
        (proj.at[2, length - some :, here], tails.at[1]),
        (proj.at[0, :some, here], heads.at[0]),
        (cot.at[:some, here], heads.at[1]),
        (proj.at[0, length - 16 :, here], few.at[0]),
        (proj.at[1, :16, here], few.at[1]),
        (proj.at[2, :16, here], few.at[2]),
        (short.at[:, :, here], taps_held),
    ]
    copies = fetch(pairs + [(taps, all_taps)] if with_taps else pairs, semaphores)
    p_tail[...] = picked(tail, some - 128, some)
    p_head[...] = picked(head, 0, some)
    if with_taps:
        copies.pop().wait()
        all_spread[...] = jnp.broadcast_to(all_taps[...].astype(BF16)[None], all_spread.shape)
        sent = pltpu.make_async_copy(all_spread, spread, semaphores.at[9])
        sent.start()
    for copy in copies:
        copy.wait()

    def block(c, _):
        columns = window(c, width)
        first[...] = mm(p_tail[...], tails[0, :, columns])
        second[...] = mm(p_tail[...], tails[1, :, columns])
        zeroth[...] = mm(p_head[...], heads[0, :, columns])
        held[...] = mm(p_head[(FK - 1) * 8 :, :], heads[1, :, columns])
        for lane in lanes_of(width):
            wide = pl.ds(pl.multiple_of(c * width + lane.start, 128), 128)
            taps = [spread_taps(taps_held, i, wide) for i in range(3)]
            for r in range(0, 8 * tail, STEP):
                mixed = featurized(first, taps[1], lane, r, STEP) * featurized(second, taps[2], lane, r, STEP)
                forward[r : r + STEP, wide] = mixed.reshape(STEP, 128).astype(BF16)
            ends = [few[0, :, wide], tails[0, some - 16 :, wide], tails[1, some - 16 :, wide]]
            ends = [end.astype(F32)[8:] for end in ends]
            forward[8 * tail :, wide] = jnp.concatenate(ends, axis=0).astype(BF16)
            for r in range(0, 8 * head, STEP):
                rows = min(STEP, 8 * head - r)
                grad = featurized(zeroth, taps[0], lane, r, rows).reshape(rows, 128) * held[r : r + rows, lane]
                if rows < STEP:
                    starts = [heads[1, :16, wide], few[1, :, wide], few[2, :, wide]]
                    starts = [start.astype(F32)[:8] for start in starts]
                    backward[r:, wide] = jnp.concatenate([grad] + starts, axis=0).astype(BF16)
                else:
                    backward[r : r + rows, wide] = grad.astype(BF16)
        return 0

    lax.fori_loop(0, channels // width, block, 0)
    if with_taps:
        sent.wait()


def operator_kernel(
    first, proj, cot, prev, later, short, taps, decay,
    e_own, e_prev, e_next, e_taps, s_own, s_lags, p_in, *refs,
):
    product, grad, sums_out, px, feat, cots, filter_held, short_held, done = refs[-9:]
    grad = grad.at[0]
    length, width = cot.shape
    span = length // 8
    edge = FK - 1
    lanes = [slice(at, at + 128) for at in range(0, width, 128)]
    row8 = lax.broadcasted_iota(jnp.int32, (8, width), 0)

    before = prev[...].astype(F32)
    after = later[...].astype(F32)
    prev8 = [before[128 + 8 * i : 136 + 8 * i] for i in range(3)]
    cot_next = after[136:144]
    next8 = [None, after[144:152], after[152:160]]

    lags = lax.broadcasted_iota(jnp.int32, (taps.shape[0], width), 0).astype(F32)
    falloff = jnp.exp(-decay[...] * lags)
    kernel = taps[...].astype(F32) * falloff
    high = kernel.astype(BF16)
    low = (kernel - high.astype(F32)).astype(BF16)
    k_spec = mm(e_taps[...], jnp.concatenate([high, high, low], axis=0))

    for i in range(3):
        x = mm(p_in[...], proj[i]).reshape(span + edge, 8, width)
        px[i, edge:] = x[edge:]
        for k in range(1, FK):
            px[i, edge - k] = jnp.where(row8 == 0, pltpu.roll(prev8[i], k, 0), x[edge - k])
    cots[...] = mm(p_in[edge * 8 :, :], cot[...]).reshape(span, 8, width)

    step = 8
    for i in range(3):
        for lane in lanes:
            weights = [jnp.broadcast_to(short[i, lag : lag + 1, lane], (8, 128)) for lag in range(FK)]
            for r in range(0, span, step):
                total = weights[0] * px[i, r + edge : r + edge + step, :, lane]
                for lag in range(1, FK):
                    total = total + weights[lag] * px[i, r + edge - lag : r + edge - lag + step, :, lane]
                feat[i, r : r + step, :, lane] = total

    def conv8(last, first, weights, whole):
        total = weights[0:1] * first if whole else jnp.zeros((8, width), F32)
        for lag in range(1, FK):
            rolled = pltpu.roll(first, lag, 0) if whole else 0.0
            total = total + weights[lag : lag + 1] * jnp.where(row8 < lag, pltpu.roll(last, lag, 0), rolled)
        return total

    ends = [proj[i, length - 16 :, :].astype(F32)[8:] for i in range(3)]
    feat_next = [None] + [conv8(ends[i], next8[i], short[i], True) for i in (1, 2)]
    mixed_next = feat_next[1] * feat_next[2]
    grad_next = after[:136]
    fix = cot_next * conv8(ends[0], None, short[0], False)
    rows = [grad_next[8 * r : 8 * r + 8] for r in range(17)]
    for r in range(edge):
        rows[r] = rows[r] + jnp.where(row8 == 0, pltpu.roll(fix, (8 - r) % 8, 0), 0.0)
    grad_next = jnp.concatenate(rows + [jnp.zeros((8, width), F32)], axis=0).astype(BF16)
    mixed_edge = jnp.concatenate([before[:128], mixed_next, jnp.zeros((8, width), F32)], axis=0).astype(BF16)

    flat = lambda value: value.reshape(length, width)
    mixed = flat(feat[1] * feat[2]).astype(BF16)
    grad_own = flat(cots[...] * feat[0]).astype(BF16)
    m_spec = mm(e_own[...], jnp.concatenate([mixed, mixed], axis=0)) + mm(e_prev[...], mixed_edge)
    g_own = mm(e_own[...], jnp.concatenate([grad_own, grad_own], axis=0))
    g_spec = g_own + mm(e_next[...], grad_next)

    half = k_spec.shape[0] // 2
    parts = lambda value: (value[:half], value[half:])
    (kr, ki), (mr, mi), (gr, gi), (hr, hi) = parts(k_spec), parts(m_spec), parts(g_spec), parts(g_own)

    def back_to(matrix, real, imaginary):
        spectrum = jnp.concatenate([real, imaginary], axis=0).astype(BF16)
        return mm(matrix[...], jnp.concatenate([spectrum, spectrum], axis=0))

    filtered = back_to(s_own, mr * kr - mi * ki, mr * ki + mi * kr)
    grad_mixed = back_to(s_own, gr * kr + gi * ki, gi * kr - gr * ki)
    filter_sums = back_to(s_lags, hr * mr + hi * mi, hi * mr - hr * mi) * falloff

    own = filtered[:length].reshape(span, 8, width)
    product[0] = flat(feat[0] * own).astype(BF16)
    back = grad_mixed[:length].reshape(span, 8, width)
    grad[0, :span] = cots[...] * own
    grad[1, :span] = back * feat[2]
    grad[2, :span] = back * feat[1]
    back_next = grad_mixed[length:]
    edge_next = [cot_next * filtered[length:], back_next * feat_next[2], back_next * feat_next[1]]
    for i in range(3):
        for k in range(edge):
            grad[i, span + k] = jnp.where(row8 == 7, pltpu.roll(edge_next[i], 7 - k, 0), pltpu.roll(grad[i, k], 7, 0))

    short_rows = []
    for i in range(3):
        rows = [[] for _ in range(FK)]
        for lane in lanes:
            sums = [jnp.zeros((8, 128), F32)] * FK
            for r in range(0, span, step):
                here = px[i, r + edge : r + edge + step, :, lane]
                for lag in range(FK):
                    value = grad[i, r + lag : r + lag + step, :, lane]
                    sums[lag] = sums[lag] + jnp.sum(here * value, axis=0)
            for lag in range(FK):
                rows[lag].append(jnp.sum(sums[lag], axis=0, keepdims=True))
        short_rows += [jnp.concatenate(row, axis=1) for row in rows]

    step, block = pl.program_id(0), first + pl.program_id(0)
    ranks, slot, _ = filter_held.shape
    per, share = filter_sums.shape[0] // ranks, short_held.shape[0]
    copies = [
        pltpu.make_async_copy(
            filter_held, sums_out.at[:, pl.ds(pl.multiple_of(block * slot, slot), slot), :], done.at[0]
        ),
        pltpu.make_async_copy(
            short_held,
            sums_out.at[pl.ds(block * share, share), pl.ds(sums_out.shape[1] - SHORT, SHORT), :],
            done.at[1],
        ),
    ]

    @pl.when(step > 0)
    def _():
        for copy in copies:
            copy.wait()

    by_rank = filter_sums.reshape(ranks, per, width) if per % 8 == 0 else jnp.stack(
        [filter_sums[rank * per : rank * per + per] for rank in range(ranks)]
    )
    if slot > per:
        by_rank = jnp.concatenate([by_rank, jnp.zeros((ranks, slot - per, width), F32)], axis=1)
    filter_held[...] = by_rank.astype(BF16)
    sums = jnp.concatenate(short_rows + [jnp.zeros((SHORT - len(short_rows), width), F32)], axis=0)
    for rank in range(share):
        held = pltpu.roll(sums, width - rank * (width // share), 1) if rank else sums
        short_held[rank] = held.astype(BF16)
    for copy in copies:
        copy.start()

    @pl.when(step == pl.num_programs(0) - 1)
    def _():
        for copy in copies:
            copy.wait()


def outputs_kernel(product, grad, short, p_out, gated, grad_proj):
    length, width = product.shape[1:]
    span = length // 8
    gated[...] = mm(p_out[...], product[0]).astype(BF16)
    for i in range(3):
        lanes = []
        for lane in lanes_of(width):
            taps = spread_taps(short, i, lane)
            chunks = []
            for r in range(0, span, 8):
                total = None
                for lag in range(FK):
                    part = grad[0, i, r + lag : r + lag + 8, :, lane] * taps[lag]
                    total = part if total is None else total + part
                chunks.append(total)
            lanes.append(jnp.concatenate(chunks, axis=0))
        result = jnp.concatenate(lanes, axis=2).reshape(length, width).astype(BF16)
        grad_proj[i] = mm(p_out[...], result).astype(BF16)


def whole(array):
    return pl.BlockSpec(array.shape, lambda c: (0,) * array.ndim)


def columns(rows, width, first=0):
    lead = (0,) * len(rows)
    return pl.BlockSpec(tuple(rows) + (width,), lambda c: lead + (first + c,))


def one_of(array, first=0):
    tail = (0,) * (len(array.shape) - 1)
    return pl.BlockSpec((1,) + tuple(array.shape[1:]), lambda c: (first + c,) + tail)


IN_VMEM = pl.BlockSpec(memory_space=pltpu.VMEM)
FAR = pl.BlockSpec(memory_space=pl.ANY)


def call(kernel, name, operands, outputs, cost=1, held=(), free=(), **options):
    arrays = [
        array if at in free else pltpu.with_memory_space_constraint(array, pltpu.HBM)
        for at, (array, _) in enumerate(operands)
    ]
    return pl.pallas_call(
        kernel,
        in_specs=[spec for _, spec in operands] + [FAR] * len(held),
        out_specs=[spec for _, spec in outputs],
        out_shape=[shape for shape, _ in outputs],
        input_output_aliases={len(operands) + at: at for at in range(len(held))},
        compiler_params=pltpu.CompilerParams(vmem_limit_bytes=40 << 20),
        cost_estimate=pl.CostEstimate(flops=cost * 10**9, bytes_accessed=10**6, transcendentals=0),
        name=name,
        **options,
    )(*arrays, *held)


def squares_kernel(rows, share, sums, raw, payload):
    ranks, slots, width = sums.shape
    total = sums[0].astype(F32)
    for rank in range(1, ranks):
        total = total + sums[rank].astype(F32)
    slot = -(-rows // 16) * 16
    pieces = [total[at : at + rows] for at in range(0, slots - SHORT, slot)]
    raw[...] = jnp.concatenate(pieces, axis=1)
    lane = lax.broadcasted_iota(jnp.int32, (SHORT, width), 1)
    short = jnp.where(lane < share, total[slots - SHORT :], 0.0)
    squares = jnp.sum(short * short, keepdims=True)
    for piece in pieces:
        squares = squares + jnp.sum(piece * piece, keepdims=True)
    high = squares.astype(BF16).astype(F32)
    row = lax.broadcasted_iota(jnp.int32, (24, width), 0)
    block = jnp.where(row < 3 * FK, short[:24], jnp.where(row == 3 * FK, high, squares - high)).astype(BF16)
    for other in range(payload.shape[0]):
        payload[other] = block


def scale_kernel(entries, share, mine, raw, gathered, grad_short, grad_filter):
    everyone, rows, width = gathered.shape
    total = jnp.zeros((8, width), F32)
    for other in range(everyone):
        total = total + gathered[other].astype(F32)[16:]
    total = total[5:6, :1] + total[6:7, :1]
    scale = jnp.minimum(1.0, math.sqrt(entries) / jnp.sqrt(total))
    grad_filter[...] = scale * raw[...]
    step = mine[1]
    for rank in range(raw.shape[1] // share):
        block = gathered[rank * step + mine[0]].astype(F32) * scale
        for i in range(3):
            grad_short[i, :, rank * share : (rank + 1) * share] = block[i * FK : (i + 1) * FK, :share]


def shards(projected, short_taps, filter_taps, decay, cotangent):
    length, _, channels = projected.shape
    ranks, groups = lax.axis_size("seq"), lax.axis_size("ch")
    rows = filter_taps.shape[0]
    count = rows * ranks
    width = min(256, channels // CHUNKS)
    share = channels // ranks
    slot = -(-rows // 16) * 16
    size, span = 2 * length, length // 8
    some = 144
    proj, cot, short, decay = jnp.transpose(projected, (1, 0, 2)), cotangent, short_taps, decay[None]
    full = lambda kind, *shape: (jax.ShapeDtypeStruct(shape, kind), IN_VMEM)
    vmem = lambda kind, *shape: pltpu.VMEM(shape, kind)
    far = lambda *arrays: [(array, FAR) for array in arrays]
    semaphores = pltpu.SemaphoreType.DMA((10,))
    own = interleaved(span)
    after = length + np.arange(8)
    chunk = channels // CHUNKS
    blocks = chunk // width

    prev, later, taps = [], [], None
    for k in range(CHUNKS):
        operands = far(proj, cot, short)
        results = [full(BF16, 152, chunk), full(BF16, 160, chunk)]
        scratch = [
            vmem(BF16, 2, some, chunk), vmem(BF16, 2, some, chunk), vmem(BF16, 3, 16, chunk), vmem(F32, 3, FK, chunk),
            vmem(BF16, 8 * (15 + FK), some), vmem(BF16, 8 * (16 + FK), some), vmem(F32, 8 * (15 + FK), width),
            vmem(F32, 8 * (15 + FK), width), vmem(F32, 8 * (16 + FK), width), vmem(F32, 8 * 17, width), semaphores,
        ]
        if k == CHUNKS - 1:
            operands += far(filter_taps)
            results.append((pltpu.HBM((ranks, rows, channels), BF16), FAR))
            scratch = [vmem(F32, rows, channels), vmem(BF16, ranks, rows, channels)] + scratch
        forward, backward, *spread = call(
            functools.partial(edges_kernel, k * chunk), "edges", operands, results, cost=10 if k else 1,
            scratch_shapes=scratch,
        )
        if k == CHUNKS - 1:
            taps = lax.all_to_all(spread[0], "seq", 0, 0).reshape(count, channels)
        if k:
            forward, backward, prev[-1], later[-1] = lax.optimization_barrier((forward, backward, prev[-1], later[-1]))
        prev.append(from_behind(forward, "seq", 1))
        later.append(from_behind(backward, "seq", -1))

    high, low = analysis(own, size)
    k_high, k_low = analysis(np.arange(count), size)
    constants = [
        np.concatenate([high, low], axis=1),
        analysis(np.concatenate([interleaved(16, -128), after]), size, 8)[0],
        analysis(interleaved(17, length), size, 8)[0],
        np.concatenate([k_high, k_low, k_high], axis=1),
        np.concatenate(list(synthesis(np.concatenate([own, after]), size)), axis=1),
        np.concatenate(list(synthesis(np.arange(count), size)), axis=1),
        pick(interleaved(span, 0, 1 - FK), length),
    ]
    constants = [(jnp.asarray(constant), whole(constant)) for constant in constants]
    held = ()
    for k in range(CHUNKS):
        first = k * blocks
        results = [
            pltpu.HBM((CHUNKS * blocks, length, width), BF16),
            pltpu.HBM((CHUNKS * blocks, 3, span + FK - 1, 8, width), F32),
        ]
        held = call(
            functools.partial(operator_kernel, first), "operator",
            [
                (proj, columns((3, length), width, first)), (cot, columns((length,), width, first)),
                (prev[k], columns((152,), width)), (later[k], columns((160,), width)),
                (short, columns((3, FK), width, first)), (taps, columns((count,), width, first)),
                (decay, columns((1,), width, first)),
            ] + constants,
            [(result, one_of(result, first)) for result in results]
            + [(pltpu.HBM((ranks, CHUNKS * blocks * slot + SHORT, width), BF16), FAR)],
            cost=12,
            held=held,
            free=(2, 3, 5),
            grid=(blocks,),
            scratch_shapes=[
                vmem(F32, 3, span + FK - 1, 8, width), vmem(F32, 3, span, 8, width), vmem(F32, span, 8, width),
                vmem(BF16, ranks, slot, width), vmem(BF16, ranks * width // channels, SHORT, width),
                pltpu.SemaphoreType.DMA((2,)),
            ],
        )
    product, grad, sums = held
    p_out = jnp.asarray(pick(own, length).T)
    gated, grad_proj = call(
        outputs_kernel, "outputs",
        [(product, one_of(product)), (grad, one_of(grad)), (short, columns((3, FK), width)), (p_out, whole(p_out))],
        [
            (jax.ShapeDtypeStruct((length, channels), BF16), columns((length,), width)),
            (jax.ShapeDtypeStruct((3, length, channels), BF16), columns((3, length), width)),
        ],
        cost=8,
        grid=(CHUNKS * blocks,),
    )
    sums, gated, grad_proj = lax.optimization_barrier((lax.all_to_all(sums, "seq", 0, 0), gated, grad_proj))

    vmem = pl.BlockSpec(memory_space=pltpu.VMEM)
    raw, payload = pl.pallas_call(
        functools.partial(squares_kernel, rows, share),
        in_specs=[vmem],
        out_specs=[vmem] * 2,
        out_shape=[
            jax.ShapeDtypeStruct((rows, channels), F32),
            jax.ShapeDtypeStruct((ranks * groups, 24, width), BF16),
        ],
        compiler_params=pltpu.CompilerParams(vmem_limit_bytes=32 << 20),
        name="squares",
    )(sums)
    gathered = lax.all_to_all(payload, ("seq", "ch"), 0, 0)
    mine = jnp.stack([lax.axis_index("ch"), jnp.int32(groups)])
    entries = (rows * ranks + 3 * FK) * channels * groups
    grad_short, grad_filter = pl.pallas_call(
        functools.partial(scale_kernel, entries, share),
        in_specs=[pl.BlockSpec(memory_space=pltpu.SMEM), vmem, vmem],
        out_specs=[vmem] * 2,
        out_shape=[
            jax.ShapeDtypeStruct((3, FK, channels), F32),
            jax.ShapeDtypeStruct((rows, channels), F32),
        ],
        compiler_params=pltpu.CompilerParams(vmem_limit_bytes=32 << 20),
        name="scale",
    )(mine, raw, gathered)
    return (gated, jnp.transpose(grad_proj, (1, 0, 2)), grad_short, grad_filter)


def solution(mesh):
    placed = (P("seq", None, "ch"), P(None, None, "ch"), P("seq", "ch"), P("ch"), P("seq", "ch"))
    return jax.shard_map(
        shards,
        mesh=mesh,
        in_specs=placed,
        out_specs=(P("seq", "ch"), P("seq", None, "ch"), P(None, None, "ch"), P("seq", "ch")),
        check_vma=False,
    )
```

```python
import functools
import math

import jax
import jax.numpy as jnp
import ml_dtypes
import numpy as np
from jax import lax
from jax.experimental import pallas as pl
from jax.experimental.pallas import tpu as pltpu
from jax.sharding import PartitionSpec as P


FK = 7
BF16 = jnp.bfloat16
F32 = jnp.float32
CHUNKS = 2
PAIR = 2
SHORT = 32
STEP = 64


def from_behind(value, axis, by):
    count = lax.axis_size(axis)
    pairs = [(i, i + by) for i in range(count) if 0 <= i + by < count]
    return lax.ppermute(value, axis, pairs)


def interleaved(span, first=0, low=0):
    return np.array([first + s * span + r for r in range(low, span) for s in range(8)])


def pick(positions, count):
    out = np.zeros((len(positions), count), np.float32)
    for row, at in enumerate(positions):
        if 0 <= at < count:
            out[row, at] = 1.0
    return out.astype(ml_dtypes.bfloat16)


def halves(matrix):
    high = matrix.astype(np.float32).astype(ml_dtypes.bfloat16)
    low = (matrix - high.astype(np.float64)).astype(np.float32).astype(ml_dtypes.bfloat16)
    return np.stack([high, low])


def analysis(positions, size, pad=0):
    freq = np.arange(size // 2)[:, None]
    angle = np.pi * (((2 * freq + 1) * np.asarray(positions)[None, :]) % (2 * size)) / size
    matrix = np.concatenate([np.cos(angle), -np.sin(angle)], axis=0)
    return halves(np.pad(matrix, ((0, 0), (0, pad))))


def synthesis(positions, size):
    freq = np.arange(size // 2)[None, :]
    angle = np.pi * (((2 * freq + 1) * np.asarray(positions)[:, None]) % (2 * size)) / size
    return halves(np.concatenate([np.cos(angle), -np.sin(angle)], axis=1) * (2.0 / size))


def mm(a, b):
    return jnp.dot(a, b, preferred_element_type=F32)


def picked(span, first, length):
    shape = ((span + FK - 1) * 8, length)
    row, column = (lax.broadcasted_iota(jnp.int32, shape, axis) for axis in (0, 1))
    position = first + (row & 7) * span + (row >> 3) - (FK - 1)
    return jnp.where(position == column, 1.0, 0.0).astype(BF16)


def lanes_of(width):
    return [slice(at, at + 128) for at in range(0, width, 128)]


def featurized(x, taps, lane, row, rows):
    total = None
    for lag in range(FK):
        at = row + 8 * (FK - 1 - lag)
        part = x[at : at + rows, lane].reshape(rows // 8, 8, 128) * taps[lag]
        total = part if total is None else total + part
    return total


def spread_taps(short, i, lane):
    return [jnp.broadcast_to(short[i, lag : lag + 1, lane], (8, 128)) for lag in range(FK)]


def fetch(pairs, semaphores):
    copies = [pltpu.make_async_copy(source, into, semaphores.at[at]) for at, (source, into) in enumerate(pairs)]
    for copy in copies:
        copy.start()
    return copies


def window(block, width):
    return pl.ds(pl.multiple_of(block * width, width), width)


def edges_kernel(at, proj, cot, short, *refs):
    tails, heads, few, taps_held, p_tail, p_head, first, second, zeroth, held, semaphores = refs[-11:]
    with_taps = len(refs) > 13
    if with_taps:
        taps, forward, backward, spread, all_taps, all_spread = refs[:6]
    else:
        forward, backward = refs[:2]
    length, channels = cot.shape[0], forward.shape[1]
    here = pl.ds(at, channels)
    some, width = p_tail.shape[1], first.shape[1]
    tail, head = 16, 17
    pairs = [
        (proj.at[1, length - some :, here], tails.at[0]),
        (proj.at[2, length - some :, here], tails.at[1]),
        (proj.at[0, :some, here], heads.at[0]),
        (cot.at[:some, here], heads.at[1]),
        (proj.at[0, length - 16 :, here], few.at[0]),
        (proj.at[1, :16, here], few.at[1]),
        (proj.at[2, :16, here], few.at[2]),
        (short.at[:, :, here], taps_held),
    ]
    copies = fetch(pairs + [(taps, all_taps)] if with_taps else pairs, semaphores)
    p_tail[...] = picked(tail, some - 128, some)
    p_head[...] = picked(head, 0, some)
    if with_taps:
        copies.pop().wait()
        all_spread[...] = jnp.broadcast_to(all_taps[...].astype(BF16)[None], all_spread.shape)
        sent = pltpu.make_async_copy(all_spread, spread, semaphores.at[9])
        sent.start()
    for copy in copies:
        copy.wait()

    def block(c, _):
        columns = window(c, width)
        first[...] = mm(p_tail[...], tails[0, :, columns])
        second[...] = mm(p_tail[...], tails[1, :, columns])
        zeroth[...] = mm(p_head[...], heads[0, :, columns])
        held[...] = mm(p_head[(FK - 1) * 8 :, :], heads[1, :, columns])
        for lane in lanes_of(width):
            wide = pl.ds(pl.multiple_of(c * width + lane.start, 128), 128)
            taps = [spread_taps(taps_held, i, wide) for i in range(3)]
            for r in range(0, 8 * tail, STEP):
                mixed = featurized(first, taps[1], lane, r, STEP) * featurized(second, taps[2], lane, r, STEP)
                forward[r : r + STEP, wide] = mixed.reshape(STEP, 128).astype(BF16)
            ends = [few[0, :, wide], tails[0, some - 16 :, wide], tails[1, some - 16 :, wide]]
            ends = [end.astype(F32)[8:] for end in ends]
            forward[8 * tail :, wide] = jnp.concatenate(ends, axis=0).astype(BF16)
            for r in range(0, 8 * head, STEP):
                rows = min(STEP, 8 * head - r)
                grad = featurized(zeroth, taps[0], lane, r, rows).reshape(rows, 128) * held[r : r + rows, lane]
                if rows < STEP:
                    starts = [heads[1, :16, wide], few[1, :, wide], few[2, :, wide]]
                    starts = [start.astype(F32)[:8] for start in starts]
                    backward[r:, wide] = jnp.concatenate([grad] + starts, axis=0).astype(BF16)
                else:
                    backward[r : r + rows, wide] = grad.astype(BF16)
        return 0

    lax.fori_loop(0, channels // width, block, 0)
    if with_taps:
        sent.wait()


def operator_block(
    proj, cot, prev, later, short, taps, decay,
    e_own, e_prev, e_next, e_taps, s_own, s_lags, p_in, product, grad, px, feat, cots,
):
    length, width = cot.shape
    span = length // 8
    edge = FK - 1
    lanes = [slice(at, at + 128) for at in range(0, width, 128)]
    row8 = lax.broadcasted_iota(jnp.int32, (8, width), 0)

    before = prev[...].astype(F32)
    after = later[...].astype(F32)
    prev8 = [before[128 + 8 * i : 136 + 8 * i] for i in range(3)]
    cot_next = after[136:144]
    next8 = [None, after[144:152], after[152:160]]

    lags = lax.broadcasted_iota(jnp.int32, (taps.shape[0], width), 0).astype(F32)
    falloff = jnp.exp(-decay[...] * lags)
    kernel = taps[...].astype(F32) * falloff
    high = kernel.astype(BF16)
    low = (kernel - high.astype(F32)).astype(BF16)
    k_spec = mm(e_taps[...], jnp.concatenate([high, high, low], axis=0))

    for i in range(3):
        x = mm(p_in[...], proj[i]).reshape(span + edge, 8, width)
        px[i, edge:] = x[edge:]
        for k in range(1, FK):
            px[i, edge - k] = jnp.where(row8 == 0, pltpu.roll(prev8[i], k, 0), x[edge - k])
    cots[...] = mm(p_in[edge * 8 :, :], cot[...]).reshape(span, 8, width)

    yield
    step = 8
    for i in range(3):
        for lane in lanes:
            weights = [jnp.broadcast_to(short[i, lag : lag + 1, lane], (8, 128)) for lag in range(FK)]
            for r in range(0, span, step):
                total = weights[0] * px[i, r + edge : r + edge + step, :, lane]
                for lag in range(1, FK):
                    total = total + weights[lag] * px[i, r + edge - lag : r + edge - lag + step, :, lane]
                feat[i, r : r + step, :, lane] = total

    def conv8(last, first, weights, whole):
        total = weights[0:1] * first if whole else jnp.zeros((8, width), F32)
        for lag in range(1, FK):
            rolled = pltpu.roll(first, lag, 0) if whole else 0.0
            total = total + weights[lag : lag + 1] * jnp.where(row8 < lag, pltpu.roll(last, lag, 0), rolled)
        return total

    ends = [proj[i, length - 16 :, :].astype(F32)[8:] for i in range(3)]
    feat_next = [None] + [conv8(ends[i], next8[i], short[i], True) for i in (1, 2)]
    mixed_next = feat_next[1] * feat_next[2]
    grad_next = after[:136]
    fix = cot_next * conv8(ends[0], None, short[0], False)
    rows = [grad_next[8 * r : 8 * r + 8] for r in range(17)]
    for r in range(edge):
        rows[r] = rows[r] + jnp.where(row8 == 0, pltpu.roll(fix, (8 - r) % 8, 0), 0.0)
    grad_next = jnp.concatenate(rows + [jnp.zeros((8, width), F32)], axis=0).astype(BF16)
    mixed_edge = jnp.concatenate([before[:128], mixed_next, jnp.zeros((8, width), F32)], axis=0).astype(BF16)

    flat = lambda value: value.reshape(length, width)
    mixed = flat(feat[1] * feat[2]).astype(BF16)
    grad_own = flat(cots[...] * feat[0]).astype(BF16)
    yield
    m_spec = mm(e_own[...], jnp.concatenate([mixed, mixed], axis=0)) + mm(e_prev[...], mixed_edge)
    g_own = mm(e_own[...], jnp.concatenate([grad_own, grad_own], axis=0))
    g_spec = g_own + mm(e_next[...], grad_next)

    yield
    half = k_spec.shape[0] // 2
    parts = lambda value: (value[:half], value[half:])
    (kr, ki), (mr, mi), (gr, gi), (hr, hi) = parts(k_spec), parts(m_spec), parts(g_spec), parts(g_own)

    def joined(real, imaginary):
        spectrum = jnp.concatenate([real, imaginary], axis=0).astype(BF16)
        return jnp.concatenate([spectrum, spectrum], axis=0)

    filtered = joined(mr * kr - mi * ki, mr * ki + mi * kr)
    grad_mixed = joined(gr * kr + gi * ki, gi * kr - gr * ki)
    filter_sums = joined(hr * mr + hi * mi, hi * mr - hr * mi)
    yield
    filtered, grad_mixed = mm(s_own[...], filtered), mm(s_own[...], grad_mixed)
    filter_sums = mm(s_lags[...], filter_sums) * falloff
    yield

    own = filtered[:length].reshape(span, 8, width)
    product[...] = flat(feat[0] * own).astype(BF16)
    back = grad_mixed[:length].reshape(span, 8, width)
    grad[0, :span] = cots[...] * own
    grad[1, :span] = back * feat[2]
    grad[2, :span] = back * feat[1]
    back_next = grad_mixed[length:]
    edge_next = [cot_next * filtered[length:], back_next * feat_next[2], back_next * feat_next[1]]
    for i in range(3):
        for k in range(edge):
            grad[i, span + k] = jnp.where(row8 == 7, pltpu.roll(edge_next[i], 7 - k, 0), pltpu.roll(grad[i, k], 7, 0))

    short_rows = []
    for i in range(3):
        rows = [[] for _ in range(FK)]
        for lane in lanes:
            sums = [jnp.zeros((8, 128), F32)] * FK
            for r in range(0, span, step):
                here = px[i, r + edge : r + edge + step, :, lane]
                for lag in range(FK):
                    value = grad[i, r + lag : r + lag + step, :, lane]
                    sums[lag] = sums[lag] + jnp.sum(here * value, axis=0)
            for lag in range(FK):
                rows[lag].append(jnp.sum(sums[lag], axis=0, keepdims=True))
        short_rows += [jnp.concatenate(row, axis=1) for row in rows]
    yield filter_sums, short_rows


def operator_kernel(first, proj, cot, prev, later, short, taps, decay, *refs):
    constants, (product, grad, sums_out, px, feat, cots, filter_held, short_held, done) = refs[:7], refs[-9:]
    width = px.shape[-1]
    pair = []
    for at in range(PAIR):
        here = slice(at * width, (at + 1) * width)
        views = [proj.at[:, :, here], cot.at[:, here], prev.at[:, here], later.at[:, here], short.at[:, :, here]]
        views += [taps.at[:, here], decay.at[:, here], *constants]
        pair.append(operator_block(*views, product.at[at], grad.at[at], px.at[at], feat.at[at], cots.at[at]))
    results = [None] * PAIR
    for turn in range(6 + PAIR - 1):
        for at in range(PAIR):
            if 0 <= turn - at < 6:
                results[at] = next(pair[at])

    step = pl.program_id(0)
    _, ranks, slot, width = filter_held.shape
    per, share = results[0][0].shape[0] // ranks, short_held.shape[1]
    copies = []
    for at in range(PAIR):
        block = first + PAIR * step + at
        rows = pl.ds(pl.multiple_of(block * slot, slot), slot)
        few = pl.ds(sums_out.shape[1] - SHORT, SHORT)
        copies += [
            pltpu.make_async_copy(filter_held.at[at], sums_out.at[:, rows, :], done.at[2 * at]),
            pltpu.make_async_copy(
                short_held.at[at], sums_out.at[pl.ds(block * share, share), few, :], done.at[2 * at + 1]
            ),
        ]

    @pl.when(step > 0)
    def _():
        for copy in copies:
            copy.wait()

    for at, (filter_sums, short_rows) in enumerate(results):
        if per % 8 == 0:
            by_rank = filter_sums.reshape(ranks, per, width)
        else:
            by_rank = jnp.stack([filter_sums[rank * per : rank * per + per] for rank in range(ranks)])
        if slot > per:
            by_rank = jnp.concatenate([by_rank, jnp.zeros((ranks, slot - per, width), F32)], axis=1)
        filter_held[at] = by_rank.astype(BF16)
        sums = jnp.concatenate(short_rows + [jnp.zeros((SHORT - len(short_rows), width), F32)], axis=0)
        for rank in range(share):
            held = pltpu.roll(sums, width - rank * (width // share), 1) if rank else sums
            short_held[at, rank] = held.astype(BF16)
    for copy in copies:
        copy.start()

    @pl.when(step == pl.num_programs(0) - 1)
    def _():
        for copy in copies:
            copy.wait()


def outputs_kernel(product, grad, short, p_out, gated, grad_proj):
    length, width = product.shape[1:]
    span = length // 8
    gated[...] = mm(p_out[...], product[0]).astype(BF16)
    for i in range(3):
        lanes = []
        for lane in lanes_of(width):
            taps = spread_taps(short, i, lane)
            chunks = []
            for r in range(0, span, 8):
                total = None
                for lag in range(FK):
                    part = grad[0, i, r + lag : r + lag + 8, :, lane] * taps[lag]
                    total = part if total is None else total + part
                chunks.append(total)
            lanes.append(jnp.concatenate(chunks, axis=0))
        result = jnp.concatenate(lanes, axis=2).reshape(length, width).astype(BF16)
        grad_proj[i] = mm(p_out[...], result).astype(BF16)


def whole(array):
    return pl.BlockSpec(array.shape, lambda c: (0,) * array.ndim)


def columns(rows, width, first=0):
    lead = (0,) * len(rows)
    return pl.BlockSpec(tuple(rows) + (width,), lambda c: lead + (first + c,))


def one_of(array, first=0, some=1):
    tail = (0,) * (len(array.shape) - 1)
    return pl.BlockSpec((some,) + tuple(array.shape[1:]), lambda c: (first + c,) + tail)


IN_VMEM = pl.BlockSpec(memory_space=pltpu.VMEM)
FAR = pl.BlockSpec(memory_space=pl.ANY)


def call(kernel, name, operands, outputs, cost=1, held=(), free=(), **options):
    arrays = [
        array if at in free else pltpu.with_memory_space_constraint(array, pltpu.HBM)
        for at, (array, _) in enumerate(operands)
    ]
    return pl.pallas_call(
        kernel,
        in_specs=[spec for _, spec in operands] + [FAR] * len(held),
        out_specs=[spec for _, spec in outputs],
        out_shape=[shape for shape, _ in outputs],
        input_output_aliases={len(operands) + at: at for at in range(len(held))},
        compiler_params=pltpu.CompilerParams(vmem_limit_bytes=40 << 20),
        cost_estimate=pl.CostEstimate(flops=cost * 10**9, bytes_accessed=10**6, transcendentals=0),
        name=name,
        **options,
    )(*arrays, *held)


def squares_kernel(rows, share, sums, raw, payload):
    ranks, slots, width = sums.shape
    total = sums[0].astype(F32)
    for rank in range(1, ranks):
        total = total + sums[rank].astype(F32)
    slot = -(-rows // 16) * 16
    pieces = [total[at : at + rows] for at in range(0, slots - SHORT, slot)]
    raw[...] = jnp.concatenate(pieces, axis=1)
    lane = lax.broadcasted_iota(jnp.int32, (SHORT, width), 1)
    short = jnp.where(lane < share, total[slots - SHORT :], 0.0)
    squares = jnp.sum(short * short, keepdims=True)
    for piece in pieces:
        squares = squares + jnp.sum(piece * piece, keepdims=True)
    high = squares.astype(BF16).astype(F32)
    row = lax.broadcasted_iota(jnp.int32, (24, width), 0)
    block = jnp.where(row < 3 * FK, short[:24], jnp.where(row == 3 * FK, high, squares - high)).astype(BF16)
    for other in range(payload.shape[0]):
        payload[other] = block


def scale_kernel(entries, share, mine, raw, gathered, grad_short, grad_filter):
    everyone, rows, width = gathered.shape
    total = jnp.zeros((8, width), F32)
    for other in range(everyone):
        total = total + gathered[other].astype(F32)[16:]
    total = total[5:6, :1] + total[6:7, :1]
    scale = jnp.minimum(1.0, math.sqrt(entries) / jnp.sqrt(total))
    grad_filter[...] = scale * raw[...]
    step = mine[1]
    for rank in range(raw.shape[1] // share):
        block = gathered[rank * step + mine[0]].astype(F32) * scale
        for i in range(3):
            grad_short[i, :, rank * share : (rank + 1) * share] = block[i * FK : (i + 1) * FK, :share]


def shards(projected, short_taps, filter_taps, decay, cotangent):
    length, _, channels = projected.shape
    ranks, groups = lax.axis_size("seq"), lax.axis_size("ch")
    rows = filter_taps.shape[0]
    count = rows * ranks
    width = min(256, channels // CHUNKS // PAIR)
    share = channels // ranks
    slot = -(-rows // 16) * 16
    size, span = 2 * length, length // 8
    some = 144
    proj, cot, short, decay = jnp.transpose(projected, (1, 0, 2)), cotangent, short_taps, decay[None]
    full = lambda kind, *shape: (jax.ShapeDtypeStruct(shape, kind), IN_VMEM)
    vmem = lambda kind, *shape: pltpu.VMEM(shape, kind)
    far = lambda *arrays: [(array, FAR) for array in arrays]
    semaphores = pltpu.SemaphoreType.DMA((10,))
    own = interleaved(span)
    after = length + np.arange(8)
    chunk = channels // CHUNKS
    blocks = chunk // width

    prev, later, taps = [], [], None
    for k in range(CHUNKS):
        operands = far(proj, cot, short)
        results = [full(BF16, 152, chunk), full(BF16, 160, chunk)]
        scratch = [
            vmem(BF16, 2, some, chunk), vmem(BF16, 2, some, chunk), vmem(BF16, 3, 16, chunk), vmem(F32, 3, FK, chunk),
            vmem(BF16, 8 * (15 + FK), some), vmem(BF16, 8 * (16 + FK), some), vmem(F32, 8 * (15 + FK), width),
            vmem(F32, 8 * (15 + FK), width), vmem(F32, 8 * (16 + FK), width), vmem(F32, 8 * 17, width), semaphores,
        ]
        if k == 0:
            operands += far(filter_taps)
            results.append((pltpu.HBM((ranks, rows, channels), BF16), FAR))
            scratch = [vmem(F32, rows, channels), vmem(BF16, ranks, rows, channels)] + scratch
        forward, backward, *spread = call(
            functools.partial(edges_kernel, k * chunk), "edges", operands, results, cost=10 if k else 1,
            scratch_shapes=scratch,
        )
        if k == 0:
            taps = lax.all_to_all(spread[0], "seq", 0, 0).reshape(count, channels)
        else:
            forward, backward, prev[-1], later[-1] = lax.optimization_barrier((forward, backward, prev[-1], later[-1]))
        prev.append(from_behind(forward, "seq", 1))
        later.append(from_behind(backward, "seq", -1))

    high, low = analysis(own, size)
    k_high, k_low = analysis(np.arange(count), size)
    constants = [
        np.concatenate([high, low], axis=1),
        analysis(np.concatenate([interleaved(16, -128), after]), size, 8)[0],
        analysis(interleaved(17, length), size, 8)[0],
        np.concatenate([k_high, k_low, k_high], axis=1),
        np.concatenate(list(synthesis(np.concatenate([own, after]), size)), axis=1),
        np.concatenate(list(synthesis(np.arange(count), size)), axis=1),
        pick(interleaved(span, 0, 1 - FK), length),
    ]
    constants = [(jnp.asarray(constant), whole(constant)) for constant in constants]
    held = ()
    for k in range(CHUNKS):
        first, wide = k * blocks // PAIR, PAIR * width
        results = [
            pltpu.HBM((CHUNKS * blocks, length, width), BF16),
            pltpu.HBM((CHUNKS * blocks, 3, span + FK - 1, 8, width), F32),
        ]
        held = call(
            functools.partial(operator_kernel, k * blocks), "operator",
            [
                (proj, columns((3, length), wide, first)), (cot, columns((length,), wide, first)),
                (prev[k], columns((152,), wide)), (later[k], columns((160,), wide)),
                (short, columns((3, FK), wide, first)), (taps, columns((count,), wide, first)),
                (decay, columns((1,), wide, first)),
            ] + constants,
            [(result, one_of(result, first, PAIR)) for result in results]
            + [(pltpu.HBM((ranks, CHUNKS * blocks * slot + SHORT, width), BF16), FAR)],
            cost=12,
            held=held,
            free=(2, 3, 5),
            grid=(blocks // PAIR,),
            scratch_shapes=[
                vmem(F32, PAIR, 3, span + FK - 1, 8, width), vmem(F32, PAIR, 3, span, 8, width),
                vmem(F32, PAIR, span, 8, width), vmem(BF16, PAIR, ranks, slot, width),
                vmem(BF16, PAIR, ranks * width // channels, SHORT, width), pltpu.SemaphoreType.DMA((2 * PAIR,)),
            ],
        )
    product, grad, sums = held
    p_out = jnp.asarray(pick(own, length).T)
    gated, grad_proj = call(
        outputs_kernel, "outputs",
        [(product, one_of(product)), (grad, one_of(grad)), (short, columns((3, FK), width)), (p_out, whole(p_out))],
        [
            (jax.ShapeDtypeStruct((length, channels), BF16), columns((length,), width)),
            (jax.ShapeDtypeStruct((3, length, channels), BF16), columns((3, length), width)),
        ],
        cost=8,
        grid=(CHUNKS * blocks,),
    )
    sums, gated, grad_proj = lax.optimization_barrier((lax.all_to_all(sums, "seq", 0, 0), gated, grad_proj))

    vmem = pl.BlockSpec(memory_space=pltpu.VMEM)
    raw, payload = pl.pallas_call(
        functools.partial(squares_kernel, rows, share),
        in_specs=[vmem],
        out_specs=[vmem] * 2,
        out_shape=[
            jax.ShapeDtypeStruct((rows, channels), F32),
            jax.ShapeDtypeStruct((ranks * groups, 24, width), BF16),
        ],
        compiler_params=pltpu.CompilerParams(vmem_limit_bytes=32 << 20),
        name="squares",
    )(sums)
    gathered = lax.all_to_all(payload, ("seq", "ch"), 0, 0)
    mine = jnp.stack([lax.axis_index("ch"), jnp.int32(groups)])
    entries = (rows * ranks + 3 * FK) * channels * groups
    grad_short, grad_filter = pl.pallas_call(
        functools.partial(scale_kernel, entries, share),
        in_specs=[pl.BlockSpec(memory_space=pltpu.SMEM), vmem, vmem],
        out_specs=[vmem] * 2,
        out_shape=[
            jax.ShapeDtypeStruct((3, FK, channels), F32),
            jax.ShapeDtypeStruct((rows, channels), F32),
        ],
        compiler_params=pltpu.CompilerParams(vmem_limit_bytes=32 << 20),
        name="scale",
    )(mine, raw, gathered)
    return (gated, jnp.transpose(grad_proj, (1, 0, 2)), grad_short, grad_filter)


def solution(mesh):
    placed = (P("seq", None, "ch"), P(None, None, "ch"), P("seq", "ch"), P("ch"), P("seq", "ch"))
    return jax.shard_map(
        shards,
        mesh=mesh,
        in_specs=placed,
        out_specs=(P("seq", "ch"), P("seq", None, "ch"), P(None, None, "ch"), P("seq", "ch")),
        check_vma=False,
    )
```

```python
import functools
import math

import jax
import jax.numpy as jnp
import ml_dtypes
import numpy as np
from jax import lax
from jax.experimental import pallas as pl
from jax.experimental.pallas import tpu as pltpu
from jax.sharding import PartitionSpec as P


FK = 7
BF16 = jnp.bfloat16
F32 = jnp.float32
CHUNKS = 2
PAIR = 2
SHORT = 32
STEP = 64


def from_behind(value, axis, by):
    count = lax.axis_size(axis)
    pairs = [(i, i + by) for i in range(count) if 0 <= i + by < count]
    return lax.ppermute(value, axis, pairs)


def interleaved(span, first=0, low=0):
    return np.array([first + s * span + r for r in range(low, span) for s in range(8)])


def pick(positions, count):
    out = np.zeros((len(positions), count), np.float32)
    for row, at in enumerate(positions):
        if 0 <= at < count:
            out[row, at] = 1.0
    return out.astype(ml_dtypes.bfloat16)


def halves(matrix):
    high = matrix.astype(np.float32).astype(ml_dtypes.bfloat16)
    low = (matrix - high.astype(np.float64)).astype(np.float32).astype(ml_dtypes.bfloat16)
    return np.stack([high, low])


def analysis(positions, size, pad=0):
    freq = np.arange(size // 2)[:, None]
    angle = np.pi * (((2 * freq + 1) * np.asarray(positions)[None, :]) % (2 * size)) / size
    matrix = np.concatenate([np.cos(angle), -np.sin(angle)], axis=0)
    return halves(np.pad(matrix, ((0, 0), (0, pad))))


def synthesis(positions, size):
    freq = np.arange(size // 2)[None, :]
    angle = np.pi * (((2 * freq + 1) * np.asarray(positions)[:, None]) % (2 * size)) / size
    return halves(np.concatenate([np.cos(angle), -np.sin(angle)], axis=1) * (2.0 / size))


def mm(a, b):
    return jnp.dot(a, b, preferred_element_type=F32)


def picked(span, first, length):
    shape = ((span + FK - 1) * 8, length)
    row, column = (lax.broadcasted_iota(jnp.int32, shape, axis) for axis in (0, 1))
    position = first + (row & 7) * span + (row >> 3) - (FK - 1)
    return jnp.where(position == column, 1.0, 0.0).astype(BF16)


def lanes_of(width):
    return [slice(at, at + 128) for at in range(0, width, 128)]


def featurized(x, taps, lane, row, rows):
    total = None
    for lag in range(FK):
        at = row + 8 * (FK - 1 - lag)
        part = x[at : at + rows, lane].reshape(rows // 8, 8, 128) * taps[lag]
        total = part if total is None else total + part
    return total


def spread_taps(short, i, lane):
    return [jnp.broadcast_to(short[i, lag : lag + 1, lane], (8, 128)) for lag in range(FK)]


def fetch(pairs, semaphores):
    copies = [pltpu.make_async_copy(source, into, semaphores.at[at]) for at, (source, into) in enumerate(pairs)]
    for copy in copies:
        copy.start()
    return copies


def window(block, width):
    return pl.ds(pl.multiple_of(block * width, width), width)


def edges_kernel(at, proj, cot, short, *refs):
    tails, heads, few, taps_held, p_tail, p_head, first, second, zeroth, held, semaphores = refs[-11:]
    with_taps = len(refs) > 13
    if with_taps:
        taps, forward, backward, spread, all_taps, all_spread = refs[:6]
    else:
        forward, backward = refs[:2]
    length, channels = cot.shape[0], forward.shape[1]
    here = pl.ds(at, channels)
    some, width = p_tail.shape[1], first.shape[1]
    tail, head = 16, 17
    pairs = [
        (proj.at[1, length - some :, here], tails.at[0]),
        (proj.at[2, length - some :, here], tails.at[1]),
        (proj.at[0, :some, here], heads.at[0]),
        (cot.at[:some, here], heads.at[1]),
        (proj.at[0, length - 16 :, here], few.at[0]),
        (proj.at[1, :16, here], few.at[1]),
        (proj.at[2, :16, here], few.at[2]),
        (short.at[:, :, here], taps_held),
    ]
    copies = fetch(pairs + [(taps, all_taps)] if with_taps else pairs, semaphores)
    p_tail[...] = picked(tail, some - 128, some)
    p_head[...] = picked(head, 0, some)
    if with_taps:
        copies.pop().wait()
        all_spread[...] = jnp.broadcast_to(all_taps[...].astype(BF16)[None], all_spread.shape)
        sent = pltpu.make_async_copy(all_spread, spread, semaphores.at[9])
        sent.start()
    for copy in copies:
        copy.wait()

    def block(c, _):
        columns = window(c, width)
        first[...] = mm(p_tail[...], tails[0, :, columns])
        second[...] = mm(p_tail[...], tails[1, :, columns])
        zeroth[...] = mm(p_head[...], heads[0, :, columns])
        held[...] = mm(p_head[(FK - 1) * 8 :, :], heads[1, :, columns])
        for lane in lanes_of(width):
            wide = pl.ds(pl.multiple_of(c * width + lane.start, 128), 128)
            taps = [spread_taps(taps_held, i, wide) for i in range(3)]
            for r in range(0, 8 * tail, STEP):
                mixed = featurized(first, taps[1], lane, r, STEP) * featurized(second, taps[2], lane, r, STEP)
                forward[r : r + STEP, wide] = mixed.reshape(STEP, 128).astype(BF16)
            ends = [few[0, :, wide], tails[0, some - 16 :, wide], tails[1, some - 16 :, wide]]
            ends = [end.astype(F32)[8:] for end in ends]
            forward[8 * tail :, wide] = jnp.concatenate(ends, axis=0).astype(BF16)
            for r in range(0, 8 * head, STEP):
                rows = min(STEP, 8 * head - r)
                grad = featurized(zeroth, taps[0], lane, r, rows).reshape(rows, 128) * held[r : r + rows, lane]
                if rows < STEP:
                    starts = [heads[1, :16, wide], few[1, :, wide], few[2, :, wide]]
                    starts = [start.astype(F32)[:8] for start in starts]
                    backward[r:, wide] = jnp.concatenate([grad] + starts, axis=0).astype(BF16)
                else:
                    backward[r : r + rows, wide] = grad.astype(BF16)
        return 0

    lax.fori_loop(0, channels // width, block, 0)
    if with_taps:
        sent.wait()


def operator_block(
    proj, cot, prev, later, short, taps, decay,
    e_own, e_prev, e_next, e_taps, s_own, s_lags, p_in, product, grad, px, feat, cots,
):
    length, width = cot.shape
    span = length // 8
    edge = FK - 1
    lanes = [slice(at, at + 128) for at in range(0, width, 128)]
    row8 = lax.broadcasted_iota(jnp.int32, (8, width), 0)

    before = prev[...].astype(F32)
    after = later[...].astype(F32)
    prev8 = [before[128 + 8 * i : 136 + 8 * i] for i in range(3)]
    cot_next = after[136:144]
    next8 = [None, after[144:152], after[152:160]]

    lags = lax.broadcasted_iota(jnp.int32, (taps.shape[0], width), 0).astype(F32)
    falloff = jnp.exp(-decay[...] * lags)
    kernel = taps[...].astype(F32) * falloff
    high = kernel.astype(BF16)
    low = (kernel - high.astype(F32)).astype(BF16)
    k_spec = mm(e_taps[...], jnp.concatenate([high, high, low], axis=0))

    for i in range(3):
        x = mm(p_in[...], proj[i]).reshape(span + edge, 8, width)
        px[i, edge:] = x[edge:]
        for k in range(1, FK):
            px[i, edge - k] = jnp.where(row8 == 0, pltpu.roll(prev8[i], k, 0), x[edge - k])
    cots[...] = mm(p_in[edge * 8 :, :], cot[...]).reshape(span, 8, width)

    yield
    step = 8
    for i in range(3):
        for lane in lanes:
            weights = [jnp.broadcast_to(short[i, lag : lag + 1, lane], (8, 128)) for lag in range(FK)]
            for r in range(0, span, step):
                total = weights[0] * px[i, r + edge : r + edge + step, :, lane]
                for lag in range(1, FK):
                    total = total + weights[lag] * px[i, r + edge - lag : r + edge - lag + step, :, lane]
                feat[i, r : r + step, :, lane] = total

    def conv8(last, first, weights, whole):
        total = weights[0:1] * first if whole else jnp.zeros((8, width), F32)
        for lag in range(1, FK):
            rolled = pltpu.roll(first, lag, 0) if whole else 0.0
            total = total + weights[lag : lag + 1] * jnp.where(row8 < lag, pltpu.roll(last, lag, 0), rolled)
        return total

    ends = [proj[i, length - 16 :, :].astype(F32)[8:] for i in range(3)]
    feat_next = [None] + [conv8(ends[i], next8[i], short[i], True) for i in (1, 2)]
    mixed_next = feat_next[1] * feat_next[2]
    grad_next = after[:136]
    fix = cot_next * conv8(ends[0], None, short[0], False)
    rows = [grad_next[8 * r : 8 * r + 8] for r in range(17)]
    for r in range(edge):
        rows[r] = rows[r] + jnp.where(row8 == 0, pltpu.roll(fix, (8 - r) % 8, 0), 0.0)
    grad_next = jnp.concatenate(rows + [jnp.zeros((8, width), F32)], axis=0).astype(BF16)
    mixed_edge = jnp.concatenate([before[:128], mixed_next, jnp.zeros((8, width), F32)], axis=0).astype(BF16)

    flat = lambda value: value.reshape(length, width)
    mixed = flat(feat[1] * feat[2]).astype(BF16)
    grad_own = flat(cots[...] * feat[0]).astype(BF16)
    yield
    m_spec = mm(e_own[...], jnp.concatenate([mixed, mixed], axis=0)) + mm(e_prev[...], mixed_edge)
    g_own = mm(e_own[...], jnp.concatenate([grad_own, grad_own], axis=0))
    g_spec = g_own + mm(e_next[...], grad_next)

    yield
    half = k_spec.shape[0] // 2
    parts = lambda value: (value[:half], value[half:])
    (kr, ki), (mr, mi), (gr, gi), (hr, hi) = parts(k_spec), parts(m_spec), parts(g_spec), parts(g_own)

    def joined(real, imaginary):
        spectrum = jnp.concatenate([real, imaginary], axis=0).astype(BF16)
        return jnp.concatenate([spectrum, spectrum], axis=0)

    filtered = joined(mr * kr - mi * ki, mr * ki + mi * kr)
    grad_mixed = joined(gr * kr + gi * ki, gi * kr - gr * ki)
    filter_sums = joined(hr * mr + hi * mi, hi * mr - hr * mi)
    yield
    filtered, grad_mixed = mm(s_own[...], filtered), mm(s_own[...], grad_mixed)
    filter_sums = mm(s_lags[...], filter_sums) * falloff
    yield

    own = filtered[:length].reshape(span, 8, width)
    product[...] = flat(feat[0] * own).astype(BF16)
    back = grad_mixed[:length].reshape(span, 8, width)
    grad[0, :span] = cots[...] * own
    grad[1, :span] = back * feat[2]
    grad[2, :span] = back * feat[1]
    back_next = grad_mixed[length:]
    edge_next = [cot_next * filtered[length:], back_next * feat_next[2], back_next * feat_next[1]]
    for i in range(3):
        for k in range(edge):
            grad[i, span + k] = jnp.where(row8 == 7, pltpu.roll(edge_next[i], 7 - k, 0), pltpu.roll(grad[i, k], 7, 0))

    short_rows = []
    for i in range(3):
        rows = [[] for _ in range(FK)]
        for lane in lanes:
            sums = [jnp.zeros((8, 128), F32)] * FK
            for r in range(0, span, step):
                here = px[i, r + edge : r + edge + step, :, lane]
                for lag in range(FK):
                    value = grad[i, r + lag : r + lag + step, :, lane]
                    sums[lag] = sums[lag] + jnp.sum(here * value, axis=0)
            for lag in range(FK):
                rows[lag].append(jnp.sum(sums[lag], axis=0, keepdims=True))
        short_rows += [jnp.concatenate(row, axis=1) for row in rows]
    yield filter_sums, short_rows


def operator_kernel(first, proj, cot, prev, later, short, taps, decay, *refs):
    constants, (product, grad, sums_out, px, feat, cots, filter_held, short_held, done) = refs[:7], refs[-9:]
    width = px.shape[-1]
    pair = []
    for at in range(PAIR):
        here = slice(at * width, (at + 1) * width)
        views = [proj.at[:, :, here], cot.at[:, here], prev.at[:, here], later.at[:, here], short.at[:, :, here]]
        views += [taps.at[:, here], decay.at[:, here], *constants]
        pair.append(operator_block(*views, product.at[at], grad.at[at], px.at[at], feat.at[at], cots.at[at]))
    results = [None] * PAIR
    for turn in range(6 + PAIR - 1):
        for at in range(PAIR):
            if 0 <= turn - at < 6:
                results[at] = next(pair[at])

    step = pl.program_id(0)
    _, ranks, slot, width = filter_held.shape
    per, share = results[0][0].shape[0] // ranks, short_held.shape[1]
    copies = []
    for at in range(PAIR):
        block = first + PAIR * step + at
        rows = pl.ds(pl.multiple_of(block * slot, slot), slot)
        few = pl.ds(sums_out.shape[1] - SHORT, SHORT)
        copies += [
            pltpu.make_async_copy(filter_held.at[at], sums_out.at[:, rows, :], done.at[2 * at]),
            pltpu.make_async_copy(
                short_held.at[at], sums_out.at[pl.ds(block * share, share), few, :], done.at[2 * at + 1]
            ),
        ]

    @pl.when(step > 0)
    def _():
        for copy in copies:
            copy.wait()

    for at, (filter_sums, short_rows) in enumerate(results):
        if per % 8 == 0:
            by_rank = filter_sums.reshape(ranks, per, width)
        else:
            by_rank = jnp.stack([filter_sums[rank * per : rank * per + per] for rank in range(ranks)])
        if slot > per:
            by_rank = jnp.concatenate([by_rank, jnp.zeros((ranks, slot - per, width), F32)], axis=1)
        filter_held[at] = by_rank.astype(BF16)
        sums = jnp.concatenate(short_rows + [jnp.zeros((SHORT - len(short_rows), width), F32)], axis=0)
        for rank in range(share):
            held = pltpu.roll(sums, width - rank * (width // share), 1) if rank else sums
            short_held[at, rank] = held.astype(BF16)
    for copy in copies:
        copy.start()

    @pl.when(step == pl.num_programs(0) - 1)
    def _():
        for copy in copies:
            copy.wait()


def outputs_kernel(product, grad, short, p_out, gated, grad_proj):
    length, width = product.shape[1:]
    span = length // 8
    gated[...] = mm(p_out[...], product[0]).astype(BF16)
    for i in range(3):
        lanes = []
        for lane in lanes_of(width):
            taps = spread_taps(short, i, lane)
            chunks = []
            for r in range(0, span, 8):
                total = None
                for lag in range(FK):
                    part = grad[0, i, r + lag : r + lag + 8, :, lane] * taps[lag]
                    total = part if total is None else total + part
                chunks.append(total)
            lanes.append(jnp.concatenate(chunks, axis=0))
        result = jnp.concatenate(lanes, axis=2).reshape(length, width).astype(BF16)
        grad_proj[i] = mm(p_out[...], result).astype(BF16)


def whole(array):
    return pl.BlockSpec(array.shape, lambda c: (0,) * array.ndim)


def columns(rows, width, first=0):
    lead = (0,) * len(rows)
    return pl.BlockSpec(tuple(rows) + (width,), lambda c: lead + (first + c,))


def one_of(array, first=0, some=1):
    tail = (0,) * (len(array.shape) - 1)
    return pl.BlockSpec((some,) + tuple(array.shape[1:]), lambda c: (first + c,) + tail)


IN_VMEM = pl.BlockSpec(memory_space=pltpu.VMEM)
FAR = pl.BlockSpec(memory_space=pl.ANY)


def call(kernel, name, operands, outputs, cost=1, held=(), free=(), **options):
    arrays = [
        array if at in free else pltpu.with_memory_space_constraint(array, pltpu.HBM)
        for at, (array, _) in enumerate(operands)
    ]
    return pl.pallas_call(
        kernel,
        in_specs=[spec for _, spec in operands] + [FAR] * len(held),
        out_specs=[spec for _, spec in outputs],
        out_shape=[shape for shape, _ in outputs],
        input_output_aliases={len(operands) + at: at for at in range(len(held))},
        compiler_params=pltpu.CompilerParams(vmem_limit_bytes=40 << 20),
        cost_estimate=pl.CostEstimate(flops=cost * 10**9, bytes_accessed=10**6, transcendentals=0),
        name=name,
        **options,
    )(*arrays, *held)


def squares_kernel(rows, share, sums, raw, payload):
    ranks, slots, width = sums.shape
    total = sums[0].astype(F32)
    for rank in range(1, ranks):
        total = total + sums[rank].astype(F32)
    slot = -(-rows // 16) * 16
    pieces = [total[at : at + rows] for at in range(0, slots - SHORT, slot)]
    raw[...] = jnp.concatenate(pieces, axis=1)
    lane = lax.broadcasted_iota(jnp.int32, (SHORT, width), 1)
    short = jnp.where(lane < share, total[slots - SHORT :], 0.0)
    squares = jnp.sum(short * short, keepdims=True)
    for piece in pieces:
        squares = squares + jnp.sum(piece * piece, keepdims=True)
    high = squares.astype(BF16).astype(F32)
    row = lax.broadcasted_iota(jnp.int32, (24, width), 0)
    block = jnp.where(row < 3 * FK, short[:24], jnp.where(row == 3 * FK, high, squares - high)).astype(BF16)
    for other in range(payload.shape[0]):
        payload[other] = block


def scale_kernel(entries, share, mine, raw, gathered, grad_short, grad_filter):
    everyone, rows, width = gathered.shape
    total = jnp.zeros((8, width), F32)
    for other in range(everyone):
        total = total + gathered[other].astype(F32)[16:]
    total = total[5:6, :1] + total[6:7, :1]
    scale = jnp.minimum(1.0, math.sqrt(entries) / jnp.sqrt(total))
    grad_filter[...] = scale * raw[...]
    step = mine[1]
    for rank in range(raw.shape[1] // share):
        block = gathered[rank * step + mine[0]].astype(F32) * scale
        for i in range(3):
            grad_short[i, :, rank * share : (rank + 1) * share] = block[i * FK : (i + 1) * FK, :share]


def shards(projected, short_taps, filter_taps, decay, cotangent):
    length, _, channels = projected.shape
    ranks, groups = lax.axis_size("seq"), lax.axis_size("ch")
    rows = filter_taps.shape[0]
    count = rows * ranks
    width = min(256, channels // CHUNKS // PAIR)
    share = channels // ranks
    slot = -(-rows // 16) * 16
    size, span = 2 * length, length // 8
    some = 144
    proj, cot, short, decay = jnp.transpose(projected, (1, 0, 2)), cotangent, short_taps, decay[None]
    full = lambda kind, *shape: (jax.ShapeDtypeStruct(shape, kind), IN_VMEM)
    vmem = lambda kind, *shape: pltpu.VMEM(shape, kind)
    far = lambda *arrays: [(array, FAR) for array in arrays]
    semaphores = pltpu.SemaphoreType.DMA((10,))
    own = interleaved(span)
    after = length + np.arange(8)
    chunk = channels // CHUNKS
    blocks = chunk // width

    prev, later, taps = [], [], None
    for k in range(CHUNKS):
        operands = far(proj, cot, short)
        results = [full(BF16, 152, chunk), full(BF16, 160, chunk)]
        scratch = [
            vmem(BF16, 2, some, chunk), vmem(BF16, 2, some, chunk), vmem(BF16, 3, 16, chunk), vmem(F32, 3, FK, chunk),
            vmem(BF16, 8 * (15 + FK), some), vmem(BF16, 8 * (16 + FK), some), vmem(F32, 8 * (15 + FK), width),
            vmem(F32, 8 * (15 + FK), width), vmem(F32, 8 * (16 + FK), width), vmem(F32, 8 * 17, width), semaphores,
        ]
        if k == 0:
            operands += far(filter_taps)
            results.append((pltpu.HBM((ranks, rows, channels), BF16), FAR))
            scratch = [vmem(F32, rows, channels), vmem(BF16, ranks, rows, channels)] + scratch
        forward, backward, *spread = call(
            functools.partial(edges_kernel, k * chunk), "edges", operands, results, cost=10 if k else 1,
            scratch_shapes=scratch,
        )
        if k == 0:
            taps = lax.all_to_all(spread[0], "seq", 0, 0).reshape(count, channels)
        else:
            backward, prev[-1], later[-1] = lax.optimization_barrier((backward, prev[-1], later[-1]))
        later.append(from_behind(backward, "seq", -1))
        prev.append(from_behind(forward, "seq", 1))

    high, low = analysis(own, size)
    k_high, k_low = analysis(np.arange(count), size)
    constants = [
        np.concatenate([high, low], axis=1),
        analysis(np.concatenate([interleaved(16, -128), after]), size, 8)[0],
        analysis(interleaved(17, length), size, 8)[0],
        np.concatenate([k_high, k_low, k_high], axis=1),
        np.concatenate(list(synthesis(np.concatenate([own, after]), size)), axis=1),
        np.concatenate(list(synthesis(np.arange(count), size)), axis=1),
        pick(interleaved(span, 0, 1 - FK), length),
    ]
    constants = [(jnp.asarray(constant), whole(constant)) for constant in constants]
    held = ()
    for k in range(CHUNKS):
        first, wide = k * blocks // PAIR, PAIR * width
        results = [
            pltpu.HBM((CHUNKS * blocks, length, width), BF16),
            pltpu.HBM((CHUNKS * blocks, 3, span + FK - 1, 8, width), F32),
        ]
        held = call(
            functools.partial(operator_kernel, k * blocks), "operator",
            [
                (proj, columns((3, length), wide, first)), (cot, columns((length,), wide, first)),
                (prev[k], columns((152,), wide)), (later[k], columns((160,), wide)),
                (short, columns((3, FK), wide, first)), (taps, columns((count,), wide, first)),
                (decay, columns((1,), wide, first)),
            ] + constants,
            [(result, one_of(result, first, PAIR)) for result in results]
            + [(pltpu.HBM((ranks, CHUNKS * blocks * slot + SHORT, width), BF16), FAR)],
            cost=12,
            held=held,
            free=(2, 3, 5),
            grid=(blocks // PAIR,),
            scratch_shapes=[
                vmem(F32, PAIR, 3, span + FK - 1, 8, width), vmem(F32, PAIR, 3, span, 8, width),
                vmem(F32, PAIR, span, 8, width), vmem(BF16, PAIR, ranks, slot, width),
                vmem(BF16, PAIR, ranks * width // channels, SHORT, width), pltpu.SemaphoreType.DMA((2 * PAIR,)),
            ],
        )
    product, grad, sums = held
    p_out = jnp.asarray(pick(own, length).T)
    gated, grad_proj = call(
        outputs_kernel, "outputs",
        [(product, one_of(product)), (grad, one_of(grad)), (short, columns((3, FK), width)), (p_out, whole(p_out))],
        [
            (jax.ShapeDtypeStruct((length, channels), BF16), columns((length,), width)),
            (jax.ShapeDtypeStruct((3, length, channels), BF16), columns((3, length), width)),
        ],
        cost=8,
        grid=(CHUNKS * blocks,),
    )
    sums, gated, grad_proj = lax.optimization_barrier((lax.all_to_all(sums, "seq", 0, 0), gated, grad_proj))

    vmem = pl.BlockSpec(memory_space=pltpu.VMEM)
    raw, payload = pl.pallas_call(
        functools.partial(squares_kernel, rows, share),
        in_specs=[vmem],
        out_specs=[vmem] * 2,
        out_shape=[
            jax.ShapeDtypeStruct((rows, channels), F32),
            jax.ShapeDtypeStruct((ranks * groups, 24, width), BF16),
        ],
        compiler_params=pltpu.CompilerParams(vmem_limit_bytes=32 << 20),
        name="squares",
    )(sums)
    gathered = lax.all_to_all(payload, ("seq", "ch"), 0, 0)
    mine = jnp.stack([lax.axis_index("ch"), jnp.int32(groups)])
    entries = (rows * ranks + 3 * FK) * channels * groups
    grad_short, grad_filter = pl.pallas_call(
        functools.partial(scale_kernel, entries, share),
        in_specs=[pl.BlockSpec(memory_space=pltpu.SMEM), vmem, vmem],
        out_specs=[vmem] * 2,
        out_shape=[
            jax.ShapeDtypeStruct((3, FK, channels), F32),
            jax.ShapeDtypeStruct((rows, channels), F32),
        ],
        compiler_params=pltpu.CompilerParams(vmem_limit_bytes=32 << 20),
        name="scale",
    )(mine, raw, gathered)
    return (gated, jnp.transpose(grad_proj, (1, 0, 2)), grad_short, grad_filter)


def solution(mesh):
    placed = (P("seq", None, "ch"), P(None, None, "ch"), P("seq", "ch"), P("ch"), P("seq", "ch"))
    return jax.shard_map(
        shards,
        mesh=mesh,
        in_specs=placed,
        out_specs=(P("seq", "ch"), P("seq", None, "ch"), P(None, None, "ch"), P("seq", "ch")),
        check_vma=False,
    )
```

```python
import functools
import math

import jax
import jax.numpy as jnp
import ml_dtypes
import numpy as np
from jax import lax
from jax.experimental import pallas as pl
from jax.experimental.pallas import tpu as pltpu
from jax.sharding import PartitionSpec as P


FK = 7
BF16 = jnp.bfloat16
F32 = jnp.float32
CHUNKS = 2
PAIR = 2
SHORT = 32
STEP = 64


def from_behind(value, axis, by):
    count = lax.axis_size(axis)
    pairs = [(i, i + by) for i in range(count) if 0 <= i + by < count]
    return lax.ppermute(value, axis, pairs)


def interleaved(span, first=0, low=0):
    return np.array([first + s * span + r for r in range(low, span) for s in range(8)])


def pick(positions, count):
    out = np.zeros((len(positions), count), np.float32)
    for row, at in enumerate(positions):
        if 0 <= at < count:
            out[row, at] = 1.0
    return out.astype(ml_dtypes.bfloat16)


def halves(matrix):
    high = matrix.astype(np.float32).astype(ml_dtypes.bfloat16)
    low = (matrix - high.astype(np.float64)).astype(np.float32).astype(ml_dtypes.bfloat16)
    return np.stack([high, low])


def analysis(positions, size, pad=0):
    freq = np.arange(size // 2)[:, None]
    angle = np.pi * (((2 * freq + 1) * np.asarray(positions)[None, :]) % (2 * size)) / size
    matrix = np.concatenate([np.cos(angle), -np.sin(angle)], axis=0)
    return halves(np.pad(matrix, ((0, 0), (0, pad))))


def synthesis(positions, size):
    freq = np.arange(size // 2)[None, :]
    angle = np.pi * (((2 * freq + 1) * np.asarray(positions)[:, None]) % (2 * size)) / size
    return halves(np.concatenate([np.cos(angle), -np.sin(angle)], axis=1) * (2.0 / size))


def mm(a, b):
    return jnp.dot(a, b, preferred_element_type=F32)


def picked(span, first, length):
    shape = ((span + FK - 1) * 8, length)
    row, column = (lax.broadcasted_iota(jnp.int32, shape, axis) for axis in (0, 1))
    position = first + (row & 7) * span + (row >> 3) - (FK - 1)
    return jnp.where(position == column, 1.0, 0.0).astype(BF16)


def lanes_of(width):
    return [slice(at, at + 128) for at in range(0, width, 128)]


def featurized(x, taps, lane, row, rows):
    total = None
    for lag in range(FK):
        at = row + 8 * (FK - 1 - lag)
        part = x[at : at + rows, lane].reshape(rows // 8, 8, 128) * taps[lag]
        total = part if total is None else total + part
    return total


def spread_taps(short, i, lane):
    return [jnp.broadcast_to(short[i, lag : lag + 1, lane], (8, 128)) for lag in range(FK)]


def fetch(pairs, semaphores):
    copies = [pltpu.make_async_copy(source, into, semaphores.at[at]) for at, (source, into) in enumerate(pairs)]
    for copy in copies:
        copy.start()
    return copies


def window(block, width):
    return pl.ds(pl.multiple_of(block * width, width), width)


def edges_kernel(at, proj, cot, short, *refs):
    tails, heads, few, taps_held, p_tail, p_head, first, second, zeroth, held, semaphores = refs[-11:]
    with_taps = len(refs) == 17
    if with_taps:
        taps, forward, backward, spread, all_taps, all_spread = refs[:6]
    elif len(refs) == 16:
        decay, forward, backward, falloff, all_decay = refs[:5]
    else:
        forward, backward = refs[:2]
    with_decay = len(refs) == 16
    length, channels = cot.shape[0], forward.shape[1]
    here = pl.ds(at, channels)
    some, width = p_tail.shape[1], first.shape[1]
    tail, head = 16, 17
    pairs = [
        (proj.at[1, length - some :, here], tails.at[0]),
        (proj.at[2, length - some :, here], tails.at[1]),
        (proj.at[0, :some, here], heads.at[0]),
        (cot.at[:some, here], heads.at[1]),
        (proj.at[0, length - 16 :, here], few.at[0]),
        (proj.at[1, :16, here], few.at[1]),
        (proj.at[2, :16, here], few.at[2]),
        (short.at[:, :, here], taps_held),
    ]
    if with_taps:
        pairs.append((taps, all_taps))
    if with_decay:
        pairs.append((decay, all_decay))
    copies = fetch(pairs, semaphores)
    p_tail[...] = picked(tail, some - 128, some)
    p_head[...] = picked(head, 0, some)
    if with_taps:
        copies.pop().wait()
        all_spread[...] = jnp.broadcast_to(all_taps[...].astype(BF16)[None], all_spread.shape)
        sent = pltpu.make_async_copy(all_spread, spread, semaphores.at[9])
        sent.start()
    for copy in copies:
        copy.wait()

    def block(c, _):
        columns = window(c, width)
        first[...] = mm(p_tail[...], tails[0, :, columns])
        second[...] = mm(p_tail[...], tails[1, :, columns])
        zeroth[...] = mm(p_head[...], heads[0, :, columns])
        held[...] = mm(p_head[(FK - 1) * 8 :, :], heads[1, :, columns])
        for lane in lanes_of(width):
            wide = pl.ds(pl.multiple_of(c * width + lane.start, 128), 128)
            taps = [spread_taps(taps_held, i, wide) for i in range(3)]
            for r in range(0, 8 * tail, STEP):
                mixed = featurized(first, taps[1], lane, r, STEP) * featurized(second, taps[2], lane, r, STEP)
                forward[r : r + STEP, wide] = mixed.reshape(STEP, 128).astype(BF16)
            ends = [few[0, :, wide], tails[0, some - 16 :, wide], tails[1, some - 16 :, wide]]
            ends = [end.astype(F32)[8:] for end in ends]
            forward[8 * tail :, wide] = jnp.concatenate(ends, axis=0).astype(BF16)
            for r in range(0, 8 * head, STEP):
                rows = min(STEP, 8 * head - r)
                grad = featurized(zeroth, taps[0], lane, r, rows).reshape(rows, 128) * held[r : r + rows, lane]
                if rows < STEP:
                    starts = [heads[1, :16, wide], few[1, :, wide], few[2, :, wide]]
                    starts = [start.astype(F32)[:8] for start in starts]
                    backward[r:, wide] = jnp.concatenate([grad] + starts, axis=0).astype(BF16)
                else:
                    backward[r : r + rows, wide] = grad.astype(BF16)
        return 0

    lax.fori_loop(0, channels // width, block, 0)
    if with_taps:
        sent.wait()
    if with_decay:

        def factors(c, _):
            columns = window(c, width)
            lags = lax.broadcasted_iota(jnp.int32, (falloff.shape[0], width), 0).astype(F32)
            falloff[:, columns] = jnp.exp(-all_decay[:, columns] * lags)
            return 0

        lax.fori_loop(0, falloff.shape[1] // width, factors, 0)


def operator_block(
    proj, cot, prev, later, short, taps, decay,
    e_own, e_prev, e_next, e_taps, s_own, s_lags, p_in, product, grad, px, feat, cots,
):
    length, width = cot.shape
    span = length // 8
    edge = FK - 1
    lanes = [slice(at, at + 128) for at in range(0, width, 128)]
    row8 = lax.broadcasted_iota(jnp.int32, (8, width), 0)

    before = prev[...].astype(F32)
    after = later[...].astype(F32)
    prev8 = [before[128 + 8 * i : 136 + 8 * i] for i in range(3)]
    cot_next = after[136:144]
    next8 = [None, after[144:152], after[152:160]]

    falloff = decay[...]
    kernel = taps[...].astype(F32) * falloff
    high = kernel.astype(BF16)
    low = (kernel - high.astype(F32)).astype(BF16)
    k_spec = mm(e_taps[...], jnp.concatenate([high, high, low], axis=0))

    for i in range(3):
        x = mm(p_in[...], proj[i]).reshape(span + edge, 8, width)
        px[i, edge:] = x[edge:]
        for k in range(1, FK):
            px[i, edge - k] = jnp.where(row8 == 0, pltpu.roll(prev8[i], k, 0), x[edge - k])
    cots[...] = mm(p_in[edge * 8 :, :], cot[...]).reshape(span, 8, width)

    yield
    step = 8
    for i in range(3):
        for lane in lanes:
            weights = [jnp.broadcast_to(short[i, lag : lag + 1, lane], (8, 128)) for lag in range(FK)]
            for r in range(0, span, step):
                total = weights[0] * px[i, r + edge : r + edge + step, :, lane]
                for lag in range(1, FK):
                    total = total + weights[lag] * px[i, r + edge - lag : r + edge - lag + step, :, lane]
                feat[i, r : r + step, :, lane] = total

    def conv8(last, first, weights, whole):
        total = weights[0:1] * first if whole else jnp.zeros((8, width), F32)
        for lag in range(1, FK):
            rolled = pltpu.roll(first, lag, 0) if whole else 0.0
            total = total + weights[lag : lag + 1] * jnp.where(row8 < lag, pltpu.roll(last, lag, 0), rolled)
        return total

    ends = [proj[i, length - 16 :, :].astype(F32)[8:] for i in range(3)]
    feat_next = [None] + [conv8(ends[i], next8[i], short[i], True) for i in (1, 2)]
    mixed_next = feat_next[1] * feat_next[2]
    grad_next = after[:136]
    fix = cot_next * conv8(ends[0], None, short[0], False)
    rows = [grad_next[8 * r : 8 * r + 8] for r in range(17)]
    for r in range(edge):
        rows[r] = rows[r] + jnp.where(row8 == 0, pltpu.roll(fix, (8 - r) % 8, 0), 0.0)
    grad_next = jnp.concatenate(rows + [jnp.zeros((8, width), F32)], axis=0).astype(BF16)
    mixed_edge = jnp.concatenate([before[:128], mixed_next, jnp.zeros((8, width), F32)], axis=0).astype(BF16)

    flat = lambda value: value.reshape(length, width)
    mixed = flat(feat[1] * feat[2]).astype(BF16)
    grad_own = flat(cots[...] * feat[0]).astype(BF16)
    yield
    m_spec = mm(e_own[...], jnp.concatenate([mixed, mixed], axis=0)) + mm(e_prev[...], mixed_edge)
    g_own = mm(e_own[...], jnp.concatenate([grad_own, grad_own], axis=0))
    g_spec = g_own + mm(e_next[...], grad_next)

    yield
    half = k_spec.shape[0] // 2
    parts = lambda value: (value[:half], value[half:])
    (kr, ki), (mr, mi), (gr, gi), (hr, hi) = parts(k_spec), parts(m_spec), parts(g_spec), parts(g_own)

    def joined(real, imaginary):
        spectrum = jnp.concatenate([real, imaginary], axis=0).astype(BF16)
        return jnp.concatenate([spectrum, spectrum], axis=0)

    filtered = joined(mr * kr - mi * ki, mr * ki + mi * kr)
    grad_mixed = joined(gr * kr + gi * ki, gi * kr - gr * ki)
    filter_sums = joined(hr * mr + hi * mi, hi * mr - hr * mi)
    yield
    filtered, grad_mixed = mm(s_own[...], filtered), mm(s_own[...], grad_mixed)
    filter_sums = mm(s_lags[...], filter_sums) * falloff
    yield

    own = filtered[:length].reshape(span, 8, width)
    product[...] = flat(feat[0] * own).astype(BF16)
    back = grad_mixed[:length].reshape(span, 8, width)
    grad[0, :span] = cots[...] * own
    grad[1, :span] = back * feat[2]
    grad[2, :span] = back * feat[1]
    back_next = grad_mixed[length:]
    edge_next = [cot_next * filtered[length:], back_next * feat_next[2], back_next * feat_next[1]]
    for i in range(3):
        for k in range(edge):
            grad[i, span + k] = jnp.where(row8 == 7, pltpu.roll(edge_next[i], 7 - k, 0), pltpu.roll(grad[i, k], 7, 0))

    short_rows = []
    for i in range(3):
        rows = [[] for _ in range(FK)]
        for lane in lanes:
            sums = [jnp.zeros((8, 128), F32)] * FK
            for r in range(0, span, step):
                here = px[i, r + edge : r + edge + step, :, lane]
                for lag in range(FK):
                    value = grad[i, r + lag : r + lag + step, :, lane]
                    sums[lag] = sums[lag] + jnp.sum(here * value, axis=0)
            for lag in range(FK):
                rows[lag].append(jnp.sum(sums[lag], axis=0, keepdims=True))
        short_rows += [jnp.concatenate(row, axis=1) for row in rows]
    yield filter_sums, short_rows


def operator_kernel(first, proj, cot, prev, later, short, taps, decay, *refs):
    constants, (product, grad, sums_out, px, feat, cots, filter_held, short_held, done) = refs[:7], refs[-9:]
    width = px.shape[-1]
    pair = []
    for at in range(PAIR):
        here = slice(at * width, (at + 1) * width)
        views = [proj.at[:, :, here], cot.at[:, here], prev.at[:, here], later.at[:, here], short.at[:, :, here]]
        views += [taps.at[:, here], decay.at[:, here], *constants]
        pair.append(operator_block(*views, product.at[at], grad.at[at], px.at[at], feat.at[at], cots.at[at]))
    results = [None] * PAIR
    for turn in range(6 + PAIR - 1):
        for at in range(PAIR):
            if 0 <= turn - at < 6:
                results[at] = next(pair[at])

    step = pl.program_id(0)
    _, ranks, slot, width = filter_held.shape
    per, share = results[0][0].shape[0] // ranks, short_held.shape[1]
    copies = []
    for at in range(PAIR):
        block = first + PAIR * step + at
        rows = pl.ds(pl.multiple_of(block * slot, slot), slot)
        few = pl.ds(sums_out.shape[1] - SHORT, SHORT)
        copies += [
            pltpu.make_async_copy(filter_held.at[at], sums_out.at[:, rows, :], done.at[2 * at]),
            pltpu.make_async_copy(
                short_held.at[at], sums_out.at[pl.ds(block * share, share), few, :], done.at[2 * at + 1]
            ),
        ]

    @pl.when(step > 0)
    def _():
        for copy in copies:
            copy.wait()

    for at, (filter_sums, short_rows) in enumerate(results):
        if per % 8 == 0:
            by_rank = filter_sums.reshape(ranks, per, width)
        else:
            by_rank = jnp.stack([filter_sums[rank * per : rank * per + per] for rank in range(ranks)])
        if slot > per:
            by_rank = jnp.concatenate([by_rank, jnp.zeros((ranks, slot - per, width), F32)], axis=1)
        filter_held[at] = by_rank.astype(BF16)
        sums = jnp.concatenate(short_rows + [jnp.zeros((SHORT - len(short_rows), width), F32)], axis=0)
        for rank in range(share):
            held = pltpu.roll(sums, width - rank * (width // share), 1) if rank else sums
            short_held[at, rank] = held.astype(BF16)
    for copy in copies:
        copy.start()

    @pl.when(step == pl.num_programs(0) - 1)
    def _():
        for copy in copies:
            copy.wait()


def outputs_kernel(product, grad, short, p_out, gated, grad_proj):
    length, width = product.shape[1:]
    span = length // 8
    gated[...] = mm(p_out[...], product[0]).astype(BF16)
    for i in range(3):
        lanes = []
        for lane in lanes_of(width):
            taps = spread_taps(short, i, lane)
            chunks = []
            for r in range(0, span, 8):
                total = None
                for lag in range(FK):
                    part = grad[0, i, r + lag : r + lag + 8, :, lane] * taps[lag]
                    total = part if total is None else total + part
                chunks.append(total)
            lanes.append(jnp.concatenate(chunks, axis=0))
        result = jnp.concatenate(lanes, axis=2).reshape(length, width).astype(BF16)
        grad_proj[i] = mm(p_out[...], result).astype(BF16)


def whole(array):
    return pl.BlockSpec(array.shape, lambda c: (0,) * array.ndim)


def columns(rows, width, first=0):
    lead = (0,) * len(rows)
    return pl.BlockSpec(tuple(rows) + (width,), lambda c: lead + (first + c,))


def one_of(array, first=0, some=1):
    tail = (0,) * (len(array.shape) - 1)
    return pl.BlockSpec((some,) + tuple(array.shape[1:]), lambda c: (first + c,) + tail)


IN_VMEM = pl.BlockSpec(memory_space=pltpu.VMEM)
FAR = pl.BlockSpec(memory_space=pl.ANY)


def call(kernel, name, operands, outputs, cost=1, held=(), free=(), **options):
    arrays = [
        array if at in free else pltpu.with_memory_space_constraint(array, pltpu.HBM)
        for at, (array, _) in enumerate(operands)
    ]
    return pl.pallas_call(
        kernel,
        in_specs=[spec for _, spec in operands] + [FAR] * len(held),
        out_specs=[spec for _, spec in outputs],
        out_shape=[shape for shape, _ in outputs],
        input_output_aliases={len(operands) + at: at for at in range(len(held))},
        compiler_params=pltpu.CompilerParams(vmem_limit_bytes=40 << 20),
        cost_estimate=pl.CostEstimate(flops=cost * 10**9, bytes_accessed=10**6, transcendentals=0),
        name=name,
        **options,
    )(*arrays, *held)


def squares_kernel(rows, share, sums, raw, payload):
    ranks, slots, width = sums.shape
    total = sums[0].astype(F32)
    for rank in range(1, ranks):
        total = total + sums[rank].astype(F32)
    slot = -(-rows // 16) * 16
    pieces = [total[at : at + rows] for at in range(0, slots - SHORT, slot)]
    raw[...] = jnp.concatenate(pieces, axis=1)
    lane = lax.broadcasted_iota(jnp.int32, (SHORT, width), 1)
    short = jnp.where(lane < share, total[slots - SHORT :], 0.0)
    squares = jnp.sum(short * short, keepdims=True)
    for piece in pieces:
        squares = squares + jnp.sum(piece * piece, keepdims=True)
    high = squares.astype(BF16).astype(F32)
    row = lax.broadcasted_iota(jnp.int32, (24, width), 0)
    block = jnp.where(row < 3 * FK, short[:24], jnp.where(row == 3 * FK, high, squares - high)).astype(BF16)
    for other in range(payload.shape[0]):
        payload[other] = block


def scale_kernel(entries, share, mine, raw, gathered, grad_short, grad_filter):
    everyone, rows, width = gathered.shape
    total = jnp.zeros((8, width), F32)
    for other in range(everyone):
        total = total + gathered[other].astype(F32)[16:]
    total = total[5:6, :1] + total[6:7, :1]
    scale = jnp.minimum(1.0, math.sqrt(entries) / jnp.sqrt(total))
    grad_filter[...] = scale * raw[...]
    step = mine[1]
    for rank in range(raw.shape[1] // share):
        block = gathered[rank * step + mine[0]].astype(F32) * scale
        for i in range(3):
            grad_short[i, :, rank * share : (rank + 1) * share] = block[i * FK : (i + 1) * FK, :share]


def shards(projected, short_taps, filter_taps, decay, cotangent):
    length, _, channels = projected.shape
    ranks, groups = lax.axis_size("seq"), lax.axis_size("ch")
    rows = filter_taps.shape[0]
    count = rows * ranks
    width = min(256, channels // CHUNKS // PAIR)
    share = channels // ranks
    slot = -(-rows // 16) * 16
    size, span = 2 * length, length // 8
    some = 144
    proj, cot, short, decay = jnp.transpose(projected, (1, 0, 2)), cotangent, short_taps, decay[None]
    full = lambda kind, *shape: (jax.ShapeDtypeStruct(shape, kind), IN_VMEM)
    vmem = lambda kind, *shape: pltpu.VMEM(shape, kind)
    far = lambda *arrays: [(array, FAR) for array in arrays]
    semaphores = pltpu.SemaphoreType.DMA((10,))
    own = interleaved(span)
    after = length + np.arange(8)
    chunk = channels // CHUNKS
    blocks = chunk // width

    prev, later, taps = [], [], None
    for k in range(CHUNKS):
        operands = far(proj, cot, short)
        results = [full(BF16, 152, chunk), full(BF16, 160, chunk)]
        scratch = [
            vmem(BF16, 2, some, chunk), vmem(BF16, 2, some, chunk), vmem(BF16, 3, 16, chunk), vmem(F32, 3, FK, chunk),
            vmem(BF16, 8 * (15 + FK), some), vmem(BF16, 8 * (16 + FK), some), vmem(F32, 8 * (15 + FK), width),
            vmem(F32, 8 * (15 + FK), width), vmem(F32, 8 * (16 + FK), width), vmem(F32, 8 * 17, width), semaphores,
        ]
        if k == 0:
            operands += far(filter_taps)
            results.append((pltpu.HBM((ranks, rows, channels), BF16), FAR))
            scratch = [vmem(F32, rows, channels), vmem(BF16, ranks, rows, channels)] + scratch
        elif k == CHUNKS - 1:
            operands += far(decay)
            results.append((pltpu.HBM((count, channels), F32), IN_VMEM))
            scratch = [vmem(F32, 1, channels)] + scratch
        forward, backward, *spread = call(
            functools.partial(edges_kernel, k * chunk), "edges", operands, results, cost=10 if k else 1,
            scratch_shapes=scratch,
        )
        if k == CHUNKS - 1:
            falloff = spread[0]
        if k == 0:
            taps = lax.all_to_all(spread[0], "seq", 0, 0).reshape(count, channels)
        else:
            backward, prev[-1], later[-1] = lax.optimization_barrier((backward, prev[-1], later[-1]))
        later.append(from_behind(backward, "seq", -1))
        prev.append(from_behind(forward, "seq", 1))

    high, low = analysis(own, size)
    k_high, k_low = analysis(np.arange(count), size)
    constants = [
        np.concatenate([high, low], axis=1),
        analysis(np.concatenate([interleaved(16, -128), after]), size, 8)[0],
        analysis(interleaved(17, length), size, 8)[0],
        np.concatenate([k_high, k_low, k_high], axis=1),
        np.concatenate(list(synthesis(np.concatenate([own, after]), size)), axis=1),
        np.concatenate(list(synthesis(np.arange(count), size)), axis=1),
        pick(interleaved(span, 0, 1 - FK), length),
    ]
    constants = [(jnp.asarray(constant), whole(constant)) for constant in constants]
    held = ()
    for k in range(CHUNKS):
        first, wide = k * blocks // PAIR, PAIR * width
        results = [
            pltpu.HBM((CHUNKS * blocks, length, width), BF16),
            pltpu.HBM((CHUNKS * blocks, 3, span + FK - 1, 8, width), F32),
        ]
        held = call(
            functools.partial(operator_kernel, k * blocks), "operator",
            [
                (proj, columns((3, length), wide, first)), (cot, columns((length,), wide, first)),
                (prev[k], columns((152,), wide)), (later[k], columns((160,), wide)),
                (short, columns((3, FK), wide, first)), (taps, columns((count,), wide, first)),
                (falloff, columns((count,), wide, first)),
            ] + constants,
            [(result, one_of(result, first, PAIR)) for result in results]
            + [(pltpu.HBM((ranks, CHUNKS * blocks * slot + SHORT, width), BF16), FAR)],
            cost=12,
            held=held,
            free=(2, 3, 5),
            grid=(blocks // PAIR,),
            scratch_shapes=[
                vmem(F32, PAIR, 3, span + FK - 1, 8, width), vmem(F32, PAIR, 3, span, 8, width),
                vmem(F32, PAIR, span, 8, width), vmem(BF16, PAIR, ranks, slot, width),
                vmem(BF16, PAIR, ranks * width // channels, SHORT, width), pltpu.SemaphoreType.DMA((2 * PAIR,)),
            ],
        )
    product, grad, sums = held
    p_out = jnp.asarray(pick(own, length).T)
    gated, grad_proj = call(
        outputs_kernel, "outputs",
        [(product, one_of(product)), (grad, one_of(grad)), (short, columns((3, FK), width)), (p_out, whole(p_out))],
        [
            (jax.ShapeDtypeStruct((length, channels), BF16), columns((length,), width)),
            (jax.ShapeDtypeStruct((3, length, channels), BF16), columns((3, length), width)),
        ],
        cost=8,
        grid=(CHUNKS * blocks,),
    )
    sums, gated, grad_proj = lax.optimization_barrier((lax.all_to_all(sums, "seq", 0, 0), gated, grad_proj))

    vmem = pl.BlockSpec(memory_space=pltpu.VMEM)
    raw, payload = pl.pallas_call(
        functools.partial(squares_kernel, rows, share),
        in_specs=[vmem],
        out_specs=[vmem] * 2,
        out_shape=[
            jax.ShapeDtypeStruct((rows, channels), F32),
            jax.ShapeDtypeStruct((ranks * groups, 24, width), BF16),
        ],
        compiler_params=pltpu.CompilerParams(vmem_limit_bytes=32 << 20),
        name="squares",
    )(sums)
    gathered = lax.all_to_all(payload, ("seq", "ch"), 0, 0)
    mine = jnp.stack([lax.axis_index("ch"), jnp.int32(groups)])
    entries = (rows * ranks + 3 * FK) * channels * groups
    grad_short, grad_filter = pl.pallas_call(
        functools.partial(scale_kernel, entries, share),
        in_specs=[pl.BlockSpec(memory_space=pltpu.SMEM), vmem, vmem],
        out_specs=[vmem] * 2,
        out_shape=[
            jax.ShapeDtypeStruct((3, FK, channels), F32),
            jax.ShapeDtypeStruct((rows, channels), F32),
        ],
        compiler_params=pltpu.CompilerParams(vmem_limit_bytes=32 << 20),
        name="scale",
    )(mine, raw, gathered)
    return (gated, jnp.transpose(grad_proj, (1, 0, 2)), grad_short, grad_filter)


def solution(mesh):
    placed = (P("seq", None, "ch"), P(None, None, "ch"), P("seq", "ch"), P("ch"), P("seq", "ch"))
    return jax.shard_map(
        shards,
        mesh=mesh,
        in_specs=placed,
        out_specs=(P("seq", "ch"), P("seq", None, "ch"), P(None, None, "ch"), P("seq", "ch")),
        check_vma=False,
    )
```

```python
import functools
import math

import jax
import jax.numpy as jnp
import ml_dtypes
import numpy as np
from jax import lax
from jax.experimental import pallas as pl
from jax.experimental.pallas import tpu as pltpu
from jax.sharding import PartitionSpec as P


FK = 7
BF16 = jnp.bfloat16
F32 = jnp.float32
CHUNKS = 2
PAIR = 2
SHORT = 32
STEP = 64


def from_behind(value, axis, by):
    count = lax.axis_size(axis)
    pairs = [(i, i + by) for i in range(count) if 0 <= i + by < count]
    return lax.ppermute(value, axis, pairs)


def interleaved(span, first=0, low=0):
    return np.array([first + s * span + r for r in range(low, span) for s in range(8)])


def pick(positions, count):
    out = np.zeros((len(positions), count), np.float32)
    for row, at in enumerate(positions):
        if 0 <= at < count:
            out[row, at] = 1.0
    return out.astype(ml_dtypes.bfloat16)


def halves(matrix):
    high = matrix.astype(np.float32).astype(ml_dtypes.bfloat16)
    low = (matrix - high.astype(np.float64)).astype(np.float32).astype(ml_dtypes.bfloat16)
    return np.stack([high, low])


def analysis(positions, size, pad=0):
    freq = np.arange(size // 2)[:, None]
    angle = np.pi * (((2 * freq + 1) * np.asarray(positions)[None, :]) % (2 * size)) / size
    matrix = np.concatenate([np.cos(angle), -np.sin(angle)], axis=0)
    return halves(np.pad(matrix, ((0, 0), (0, pad))))


def synthesis(positions, size):
    freq = np.arange(size // 2)[None, :]
    angle = np.pi * (((2 * freq + 1) * np.asarray(positions)[:, None]) % (2 * size)) / size
    return halves(np.concatenate([np.cos(angle), -np.sin(angle)], axis=1) * (2.0 / size))


def mm(a, b):
    return jnp.dot(a, b, preferred_element_type=F32)


def picked(span, first, length):
    shape = ((span + FK - 1) * 8, length)
    row, column = (lax.broadcasted_iota(jnp.int32, shape, axis) for axis in (0, 1))
    position = first + (row & 7) * span + (row >> 3) - (FK - 1)
    return jnp.where(position == column, 1.0, 0.0).astype(BF16)


def lanes_of(width):
    return [slice(at, at + 128) for at in range(0, width, 128)]


def featurized(x, taps, lane, row, rows):
    total = None
    for lag in range(FK):
        at = row + 8 * (FK - 1 - lag)
        part = x[at : at + rows, lane].reshape(rows // 8, 8, 128) * taps[lag]
        total = part if total is None else total + part
    return total


def spread_taps(short, i, lane):
    return [jnp.broadcast_to(short[i, lag : lag + 1, lane], (8, 128)) for lag in range(FK)]


def fetch(pairs, semaphores):
    copies = [pltpu.make_async_copy(source, into, semaphores.at[at]) for at, (source, into) in enumerate(pairs)]
    for copy in copies:
        copy.start()
    return copies


def window(block, width):
    return pl.ds(pl.multiple_of(block * width, width), width)


def edges_kernel(at, proj, cot, short, *refs):
    tails, heads, few, taps_held, p_tail, p_head, first, second, zeroth, held, semaphores = refs[-11:]
    with_taps = len(refs) == 17
    if with_taps:
        taps, forward, backward, spread, all_taps, all_spread = refs[:6]
    elif len(refs) == 16:
        decay, forward, backward, falloff, all_decay = refs[:5]
    else:
        forward, backward = refs[:2]
    with_decay = len(refs) == 16
    length, channels = cot.shape[0], forward.shape[1]
    here = pl.ds(at, channels)
    some, width = p_tail.shape[1], first.shape[1]
    tail, head = 16, 17
    pairs = [
        (proj.at[1, length - some :, here], tails.at[0]),
        (proj.at[2, length - some :, here], tails.at[1]),
        (proj.at[0, :some, here], heads.at[0]),
        (cot.at[:some, here], heads.at[1]),
        (proj.at[0, length - 16 :, here], few.at[0]),
        (proj.at[1, :16, here], few.at[1]),
        (proj.at[2, :16, here], few.at[2]),
        (short.at[:, :, here], taps_held),
    ]
    if with_taps:
        pairs.append((taps, all_taps))
    if with_decay:
        pairs.append((decay, all_decay))
    copies = fetch(pairs, semaphores)
    p_tail[...] = picked(tail, some - 128, some)
    p_head[...] = picked(head, 0, some)
    if with_taps:
        copies.pop().wait()
        all_spread[...] = jnp.broadcast_to(all_taps[...].astype(BF16)[None], all_spread.shape)
        sent = pltpu.make_async_copy(all_spread, spread, semaphores.at[9])
        sent.start()
    for copy in copies:
        copy.wait()

    def block(c, _):
        columns = window(c, width)
        first[...] = mm(p_tail[...], tails[0, :, columns])
        second[...] = mm(p_tail[...], tails[1, :, columns])
        zeroth[...] = mm(p_head[...], heads[0, :, columns])
        held[...] = mm(p_head[(FK - 1) * 8 :, :], heads[1, :, columns])
        for lane in lanes_of(width):
            wide = pl.ds(pl.multiple_of(c * width + lane.start, 128), 128)
            taps = [spread_taps(taps_held, i, wide) for i in range(3)]
            for r in range(0, 8 * tail, STEP):
                mixed = featurized(first, taps[1], lane, r, STEP) * featurized(second, taps[2], lane, r, STEP)
                forward[r : r + STEP, wide] = mixed.reshape(STEP, 128).astype(BF16)
            ends = [few[0, :, wide], tails[0, some - 16 :, wide], tails[1, some - 16 :, wide]]
            ends = [end.astype(F32)[8:] for end in ends]
            forward[8 * tail :, wide] = jnp.concatenate(ends, axis=0).astype(BF16)
            for r in range(0, 8 * head, STEP):
                rows = min(STEP, 8 * head - r)
                grad = featurized(zeroth, taps[0], lane, r, rows).reshape(rows, 128) * held[r : r + rows, lane]
                if rows < STEP:
                    starts = [heads[1, :16, wide], few[1, :, wide], few[2, :, wide]]
                    starts = [start.astype(F32)[:8] for start in starts]
                    backward[r:, wide] = jnp.concatenate([grad] + starts, axis=0).astype(BF16)
                else:
                    backward[r : r + rows, wide] = grad.astype(BF16)
        return 0

    lax.fori_loop(0, channels // width, block, 0)
    if with_taps:
        sent.wait()
    if with_decay:

        def factors(c, _):
            columns = window(c, width)
            lags = lax.broadcasted_iota(jnp.int32, (falloff.shape[0], width), 0).astype(F32)
            falloff[:, columns] = jnp.exp(-all_decay[:, columns] * lags)
            return 0

        lax.fori_loop(0, falloff.shape[1] // width, factors, 0)


def operator_block(
    proj, cot, prev, later, short, taps, decay,
    e_own, e_prev, e_next, e_taps, s_own, s_lags, p_in, product, grad, px, feat, cots,
):
    length, width = cot.shape
    span = length // 8
    edge = FK - 1
    lanes = [slice(at, at + 128) for at in range(0, width, 128)]
    row8 = lax.broadcasted_iota(jnp.int32, (8, width), 0)

    before = prev[...].astype(F32)
    after = later[...].astype(F32)
    prev8 = [before[128 + 8 * i : 136 + 8 * i] for i in range(3)]
    cot_next = after[136:144]
    next8 = [None, after[144:152], after[152:160]]

    falloff = decay[...]
    kernel = taps[...].astype(F32) * falloff
    high = kernel.astype(BF16)
    low = (kernel - high.astype(F32)).astype(BF16)
    k_spec = mm(e_taps[...], jnp.concatenate([high, high, low], axis=0))

    for i in range(3):
        x = mm(p_in[...], proj[i]).reshape(span + edge, 8, width)
        px[i, edge:] = x[edge:]
        for k in range(1, FK):
            px[i, edge - k] = jnp.where(row8 == 0, pltpu.roll(prev8[i], k, 0), x[edge - k])
    cots[...] = mm(p_in[edge * 8 :, :], cot[...]).reshape(span, 8, width)

    yield
    step = 8
    for i in range(3):
        for lane in lanes:
            weights = [jnp.broadcast_to(short[i, lag : lag + 1, lane], (8, 128)) for lag in range(FK)]
            for r in range(0, span, step):
                total = weights[0] * px[i, r + edge : r + edge + step, :, lane]
                for lag in range(1, FK):
                    total = total + weights[lag] * px[i, r + edge - lag : r + edge - lag + step, :, lane]
                feat[i, r : r + step, :, lane] = total

    def conv8(last, first, weights, whole):
        total = weights[0:1] * first if whole else jnp.zeros((8, width), F32)
        for lag in range(1, FK):
            rolled = pltpu.roll(first, lag, 0) if whole else 0.0
            total = total + weights[lag : lag + 1] * jnp.where(row8 < lag, pltpu.roll(last, lag, 0), rolled)
        return total

    ends = [proj[i, length - 16 :, :].astype(F32)[8:] for i in range(3)]
    feat_next = [None] + [conv8(ends[i], next8[i], short[i], True) for i in (1, 2)]
    mixed_next = feat_next[1] * feat_next[2]
    grad_next = after[:136]
    fix = cot_next * conv8(ends[0], None, short[0], False)
    rows = [grad_next[8 * r : 8 * r + 8] for r in range(17)]
    for r in range(edge):
        rows[r] = rows[r] + jnp.where(row8 == 0, pltpu.roll(fix, (8 - r) % 8, 0), 0.0)
    grad_next = jnp.concatenate(rows + [jnp.zeros((8, width), F32)], axis=0).astype(BF16)
    mixed_edge = jnp.concatenate([before[:128], mixed_next, jnp.zeros((8, width), F32)], axis=0).astype(BF16)

    flat = lambda value: value.reshape(length, width)
    mixed = flat(feat[1] * feat[2]).astype(BF16)
    grad_own = flat(cots[...] * feat[0]).astype(BF16)
    yield
    m_spec = mm(e_own[...], jnp.concatenate([mixed, mixed], axis=0)) + mm(e_prev[...], mixed_edge)
    g_own = mm(e_own[...], jnp.concatenate([grad_own, grad_own], axis=0))
    g_spec = g_own + mm(e_next[...], grad_next)

    yield
    half = k_spec.shape[0] // 2
    parts = lambda value: (value[:half], value[half:])
    (kr, ki), (mr, mi), (gr, gi), (hr, hi) = parts(k_spec), parts(m_spec), parts(g_spec), parts(g_own)

    def joined(real, imaginary):
        spectrum = jnp.concatenate([real, imaginary], axis=0).astype(BF16)
        return jnp.concatenate([spectrum, spectrum], axis=0)

    filtered = joined(mr * kr - mi * ki, mr * ki + mi * kr)
    grad_mixed = joined(gr * kr + gi * ki, gi * kr - gr * ki)
    filter_sums = joined(hr * mr + hi * mi, hi * mr - hr * mi)
    yield
    filtered, grad_mixed = mm(s_own[...], filtered), mm(s_own[...], grad_mixed)
    filter_sums = mm(s_lags[...], filter_sums) * falloff
    yield

    own = filtered[:length].reshape(span, 8, width)
    product[...] = flat(feat[0] * own).astype(BF16)
    back = grad_mixed[:length].reshape(span, 8, width)
    grad[0, :span] = cots[...] * own
    grad[1, :span] = back * feat[2]
    grad[2, :span] = back * feat[1]
    back_next = grad_mixed[length:]
    edge_next = [cot_next * filtered[length:], back_next * feat_next[2], back_next * feat_next[1]]
    for i in range(3):
        for k in range(edge):
            grad[i, span + k] = jnp.where(row8 == 7, pltpu.roll(edge_next[i], 7 - k, 0), pltpu.roll(grad[i, k], 7, 0))

    short_rows = []
    for i in range(3):
        rows = [[] for _ in range(FK)]
        for lane in lanes:
            sums = [jnp.zeros((8, 128), F32)] * FK
            for r in range(0, span, step):
                here = px[i, r + edge : r + edge + step, :, lane]
                for lag in range(FK):
                    value = grad[i, r + lag : r + lag + step, :, lane]
                    sums[lag] = sums[lag] + jnp.sum(here * value, axis=0)
            for lag in range(FK):
                rows[lag].append(jnp.sum(sums[lag], axis=0, keepdims=True))
        short_rows += [jnp.concatenate(row, axis=1) for row in rows]
    yield filter_sums, short_rows


def operator_kernel(first, proj, cot, prev, later, short, taps, decay, *refs):
    constants, (product, grad, sums_out, px, feat, cots, filter_held, short_held, done) = refs[:7], refs[-9:]
    width = px.shape[-1]
    pair = []
    for at in range(PAIR):
        here = slice(at * width, (at + 1) * width)
        views = [proj.at[:, :, here], cot.at[:, here], prev.at[:, here], later.at[:, here], short.at[:, :, here]]
        views += [taps.at[:, here], decay.at[:, here], *constants]
        pair.append(operator_block(*views, product.at[at], grad.at[at], px.at[at], feat.at[at], cots.at[at]))
    results = [None] * PAIR
    for turn in range(6 + PAIR - 1):
        for at in range(PAIR):
            if 0 <= turn - at < 6:
                results[at] = next(pair[at])

    step = pl.program_id(0)
    _, ranks, slot, width = filter_held.shape
    per, share = results[0][0].shape[0] // ranks, short_held.shape[1]
    copies = []
    for at in range(PAIR):
        block = first + PAIR * step + at
        rows = pl.ds(pl.multiple_of(block * slot, slot), slot)
        few = pl.ds(sums_out.shape[1] - SHORT, SHORT)
        copies += [
            pltpu.make_async_copy(filter_held.at[at], sums_out.at[:, rows, :], done.at[2 * at]),
            pltpu.make_async_copy(
                short_held.at[at], sums_out.at[pl.ds(block * share, share), few, :], done.at[2 * at + 1]
            ),
        ]

    @pl.when(step > 0)
    def _():
        for copy in copies:
            copy.wait()

    for at, (filter_sums, short_rows) in enumerate(results):
        if per % 8 == 0:
            by_rank = filter_sums.reshape(ranks, per, width)
        else:
            by_rank = jnp.stack([filter_sums[rank * per : rank * per + per] for rank in range(ranks)])
        if slot > per:
            by_rank = jnp.concatenate([by_rank, jnp.zeros((ranks, slot - per, width), F32)], axis=1)
        filter_held[at] = by_rank.astype(BF16)
        sums = jnp.concatenate(short_rows + [jnp.zeros((SHORT - len(short_rows), width), F32)], axis=0)
        for rank in range(share):
            held = pltpu.roll(sums, width - rank * (width // share), 1) if rank else sums
            short_held[at, rank] = held.astype(BF16)
    for copy in copies:
        copy.start()

    @pl.when(step == pl.num_programs(0) - 1)
    def _():
        for copy in copies:
            copy.wait()


def outputs_kernel(product, grad, short, p_out, gated, grad_proj):
    length, width = product.shape[1:]
    span = length // 8
    gated[...] = mm(p_out[...], product[0]).astype(BF16)
    for i in range(3):
        lanes = []
        for lane in lanes_of(width):
            taps = spread_taps(short, i, lane)
            chunks = []
            for r in range(0, span, 8):
                total = None
                for lag in range(FK):
                    part = grad[0, i, r + lag : r + lag + 8, :, lane] * taps[lag]
                    total = part if total is None else total + part
                chunks.append(total)
            lanes.append(jnp.concatenate(chunks, axis=0))
        result = jnp.concatenate(lanes, axis=2).reshape(length, width).astype(BF16)
        grad_proj[i] = mm(p_out[...], result).astype(BF16)


def whole(array):
    return pl.BlockSpec(array.shape, lambda c: (0,) * array.ndim)


def columns(rows, width, first=0):
    lead = (0,) * len(rows)
    return pl.BlockSpec(tuple(rows) + (width,), lambda c: lead + (first + c,))


def one_of(array, first=0, some=1):
    tail = (0,) * (len(array.shape) - 1)
    return pl.BlockSpec((some,) + tuple(array.shape[1:]), lambda c: (first + c,) + tail)


IN_VMEM = pl.BlockSpec(memory_space=pltpu.VMEM)
FAR = pl.BlockSpec(memory_space=pl.ANY)


def call(kernel, name, operands, outputs, cost=1, held=(), free=(), **options):
    arrays = [
        array if at in free else pltpu.with_memory_space_constraint(array, pltpu.HBM)
        for at, (array, _) in enumerate(operands)
    ]
    return pl.pallas_call(
        kernel,
        in_specs=[spec for _, spec in operands] + [FAR] * len(held),
        out_specs=[spec for _, spec in outputs],
        out_shape=[shape for shape, _ in outputs],
        input_output_aliases={len(operands) + at: at for at in range(len(held))},
        compiler_params=pltpu.CompilerParams(vmem_limit_bytes=40 << 20),
        cost_estimate=pl.CostEstimate(flops=cost * 10**9, bytes_accessed=10**6, transcendentals=0),
        name=name,
        **options,
    )(*arrays, *held)


def squares_kernel(rows, share, sums, raw, payload):
    ranks, slots, width = sums.shape
    total = sums[0].astype(F32)
    for rank in range(1, ranks):
        total = total + sums[rank].astype(F32)
    slot = -(-rows // 16) * 16
    pieces = [total[at : at + rows] for at in range(0, slots - SHORT, slot)]
    raw[...] = jnp.concatenate(pieces, axis=1)
    lane = lax.broadcasted_iota(jnp.int32, (SHORT, width), 1)
    short = jnp.where(lane < share, total[slots - SHORT :], 0.0)
    squares = jnp.sum(short * short, keepdims=True)
    for piece in pieces:
        squares = squares + jnp.sum(piece * piece, keepdims=True)
    high = squares.astype(BF16).astype(F32)
    row = lax.broadcasted_iota(jnp.int32, (24, width), 0)
    block = jnp.where(row < 3 * FK, short[:24], jnp.where(row == 3 * FK, high, squares - high)).astype(BF16)
    for other in range(payload.shape[0]):
        payload[other] = block


def scale_kernel(entries, share, mine, raw, gathered, grad_short, grad_filter):
    everyone, rows, width = gathered.shape
    total = jnp.zeros((8, width), F32)
    for other in range(everyone):
        total = total + gathered[other].astype(F32)[16:]
    total = total[5:6, :1] + total[6:7, :1]
    scale = jnp.minimum(1.0, math.sqrt(entries) / jnp.sqrt(total))
    grad_filter[...] = scale * raw[...]
    step = mine[1]
    for rank in range(raw.shape[1] // share):
        block = gathered[rank * step + mine[0]].astype(F32) * scale
        for i in range(3):
            grad_short[i, :, rank * share : (rank + 1) * share] = block[i * FK : (i + 1) * FK, :share]


def shards(projected, short_taps, filter_taps, decay, cotangent):
    length, _, channels = projected.shape
    ranks, groups = lax.axis_size("seq"), lax.axis_size("ch")
    rows = filter_taps.shape[0]
    count = rows * ranks
    width = min(256, channels // CHUNKS // PAIR)
    share = channels // ranks
    slot = -(-rows // 16) * 16
    size, span = 2 * length, length // 8
    some = 144
    proj, cot, short, decay = jnp.transpose(projected, (1, 0, 2)), cotangent, short_taps, decay[None]
    full = lambda kind, *shape: (jax.ShapeDtypeStruct(shape, kind), IN_VMEM)
    vmem = lambda kind, *shape: pltpu.VMEM(shape, kind)
    far = lambda *arrays: [(array, FAR) for array in arrays]
    semaphores = pltpu.SemaphoreType.DMA((10,))
    own = interleaved(span)
    after = length + np.arange(8)
    chunk = channels // CHUNKS
    blocks = chunk // width

    prev, later, taps = [], [], None
    for k in range(CHUNKS):
        operands = far(proj, cot, short)
        results = [full(BF16, 152, chunk), full(BF16, 160, chunk)]
        scratch = [
            vmem(BF16, 2, some, chunk), vmem(BF16, 2, some, chunk), vmem(BF16, 3, 16, chunk), vmem(F32, 3, FK, chunk),
            vmem(BF16, 8 * (15 + FK), some), vmem(BF16, 8 * (16 + FK), some), vmem(F32, 8 * (15 + FK), width),
            vmem(F32, 8 * (15 + FK), width), vmem(F32, 8 * (16 + FK), width), vmem(F32, 8 * 17, width), semaphores,
        ]
        if k == 0:
            operands += far(filter_taps)
            results.append((pltpu.HBM((ranks, rows, channels), BF16), FAR))
            scratch = [vmem(F32, rows, channels), vmem(BF16, ranks, rows, channels)] + scratch
        elif k == CHUNKS - 1:
            operands += far(decay)
            results.append((pltpu.HBM((count, channels), F32), IN_VMEM))
            scratch = [vmem(F32, 1, channels)] + scratch
        forward, backward, *spread = call(
            functools.partial(edges_kernel, k * chunk), "edges", operands, results, cost=10 if k else 1,
            scratch_shapes=scratch,
        )
        if k == CHUNKS - 1:
            falloff = spread[0]
        if k == 0:
            taps = lax.all_to_all(spread[0], "seq", 0, 0).reshape(count, channels)
        else:
            backward, prev[-1] = lax.optimization_barrier((backward, prev[-1]))
        later.append(from_behind(backward, "seq", -1))
        prev.append(from_behind(forward, "seq", 1))

    high, low = analysis(own, size)
    k_high, k_low = analysis(np.arange(count), size)
    constants = [
        np.concatenate([high, low], axis=1),
        analysis(np.concatenate([interleaved(16, -128), after]), size, 8)[0],
        analysis(interleaved(17, length), size, 8)[0],
        np.concatenate([k_high, k_low, k_high], axis=1),
        np.concatenate(list(synthesis(np.concatenate([own, after]), size)), axis=1),
        np.concatenate(list(synthesis(np.arange(count), size)), axis=1),
        pick(interleaved(span, 0, 1 - FK), length),
    ]
    constants = [(jnp.asarray(constant), whole(constant)) for constant in constants]
    held = ()
    for k in range(CHUNKS):
        first, wide = k * blocks // PAIR, PAIR * width
        results = [
            pltpu.HBM((CHUNKS * blocks, length, width), BF16),
            pltpu.HBM((CHUNKS * blocks, 3, span + FK - 1, 8, width), F32),
        ]
        held = call(
            functools.partial(operator_kernel, k * blocks), "operator",
            [
                (proj, columns((3, length), wide, first)), (cot, columns((length,), wide, first)),
                (prev[k], columns((152,), wide)), (later[k], columns((160,), wide)),
                (short, columns((3, FK), wide, first)), (taps, columns((count,), wide, first)),
                (falloff, columns((count,), wide, first)),
            ] + constants,
            [(result, one_of(result, first, PAIR)) for result in results]
            + [(pltpu.HBM((ranks, CHUNKS * blocks * slot + SHORT, width), BF16), FAR)],
            cost=12,
            held=held,
            free=(2, 3, 5),
            grid=(blocks // PAIR,),
            scratch_shapes=[
                vmem(F32, PAIR, 3, span + FK - 1, 8, width), vmem(F32, PAIR, 3, span, 8, width),
                vmem(F32, PAIR, span, 8, width), vmem(BF16, PAIR, ranks, slot, width),
                vmem(BF16, PAIR, ranks * width // channels, SHORT, width), pltpu.SemaphoreType.DMA((2 * PAIR,)),
            ],
        )
    product, grad, sums = held
    p_out = jnp.asarray(pick(own, length).T)
    gated, grad_proj = call(
        outputs_kernel, "outputs",
        [(product, one_of(product)), (grad, one_of(grad)), (short, columns((3, FK), width)), (p_out, whole(p_out))],
        [
            (jax.ShapeDtypeStruct((length, channels), BF16), columns((length,), width)),
            (jax.ShapeDtypeStruct((3, length, channels), BF16), columns((3, length), width)),
        ],
        cost=8,
        grid=(CHUNKS * blocks,),
    )
    sums, gated, grad_proj = lax.optimization_barrier((lax.all_to_all(sums, "seq", 0, 0), gated, grad_proj))

    vmem = pl.BlockSpec(memory_space=pltpu.VMEM)
    raw, payload = pl.pallas_call(
        functools.partial(squares_kernel, rows, share),
        in_specs=[vmem],
        out_specs=[vmem] * 2,
        out_shape=[
            jax.ShapeDtypeStruct((rows, channels), F32),
            jax.ShapeDtypeStruct((ranks * groups, 24, width), BF16),
        ],
        compiler_params=pltpu.CompilerParams(vmem_limit_bytes=32 << 20),
        name="squares",
    )(sums)
    gathered = lax.all_to_all(payload, ("seq", "ch"), 0, 0)
    mine = jnp.stack([lax.axis_index("ch"), jnp.int32(groups)])
    entries = (rows * ranks + 3 * FK) * channels * groups
    grad_short, grad_filter = pl.pallas_call(
        functools.partial(scale_kernel, entries, share),
        in_specs=[pl.BlockSpec(memory_space=pltpu.SMEM), vmem, vmem],
        out_specs=[vmem] * 2,
        out_shape=[
            jax.ShapeDtypeStruct((3, FK, channels), F32),
            jax.ShapeDtypeStruct((rows, channels), F32),
        ],
        compiler_params=pltpu.CompilerParams(vmem_limit_bytes=32 << 20),
        name="scale",
    )(mine, raw, gathered)
    return (gated, jnp.transpose(grad_proj, (1, 0, 2)), grad_short, grad_filter)


def solution(mesh):
    placed = (P("seq", None, "ch"), P(None, None, "ch"), P("seq", "ch"), P("ch"), P("seq", "ch"))
    return jax.shard_map(
        shards,
        mesh=mesh,
        in_specs=placed,
        out_specs=(P("seq", "ch"), P("seq", None, "ch"), P(None, None, "ch"), P("seq", "ch")),
        check_vma=False,
    )
```

```python
import functools
import math

import jax
import jax.numpy as jnp
import ml_dtypes
import numpy as np
from jax import lax
from jax.experimental import pallas as pl
from jax.experimental.pallas import tpu as pltpu
from jax.sharding import PartitionSpec as P


FK = 7
BF16 = jnp.bfloat16
F32 = jnp.float32
CHUNKS = 2
PAIR = 2
SHORT = 32
STEP = 64


def from_behind(value, axis, by):
    count = lax.axis_size(axis)
    pairs = [(i, i + by) for i in range(count) if 0 <= i + by < count]
    return lax.ppermute(value, axis, pairs)


def interleaved(span, first=0, low=0):
    return np.array([first + s * span + r for r in range(low, span) for s in range(8)])


def pick(positions, count):
    out = np.zeros((len(positions), count), np.float32)
    for row, at in enumerate(positions):
        if 0 <= at < count:
            out[row, at] = 1.0
    return out.astype(ml_dtypes.bfloat16)


def halves(matrix):
    high = matrix.astype(np.float32).astype(ml_dtypes.bfloat16)
    low = (matrix - high.astype(np.float64)).astype(np.float32).astype(ml_dtypes.bfloat16)
    return np.stack([high, low])


def analysis(positions, size, pad=0):
    freq = np.arange(size // 2)[:, None]
    angle = np.pi * (((2 * freq + 1) * np.asarray(positions)[None, :]) % (2 * size)) / size
    matrix = np.concatenate([np.cos(angle), -np.sin(angle)], axis=0)
    return halves(np.pad(matrix, ((0, 0), (0, pad))))


def synthesis(positions, size):
    freq = np.arange(size // 2)[None, :]
    angle = np.pi * (((2 * freq + 1) * np.asarray(positions)[:, None]) % (2 * size)) / size
    return halves(np.concatenate([np.cos(angle), -np.sin(angle)], axis=1) * (2.0 / size))


def mm(a, b):
    return jnp.dot(a, b, preferred_element_type=F32)


def picked(span, first, length):
    shape = ((span + FK - 1) * 8, length)
    row, column = (lax.broadcasted_iota(jnp.int32, shape, axis) for axis in (0, 1))
    position = first + (row & 7) * span + (row >> 3) - (FK - 1)
    return jnp.where(position == column, 1.0, 0.0).astype(BF16)


def lanes_of(width):
    return [slice(at, at + 128) for at in range(0, width, 128)]


def featurized(x, taps, lane, row, rows):
    total = None
    for lag in range(FK):
        at = row + 8 * (FK - 1 - lag)
        part = x[at : at + rows, lane].reshape(rows // 8, 8, 128) * taps[lag]
        total = part if total is None else total + part
    return total


def spread_taps(short, i, lane):
    return [jnp.broadcast_to(short[i, lag : lag + 1, lane], (8, 128)) for lag in range(FK)]


def fetch(pairs, semaphores):
    copies = [pltpu.make_async_copy(source, into, semaphores.at[at]) for at, (source, into) in enumerate(pairs)]
    for copy in copies:
        copy.start()
    return copies


def window(block, width):
    return pl.ds(pl.multiple_of(block * width, width), width)


def edges_kernel(at, proj, cot, short, *refs):
    tails, heads, few, taps_held, p_tail, p_head, first, second, zeroth, held, semaphores = refs[-11:]
    with_taps = len(refs) == 17
    if with_taps:
        taps, forward, backward, spread, all_taps, all_spread = refs[:6]
    elif len(refs) == 16:
        decay, forward, backward, falloff, all_decay = refs[:5]
    else:
        forward, backward = refs[:2]
    with_decay = len(refs) == 16
    length, channels = cot.shape[0], forward.shape[1]
    here = pl.ds(at, channels)
    some, width = p_tail.shape[1], first.shape[1]
    tail, head = 16, 17
    pairs = [
        (proj.at[1, length - some :, here], tails.at[0]),
        (proj.at[2, length - some :, here], tails.at[1]),
        (proj.at[0, :some, here], heads.at[0]),
        (cot.at[:some, here], heads.at[1]),
        (proj.at[0, length - 16 :, here], few.at[0]),
        (proj.at[1, :16, here], few.at[1]),
        (proj.at[2, :16, here], few.at[2]),
        (short.at[:, :, here], taps_held),
    ]
    if with_taps:
        pairs.append((taps, all_taps))
    if with_decay:
        pairs.append((decay, all_decay))
    copies = fetch(pairs, semaphores)
    p_tail[...] = picked(tail, some - 128, some)
    p_head[...] = picked(head, 0, some)
    if with_taps:
        copies.pop().wait()
        all_spread[...] = jnp.broadcast_to(all_taps[...].astype(BF16)[None], all_spread.shape)
        sent = pltpu.make_async_copy(all_spread, spread, semaphores.at[9])
        sent.start()
    for copy in copies:
        copy.wait()

    def block(c, _):
        columns = window(c, width)
        first[...] = mm(p_tail[...], tails[0, :, columns])
        second[...] = mm(p_tail[...], tails[1, :, columns])
        zeroth[...] = mm(p_head[...], heads[0, :, columns])
        held[...] = mm(p_head[(FK - 1) * 8 :, :], heads[1, :, columns])
        for lane in lanes_of(width):
            wide = pl.ds(pl.multiple_of(c * width + lane.start, 128), 128)
            taps = [spread_taps(taps_held, i, wide) for i in range(3)]
            for r in range(0, 8 * tail, STEP):
                mixed = featurized(first, taps[1], lane, r, STEP) * featurized(second, taps[2], lane, r, STEP)
                forward[r : r + STEP, wide] = mixed.reshape(STEP, 128).astype(BF16)
            ends = [few[0, :, wide], tails[0, some - 16 :, wide], tails[1, some - 16 :, wide]]
            ends = [end.astype(F32)[8:] for end in ends]
            forward[8 * tail :, wide] = jnp.concatenate(ends, axis=0).astype(BF16)
            for r in range(0, 8 * head, STEP):
                rows = min(STEP, 8 * head - r)
                grad = featurized(zeroth, taps[0], lane, r, rows).reshape(rows, 128) * held[r : r + rows, lane]
                if rows < STEP:
                    starts = [heads[1, :16, wide], few[1, :, wide], few[2, :, wide]]
                    starts = [start.astype(F32)[:8] for start in starts]
                    backward[r:, wide] = jnp.concatenate([grad] + starts, axis=0).astype(BF16)
                else:
                    backward[r : r + rows, wide] = grad.astype(BF16)
        return 0

    lax.fori_loop(0, channels // width, block, 0)
    if with_taps:
        sent.wait()
    if with_decay:

        def factors(c, _):
            columns = window(c, width)
            lags = lax.broadcasted_iota(jnp.int32, (falloff.shape[0], width), 0).astype(F32)
            falloff[:, columns] = jnp.exp(-all_decay[:, columns] * lags)
            return 0

        lax.fori_loop(0, falloff.shape[1] // width, factors, 0)


def operator_block(
    proj, cot, prev, later, short, taps, decay,
    e_own, e_prev, e_next, e_taps, s_own, s_lags, p_in, product, grad, px, feat, cots,
):
    length, width = cot.shape
    span = length // 8
    edge = FK - 1
    lanes = [slice(at, at + 128) for at in range(0, width, 128)]
    row8 = lax.broadcasted_iota(jnp.int32, (8, width), 0)

    before = prev[...].astype(F32)
    after = later[...].astype(F32)
    prev8 = [before[128 + 8 * i : 136 + 8 * i] for i in range(3)]
    cot_next = after[136:144]
    next8 = [None, after[144:152], after[152:160]]

    falloff = decay[...]
    kernel = taps[...].astype(F32) * falloff
    high = kernel.astype(BF16)
    k_spec = mm(e_taps[...], jnp.concatenate([high, high], axis=0))

    for i in range(3):
        x = mm(p_in[...], proj[i]).reshape(span + edge, 8, width)
        px[i, edge:] = x[edge:]
        for k in range(1, FK):
            px[i, edge - k] = jnp.where(row8 == 0, pltpu.roll(prev8[i], k, 0), x[edge - k])
    cots[...] = mm(p_in[edge * 8 :, :], cot[...]).reshape(span, 8, width)

    yield
    step = 8
    for i in range(3):
        for lane in lanes:
            weights = [jnp.broadcast_to(short[i, lag : lag + 1, lane], (8, 128)) for lag in range(FK)]
            for r in range(0, span, step):
                total = weights[0] * px[i, r + edge : r + edge + step, :, lane]
                for lag in range(1, FK):
                    total = total + weights[lag] * px[i, r + edge - lag : r + edge - lag + step, :, lane]
                feat[i, r : r + step, :, lane] = total

    def conv8(last, first, weights, whole):
        total = weights[0:1] * first if whole else jnp.zeros((8, width), F32)
        for lag in range(1, FK):
            rolled = pltpu.roll(first, lag, 0) if whole else 0.0
            total = total + weights[lag : lag + 1] * jnp.where(row8 < lag, pltpu.roll(last, lag, 0), rolled)
        return total

    ends = [proj[i, length - 16 :, :].astype(F32)[8:] for i in range(3)]
    feat_next = [None] + [conv8(ends[i], next8[i], short[i], True) for i in (1, 2)]
    mixed_next = feat_next[1] * feat_next[2]
    grad_next = after[:136]
    fix = cot_next * conv8(ends[0], None, short[0], False)
    rows = [grad_next[8 * r : 8 * r + 8] for r in range(17)]
    for r in range(edge):
        rows[r] = rows[r] + jnp.where(row8 == 0, pltpu.roll(fix, (8 - r) % 8, 0), 0.0)
    grad_next = jnp.concatenate(rows + [jnp.zeros((8, width), F32)], axis=0).astype(BF16)
    mixed_edge = jnp.concatenate([before[:128], mixed_next, jnp.zeros((8, width), F32)], axis=0).astype(BF16)

    flat = lambda value: value.reshape(length, width)
    mixed = flat(feat[1] * feat[2]).astype(BF16)
    grad_own = flat(cots[...] * feat[0]).astype(BF16)
    yield
    m_spec = mm(e_own[...], jnp.concatenate([mixed, mixed], axis=0)) + mm(e_prev[...], mixed_edge)
    g_own = mm(e_own[...], jnp.concatenate([grad_own, grad_own], axis=0))
    g_spec = g_own + mm(e_next[...], grad_next)

    yield
    half = k_spec.shape[0] // 2
    parts = lambda value: (value[:half], value[half:])
    (kr, ki), (mr, mi), (gr, gi), (hr, hi) = parts(k_spec), parts(m_spec), parts(g_spec), parts(g_own)

    twice = lambda spectrum: jnp.concatenate([spectrum, spectrum], axis=0)

    def joined(real, imaginary):
        return jnp.concatenate([real, imaginary], axis=0).astype(BF16)

    filtered = joined(mr * kr - mi * ki, mr * ki + mi * kr)
    grad_mixed = joined(gr * kr + gi * ki, gi * kr - gr * ki)
    filter_sums = joined(hr * mr + hi * mi, hi * mr - hr * mi)
    yield
    filtered, grad_mixed = mm(s_own[...], twice(filtered)), mm(s_own[...], twice(grad_mixed))
    filter_sums = mm(s_lags[...], filter_sums) * falloff
    yield

    own = filtered[:length].reshape(span, 8, width)
    product[...] = flat(feat[0] * own).astype(BF16)
    back = grad_mixed[:length].reshape(span, 8, width)
    grad[0, :span] = cots[...] * own
    grad[1, :span] = back * feat[2]
    grad[2, :span] = back * feat[1]
    back_next = grad_mixed[length:]
    edge_next = [cot_next * filtered[length:], back_next * feat_next[2], back_next * feat_next[1]]
    for i in range(3):
        for k in range(edge):
            grad[i, span + k] = jnp.where(row8 == 7, pltpu.roll(edge_next[i], 7 - k, 0), pltpu.roll(grad[i, k], 7, 0))

    short_rows = []
    for i in range(3):
        rows = [[] for _ in range(FK)]
        for lane in lanes:
            sums = [jnp.zeros((8, 128), F32)] * FK
            for r in range(0, span, step):
                here = px[i, r + edge : r + edge + step, :, lane]
                for lag in range(FK):
                    value = grad[i, r + lag : r + lag + step, :, lane]
                    sums[lag] = sums[lag] + jnp.sum(here * value, axis=0)
            for lag in range(FK):
                rows[lag].append(jnp.sum(sums[lag], axis=0, keepdims=True))
        short_rows += [jnp.concatenate(row, axis=1) for row in rows]
    yield filter_sums, short_rows


def operator_kernel(first, proj, cot, prev, later, short, taps, decay, *refs):
    constants, (product, grad, sums_out, px, feat, cots, filter_held, short_held, done) = refs[:7], refs[-9:]
    width = px.shape[-1]
    pair = []
    for at in range(PAIR):
        here = slice(at * width, (at + 1) * width)
        views = [proj.at[:, :, here], cot.at[:, here], prev.at[:, here], later.at[:, here], short.at[:, :, here]]
        views += [taps.at[:, here], decay.at[:, here], *constants]
        pair.append(operator_block(*views, product.at[at], grad.at[at], px.at[at], feat.at[at], cots.at[at]))
    results = [None] * PAIR
    for turn in range(6 + PAIR - 1):
        for at in range(PAIR):
            if 0 <= turn - at < 6:
                results[at] = next(pair[at])

    step = pl.program_id(0)
    _, ranks, slot, width = filter_held.shape
    per, share = results[0][0].shape[0] // ranks, short_held.shape[1]
    copies = []
    for at in range(PAIR):
        block = first + PAIR * step + at
        rows = pl.ds(pl.multiple_of(block * slot, slot), slot)
        few = pl.ds(sums_out.shape[1] - SHORT, SHORT)
        copies += [
            pltpu.make_async_copy(filter_held.at[at], sums_out.at[:, rows, :], done.at[2 * at]),
            pltpu.make_async_copy(
                short_held.at[at], sums_out.at[pl.ds(block * share, share), few, :], done.at[2 * at + 1]
            ),
        ]

    @pl.when(step > 0)
    def _():
        for copy in copies:
            copy.wait()

    for at, (filter_sums, short_rows) in enumerate(results):
        if per % 8 == 0:
            by_rank = filter_sums.reshape(ranks, per, width)
        else:
            by_rank = jnp.stack([filter_sums[rank * per : rank * per + per] for rank in range(ranks)])
        if slot > per:
            by_rank = jnp.concatenate([by_rank, jnp.zeros((ranks, slot - per, width), F32)], axis=1)
        filter_held[at] = by_rank.astype(BF16)
        sums = jnp.concatenate(short_rows + [jnp.zeros((SHORT - len(short_rows), width), F32)], axis=0)
        for rank in range(share):
            held = pltpu.roll(sums, width - rank * (width // share), 1) if rank else sums
            short_held[at, rank] = held.astype(BF16)
    for copy in copies:
        copy.start()

    @pl.when(step == pl.num_programs(0) - 1)
    def _():
        for copy in copies:
            copy.wait()


def outputs_kernel(product, grad, short, p_out, gated, grad_proj):
    length, width = product.shape[1:]
    span = length // 8
    gated[...] = mm(p_out[...], product[0]).astype(BF16)
    for i in range(3):
        lanes = []
        for lane in lanes_of(width):
            taps = spread_taps(short, i, lane)
            chunks = []
            for r in range(0, span, 8):
                total = None
                for lag in range(FK):
                    part = grad[0, i, r + lag : r + lag + 8, :, lane] * taps[lag]
                    total = part if total is None else total + part
                chunks.append(total)
            lanes.append(jnp.concatenate(chunks, axis=0))
        result = jnp.concatenate(lanes, axis=2).reshape(length, width).astype(BF16)
        grad_proj[i] = mm(p_out[...], result).astype(BF16)


def whole(array):
    return pl.BlockSpec(array.shape, lambda c: (0,) * array.ndim)


def columns(rows, width, first=0):
    lead = (0,) * len(rows)
    return pl.BlockSpec(tuple(rows) + (width,), lambda c: lead + (first + c,))


def one_of(array, first=0, some=1):
    tail = (0,) * (len(array.shape) - 1)
    return pl.BlockSpec((some,) + tuple(array.shape[1:]), lambda c: (first + c,) + tail)


IN_VMEM = pl.BlockSpec(memory_space=pltpu.VMEM)
FAR = pl.BlockSpec(memory_space=pl.ANY)


def call(kernel, name, operands, outputs, cost=1, held=(), free=(), **options):
    arrays = [
        array if at in free else pltpu.with_memory_space_constraint(array, pltpu.HBM)
        for at, (array, _) in enumerate(operands)
    ]
    return pl.pallas_call(
        kernel,
        in_specs=[spec for _, spec in operands] + [FAR] * len(held),
        out_specs=[spec for _, spec in outputs],
        out_shape=[shape for shape, _ in outputs],
        input_output_aliases={len(operands) + at: at for at in range(len(held))},
        compiler_params=pltpu.CompilerParams(vmem_limit_bytes=40 << 20),
        cost_estimate=pl.CostEstimate(flops=cost * 10**9, bytes_accessed=10**6, transcendentals=0),
        name=name,
        **options,
    )(*arrays, *held)


def squares_kernel(rows, share, sums, raw, payload):
    ranks, slots, width = sums.shape
    total = sums[0].astype(F32)
    for rank in range(1, ranks):
        total = total + sums[rank].astype(F32)
    slot = -(-rows // 16) * 16
    pieces = [total[at : at + rows] for at in range(0, slots - SHORT, slot)]
    raw[...] = jnp.concatenate(pieces, axis=1)
    lane = lax.broadcasted_iota(jnp.int32, (SHORT, width), 1)
    short = jnp.where(lane < share, total[slots - SHORT :], 0.0)
    squares = jnp.sum(short * short, keepdims=True)
    for piece in pieces:
        squares = squares + jnp.sum(piece * piece, keepdims=True)
    high = squares.astype(BF16).astype(F32)
    row = lax.broadcasted_iota(jnp.int32, (24, width), 0)
    block = jnp.where(row < 3 * FK, short[:24], jnp.where(row == 3 * FK, high, squares - high)).astype(BF16)
    for other in range(payload.shape[0]):
        payload[other] = block


def scale_kernel(entries, share, mine, raw, gathered, grad_short, grad_filter):
    everyone, rows, width = gathered.shape
    total = jnp.zeros((8, width), F32)
    for other in range(everyone):
        total = total + gathered[other].astype(F32)[16:]
    total = total[5:6, :1] + total[6:7, :1]
    scale = jnp.minimum(1.0, math.sqrt(entries) / jnp.sqrt(total))
    grad_filter[...] = scale * raw[...]
    step = mine[1]
    for rank in range(raw.shape[1] // share):
        block = gathered[rank * step + mine[0]].astype(F32) * scale
        for i in range(3):
            grad_short[i, :, rank * share : (rank + 1) * share] = block[i * FK : (i + 1) * FK, :share]


def shards(projected, short_taps, filter_taps, decay, cotangent):
    length, _, channels = projected.shape
    ranks, groups = lax.axis_size("seq"), lax.axis_size("ch")
    rows = filter_taps.shape[0]
    count = rows * ranks
    width = min(256, channels // CHUNKS // PAIR)
    share = channels // ranks
    slot = -(-rows // 16) * 16
    size, span = 2 * length, length // 8
    some = 144
    proj, cot, short, decay = jnp.transpose(projected, (1, 0, 2)), cotangent, short_taps, decay[None]
    full = lambda kind, *shape: (jax.ShapeDtypeStruct(shape, kind), IN_VMEM)
    vmem = lambda kind, *shape: pltpu.VMEM(shape, kind)
    far = lambda *arrays: [(array, FAR) for array in arrays]
    semaphores = pltpu.SemaphoreType.DMA((10,))
    own = interleaved(span)
    after = length + np.arange(8)
    chunk = channels // CHUNKS
    blocks = chunk // width

    prev, later, taps = [], [], None
    for k in range(CHUNKS):
        operands = far(proj, cot, short)
        results = [full(BF16, 152, chunk), full(BF16, 160, chunk)]
        scratch = [
            vmem(BF16, 2, some, chunk), vmem(BF16, 2, some, chunk), vmem(BF16, 3, 16, chunk), vmem(F32, 3, FK, chunk),
            vmem(BF16, 8 * (15 + FK), some), vmem(BF16, 8 * (16 + FK), some), vmem(F32, 8 * (15 + FK), width),
            vmem(F32, 8 * (15 + FK), width), vmem(F32, 8 * (16 + FK), width), vmem(F32, 8 * 17, width), semaphores,
        ]
        if k == 0:
            operands += far(filter_taps)
            results.append((pltpu.HBM((ranks, rows, channels), BF16), FAR))
            scratch = [vmem(F32, rows, channels), vmem(BF16, ranks, rows, channels)] + scratch
        elif k == CHUNKS - 1:
            operands += far(decay)
            results.append((pltpu.HBM((count, channels), F32), IN_VMEM))
            scratch = [vmem(F32, 1, channels)] + scratch
        forward, backward, *spread = call(
            functools.partial(edges_kernel, k * chunk), "edges", operands, results, cost=10 if k else 1,
            scratch_shapes=scratch,
        )
        if k == CHUNKS - 1:
            falloff = spread[0]
        if k == 0:
            taps = lax.all_to_all(spread[0], "seq", 0, 0).reshape(count, channels)
        else:
            backward, prev[-1], later[-1] = lax.optimization_barrier((backward, prev[-1], later[-1]))
        later.append(from_behind(backward, "seq", -1))
        prev.append(from_behind(forward, "seq", 1))

    high, low = analysis(own, size)
    k_high, k_low = analysis(np.arange(count), size)
    constants = [
        np.concatenate([high, low], axis=1),
        analysis(np.concatenate([interleaved(16, -128), after]), size, 8)[0],
        analysis(interleaved(17, length), size, 8)[0],
        np.concatenate([k_high, k_low], axis=1),
        np.concatenate(list(synthesis(np.concatenate([own, after]), size)), axis=1),
        synthesis(np.arange(count), size)[0],
        pick(interleaved(span, 0, 1 - FK), length),
    ]
    constants = [(jnp.asarray(constant), whole(constant)) for constant in constants]
    held = ()
    for k in range(CHUNKS):
        first, wide = k * blocks // PAIR, PAIR * width
        results = [
            pltpu.HBM((CHUNKS * blocks, length, width), BF16),
            pltpu.HBM((CHUNKS * blocks, 3, span + FK - 1, 8, width), F32),
        ]
        held = call(
            functools.partial(operator_kernel, k * blocks), "operator",
            [
                (proj, columns((3, length), wide, first)), (cot, columns((length,), wide, first)),
                (prev[k], columns((152,), wide)), (later[k], columns((160,), wide)),
                (short, columns((3, FK), wide, first)), (taps, columns((count,), wide, first)),
                (falloff, columns((count,), wide, first)),
            ] + constants,
            [(result, one_of(result, first, PAIR)) for result in results]
            + [(pltpu.HBM((ranks, CHUNKS * blocks * slot + SHORT, width), BF16), FAR)],
            cost=12,
            held=held,
            free=(2, 3, 5),
            grid=(blocks // PAIR,),
            scratch_shapes=[
                vmem(F32, PAIR, 3, span + FK - 1, 8, width), vmem(F32, PAIR, 3, span, 8, width),
                vmem(F32, PAIR, span, 8, width), vmem(BF16, PAIR, ranks, slot, width),
                vmem(BF16, PAIR, ranks * width // channels, SHORT, width), pltpu.SemaphoreType.DMA((2 * PAIR,)),
            ],
        )
    product, grad, sums = held
    p_out = jnp.asarray(pick(own, length).T)
    gated, grad_proj = call(
        outputs_kernel, "outputs",
        [(product, one_of(product)), (grad, one_of(grad)), (short, columns((3, FK), width)), (p_out, whole(p_out))],
        [
            (jax.ShapeDtypeStruct((length, channels), BF16), columns((length,), width)),
            (jax.ShapeDtypeStruct((3, length, channels), BF16), columns((3, length), width)),
        ],
        cost=8,
        grid=(CHUNKS * blocks,),
    )
    sums, gated, grad_proj = lax.optimization_barrier((lax.all_to_all(sums, "seq", 0, 0), gated, grad_proj))

    vmem = pl.BlockSpec(memory_space=pltpu.VMEM)
    raw, payload = pl.pallas_call(
        functools.partial(squares_kernel, rows, share),
        in_specs=[vmem],
        out_specs=[vmem] * 2,
        out_shape=[
            jax.ShapeDtypeStruct((rows, channels), F32),
            jax.ShapeDtypeStruct((ranks * groups, 24, width), BF16),
        ],
        compiler_params=pltpu.CompilerParams(vmem_limit_bytes=32 << 20),
        name="squares",
    )(sums)
    gathered = lax.all_to_all(payload, ("seq", "ch"), 0, 0)
    mine = jnp.stack([lax.axis_index("ch"), jnp.int32(groups)])
    entries = (rows * ranks + 3 * FK) * channels * groups
    grad_short, grad_filter = pl.pallas_call(
        functools.partial(scale_kernel, entries, share),
        in_specs=[pl.BlockSpec(memory_space=pltpu.SMEM), vmem, vmem],
        out_specs=[vmem] * 2,
        out_shape=[
            jax.ShapeDtypeStruct((3, FK, channels), F32),
            jax.ShapeDtypeStruct((rows, channels), F32),
        ],
        compiler_params=pltpu.CompilerParams(vmem_limit_bytes=32 << 20),
        name="scale",
    )(mine, raw, gathered)
    return (gated, jnp.transpose(grad_proj, (1, 0, 2)), grad_short, grad_filter)


def solution(mesh):
    placed = (P("seq", None, "ch"), P(None, None, "ch"), P("seq", "ch"), P("ch"), P("seq", "ch"))
    return jax.shard_map(
        shards,
        mesh=mesh,
        in_specs=placed,
        out_specs=(P("seq", "ch"), P("seq", None, "ch"), P(None, None, "ch"), P("seq", "ch")),
        check_vma=False,
    )
```
